32 devices in a mesh: gx: 8 (over z, x), gy: 4 (over y, core).
Axes of the slice: x: 2, y: 2, z: 4, core: 2. Of those that a mesh axis runs over, the one named last changes fastest.
Arguments:
- field: bfloat16 [20, 16, 16, 512], P(None, 'gx', 'gy'), may hold values from -6 to 6
- cotangent: bfloat16 [20, 16, 16, 512], P(None, 'gx', 'gy'), may hold values from -6 to 6
- spectral_weight: float32 [64, 2, 20, 20, 16, 16], P('gx', None, None, None, 'gy'), may hold values from -3 to 3
- pointwise_weight: bfloat16 [20, 20], replicated, may hold values from -1.25 to 1.25
- channel_bias: float32 [20], replicated, may hold values from -3 to 3
Outputs:
- layer_out: bfloat16 [20, 16, 16, 512], P(None, 'gx', 'gy')
- grad_field: bfloat16 [20, 16, 16, 512], P(None, 'gx', 'gy')
- grad_spectral: float32 [64, 2, 20, 20, 16, 16], P('gx', None, None, None, 'gy')
The draws below stay inside these ranges and needn't reach their ends.
All inputs are finite; a program needn't handle non-finite values.
Results may differ from the reference program's by a relative error of at most 0.0061.
Values sent between devices are 32-bit elements; how exact they have to be, the bound alone decides.
No kernel may reach another device: no remote copies, remote signals or barrier semaphores. Data moves between devices by JAX's collectives and lax.ppermute only.
A program may use at most 128 MiB of HBM per device.

```python
import math
import jax
import jax.numpy as jnp
from jax import lax

W = 20
KX = 16
KY = 16
KZ = 16
KT = 4
NZ = 32
NT = 16
MZT = 64
NX = 16
NY = 16


def steps_of(key, shape, pieces, low, largest):
    def one(axis_at, blocks):
        heights = jax.random.uniform(jax.random.fold_in(jax.random.fold_in(key, 6), axis_at), (blocks,), jnp.float32, low / len(pieces), largest / len(pieces))
        return jnp.repeat(jnp.exp(heights), shape[axis_at] // blocks).reshape((-1,) + (1,) * (len(shape) - axis_at - 1))

    loudness = one(*pieces[0])
    for cut in pieces[1:]:
        loudness = loudness * one(*cut)
    return loudness


def noise(rng, dims, width, bound, shards=(), kind=jnp.bfloat16):
    drawn = width * jax.random.normal(rng, dims, jnp.float32)
    if shards:
        drawn = drawn * steps_of(rng, dims, shards, -0.22, 0.18)
    return jnp.clip(drawn, -bound, bound).astype(kind)


def setup_inputs(seed: int = 0) -> dict:
    key_of = jax.random.split(jax.random.key(seed), 6)
    field = noise(key_of[0], (W, NX, NY, NZ * NT), 1.0, 6.0, ((1, 8), (2, 4)))
    cotangent = noise(key_of[1], (W, NX, NY, NZ * NT), 1.0, 6.0, ((1, 8), (2, 4)))
    spectral_weight = noise(key_of[2], (MZT, 2, W, W, KX, KY), 0.5, 3.0, ((0, 8), (4, 4)), jnp.float32)
    pointwise_weight = noise(key_of[3], (W, W), W ** -0.5, 1.25)
    channel_bias = noise(key_of[4], (W,), 0.5, 3.0, (), jnp.float32)
    return {"field": field, "cotangent": cotangent, "spectral_weight": spectral_weight, "pointwise_weight": pointwise_weight, "channel_bias": channel_bias}


HIGHEST_PRECISION = lax.Precision.HIGHEST

def rotation(length, kept_modes, phase_sign, cell_count, offset):
    position = offset + jnp.arange(cell_count, dtype=jnp.int32)
    mode_index = jnp.arange(kept_modes, dtype=jnp.int32)
    frequency = jnp.where(mode_index < kept_modes // 2, mode_index, mode_index - kept_modes)
    phase_int = jnp.mod(position[:, None] * frequency[None, :], length)
    angles = phase_int.astype(jnp.float32) * (phase_sign * 2.0 * math.pi / length)
    factor = 1.0 / math.sqrt(length)
    cosine = jnp.cos(angles) * factor
    sine_part = jnp.sin(angles) * factor
    return jnp.stack([jnp.stack([cosine, sine_part]), jnp.stack([-sine_part, cosine])])

def depth_time_table(depth_cells, time_cells, modes_depth, modes_time):
    depth_pos = jnp.arange(depth_cells, dtype=jnp.int32)
    time_pos = jnp.arange(time_cells, dtype=jnp.int32)
    depth_index = jnp.arange(modes_depth, dtype=jnp.int32)
    depth_freq = jnp.where(depth_index < modes_depth // 2, depth_index, depth_index - modes_depth)
    time_freq = jnp.arange(modes_time, dtype=jnp.int32)
    total_cells = depth_cells * time_cells
    phase_int = depth_pos[:, None, None, None] * depth_freq[None, None, :, None] * time_cells + time_pos[None, :, None, None] * time_freq[None, None, None, :] * depth_cells
    phase_int = jnp.mod(phase_int, total_cells).reshape(total_cells, modes_depth * modes_time)
    angles = phase_int.astype(jnp.float32) * (2.0 * math.pi / total_cells)
    factor = 1.0 / math.sqrt(total_cells)
    return jnp.stack([jnp.cos(angles) * factor, -jnp.sin(angles) * factor], axis=1)

def mode_weight(first_mode, mode_count, modes_time):
    mode_ids = first_mode + jnp.arange(mode_count, dtype=jnp.int32)
    weights = jnp.where(jnp.mod(mode_ids, modes_time) == 0, 1.0, 2.0).astype(jnp.float32)
    return weights.reshape(mode_count, 1, 1, 1, 1)

def mix_pair(left_part, right_part):
    return jnp.einsum('mwkj,mwokj->mokj', left_part, right_part, precision=HIGHEST_PRECISION)

def adjoint_pair(left_part, right_part):
    return jnp.einsum('mwokj,mokj->mwkj', left_part, right_part, precision=HIGHEST_PRECISION)

def complex_mix(spectra, weights):
    real_in, imag_in = (spectra[:, 0], spectra[:, 1])
    real_w, imag_w = (weights[:, 0], weights[:, 1])
    real_out = mix_pair(real_in, real_w) - mix_pair(imag_in, imag_w)
    imag_out = mix_pair(real_in, imag_w) + mix_pair(imag_in, real_w)
    return jnp.stack([real_out, imag_out], axis=1)

def adjoint_mix(weights, spectra):
    real_w, imag_w = (weights[:, 0], weights[:, 1])
    real_in, imag_in = (spectra[:, 0], spectra[:, 1])
    real_out = adjoint_pair(real_w, real_in) + adjoint_pair(imag_w, imag_in)
    imag_out = adjoint_pair(real_w, imag_in) - adjoint_pair(imag_w, real_in)
    return jnp.stack([real_out, imag_out], axis=1)

def weight_grad(inputs, outputs):
    real_in = inputs[:, 0][:, :, None]
    imag_in = inputs[:, 1][:, :, None]
    real_out = outputs[:, 0][:, None]
    imag_out = outputs[:, 1][:, None]
    real_part = real_in * real_out + imag_in * imag_out
    imag_part = real_in * imag_out - imag_in * real_out
    return jnp.stack([real_part, imag_part], axis=1)

def forward_spectrum(values, table_half):
    first_section = jnp.einsum('wxyq,qsm->mswyx', values, table_half, preferred_element_type=jnp.float32)
    table_first = rotation(NX, KX, -1.0, NX, 0)
    second_section = jnp.einsum('mswyx,srxk->mrwky', first_section, table_first, precision=HIGHEST_PRECISION)
    table_second = rotation(NY, KY, -1.0, NY, 0)
    return jnp.einsum('mswky,sryj->mrwkj', second_section, table_second, precision=HIGHEST_PRECISION)

def inverse_modes(spectra):
    table_second = rotation(NY, KY, 1.0, NY, 0)
    first_section = jnp.einsum('msokj,sryj->mroky', spectra, table_second, precision=HIGHEST_PRECISION)
    table_first = rotation(NX, KX, 1.0, NX, 0)
    return jnp.einsum('msoky,srxk->mroyx', first_section, table_first, precision=HIGHEST_PRECISION)

def reference(field, cotangent, spectral_weight, pointwise_weight, channel_bias):
    table_float = depth_time_table(NZ, NT, KZ, KT)
    table_half = table_float.astype(jnp.bfloat16)
    weights_modes = mode_weight(0, KZ * KT, KT)
    spectra = forward_spectrum(field, table_half)
    mixed_modes = complex_mix(spectra, spectral_weight) * weights_modes
    inverse = inverse_modes(mixed_modes)

    def channel_out(inputs):
        channel_modes, column, offset_value, channel_cot = inputs
        spatial = jnp.einsum('msyx,qsm->xyq', channel_modes, table_float, precision=HIGHEST_PRECISION)
        local_term = jnp.einsum('w,wxyq->xyq', column, field, preferred_element_type=jnp.float32)
        pre_act = spatial + local_term + offset_value
        activated, pullback = jax.vjp(jax.nn.gelu, pre_act)
        scaled = pullback(channel_cot.astype(jnp.float32))[0]
        return (activated.astype(jnp.bfloat16), scaled.astype(jnp.bfloat16))
    layer_out, signal = lax.map(channel_out, (jnp.moveaxis(inverse, 2, 0), pointwise_weight.T, channel_bias, cotangent))
    back_spectra = forward_spectrum(signal, table_half) * weights_modes
    grad_spectral = weight_grad(spectra, back_spectra)
    back_inverse = inverse_modes(adjoint_mix(spectral_weight, back_spectra))

    def channel_in(inputs):
        channel_modes, row_weights = inputs
        spatial = jnp.einsum('msyx,qsm->xyq', channel_modes, table_float, precision=HIGHEST_PRECISION)
        local_term = jnp.einsum('o,oxyq->xyq', row_weights, signal, preferred_element_type=jnp.float32)
        return (spatial + local_term).astype(jnp.bfloat16)
    grad_field = lax.map(channel_in, (jnp.moveaxis(back_inverse, 2, 0), pointwise_weight))
    return (layer_out, grad_field, grad_spectral)
```

```python
import math

import jax
import jax.numpy as jnp
import ml_dtypes
import numpy as np
from jax import lax
from jax.experimental import pallas as pl
from jax.experimental.pallas import tpu as pltpu
from jax.sharding import PartitionSpec as P

KZ = 16
KT = 4
NT = 16
LANES = 128
EXACT = lax.Precision.HIGHEST
F32 = jnp.float32
BF16 = jnp.bfloat16


def round_up(value, step):
    return -(-value // step) * step


def frequencies(kept):
    index = np.arange(kept)
    return np.where(index < kept // 2, index, index - kept)


def depth_time_table(cells):
    depth_cells = cells // NT
    depth = np.arange(depth_cells)[:, None, None, None] * frequencies(KZ)[None, None, :, None] * NT
    time = np.arange(NT)[None, :, None, None] * np.arange(KT)[None, None, None, :] * depth_cells
    phase = np.mod(depth + time, cells).reshape(cells, KZ * KT)
    angles = phase.astype(np.float32) * np.float32(2.0 * math.pi / cells)
    factor = np.float32(1.0 / math.sqrt(cells))
    return np.stack([np.cos(angles) * factor, -np.sin(angles) * factor], axis=1).astype(np.float32)


def plane_table(nx, ny, cells_x, cells_y, kept_x, kept_y, half):
    length_x, length_y = nx * cells_x, ny * cells_y
    phase_x = np.arange(length_x)[:, None] * frequencies(kept_x)[None, :]
    phase_y = np.arange(length_y)[:, None] * frequencies(kept_y)[None, :]
    angle = (
        np.mod(phase_x, length_x)[:, None, :, None] / length_x
        + np.mod(phase_y, length_y)[None, :, None, :] / length_y
    )
    factor = 1.0 / math.sqrt(length_x * length_y)
    cosine = np.cos(2.0 * math.pi * angle) * factor
    sine = np.sin(2.0 * math.pi * angle) * factor
    table = np.stack([np.stack([cosine, -sine]), np.stack([sine, cosine])])
    local = kept_x // ny
    table = table.reshape(2, 2, nx, cells_x, ny // 2, 2, cells_y, ny, local * kept_y)
    table = table.transpose(7, 5, 2, 4, 3, 6, 0, 1, 8)
    padded = np.zeros(table.shape[:-1] + (half,), np.float32)
    padded[..., : local * kept_y] = table
    out = np.stack([padded[j][[j % 2, 1 - j % 2]] for j in range(ny)])
    return out.reshape(ny, nx * cells_x * ny * cells_y, 4 * half)


class Sizes:
    def __init__(self, field, weight):
        self.nx, self.ny = lax.axis_size("gx"), lax.axis_size("gy")
        self.channels, self.cells_x, self.cells_y, self.depth = field.shape
        self.modes = weight.shape[0]
        self.local_x, self.kept_y = weight.shape[4:]
        self.kept_x = self.local_x * self.ny
        self.cells = self.cells_x * self.cells_y
        self.chips = self.nx * self.ny // 2
        self.kept = self.local_x * self.kept_y
        self.half = round_up(self.kept, LANES // 2)
        self.flat = 2 * self.channels * self.modes
        self.width = round_up(self.flat, LANES)
        self.all_modes = 2 * self.modes * self.nx
        self.rows = round_up(self.channels, 8)


def gather_cells(source, scratch, sizes):
    for w in range(sizes.channels):
        for x in range(sizes.cells_x):
            first = (w * sizes.cells_x + x) * sizes.cells_y
            scratch[first : first + sizes.cells_y, :] = source[w, x].astype(F32)
    return scratch[...]


def scatter_cells(values, target, sizes):
    for w in range(sizes.channels):
        for x in range(sizes.cells_x):
            first = (w * sizes.cells_x + x) * sizes.cells_y
            target[w, x] = values[first : first + sizes.cells_y, :].astype(target.dtype)


def lane_group(sizes):
    return lax.broadcasted_iota(jnp.int32, (sizes.cells, LANES), 1) // sizes.modes


def send_modes(values, target, sizes):
    group = lane_group(sizes)
    tiles = [values[w * sizes.cells : (w + 1) * sizes.cells, :] for w in range(sizes.channels)]
    for i in range(sizes.nx):
        out = [jnp.zeros((sizes.cells, LANES), F32) for _ in range(sizes.width // LANES)]
        for s in range(2):
            have = (i * 2 + s) * sizes.modes
            for w in range(sizes.channels):
                tile, want = divmod((s * sizes.channels + w) * sizes.modes, LANES)
                moved = tiles[w]
                if want != have:
                    moved = pltpu.roll(moved, (want - have) % LANES, 1)
                out[tile] = jnp.where(group == want // sizes.modes, moved, out[tile])
        for t, value in enumerate(out):
            for y in range(sizes.ny // 2):
                target[i * (sizes.ny // 2) + y, :, t * LANES : (t + 1) * LANES] = value


def receive_modes(source, scratch, sizes):
    group = lane_group(sizes)
    tiles = []
    for i in range(sizes.nx):
        row = []
        for t in range(sizes.width // LANES):
            value = None
            for y in range(sizes.ny // 2):
                part = source[i * (sizes.ny // 2) + y, :, t * LANES : (t + 1) * LANES]
                value = part if value is None else value + part
            row.append(value)
        tiles.append(row)
    for w in range(sizes.channels):
        out = jnp.zeros((sizes.cells, LANES), F32)
        for i in range(sizes.nx):
            for s in range(2):
                want = (i * 2 + s) * sizes.modes
                tile, have = divmod((s * sizes.channels + w) * sizes.modes, LANES)
                moved = tiles[i][tile]
                if want != have:
                    moved = pltpu.roll(moved, (want - have) % LANES, 1)
                out = jnp.where(group == want // sizes.modes, moved, out)
        scratch[w * sizes.cells : (w + 1) * sizes.cells, :] = out
    return scratch[...]


def dot(left, right, **kwargs):
    return jnp.dot(left, right, preferred_element_type=F32, **kwargs)


def depth_forward(sizes, field, table, out, cells):
    values = gather_cells(field, cells, sizes).astype(BF16)
    send_modes(dot(values, table[...]), out, sizes)


def turn_weights(sizes, source, target):
    pad = jnp.zeros((sizes.rows - sizes.channels, 2 * sizes.half), F32) if sizes.rows > sizes.channels else None
    for w in range(sizes.channels):
        if sizes.half > sizes.kept:
            target[0, w] = jnp.zeros((sizes.rows, 2 * sizes.half), F32)
        elif pad is not None:
            target[0, w, sizes.channels :, :] = pad
        if sizes.half == sizes.kept:
            block = jnp.concatenate([source[0, s, w].reshape(sizes.kept, sizes.channels) for s in range(2)], 0)
            target[0, w, : sizes.channels, :] = block.T
        else:
            for s in range(2):
                block = source[0, s, w].reshape(sizes.kept, sizes.channels).T
                target[0, w, : sizes.channels, s * sizes.half : s * sizes.half + sizes.kept] = block


def plane_spectra(sizes, own, other, table, target):
    received = jnp.concatenate(
        [ref[...].reshape(sizes.chips * sizes.cells, sizes.width) for ref in (own, other)], 0
    )
    both = dot(received.T, table[...], precision=EXACT)
    count = sizes.channels * sizes.modes
    target[:count, :] = both[:count, : 2 * sizes.half] + both[count : 2 * count, 2 * sizes.half :]


def plane_cells(sizes, mixed, spread, table, own, other):
    rows, lanes = mixed.shape
    spread[...] = jnp.zeros_like(spread)
    for s in range(2):
        spread[s * rows : (s + 1) * rows, s * lanes : (s + 1) * lanes] = mixed[...]
    cells = lax.dot_general(
        table[...], spread[...], (((1,), (1,)), ((), ())), precision=EXACT, preferred_element_type=F32
    )
    count = sizes.chips * sizes.cells
    for at, ref in enumerate((own, other)):
        ref[...] = cells[at * count : (at + 1) * count, :].reshape(ref.shape)


def swap_parts(values, sizes):
    return pltpu.roll(values, sizes.half, 1)


def mode_rows(first, sizes):
    return pl.ds(first, sizes.channels, stride=sizes.modes)


def first_lanes(rows, sizes):
    return lax.broadcasted_iota(jnp.int32, (rows, 2 * sizes.half), 1) < sizes.half


def mix_forward(sizes, own, other, table, weight, spectra, out_own, out_other, mixed, spread):
    plane_spectra(sizes, own, other, table, spectra)
    real = first_lanes(sizes.rows, sizes)
    for m in range(sizes.modes):
        straight = jnp.zeros((sizes.rows, 2 * sizes.half), F32)
        crossed = jnp.zeros((sizes.rows, 2 * sizes.half), F32)
        for w in range(sizes.channels):
            row = spectra[w * sizes.modes + m : w * sizes.modes + m + 1, :]
            block = weight[m, w]
            straight = straight + row * block
            crossed = crossed + swap_parts(row, sizes) * block
        real_part = straight - swap_parts(straight, sizes)
        imag_part = crossed + swap_parts(crossed, sizes)
        result = jnp.where(real, real_part, imag_part)
        mixed[mode_rows(m, sizes), :] = result[: sizes.channels]
    plane_cells(sizes, mixed, spread, table, out_own, out_other)


def mix_back(sizes, own, other, table, weight, back, out_own, out_other, mixed, spread, spectra):
    plane_spectra(sizes, own, other, table, spectra)
    real = first_lanes(sizes.channels, sizes)
    for m in range(sizes.modes):
        rows = spectra[mode_rows(m, sizes), :]
        if sizes.rows > sizes.channels:
            rows = jnp.concatenate([rows, jnp.zeros((sizes.rows - sizes.channels, 2 * sizes.half), F32)], 0)
        back[m] = rows
        turned = swap_parts(rows, sizes)
        straight, crossed = [], []
        for w in range(sizes.channels):
            block = weight[m, w]
            straight.append(jnp.sum(block * rows, axis=0, keepdims=True))
            crossed.append(jnp.sum(block * turned, axis=0, keepdims=True))
        straight = jnp.concatenate(straight, 0)
        crossed = jnp.concatenate(crossed, 0)
        real_part = straight + swap_parts(straight, sizes)
        imag_part = swap_parts(crossed, sizes) - crossed
        mixed[mode_rows(m, sizes), :] = jnp.where(real, real_part, imag_part)
    plane_cells(sizes, mixed, spread, table, out_own, out_other)


def grad_weights(sizes, spectra, back, target):
    mode = pl.program_id(0)
    rows = back[0]
    turned = swap_parts(rows, sizes)
    real = first_lanes(1, sizes)
    for w in range(sizes.channels):
        row = spectra[pl.ds(w * sizes.modes + mode, 1), :]
        swapped = swap_parts(row, sizes)
        real_part = jnp.where(real, row, swapped)
        imag_part = jnp.where(real, swapped, -row)
        block = (real_part * rows + imag_part * turned)[: sizes.channels]
        for s in range(2):
            part = block[:, s * sizes.half : s * sizes.half + sizes.kept].T
            target[0, s, w] = part.reshape(sizes.local_x, sizes.kept_y, sizes.channels)


def activate(sizes, received, field, cotangent, inverse, forward, mixer, bias, layer_out, signal_out, out, cells, spectrum):
    spatial = dot(receive_modes(received, spectrum, sizes), inverse[...], precision=EXACT)
    values = gather_cells(field, cells, sizes).astype(BF16)
    pre = spatial + dot(mixer[...], values) + bias[...]
    slope = math.sqrt(2.0 / math.pi)
    squared = pre * pre
    bend = jnp.tanh(slope * (pre + 0.044715 * (squared * pre)))
    scatter_cells(0.5 * pre * (1.0 + bend), layer_out, sizes)
    derivative = 0.5 * (1.0 + bend) + 0.5 * pre * (1.0 - bend * bend) * (slope * (1.0 + 3.0 * 0.044715 * squared))
    signal = (gather_cells(cotangent, cells, sizes) * derivative).astype(BF16)
    signal_out[...] = signal
    send_modes(dot(signal, forward[...]), out, sizes)


def finish(sizes, received, signal, inverse, mixer, grad_field, spectrum):
    spatial = dot(receive_modes(received, spectrum, sizes), inverse[...], precision=EXACT)
    scatter_cells(spatial + dot(mixer[...], signal[...]), grad_field, sizes)


def shape_of(shape, dtype=F32):
    return jax.ShapeDtypeStruct(shape, dtype)


def whole_call(body, sizes, out_shape, scratch, *args):
    def kernel(*refs):
        body(sizes, *refs)

    vmem = pl.BlockSpec(memory_space=pltpu.VMEM)
    return pl.pallas_call(
        kernel,
        out_shape=out_shape,
        in_specs=[vmem] * len(args),
        out_specs=jax.tree.map(lambda _: vmem, out_shape),
        scratch_shapes=scratch,
        name=body.__name__,
        compiler_params=pltpu.CompilerParams(vmem_limit_bytes=32 * 1024 * 1024),
    )(*args)


def on_device(field, cotangent, spectral_weight, pointwise_weight, channel_bias):
    z = Sizes(field, spectral_weight)
    depth_table = depth_time_table(z.depth)
    modes = depth_table.shape[2]
    kappa = np.where(np.arange(modes) % KT == 0, 1.0, 2.0).astype(np.float32)
    ordered = depth_table.reshape(z.depth, 2, z.nx, z.modes).transpose(0, 2, 1, 3).reshape(z.depth, z.all_modes)
    doubled = np.repeat(kappa.reshape(z.nx, 1, z.modes), 2, axis=1).reshape(z.all_modes)
    forward_first = jnp.asarray(ordered.astype(ml_dtypes.bfloat16))
    forward_back = jnp.asarray((ordered.astype(ml_dtypes.bfloat16).astype(np.float32) * doubled).astype(ml_dtypes.bfloat16))
    inverse_back = jnp.asarray(np.ascontiguousarray(ordered.T))
    inverse_first = jnp.asarray(np.ascontiguousarray((ordered * doubled).T))
    tables = jnp.asarray(plane_table(z.nx, z.ny, z.cells_x, z.cells_y, z.kept_x, z.kept_y, z.half))
    plane = lax.dynamic_index_in_dim(tables, lax.axis_index("gy"), 0, keepdims=False)

    groups = [[gx * z.ny + 2 * y + c for gx in range(z.nx) for y in range(z.ny // 2)] for c in range(2)]
    pairs = [(s, s ^ 1) for s in range(z.ny)]

    def exchange(payload):
        return lax.all_to_all(
            payload, ("gx", "gy"), split_axis=0, concat_axis=0, tiled=True, axis_index_groups=groups
        )

    def other_core(payload):
        return lax.ppermute(payload, "gy", pairs)

    payload = shape_of((z.chips, z.cells, z.width))
    cell_rows = z.channels * z.cells
    cells_scratch = pltpu.VMEM((cell_rows, z.depth), F32)
    spectrum_scratch = pltpu.VMEM((cell_rows, z.all_modes), F32)
    mode_rows_count = z.channels * z.modes
    spectra_shape = (mode_rows_count, 2 * z.half)
    mixed_scratch = [pltpu.VMEM(spectra_shape, F32), pltpu.VMEM((z.width, 4 * z.half), F32)]

    native = jnp.transpose(spectral_weight, (0, 1, 2, 4, 5, 3))
    block_in = (1, 2, z.channels, z.local_x, z.kept_y, z.channels)
    block_turned = (1, z.channels, z.rows, 2 * z.half)
    turned = pl.pallas_call(
        lambda source, target: turn_weights(z, source, target),
        grid=(z.modes,),
        out_shape=shape_of((z.modes,) + block_turned[1:]),
        in_specs=[pl.BlockSpec(block_in, lambda m: (m, 0, 0, 0, 0, 0))],
        out_specs=pl.BlockSpec(block_turned, lambda m: (m, 0, 0, 0)),
        name="turn_weights",
        compiler_params=pltpu.CompilerParams(vmem_limit_bytes=32 * 1024 * 1024),
    )(native)

    identity = jnp.eye(z.cells, dtype=BF16)
    mixer_back = jnp.kron(pointwise_weight, identity)
    mixer_first = jnp.kron(pointwise_weight.T, identity)
    bias = jnp.repeat(channel_bias, z.cells)[:, None]

    sent = whole_call(depth_forward, z, payload, [cells_scratch], field, forward_first)
    own = exchange(sent)
    spectra, part_own, part_other = whole_call(
        mix_forward, z, (shape_of(spectra_shape), payload, payload), mixed_scratch,
        own, other_core(own), plane, turned,
    )
    returned = exchange(part_own + other_core(part_other))
    layer_out, signal, sent = whole_call(
        activate, z,
        (shape_of(field.shape, BF16), shape_of((cell_rows, z.depth), BF16), payload),
        [cells_scratch, spectrum_scratch],
        returned, field, cotangent, inverse_first, forward_back, mixer_first, bias,
    )
    own = exchange(sent)
    back, part_own, part_other = whole_call(
        mix_back, z, (shape_of((z.modes, z.rows, 2 * z.half)), payload, payload),
        mixed_scratch + [pltpu.VMEM(spectra_shape, F32)],
        own, other_core(own), plane, turned,
    )
    returned = exchange(part_own + other_core(part_other))
    gradient = pl.pallas_call(
        lambda spectra_ref, back_ref, target: grad_weights(z, spectra_ref, back_ref, target),
        grid=(z.modes,),
        out_shape=shape_of(native.shape),
        in_specs=[
            pl.BlockSpec(spectra_shape, lambda m: (0, 0)),
            pl.BlockSpec((1, z.rows, 2 * z.half), lambda m: (m, 0, 0)),
        ],
        out_specs=pl.BlockSpec(block_in, lambda m: (m, 0, 0, 0, 0, 0)),
        name="grad_weights",
        compiler_params=pltpu.CompilerParams(vmem_limit_bytes=32 * 1024 * 1024),
    )(spectra, back)
    grad_field = whole_call(
        finish, z, shape_of(field.shape, BF16), [spectrum_scratch], returned, signal, inverse_back, mixer_back
    )
    return (layer_out, grad_field, jnp.transpose(gradient, (0, 1, 2, 5, 3, 4)))


def solution(mesh):
    return jax.shard_map(
        on_device,
        mesh=mesh,
        in_specs=(
            P(None, "gx", "gy", None),
            P(None, "gx", "gy", None),
            P("gx", None, None, None, "gy", None),
            P(),
            P(),
        ),
        out_specs=(
            P(None, "gx", "gy", None),
            P(None, "gx", "gy", None),
            P("gx", None, None, None, "gy", None),
        ),
        check_vma=False,
    )
```

```python
import math

import jax
import jax.numpy as jnp
import ml_dtypes
import numpy as np
from jax import lax
from jax.experimental import pallas as pl
from jax.experimental.pallas import tpu as pltpu
from jax.sharding import PartitionSpec as P

KZ = 16
KT = 4
NT = 16
LANES = 128
EXACT = lax.Precision.HIGHEST
F32 = jnp.float32
BF16 = jnp.bfloat16


def round_up(value, step):
    return -(-value // step) * step


def frequencies(kept):
    index = np.arange(kept)
    return np.where(index < kept // 2, index, index - kept)


def depth_time_table(cells):
    depth_cells = cells // NT
    depth = np.arange(depth_cells)[:, None, None, None] * frequencies(KZ)[None, None, :, None] * NT
    time = np.arange(NT)[None, :, None, None] * np.arange(KT)[None, None, None, :] * depth_cells
    phase = np.mod(depth + time, cells).reshape(cells, KZ * KT)
    angles = phase.astype(np.float32) * np.float32(2.0 * math.pi / cells)
    factor = np.float32(1.0 / math.sqrt(cells))
    return np.stack([np.cos(angles) * factor, -np.sin(angles) * factor], axis=1).astype(np.float32)


def plane_table(sizes, place, cores, owners):
    shape = (cores * sizes.chips * sizes.cells, owners * 4 * sizes.half)
    row = lax.broadcasted_iota(jnp.int32, shape, 0)
    lane = lax.broadcasted_iota(jnp.int32, shape, 1)
    chip = row // sizes.cells % sizes.chips
    core = (place + row // (sizes.cells * sizes.chips)) % 2
    x = chip // (sizes.ny // 2) * sizes.cells_x + row // sizes.cells_y % sizes.cells_x
    y = (chip % (sizes.ny // 2) * 2 + core) * sizes.cells_y + row % sizes.cells_y
    mode = lane % sizes.half
    quarter = lane // sizes.half % 2 - lane // (2 * sizes.half) % 2
    owner = place // 2 * 2 + (place + lane // (4 * sizes.half)) % 2
    kx = owner * sizes.local_x + mode // sizes.kept_y
    ky = mode % sizes.kept_y
    kx = jnp.where(kx < sizes.kept_x // 2, kx, kx - sizes.kept_x)
    ky = jnp.where(ky < sizes.kept_y // 2, ky, ky - sizes.kept_y)
    length_x, length_y = sizes.nx * sizes.cells_x, sizes.ny * sizes.cells_y
    turn = math.lcm(length_x, length_y, 4)
    phase = jnp.mod(x * kx * (turn // length_x) + y * ky * (turn // length_y) + quarter * (turn // 4), turn)
    values = jnp.cos(phase.astype(F32) * (2.0 * math.pi / turn)) * (1.0 / math.sqrt(length_x * length_y))
    return jnp.where(mode < sizes.kept, values, 0.0)


class Sizes:
    def __init__(self, field, weight):
        self.nx, self.ny = lax.axis_size("gx"), lax.axis_size("gy")
        self.channels, self.cells_x, self.cells_y, self.depth = field.shape
        self.modes = weight.shape[0]
        self.local_x, self.kept_y = weight.shape[4:]
        self.kept_x = self.local_x * self.ny
        self.cells = self.cells_x * self.cells_y
        self.chips = self.nx * self.ny // 2
        self.kept = self.local_x * self.kept_y
        self.half = round_up(self.kept, LANES // 2)
        self.flat = 2 * self.channels * self.modes
        self.width = round_up(self.flat, LANES)
        self.all_modes = 2 * self.modes * self.nx
        self.rows = round_up(self.channels, 8)


def gather_cells(source, scratch, sizes):
    for w in range(sizes.channels):
        for x in range(sizes.cells_x):
            first = (w * sizes.cells_x + x) * sizes.cells_y
            scratch[first : first + sizes.cells_y, :] = source[w, x].astype(F32)
    return scratch[...]


def scatter_cells(values, target, sizes):
    for w in range(sizes.channels):
        for x in range(sizes.cells_x):
            first = (w * sizes.cells_x + x) * sizes.cells_y
            target[w, x] = values[first : first + sizes.cells_y, :].astype(target.dtype)


def lane_group(sizes):
    return lax.broadcasted_iota(jnp.int32, (sizes.cells, LANES), 1) // sizes.modes


def send_modes(values, target, sizes):
    group = lane_group(sizes)
    tiles = [values[w * sizes.cells : (w + 1) * sizes.cells, :] for w in range(sizes.channels)]
    for i in range(sizes.nx):
        out = [jnp.zeros((sizes.cells, LANES), F32) for _ in range(sizes.width // LANES)]
        for s in range(2):
            have = (i * 2 + s) * sizes.modes
            for w in range(sizes.channels):
                tile, want = divmod((s * sizes.channels + w) * sizes.modes, LANES)
                moved = tiles[w]
                if want != have:
                    moved = pltpu.roll(moved, (want - have) % LANES, 1)
                out[tile] = jnp.where(group == want // sizes.modes, moved, out[tile])
        for t, value in enumerate(out):
            for y in range(sizes.ny // 2):
                target[i * (sizes.ny // 2) + y, :, t * LANES : (t + 1) * LANES] = value


def receive_modes(source, scratch, sizes):
    group = lane_group(sizes)
    tiles = []
    for i in range(sizes.nx):
        row = []
        for t in range(sizes.width // LANES):
            value = None
            for y in range(sizes.ny // 2):
                part = source[i * (sizes.ny // 2) + y, :, t * LANES : (t + 1) * LANES]
                value = part if value is None else value + part
            row.append(value)
        tiles.append(row)
    for w in range(sizes.channels):
        out = jnp.zeros((sizes.cells, LANES), F32)
        for i in range(sizes.nx):
            for s in range(2):
                want = (i * 2 + s) * sizes.modes
                tile, have = divmod((s * sizes.channels + w) * sizes.modes, LANES)
                moved = tiles[i][tile]
                if want != have:
                    moved = pltpu.roll(moved, (want - have) % LANES, 1)
                out = jnp.where(group == want // sizes.modes, moved, out)
        scratch[w * sizes.cells : (w + 1) * sizes.cells, :] = out
    return scratch[...]


def dot(left, right, **kwargs):
    return jnp.dot(left, right, preferred_element_type=F32, **kwargs)


def fetch(sources, targets, semaphores):
    copies = [pltpu.make_async_copy(*pair, semaphores.at[at]) for at, pair in enumerate(zip(sources, targets))]
    for copy in copies:
        copy.start()
    for copy in copies:
        copy.wait()


def depth_forward(sizes, field, table, out, cells, field_here, table_here, semaphores):
    fetch((field, table), (field_here, table_here), semaphores)
    values = gather_cells(field_here, cells, sizes).astype(BF16)
    send_modes(dot(values, table_here[...]), out, sizes)


def one_hot(rows, columns, step, along_rows):
    row = lax.broadcasted_iota(jnp.int32, (rows, columns), 0)
    column = lax.broadcasted_iota(jnp.int32, (rows, columns), 1)
    same = row // step == column if along_rows else row == column // step
    return jnp.where(same, 1.0, 0.0).astype(BF16)


def cell_mixer(weights, sizes):
    count = sizes.channels * sizes.cells
    left = one_hot(count, sizes.channels, sizes.cells, True)
    right = one_hot(sizes.channels, count, sizes.cells, False)
    wide = dot(dot(left, weights).astype(BF16), right)
    row = lax.broadcasted_iota(jnp.int32, (count, count), 0)
    column = lax.broadcasted_iota(jnp.int32, (count, count), 1)
    same = lax.rem(row, sizes.cells) == lax.rem(column, sizes.cells)
    return jnp.where(same, wide, 0.0).astype(BF16)


def prepare(sizes, field, cotangent, turned_weight, bias, inverse, forward, local, cot_cells, inverse_out, forward_out, cells, field_here, cot_here, semaphores):
    fetch((field, cotangent, inverse, forward), (field_here, cot_here, inverse_out, forward_out), semaphores)
    values = gather_cells(field_here, cells, sizes).astype(BF16)
    bypass = dot(cell_mixer(turned_weight[...], sizes), values)
    for o in range(sizes.channels):
        rows = slice(o * sizes.cells, (o + 1) * sizes.cells)
        local[rows, :] = bypass[rows, :] + bias[o]
    gather_cells(cot_here, cot_cells, sizes)


def emit(sizes, pre, signal, weight, layer_out, local):
    scatter_cells(gelu_parts(pre[...])[0], layer_out, sizes)
    local[...] = dot(cell_mixer(weight[...], sizes), signal[...])


def turn_weights(sizes, source, target):
    pad = jnp.zeros((sizes.rows - sizes.channels, 2 * sizes.half), F32) if sizes.rows > sizes.channels else None
    for w in range(sizes.channels):
        if sizes.half > sizes.kept:
            target[0, w] = jnp.zeros((sizes.rows, 2 * sizes.half), F32)
        elif pad is not None:
            target[0, w, sizes.channels :, :] = pad
        if sizes.half == sizes.kept:
            block = jnp.concatenate([source[0, s, w].reshape(sizes.kept, sizes.channels) for s in range(2)], 0)
            target[0, w, : sizes.channels, :] = block.T
        else:
            for s in range(2):
                block = source[0, s, w].reshape(sizes.kept, sizes.channels).T
                target[0, w, : sizes.channels, s * sizes.half : s * sizes.half + sizes.kept] = block


def plane_spectra(sizes, own, other, table, target):
    received = jnp.concatenate(
        [ref[...].reshape(sizes.chips * sizes.cells, sizes.width) for ref in (own, other)], 0
    )
    both = dot(received.T, table[...], precision=EXACT)
    count = sizes.channels * sizes.modes
    target[:count, :] = both[:count, : 2 * sizes.half] + both[count : 2 * count, 2 * sizes.half :]


def plane_cells(sizes, own, other, table, out, spread):
    rows, lanes = own.shape
    spread[...] = jnp.zeros_like(spread)
    for at, ref in enumerate((own, other)):
        for s in range(2):
            first = (at * 2 + s) * lanes
            spread[s * rows : (s + 1) * rows, first : first + lanes] = ref[...]
    cells = lax.dot_general(
        table[...], spread[...], (((1,), (1,)), ((), ())), precision=EXACT, preferred_element_type=F32
    )
    out[...] = cells.reshape(out.shape)


def swap_parts(values, sizes):
    return pltpu.roll(values, sizes.half, 1)


def mode_rows(first, sizes):
    return pl.ds(first, sizes.channels, stride=sizes.modes)


def first_lanes(rows, sizes):
    return lax.broadcasted_iota(jnp.int32, (rows, 2 * sizes.half), 1) < sizes.half


def mix_forward(sizes, own, other, table, weight, spectra, mixed):
    plane_spectra(sizes, own, other, table, spectra)
    real = first_lanes(sizes.rows, sizes)
    for m in range(sizes.modes):
        straight = jnp.zeros((sizes.rows, 2 * sizes.half), F32)
        crossed = jnp.zeros((sizes.rows, 2 * sizes.half), F32)
        for w in range(sizes.channels):
            row = spectra[w * sizes.modes + m : w * sizes.modes + m + 1, :]
            block = weight[m, w]
            straight = straight + row * block
            crossed = crossed + swap_parts(row, sizes) * block
        real_part = straight - swap_parts(straight, sizes)
        imag_part = crossed + swap_parts(crossed, sizes)
        result = jnp.where(real, real_part, imag_part)
        mixed[mode_rows(m, sizes), :] = result[: sizes.channels]


def mix_back(sizes, own, other, table, weight, back, mixed, spectra):
    plane_spectra(sizes, own, other, table, spectra)
    real = first_lanes(sizes.channels, sizes)
    for m in range(sizes.modes):
        rows = spectra[mode_rows(m, sizes), :]
        if sizes.rows > sizes.channels:
            rows = jnp.concatenate([rows, jnp.zeros((sizes.rows - sizes.channels, 2 * sizes.half), F32)], 0)
        back[m] = rows
        turned = swap_parts(rows, sizes)
        straight, crossed = [], []
        for w in range(sizes.channels):
            block = weight[m, w]
            straight.append(jnp.sum(block * rows, axis=0, keepdims=True))
            crossed.append(jnp.sum(block * turned, axis=0, keepdims=True))
        straight = jnp.concatenate(straight, 0)
        crossed = jnp.concatenate(crossed, 0)
        real_part = straight + swap_parts(straight, sizes)
        imag_part = swap_parts(crossed, sizes) - crossed
        mixed[mode_rows(m, sizes), :] = jnp.where(real, real_part, imag_part)


def grad_weights(sizes, spectra, back, target):
    mode = pl.program_id(0)
    rows = back[0]
    turned = swap_parts(rows, sizes)
    real = first_lanes(1, sizes)
    for w in range(sizes.channels):
        row = spectra[pl.ds(w * sizes.modes + mode, 1), :]
        swapped = swap_parts(row, sizes)
        real_part = jnp.where(real, row, swapped)
        imag_part = jnp.where(real, swapped, -row)
        block = (real_part * rows + imag_part * turned).T
        for s in range(2):
            part = block[s * sizes.half : s * sizes.half + sizes.kept, : sizes.channels]
            target[0, s, w] = part.reshape(sizes.local_x, sizes.kept_y, sizes.channels)


def gelu_parts(pre):
    slope = math.sqrt(2.0 / math.pi)
    squared = pre * pre
    bend = jnp.tanh(slope * (pre + 0.044715 * (squared * pre)))
    value = 0.5 * pre * (1.0 + bend)
    derivative = 0.5 * (1.0 + bend) + 0.5 * pre * (1.0 - bend * bend) * (slope * (1.0 + 3.0 * 0.044715 * squared))
    return value, derivative


def activate(sizes, received, local, cotangent, inverse, forward, pre_out, signal_out, out, spectrum):
    pre = dot(receive_modes(received, spectrum, sizes), inverse[...], precision=EXACT) + local[...]
    pre_out[...] = pre
    signal = (cotangent[...] * gelu_parts(pre)[1]).astype(BF16)
    signal_out[...] = signal
    send_modes(dot(signal, forward[...]), out, sizes)


def finish(sizes, received, local, inverse, grad_field, spectrum):
    spatial = dot(receive_modes(received, spectrum, sizes), inverse[...], precision=EXACT)
    scatter_cells(spatial + local[...], grad_field, sizes)


def shape_of(shape, dtype=F32):
    return jax.ShapeDtypeStruct(shape, dtype)


VMEM = pl.BlockSpec(memory_space=pltpu.VMEM)
SMEM = pl.BlockSpec(memory_space=pltpu.SMEM)
REMOTE = pl.BlockSpec(memory_space=pl.ANY)


def settings(mebibytes):
    return pltpu.CompilerParams(vmem_limit_bytes=mebibytes * 1024 * 1024)


def cost(nanoseconds):
    return pl.CostEstimate(flops=0, bytes_accessed=3000 * nanoseconds, transcendentals=0)


def whole_call(body, sizes, nanoseconds, out_shape, scratch, *args, specs=None):
    def kernel(*refs):
        body(sizes, *refs)

    return pl.pallas_call(
        kernel,
        out_shape=out_shape,
        in_specs=specs or [VMEM] * len(args),
        out_specs=jax.tree.map(lambda _: VMEM, out_shape),
        scratch_shapes=scratch,
        name=body.__name__,
        cost_estimate=cost(nanoseconds),
        compiler_params=settings(16),
    )(*args)


def on_device(field, cotangent, spectral_weight, pointwise_weight, channel_bias):
    z = Sizes(field, spectral_weight)
    depth_table = depth_time_table(z.depth)
    modes = depth_table.shape[2]
    kappa = np.where(np.arange(modes) % KT == 0, 1.0, 2.0).astype(np.float32)
    ordered = depth_table.reshape(z.depth, 2, z.nx, z.modes).transpose(0, 2, 1, 3).reshape(z.depth, z.all_modes)
    doubled = np.repeat(kappa.reshape(z.nx, 1, z.modes), 2, axis=1).reshape(z.all_modes)
    forward_first = jnp.asarray(ordered.astype(ml_dtypes.bfloat16))
    forward_back = jnp.asarray((ordered.astype(ml_dtypes.bfloat16).astype(np.float32) * doubled).astype(ml_dtypes.bfloat16))
    inverse_back = jnp.asarray(np.ascontiguousarray(ordered.T))
    inverse_first = jnp.asarray(np.ascontiguousarray((ordered * doubled).T))
    groups = [[gx * z.ny + 2 * y + c for gx in range(z.nx) for y in range(z.ny // 2)] for c in range(2)]
    pairs = [(s, s ^ 1) for s in range(z.ny)]

    def exchange(payload):
        return lax.all_to_all(
            payload, ("gx", "gy"), split_axis=0, concat_axis=0, tiled=True, axis_index_groups=groups
        )

    def other_core(payload):
        return lax.ppermute(payload, "gy", pairs)

    payload = shape_of((z.chips, z.cells, z.width))
    cell_rows = z.channels * z.cells
    cells_shape = (cell_rows, z.depth)
    cells_scratch = pltpu.VMEM(cells_shape, F32)
    spectrum_scratch = pltpu.VMEM((cell_rows, z.all_modes), F32)
    spectra_shape = (z.channels * z.modes, 2 * z.half)
    spectra_scratch = pltpu.VMEM(spectra_shape, F32)
    spread_scratch = pltpu.VMEM((z.width, 8 * z.half), F32)
    field_scratch = pltpu.VMEM(field.shape, BF16)

    sent = whole_call(
        depth_forward, z, 1500, payload,
        [cells_scratch, field_scratch, pltpu.VMEM(forward_first.shape, BF16), pltpu.SemaphoreType.DMA((2,))],
        field, forward_first, specs=[REMOTE] * 2,
    )

    sent, field, cotangent, spectral_weight, place = lax.optimization_barrier(
        (sent, field, cotangent, spectral_weight, lax.axis_index("gy"))
    )
    own = exchange(sent)
    native = jnp.transpose(spectral_weight, (0, 1, 2, 4, 5, 3))
    block_in = (1, 2, z.channels, z.local_x, z.kept_y, z.channels)
    block_turned = (1, z.channels, z.rows, 2 * z.half)
    turned = pl.pallas_call(
        lambda source, target: turn_weights(z, source, target),
        grid=(z.modes,),
        out_shape=shape_of((z.modes,) + block_turned[1:]),
        in_specs=[pl.BlockSpec(block_in, lambda m: (m, 0, 0, 0, 0, 0))],
        out_specs=pl.BlockSpec(block_turned, lambda m: (m, 0, 0, 0)),
        name="turn_weights",
        cost_estimate=cost(5000),
        compiler_params=settings(56),
    )(native)
    local, cot_cells, inverse_here, forward_here = whole_call(
        prepare, z, 2000,
        (shape_of(cells_shape), shape_of(cells_shape), shape_of(inverse_first.shape), shape_of(forward_back.shape, BF16)),
        [cells_scratch, field_scratch, field_scratch, pltpu.SemaphoreType.DMA((4,))],
        field, cotangent, pointwise_weight.T, channel_bias, inverse_first, forward_back,
        specs=[REMOTE, REMOTE, VMEM, SMEM, REMOTE, REMOTE],
    )
    plane = plane_table(z, place, 2, 1)
    plane_back = plane_table(z, place, 1, 2)
    own, turned, local, cot_cells, inverse_here, forward_here, plane, plane_back = lax.optimization_barrier(
        (own, turned, local, cot_cells, inverse_here, forward_here, plane, plane_back)
    )

    spectra, mixed = whole_call(
        mix_forward, z, 2000, (shape_of(spectra_shape), shape_of(spectra_shape)), [],
        own, other_core(own), plane, turned,
    )
    sent = whole_call(plane_cells, z, 1000, payload, [spread_scratch], mixed, other_core(mixed), plane_back)
    returned = exchange(sent)
    pre, signal, sent = whole_call(
        activate, z, 2000,
        (shape_of(cells_shape), shape_of(cells_shape, BF16), payload), [spectrum_scratch],
        returned, local, cot_cells, inverse_here, forward_here,
    )
    sent, pre, signal = lax.optimization_barrier((sent, pre, signal))
    own = exchange(sent)
    layer_out, local = whole_call(
        emit, z, 2000, (shape_of(field.shape, BF16), shape_of(cells_shape)), [], pre, signal, pointwise_weight
    )
    own, layer_out, local = lax.optimization_barrier((own, layer_out, local))
    back, mixed = whole_call(
        mix_back, z, 2000, (shape_of((z.modes, z.rows, 2 * z.half)), shape_of(spectra_shape)), [spectra_scratch],
        own, other_core(own), plane, turned,
    )
    sent = whole_call(plane_cells, z, 1000, payload, [spread_scratch], mixed, other_core(mixed), plane_back)
    sent, back, spectra = lax.optimization_barrier((sent, back, spectra))
    returned = exchange(sent)
    gradient = pl.pallas_call(
        lambda spectra_ref, back_ref, target: grad_weights(z, spectra_ref, back_ref, target),
        grid=(z.modes,),
        out_shape=shape_of(native.shape),
        in_specs=[
            pl.BlockSpec(spectra_shape, lambda m: (0, 0)),
            pl.BlockSpec((1, z.rows, 2 * z.half), lambda m: (m, 0, 0)),
        ],
        out_specs=pl.BlockSpec(block_in, lambda m: (m, 0, 0, 0, 0, 0)),
        name="grad_weights",
        cost_estimate=cost(5000),
        compiler_params=settings(56),
    )(spectra, back)
    returned, gradient = lax.optimization_barrier((returned, gradient))
    grad_field = whole_call(
        finish, z, 1000, shape_of(field.shape, BF16), [spectrum_scratch], returned, local, inverse_back
    )
    return (layer_out, grad_field, jnp.transpose(gradient, (0, 1, 2, 5, 3, 4)))


def solution(mesh):
    return jax.shard_map(
        on_device,
        mesh=mesh,
        in_specs=(
            P(None, "gx", "gy", None),
            P(None, "gx", "gy", None),
            P("gx", None, None, None, "gy", None),
            P(),
            P(),
        ),
        out_specs=(
            P(None, "gx", "gy", None),
            P(None, "gx", "gy", None),
            P("gx", None, None, None, "gy", None),
        ),
        check_vma=False,
    )
```

```python
import math

import jax
import jax.numpy as jnp
import ml_dtypes
import numpy as np
from jax import lax
from jax.experimental import pallas as pl
from jax.experimental.pallas import tpu as pltpu
from jax.sharding import PartitionSpec as P

KZ = 16
KT = 4
NT = 16
LANES = 128
EXACT = lax.Precision.HIGHEST
F32 = jnp.float32
BF16 = jnp.bfloat16


def round_up(value, step):
    return -(-value // step) * step


def frequencies(kept):
    index = np.arange(kept)
    return np.where(index < kept // 2, index, index - kept)


def depth_time_table(cells):
    depth_cells = cells // NT
    depth = np.arange(depth_cells)[:, None, None, None] * frequencies(KZ)[None, None, :, None] * NT
    time = np.arange(NT)[None, :, None, None] * np.arange(KT)[None, None, None, :] * depth_cells
    phase = np.mod(depth + time, cells).reshape(cells, KZ * KT)
    angles = phase.astype(np.float32) * np.float32(2.0 * math.pi / cells)
    factor = np.float32(1.0 / math.sqrt(cells))
    return np.stack([np.cos(angles) * factor, -np.sin(angles) * factor], axis=1).astype(np.float32)


def plane_table(sizes, place, cores, owners):
    shape = (cores * sizes.chips * sizes.cells, owners * 4 * sizes.half)
    row = lax.broadcasted_iota(jnp.int32, shape, 0)
    lane = lax.broadcasted_iota(jnp.int32, shape, 1)
    chip = row // sizes.cells % sizes.chips
    core = (place + row // (sizes.cells * sizes.chips)) % 2
    x = chip // (sizes.ny // 2) * sizes.cells_x + row // sizes.cells_y % sizes.cells_x
    y = (chip % (sizes.ny // 2) * 2 + core) * sizes.cells_y + row % sizes.cells_y
    mode = lane % sizes.half
    quarter = lane // sizes.half % 2 - lane // (2 * sizes.half) % 2
    owner = place // 2 * 2 + (place + lane // (4 * sizes.half)) % 2
    kx = owner * sizes.local_x + mode // sizes.kept_y
    ky = mode % sizes.kept_y
    kx = jnp.where(kx < sizes.kept_x // 2, kx, kx - sizes.kept_x)
    ky = jnp.where(ky < sizes.kept_y // 2, ky, ky - sizes.kept_y)
    length_x, length_y = sizes.nx * sizes.cells_x, sizes.ny * sizes.cells_y
    turn = math.lcm(length_x, length_y, 4)
    phase = jnp.mod(x * kx * (turn // length_x) + y * ky * (turn // length_y) + quarter * (turn // 4), turn)
    values = jnp.cos(phase.astype(F32) * (2.0 * math.pi / turn)) * (1.0 / math.sqrt(length_x * length_y))
    return jnp.where(mode < sizes.kept, values, 0.0)


class Sizes:
    def __init__(self, field, weight):
        self.nx, self.ny = lax.axis_size("gx"), lax.axis_size("gy")
        self.channels, self.cells_x, self.cells_y, self.depth = field.shape
        self.modes = weight.shape[0]
        self.local_x, self.kept_y = weight.shape[4:]
        self.kept_x = self.local_x * self.ny
        self.cells = self.cells_x * self.cells_y
        self.chips = self.nx * self.ny // 2
        self.kept = self.local_x * self.kept_y
        self.half = round_up(self.kept, LANES // 2)
        self.flat = 2 * self.channels * self.modes
        self.width = round_up(self.flat, LANES)
        self.all_modes = 2 * self.modes * self.nx
        self.rows = round_up(self.channels, 8)


def gather_cells(source, scratch, sizes):
    for w in range(sizes.channels):
        for x in range(sizes.cells_x):
            first = (w * sizes.cells_x + x) * sizes.cells_y
            scratch[first : first + sizes.cells_y, :] = source[w, x].astype(F32)
    return scratch[...]


def scatter_cells(values, target, sizes):
    for w in range(sizes.channels):
        for x in range(sizes.cells_x):
            first = (w * sizes.cells_x + x) * sizes.cells_y
            target[w, x] = values[first : first + sizes.cells_y, :].astype(target.dtype)


def lane_group(sizes):
    return lax.broadcasted_iota(jnp.int32, (sizes.cells, LANES), 1) // sizes.modes


def send_modes(values, target, sizes):
    group = lane_group(sizes)
    tiles = [values[w * sizes.cells : (w + 1) * sizes.cells, :] for w in range(sizes.channels)]
    for i in range(sizes.nx):
        out = [jnp.zeros((sizes.cells, LANES), F32) for _ in range(sizes.width // LANES)]
        for s in range(2):
            have = (i * 2 + s) * sizes.modes
            for w in range(sizes.channels):
                tile, want = divmod((s * sizes.channels + w) * sizes.modes, LANES)
                moved = tiles[w]
                if want != have:
                    moved = pltpu.roll(moved, (want - have) % LANES, 1)
                out[tile] = jnp.where(group == want // sizes.modes, moved, out[tile])
        for t, value in enumerate(out):
            for y in range(sizes.ny // 2):
                target[i * (sizes.ny // 2) + y, :, t * LANES : (t + 1) * LANES] = value


def receive_modes(source, scratch, sizes):
    group = lane_group(sizes)
    tiles = []
    for i in range(sizes.nx):
        row = []
        for t in range(sizes.width // LANES):
            value = None
            for y in range(sizes.ny // 2):
                part = source[i * (sizes.ny // 2) + y, :, t * LANES : (t + 1) * LANES]
                value = part if value is None else value + part
            row.append(value)
        tiles.append(row)
    for w in range(sizes.channels):
        out = jnp.zeros((sizes.cells, LANES), F32)
        for i in range(sizes.nx):
            for s in range(2):
                want = (i * 2 + s) * sizes.modes
                tile, have = divmod((s * sizes.channels + w) * sizes.modes, LANES)
                moved = tiles[i][tile]
                if want != have:
                    moved = pltpu.roll(moved, (want - have) % LANES, 1)
                out = jnp.where(group == want // sizes.modes, moved, out)
        scratch[w * sizes.cells : (w + 1) * sizes.cells, :] = out
    return scratch[...]


def dot(left, right, **kwargs):
    return jnp.dot(left, right, preferred_element_type=F32, **kwargs)


def fetch(sources, targets, semaphores):
    copies = [pltpu.make_async_copy(*pair, semaphores.at[at]) for at, pair in enumerate(zip(sources, targets))]
    for copy in copies:
        copy.start()
    for copy in copies:
        copy.wait()


def depth_forward(sizes, field, table, out, cells, field_here, table_here, semaphores):
    fetch((field, table), (field_here, table_here), semaphores)
    values = gather_cells(field_here, cells, sizes).astype(BF16)
    send_modes(dot(values, table_here[...]), out, sizes)


def one_hot(rows, columns, step, along_rows):
    row = lax.broadcasted_iota(jnp.int32, (rows, columns), 0)
    column = lax.broadcasted_iota(jnp.int32, (rows, columns), 1)
    same = row // step == column if along_rows else row == column // step
    return jnp.where(same, 1.0, 0.0).astype(BF16)


def cell_mixer(weights, across, sizes):
    count = sizes.channels * sizes.cells
    left = one_hot(count, sizes.channels, sizes.cells, True)
    right = one_hot(sizes.channels, count, sizes.cells, False)
    tall = lax.dot_general(left, weights, (((1,), (1 if across else 0,)), ((), ())), preferred_element_type=F32)
    wide = dot(tall.astype(BF16), right)
    row = lax.broadcasted_iota(jnp.int32, (count, count), 0)
    column = lax.broadcasted_iota(jnp.int32, (count, count), 1)
    same = lax.rem(row, sizes.cells) == lax.rem(column, sizes.cells)
    return jnp.where(same, wide, 0.0).astype(BF16)


def prepare(sizes, field, cotangent, weight, bias, inverse, forward, local, cot_cells, inverse_out, forward_out, cells, field_here, cot_here, semaphores):
    fetch((field, cotangent, inverse, forward), (field_here, cot_here, inverse_out, forward_out), semaphores)
    values = gather_cells(field_here, cells, sizes).astype(BF16)
    bypass = dot(cell_mixer(weight[...], True, sizes), values)
    for o in range(sizes.channels):
        rows = slice(o * sizes.cells, (o + 1) * sizes.cells)
        local[rows, :] = bypass[rows, :] + bias[o]
    gather_cells(cot_here, cot_cells, sizes)


def emit(sizes, pre, signal, weight, layer_out, local):
    scatter_cells(gelu_parts(pre[...])[0], layer_out, sizes)
    local[...] = dot(cell_mixer(weight[...], False, sizes), signal[...])


def turn_weights(sizes, source, after, target, here, semaphores):
    del after
    copies = [pltpu.make_async_copy(source.at[at], here.at[at], semaphores.at[at]) for at in range(2 * sizes.modes)]
    for copy in copies:
        copy.start()
    if sizes.half > sizes.kept:
        target[...] = jnp.zeros_like(target)
    elif sizes.rows > sizes.channels:
        target[:, :, sizes.channels :, :] = jnp.zeros(
            (sizes.modes, sizes.channels, sizes.rows - sizes.channels, 2 * sizes.half), F32
        )

    def turn(mode, carry):
        for s in range(2):
            at = 2 * mode + s
            pltpu.make_async_copy(source.at[at], here.at[at], semaphores.at[at]).wait()
        for w in range(sizes.channels):
            blocks = [here[2 * mode + s, w].reshape(sizes.kept, sizes.channels) for s in range(2)]
            if sizes.half == sizes.kept:
                target[mode, w, : sizes.channels, :] = jnp.concatenate(blocks, 0).T
            else:
                for s, block in enumerate(blocks):
                    target[mode, w, : sizes.channels, s * sizes.half : s * sizes.half + sizes.kept] = block.T
        return carry

    lax.fori_loop(0, sizes.modes, turn, 0)


def plane_spectra(sizes, own, other, table, target):
    received = jnp.concatenate(
        [ref[...].reshape(sizes.chips * sizes.cells, sizes.width) for ref in (own, other)], 0
    )
    both = dot(received.T, table[...], precision=EXACT)
    count = sizes.channels * sizes.modes
    target[:count, :] = both[:count, : 2 * sizes.half] + both[count : 2 * count, 2 * sizes.half :]


def plane_cells(sizes, own, other, table, out, spread):
    rows, lanes = own.shape
    spread[...] = jnp.zeros_like(spread)
    for at, ref in enumerate((own, other)):
        for s in range(2):
            first = (at * 2 + s) * lanes
            spread[s * rows : (s + 1) * rows, first : first + lanes] = ref[...]
    cells = lax.dot_general(
        table[...], spread[...], (((1,), (1,)), ((), ())), precision=EXACT, preferred_element_type=F32
    )
    out[...] = cells.reshape(out.shape)


def swap_parts(values, sizes):
    return pltpu.roll(values, sizes.half, 1)


def mode_rows(first, sizes):
    return pl.ds(first, sizes.channels, stride=sizes.modes)


def first_lanes(rows, sizes):
    return lax.broadcasted_iota(jnp.int32, (rows, 2 * sizes.half), 1) < sizes.half


def mix_forward(sizes, own, other, table, weight, spectra, mixed):
    plane_spectra(sizes, own, other, table, spectra)
    real = first_lanes(sizes.rows, sizes)
    for m in range(sizes.modes):
        straight = jnp.zeros((sizes.rows, 2 * sizes.half), F32)
        crossed = jnp.zeros((sizes.rows, 2 * sizes.half), F32)
        for w in range(sizes.channels):
            row = spectra[w * sizes.modes + m : w * sizes.modes + m + 1, :]
            block = weight[m, w]
            straight = straight + row * block
            crossed = crossed + swap_parts(row, sizes) * block
        real_part = straight - swap_parts(straight, sizes)
        imag_part = crossed + swap_parts(crossed, sizes)
        result = jnp.where(real, real_part, imag_part)
        mixed[mode_rows(m, sizes), :] = result[: sizes.channels]


def mix_back(sizes, own, other, table, weight, back, mixed, spectra):
    plane_spectra(sizes, own, other, table, spectra)
    real = first_lanes(sizes.channels, sizes)
    for m in range(sizes.modes):
        rows = spectra[mode_rows(m, sizes), :]
        if sizes.rows > sizes.channels:
            rows = jnp.concatenate([rows, jnp.zeros((sizes.rows - sizes.channels, 2 * sizes.half), F32)], 0)
        back[m] = rows
        turned = swap_parts(rows, sizes)
        straight, crossed = [], []
        for w in range(sizes.channels):
            block = weight[m, w]
            straight.append(jnp.sum(block * rows, axis=0, keepdims=True))
            crossed.append(jnp.sum(block * turned, axis=0, keepdims=True))
        straight = jnp.concatenate(straight, 0)
        crossed = jnp.concatenate(crossed, 0)
        real_part = straight + swap_parts(straight, sizes)
        imag_part = swap_parts(crossed, sizes) - crossed
        mixed[mode_rows(m, sizes), :] = jnp.where(real, real_part, imag_part)


def grad_weights(sizes, spectra, back, target, here, semaphores):
    real = first_lanes(1, sizes)

    def copy(at):
        return pltpu.make_async_copy(here.at[at], target.at[at], semaphores.at[at])

    def one_mode(mode, carry):
        rows = back[mode]
        turned = swap_parts(rows, sizes)
        for w in range(sizes.channels):
            row = spectra[pl.ds(w * sizes.modes + mode, 1), :]
            swapped = swap_parts(row, sizes)
            real_part = jnp.where(real, row, swapped)
            imag_part = jnp.where(real, swapped, -row)
            block = (real_part * rows + imag_part * turned).T
            for s in range(2):
                part = block[s * sizes.half : s * sizes.half + sizes.kept, : sizes.channels]
                here[2 * mode + s, w] = part.reshape(sizes.local_x, sizes.kept_y, sizes.channels)
        for s in range(2):
            copy(2 * mode + s).start()
        return carry

    lax.fori_loop(0, sizes.modes, one_mode, 0)
    for at in range(2 * sizes.modes):
        copy(at).wait()


def gelu_parts(pre):
    slope = math.sqrt(2.0 / math.pi)
    squared = pre * pre
    bend = jnp.tanh(slope * (pre + 0.044715 * (squared * pre)))
    value = 0.5 * pre * (1.0 + bend)
    derivative = 0.5 * (1.0 + bend) + 0.5 * pre * (1.0 - bend * bend) * (slope * (1.0 + 3.0 * 0.044715 * squared))
    return value, derivative


def activate(sizes, received, local, cotangent, inverse, forward, pre_out, signal_out, out, spectrum):
    pre = dot(receive_modes(received, spectrum, sizes), inverse[...], precision=EXACT) + local[...]
    pre_out[...] = pre
    signal = (cotangent[...] * gelu_parts(pre)[1]).astype(BF16)
    signal_out[...] = signal
    send_modes(dot(signal, forward[...]), out, sizes)


def finish(sizes, received, local, inverse, grad_field, spectrum):
    spatial = dot(receive_modes(received, spectrum, sizes), inverse[...], precision=EXACT)
    scatter_cells(spatial + local[...], grad_field, sizes)


def shape_of(shape, dtype=F32):
    return jax.ShapeDtypeStruct(shape, dtype)


VMEM = pl.BlockSpec(memory_space=pltpu.VMEM)
SMEM = pl.BlockSpec(memory_space=pltpu.SMEM)
REMOTE = pl.BlockSpec(memory_space=pl.ANY)


def settings(mebibytes):
    return pltpu.CompilerParams(vmem_limit_bytes=mebibytes * 1024 * 1024)


def cost(nanoseconds):
    return pl.CostEstimate(flops=0, bytes_accessed=3000 * nanoseconds, transcendentals=0)


def whole_call(body, sizes, nanoseconds, out_shape, scratch, *args, specs=None, out_specs=None, room=16):
    def kernel(*refs):
        body(sizes, *refs)

    return pl.pallas_call(
        kernel,
        out_shape=out_shape,
        in_specs=specs or [VMEM] * len(args),
        out_specs=out_specs or jax.tree.map(lambda _: VMEM, out_shape),
        scratch_shapes=scratch,
        name=body.__name__,
        cost_estimate=cost(nanoseconds),
        compiler_params=settings(room),
    )(*args)


def on_device(field, cotangent, spectral_weight, pointwise_weight, channel_bias):
    z = Sizes(field, spectral_weight)
    depth_table = depth_time_table(z.depth)
    modes = depth_table.shape[2]
    kappa = np.where(np.arange(modes) % KT == 0, 1.0, 2.0).astype(np.float32)
    ordered = depth_table.reshape(z.depth, 2, z.nx, z.modes).transpose(0, 2, 1, 3).reshape(z.depth, z.all_modes)
    doubled = np.repeat(kappa.reshape(z.nx, 1, z.modes), 2, axis=1).reshape(z.all_modes)
    forward_first = jnp.asarray(ordered.astype(ml_dtypes.bfloat16))
    forward_back = jnp.asarray((ordered.astype(ml_dtypes.bfloat16).astype(np.float32) * doubled).astype(ml_dtypes.bfloat16))
    inverse_back = jnp.asarray(np.ascontiguousarray(ordered.T))
    inverse_first = jnp.asarray(np.ascontiguousarray((ordered * doubled).T))
    groups = [[gx * z.ny + 2 * y + c for gx in range(z.nx) for y in range(z.ny // 2)] for c in range(2)]
    pairs = [(s, s ^ 1) for s in range(z.ny)]

    def exchange(payload):
        return lax.all_to_all(
            payload, ("gx", "gy"), split_axis=0, concat_axis=0, tiled=True, axis_index_groups=groups
        )

    def other_core(payload):
        return lax.ppermute(payload, "gy", pairs)

    payload = shape_of((z.chips, z.cells, z.width))
    cell_rows = z.channels * z.cells
    cells_shape = (cell_rows, z.depth)
    cells_scratch = pltpu.VMEM(cells_shape, F32)
    spectrum_scratch = pltpu.VMEM((cell_rows, z.all_modes), F32)
    spectra_shape = (z.channels * z.modes, 2 * z.half)
    spectra_scratch = pltpu.VMEM(spectra_shape, F32)
    spread_scratch = pltpu.VMEM((z.width, 8 * z.half), F32)
    field_scratch = pltpu.VMEM(field.shape, BF16)

    native = jnp.transpose(spectral_weight, (0, 1, 2, 4, 5, 3))
    weight_shape = (2 * z.modes,) + native.shape[2:]
    weight_scratch = [pltpu.VMEM(weight_shape, F32), pltpu.SemaphoreType.DMA((2 * z.modes,))]

    sent = whole_call(
        depth_forward, z, 1500, payload,
        [cells_scratch, field_scratch, pltpu.VMEM(forward_first.shape, BF16), pltpu.SemaphoreType.DMA((2,))],
        field, forward_first, specs=[REMOTE] * 2, room=50,
    )
    own = exchange(sent)
    turned = whole_call(
        turn_weights, z, 5000, shape_of((z.modes, z.channels, z.rows, 2 * z.half)), weight_scratch,
        native.reshape(weight_shape), sent, specs=[REMOTE] * 2, room=50,
    )
    own, turned, place = lax.optimization_barrier((own, turned, lax.axis_index("gy")))

    plane = plane_table(z, place, 2, 1)
    spectra, mixed = whole_call(
        mix_forward, z, 2000, (shape_of(spectra_shape), shape_of(spectra_shape)), [],
        own, other_core(own), plane, turned,
    )
    mixed, spectra, place = lax.optimization_barrier((mixed, spectra, place))
    plane_back = plane_table(z, place, 1, 2)
    sent = whole_call(plane_cells, z, 1000, payload, [spread_scratch], mixed, other_core(mixed), plane_back)
    sent, field, cotangent = lax.optimization_barrier((sent, field, cotangent))
    returned = exchange(sent)
    local, cot_cells, inverse_here, forward_here = whole_call(
        prepare, z, 2000,
        (shape_of(cells_shape), shape_of(cells_shape), shape_of(inverse_first.shape), shape_of(forward_back.shape, BF16)),
        [cells_scratch, field_scratch, field_scratch, pltpu.SemaphoreType.DMA((4,))],
        field, cotangent, pointwise_weight, channel_bias, inverse_first, forward_back,
        specs=[REMOTE, REMOTE, VMEM, SMEM, REMOTE, REMOTE], room=50,
    )
    returned, local, cot_cells, inverse_here, forward_here = lax.optimization_barrier(
        (returned, local, cot_cells, inverse_here, forward_here)
    )
    pre, signal, sent = whole_call(
        activate, z, 2000,
        (shape_of(cells_shape), shape_of(cells_shape, BF16), payload), [spectrum_scratch],
        returned, local, cot_cells, inverse_here, forward_here,
    )
    sent, pre, signal = lax.optimization_barrier((sent, pre, signal))
    own = exchange(sent)
    layer_out, local = whole_call(
        emit, z, 2000, (shape_of(field.shape, BF16), shape_of(cells_shape)), [], pre, signal, pointwise_weight
    )
    own, layer_out, local = lax.optimization_barrier((own, layer_out, local))
    back, mixed = whole_call(
        mix_back, z, 2000, (shape_of((z.modes, z.rows, 2 * z.half)), shape_of(spectra_shape)), [spectra_scratch],
        own, other_core(own), plane, turned,
    )
    sent = whole_call(plane_cells, z, 1000, payload, [spread_scratch], mixed, other_core(mixed), plane_back)
    sent, back, spectra = lax.optimization_barrier((sent, back, spectra))
    returned = exchange(sent)
    gradient = whole_call(
        grad_weights, z, 5000, shape_of(weight_shape), weight_scratch, spectra, back, out_specs=REMOTE, room=50
    )
    returned, gradient = lax.optimization_barrier((returned, gradient))
    grad_field = whole_call(
        finish, z, 1000, shape_of(field.shape, BF16), [spectrum_scratch], returned, local, inverse_back
    )
    return (layer_out, grad_field, jnp.transpose(gradient.reshape(native.shape), (0, 1, 2, 5, 3, 4)))


def solution(mesh):
    return jax.shard_map(
        on_device,
        mesh=mesh,
        in_specs=(
            P(None, "gx", "gy", None),
            P(None, "gx", "gy", None),
            P("gx", None, None, None, "gy", None),
            P(),
            P(),
        ),
        out_specs=(
            P(None, "gx", "gy", None),
            P(None, "gx", "gy", None),
            P("gx", None, None, None, "gy", None),
        ),
        check_vma=False,
    )
```

```python
import math

import jax
import jax.numpy as jnp
import ml_dtypes
import numpy as np
from jax import lax
from jax.experimental import pallas as pl
from jax.experimental.pallas import tpu as pltpu
from jax.sharding import PartitionSpec as P

KZ = 16
KT = 4
NT = 16
LANES = 128
EXACT = lax.Precision.HIGHEST
F32 = jnp.float32
BF16 = jnp.bfloat16


def round_up(value, step):
    return -(-value // step) * step


def frequencies(kept):
    index = np.arange(kept)
    return np.where(index < kept // 2, index, index - kept)


def depth_time_table(cells):
    depth_cells = cells // NT
    depth = np.arange(depth_cells)[:, None, None, None] * frequencies(KZ)[None, None, :, None] * NT
    time = np.arange(NT)[None, :, None, None] * np.arange(KT)[None, None, None, :] * depth_cells
    phase = np.mod(depth + time, cells).reshape(cells, KZ * KT)
    angles = phase.astype(np.float32) * np.float32(2.0 * math.pi / cells)
    factor = np.float32(1.0 / math.sqrt(cells))
    return np.stack([np.cos(angles) * factor, -np.sin(angles) * factor], axis=1).astype(np.float32)


def plane_factors(sizes):
    length_x, length_y = sizes.nx * sizes.cells_x, sizes.ny * sizes.cells_y
    lane = np.arange(4 * sizes.half)
    mode = lane % sizes.half
    quarter = lane // sizes.half % 2 - lane // (2 * sizes.half)
    inside = mode < sizes.kept
    kx = np.arange(sizes.ny)[:, None] * sizes.local_x + np.where(inside, mode // sizes.kept_y, 0)
    turn_x = np.mod(np.arange(length_x)[:, None] * frequencies(sizes.kept_x)[kx][:, None, :], length_x) / length_x
    turn_y = np.mod(np.arange(length_y)[:, None] * frequencies(sizes.kept_y)[mode % sizes.kept_y], length_y) / length_y
    angle_x, angle_y = 2.0 * math.pi * turn_x, 2.0 * math.pi * (turn_y + quarter / 4.0)
    scale = inside / math.sqrt(length_x * length_y)
    factors_x = np.concatenate([np.cos(angle_x), -np.sin(angle_x)], -1)
    factors_y = np.concatenate([np.cos(angle_y) * scale, np.sin(angle_y) * scale], -1)
    return factors_x.astype(np.float32), factors_y.astype(np.float32)


class Sizes:
    def __init__(self, field, weight):
        self.nx, self.ny = lax.axis_size("gx"), lax.axis_size("gy")
        self.channels, self.cells_x, self.cells_y, self.depth = field.shape
        self.modes = weight.shape[0]
        self.local_x, self.kept_y = weight.shape[4:]
        self.kept_x = self.local_x * self.ny
        self.cells = self.cells_x * self.cells_y
        self.chips = self.nx * self.ny // 2
        self.kept = self.local_x * self.kept_y
        self.half = round_up(self.kept, LANES // 2)
        self.flat = 2 * self.channels * self.modes
        self.width = round_up(self.flat, LANES)
        self.all_modes = 2 * self.modes * self.nx
        self.rows = round_up(self.channels, 8)


def gather_cells(source, scratch, sizes):
    for w in range(sizes.channels):
        for x in range(sizes.cells_x):
            first = (w * sizes.cells_x + x) * sizes.cells_y
            scratch[first : first + sizes.cells_y, :] = source[w, x].astype(F32)
    return scratch[...]


def scatter_cells(values, target, sizes):
    for w in range(sizes.channels):
        for x in range(sizes.cells_x):
            first = (w * sizes.cells_x + x) * sizes.cells_y
            target[w, x] = values[first : first + sizes.cells_y, :].astype(target.dtype)


def lane_group(sizes):
    return lax.broadcasted_iota(jnp.int32, (sizes.cells, LANES), 1) // sizes.modes


def send_modes(values, target, sizes):
    group = lane_group(sizes)
    tiles = [values[w * sizes.cells : (w + 1) * sizes.cells, :] for w in range(sizes.channels)]
    for i in range(sizes.nx):
        out = [jnp.zeros((sizes.cells, LANES), F32) for _ in range(sizes.width // LANES)]
        for s in range(2):
            have = (i * 2 + s) * sizes.modes
            for w in range(sizes.channels):
                tile, want = divmod((s * sizes.channels + w) * sizes.modes, LANES)
                moved = tiles[w]
                if want != have:
                    moved = pltpu.roll(moved, (want - have) % LANES, 1)
                out[tile] = jnp.where(group == want // sizes.modes, moved, out[tile])
        for t, value in enumerate(out):
            for y in range(sizes.ny // 2):
                target[i * (sizes.ny // 2) + y, :, t * LANES : (t + 1) * LANES] = value


def receive_modes(source, scratch, sizes):
    group = lane_group(sizes)
    tiles = []
    for i in range(sizes.nx):
        row = []
        for t in range(sizes.width // LANES):
            value = None
            for y in range(sizes.ny // 2):
                part = source[i * (sizes.ny // 2) + y, :, t * LANES : (t + 1) * LANES]
                value = part if value is None else value + part
            row.append(value)
        tiles.append(row)
    for w in range(sizes.channels):
        out = jnp.zeros((sizes.cells, LANES), F32)
        for i in range(sizes.nx):
            for s in range(2):
                want = (i * 2 + s) * sizes.modes
                tile, have = divmod((s * sizes.channels + w) * sizes.modes, LANES)
                moved = tiles[i][tile]
                if want != have:
                    moved = pltpu.roll(moved, (want - have) % LANES, 1)
                out = jnp.where(group == want // sizes.modes, moved, out)
        scratch[w * sizes.cells : (w + 1) * sizes.cells, :] = out
    return scratch[...]


def dot(left, right, **kwargs):
    return jnp.dot(left, right, preferred_element_type=F32, **kwargs)


def fetch(sources, targets, semaphores):
    copies = [pltpu.make_async_copy(*pair, semaphores.at[at]) for at, pair in enumerate(zip(sources, targets))]
    for copy in copies:
        copy.start()
    for copy in copies:
        copy.wait()


def depth_forward(sizes, field, table, out, cells, field_here, table_here, semaphores):
    fetch((field, table), (field_here, table_here), semaphores)
    values = gather_cells(field_here, cells, sizes).astype(BF16)
    send_modes(dot(values, table_here[...]), out, sizes)


def one_hot(rows, columns, step, along_rows):
    row = lax.broadcasted_iota(jnp.int32, (rows, columns), 0)
    column = lax.broadcasted_iota(jnp.int32, (rows, columns), 1)
    same = row // step == column if along_rows else row == column // step
    return jnp.where(same, 1.0, 0.0).astype(BF16)


def cell_mixer(weights, across, sizes):
    count = sizes.channels * sizes.cells
    left = one_hot(count, sizes.channels, sizes.cells, True)
    right = one_hot(sizes.channels, count, sizes.cells, False)
    tall = lax.dot_general(left, weights, (((1,), (1 if across else 0,)), ((), ())), preferred_element_type=F32)
    wide = dot(tall.astype(BF16), right)
    row = lax.broadcasted_iota(jnp.int32, (count, count), 0)
    column = lax.broadcasted_iota(jnp.int32, (count, count), 1)
    same = lax.rem(row, sizes.cells) == lax.rem(column, sizes.cells)
    return jnp.where(same, wide, 0.0).astype(BF16)


def prepare(sizes, field, cotangent, weight, bias, inverse, forward, local, cot_cells, inverse_out, forward_out, cells, field_here, cot_here, semaphores):
    fetch((field, cotangent, inverse, forward), (field_here, cot_here, inverse_out, forward_out), semaphores)
    values = gather_cells(field_here, cells, sizes).astype(BF16)
    bypass = dot(cell_mixer(weight[...], True, sizes), values)
    for o in range(sizes.channels):
        rows = slice(o * sizes.cells, (o + 1) * sizes.cells)
        local[rows, :] = bypass[rows, :] + bias[o]
    gather_cells(cot_here, cot_cells, sizes)


def emit(sizes, pre, signal, weight, inverse, layer_out, local, inverse_out, semaphore):
    copy = pltpu.make_async_copy(inverse, inverse_out, semaphore.at[0])
    copy.start()
    scatter_cells(gelu_parts(pre[...])[0], layer_out, sizes)
    local[...] = dot(cell_mixer(weight[...], False, sizes), signal[...])
    copy.wait()


def plane_tables(sizes, place, mine, other, factors_y, table, back):
    half_rows = sizes.chips * sizes.cells
    lanes = 4 * sizes.half

    def chosen(rows, length, index):
        column = lax.broadcasted_iota(jnp.int32, (rows, length), 1)
        return jnp.where(column == index(lax.broadcasted_iota(jnp.int32, (rows, length), 0)), 1.0, 0.0)

    def at_x(row):
        chip = lax.rem(row // sizes.cells, sizes.chips)
        return chip // (sizes.ny // 2) * sizes.cells_x + lax.rem(row // sizes.cells_y, sizes.cells_x)

    def at_y(row):
        chip = lax.rem(row // sizes.cells, sizes.chips)
        core = lax.rem(place + row // half_rows, 2)
        return (lax.rem(chip, sizes.ny // 2) * 2 + core) * sizes.cells_y + lax.rem(row, sizes.cells_y)

    def product(left, right):
        return left[:, :lanes] * right[:, :lanes] + left[:, lanes:] * right[:, lanes:]

    pick_x = chosen(2 * half_rows, sizes.nx * sizes.cells_x, at_x)
    pick_y = chosen(2 * half_rows, sizes.ny * sizes.cells_y, at_y)
    spread_y = dot(pick_y, factors_y[...], precision=EXACT)
    table[...] = product(dot(pick_x, mine[...], precision=EXACT), spread_y)
    back[:, :lanes] = table[:half_rows, :]
    back[:, lanes:] = product(dot(pick_x[:half_rows], other[...], precision=EXACT), spread_y[:half_rows])


def turn_weights(sizes, source, after, place, factors_x, factors_y, target, table, back, here, mine, other, mine_y, semaphores, small):
    del after
    place = place[0]
    pair = place + 1 - 2 * lax.rem(place, 2)
    moves = ((factors_x.at[place], mine), (factors_x.at[pair], other), (factors_y, mine_y))
    tables = [pltpu.make_async_copy(*move, small.at[at]) for at, move in enumerate(moves)]
    copies = [pltpu.make_async_copy(source.at[at], here.at[at], semaphores.at[at]) for at in range(2 * sizes.modes)]
    for copy in tables + copies:
        copy.start()
    for copy in tables:
        copy.wait()
    plane_tables(sizes, place, mine, other, mine_y, table, back)
    if sizes.half > sizes.kept:
        target[...] = jnp.zeros_like(target)
    elif sizes.rows > sizes.channels:
        target[:, :, sizes.channels :, :] = jnp.zeros(
            (sizes.modes, sizes.channels, sizes.rows - sizes.channels, 2 * sizes.half), F32
        )

    def turn(mode, carry):
        for s in range(2):
            at = 2 * mode + s
            pltpu.make_async_copy(source.at[at], here.at[at], semaphores.at[at]).wait()
        for w in range(sizes.channels):
            blocks = [here[2 * mode + s, w].reshape(sizes.kept, sizes.channels) for s in range(2)]
            if sizes.half == sizes.kept:
                target[mode, w, : sizes.channels, :] = jnp.concatenate(blocks, 0).T
            else:
                for s, block in enumerate(blocks):
                    target[mode, w, : sizes.channels, s * sizes.half : s * sizes.half + sizes.kept] = block.T
        return carry

    lax.fori_loop(0, sizes.modes, turn, 0)


def plane_spectra(sizes, own, other, table, target):
    received = jnp.concatenate(
        [ref[...].reshape(sizes.chips * sizes.cells, sizes.width) for ref in (own, other)], 0
    )
    both = dot(received.T, table[...], precision=EXACT)
    count = sizes.channels * sizes.modes
    target[:count, :] = both[:count, : 2 * sizes.half] + both[count : 2 * count, 2 * sizes.half :]


def plane_cells(sizes, own, other, table, out, spread):
    rows, lanes = own.shape
    spread[...] = jnp.zeros_like(spread)
    for at, ref in enumerate((own, other)):
        for s in range(2):
            first = (at * 2 + s) * lanes
            spread[s * rows : (s + 1) * rows, first : first + lanes] = ref[...]
    cells = lax.dot_general(
        table[...], spread[...], (((1,), (1,)), ((), ())), precision=EXACT, preferred_element_type=F32
    )
    out[...] = cells.reshape(out.shape)


def swap_parts(values, sizes):
    return pltpu.roll(values, sizes.half, 1)


def mode_rows(first, sizes):
    return pl.ds(first, sizes.channels, stride=sizes.modes)


def first_lanes(rows, sizes):
    return lax.broadcasted_iota(jnp.int32, (rows, 2 * sizes.half), 1) < sizes.half


def mix_forward(sizes, own, other, table, weight, spectra, mixed):
    plane_spectra(sizes, own, other, table, spectra)
    real = first_lanes(sizes.rows, sizes)
    for m in range(sizes.modes):
        straight = jnp.zeros((sizes.rows, 2 * sizes.half), F32)
        crossed = jnp.zeros((sizes.rows, 2 * sizes.half), F32)
        for w in range(sizes.channels):
            row = spectra[w * sizes.modes + m : w * sizes.modes + m + 1, :]
            block = weight[m, w]
            straight = straight + row * block
            crossed = crossed + swap_parts(row, sizes) * block
        real_part = straight - swap_parts(straight, sizes)
        imag_part = crossed + swap_parts(crossed, sizes)
        result = jnp.where(real, real_part, imag_part)
        mixed[mode_rows(m, sizes), :] = result[: sizes.channels]


def mix_back(sizes, own, other, table, weight, back, mixed, spectra):
    plane_spectra(sizes, own, other, table, spectra)
    real = first_lanes(sizes.channels, sizes)
    for m in range(sizes.modes):
        rows = spectra[mode_rows(m, sizes), :]
        if sizes.rows > sizes.channels:
            rows = jnp.concatenate([rows, jnp.zeros((sizes.rows - sizes.channels, 2 * sizes.half), F32)], 0)
        back[m] = rows
        turned = swap_parts(rows, sizes)
        straight, crossed = [], []
        for w in range(sizes.channels):
            block = weight[m, w]
            straight.append(jnp.sum(block * rows, axis=0, keepdims=True))
            crossed.append(jnp.sum(block * turned, axis=0, keepdims=True))
        straight = jnp.concatenate(straight, 0)
        crossed = jnp.concatenate(crossed, 0)
        real_part = straight + swap_parts(straight, sizes)
        imag_part = swap_parts(crossed, sizes) - crossed
        mixed[mode_rows(m, sizes), :] = jnp.where(real, real_part, imag_part)


def grad_weights(sizes, spectra, back, target, here, semaphores):
    real = first_lanes(1, sizes)

    def copy(at):
        return pltpu.make_async_copy(here.at[at], target.at[at], semaphores.at[at])

    def one_mode(mode, carry):
        rows = back[mode]
        turned = swap_parts(rows, sizes)
        for w in range(sizes.channels):
            row = spectra[pl.ds(w * sizes.modes + mode, 1), :]
            swapped = swap_parts(row, sizes)
            real_part = jnp.where(real, row, swapped)
            imag_part = jnp.where(real, swapped, -row)
            block = (real_part * rows + imag_part * turned).T
            for s in range(2):
                part = block[s * sizes.half : s * sizes.half + sizes.kept, : sizes.channels]
                here[2 * mode + s, w] = part.reshape(sizes.local_x, sizes.kept_y, sizes.channels)
        for s in range(2):
            copy(2 * mode + s).start()
        return carry

    lax.fori_loop(0, sizes.modes, one_mode, 0)
    for at in range(2 * sizes.modes):
        copy(at).wait()


def gelu_parts(pre):
    slope = math.sqrt(2.0 / math.pi)
    squared = pre * pre
    bend = jnp.tanh(slope * (pre + 0.044715 * (squared * pre)))
    value = 0.5 * pre * (1.0 + bend)
    derivative = 0.5 * (1.0 + bend) + 0.5 * pre * (1.0 - bend * bend) * (slope * (1.0 + 3.0 * 0.044715 * squared))
    return value, derivative


def activate(sizes, received, local, cotangent, inverse, forward, pre_out, signal_out, out, spectrum):
    pre = dot(receive_modes(received, spectrum, sizes), inverse[...], precision=EXACT) + local[...]
    pre_out[...] = pre
    signal = (cotangent[...] * gelu_parts(pre)[1]).astype(BF16)
    signal_out[...] = signal
    send_modes(dot(signal, forward[...]), out, sizes)


def finish(sizes, received, local, inverse, grad_field, spectrum):
    spatial = dot(receive_modes(received, spectrum, sizes), inverse[...], precision=EXACT)
    scatter_cells(spatial + local[...], grad_field, sizes)


def shape_of(shape, dtype=F32):
    return jax.ShapeDtypeStruct(shape, dtype)


VMEM = pl.BlockSpec(memory_space=pltpu.VMEM)
SMEM = pl.BlockSpec(memory_space=pltpu.SMEM)
HBM = pl.BlockSpec(memory_space=pltpu.HBM)


def settings(mebibytes):
    return pltpu.CompilerParams(vmem_limit_bytes=mebibytes * 1024 * 1024)


def cost(nanoseconds):
    return pl.CostEstimate(flops=0, bytes_accessed=3000 * nanoseconds, transcendentals=0)


def whole_call(body, sizes, nanoseconds, out_shape, scratch, *args, specs=None, out_specs=None, room=16):
    def kernel(*refs):
        body(sizes, *refs)

    return pl.pallas_call(
        kernel,
        out_shape=out_shape,
        in_specs=specs or [VMEM] * len(args),
        out_specs=out_specs or jax.tree.map(lambda _: VMEM, out_shape),
        scratch_shapes=scratch,
        name=body.__name__,
        cost_estimate=cost(nanoseconds),
        compiler_params=settings(room),
    )(*args)


def on_device(field, cotangent, spectral_weight, pointwise_weight, channel_bias):
    z = Sizes(field, spectral_weight)
    depth_table = depth_time_table(z.depth)
    modes = depth_table.shape[2]
    kappa = np.where(np.arange(modes) % KT == 0, 1.0, 2.0).astype(np.float32)
    ordered = depth_table.reshape(z.depth, 2, z.nx, z.modes).transpose(0, 2, 1, 3).reshape(z.depth, z.all_modes)
    doubled = np.repeat(kappa.reshape(z.nx, 1, z.modes), 2, axis=1).reshape(z.all_modes)
    forward_first = jnp.asarray(ordered.astype(ml_dtypes.bfloat16))
    forward_back = jnp.asarray((ordered.astype(ml_dtypes.bfloat16).astype(np.float32) * doubled).astype(ml_dtypes.bfloat16))
    inverse_back = jnp.asarray(np.ascontiguousarray(ordered.T))
    inverse_first = jnp.asarray(np.ascontiguousarray((ordered * doubled).T))
    groups = [[gx * z.ny + 2 * y + c for gx in range(z.nx) for y in range(z.ny // 2)] for c in range(2)]
    pairs = [(s, s ^ 1) for s in range(z.ny)]

    def exchange(payload):
        return lax.all_to_all(
            payload, ("gx", "gy"), split_axis=0, concat_axis=0, tiled=True, axis_index_groups=groups
        )

    def other_core(payload):
        return lax.ppermute(payload, "gy", pairs)

    payload = shape_of((z.chips, z.cells, z.width))
    cell_rows = z.channels * z.cells
    cells_shape = (cell_rows, z.depth)
    cells_scratch = pltpu.VMEM(cells_shape, F32)
    spectrum_scratch = pltpu.VMEM((cell_rows, z.all_modes), F32)
    spectra_shape = (z.channels * z.modes, 2 * z.half)
    spectra_scratch = pltpu.VMEM(spectra_shape, F32)
    spread_scratch = pltpu.VMEM((z.width, 8 * z.half), F32)
    field_scratch = pltpu.VMEM(field.shape, BF16)

    native = jnp.transpose(spectral_weight, (0, 1, 2, 4, 5, 3))
    weight_shape = (2 * z.modes,) + native.shape[2:]
    weight_scratch = [pltpu.VMEM(weight_shape, F32), pltpu.SemaphoreType.DMA((2 * z.modes,))]

    factors_x, factors_y = plane_factors(z)
    half_rows = z.chips * z.cells

    sent = whole_call(
        depth_forward, z, 1500, payload,
        [cells_scratch, field_scratch, pltpu.VMEM(forward_first.shape, BF16), pltpu.SemaphoreType.DMA((2,))],
        field, forward_first, specs=[HBM] * 2,
    )
    own = exchange(sent)
    factor_scratch = pltpu.VMEM(factors_x.shape[1:], F32)
    turned, plane, plane_back = whole_call(
        turn_weights, z, 5000,
        (
            shape_of((z.modes, z.channels, z.rows, 2 * z.half)),
            shape_of((2 * half_rows, 4 * z.half)),
            shape_of((half_rows, 8 * z.half)),
        ),
        [
            weight_scratch[0], factor_scratch, factor_scratch, pltpu.VMEM(factors_y.shape, F32),
            weight_scratch[1], pltpu.SemaphoreType.DMA((3,)),
        ],
        native.reshape(weight_shape), sent, lax.axis_index("gy").reshape(1), jnp.asarray(factors_x), jnp.asarray(factors_y),
        specs=[HBM, HBM, SMEM, HBM, HBM], room=28,
    )
    own, turned, plane, plane_back, field, cotangent = lax.optimization_barrier(
        (own, turned, plane, plane_back, field, cotangent)
    )
    other = other_core(own)
    local, cot_cells, inverse_here, forward_here = whole_call(
        prepare, z, 1500,
        (shape_of(cells_shape), shape_of(cells_shape), shape_of(inverse_first.shape), shape_of(forward_back.shape, BF16)),
        [cells_scratch, field_scratch, field_scratch, pltpu.SemaphoreType.DMA((4,))],
        field, cotangent, pointwise_weight, channel_bias, inverse_first, forward_back,
        specs=[HBM, HBM, VMEM, SMEM, HBM, HBM],
    )
    other, local, cot_cells, inverse_here, forward_here = lax.optimization_barrier(
        (other, local, cot_cells, inverse_here, forward_here)
    )
    spectra, mixed = whole_call(
        mix_forward, z, 1000, (shape_of(spectra_shape), shape_of(spectra_shape)), [], own, other, plane, turned
    )
    sent = whole_call(plane_cells, z, 1000, payload, [spread_scratch], mixed, other_core(mixed), plane_back)
    pre, signal, sent = whole_call(
        activate, z, 2000,
        (shape_of(cells_shape), shape_of(cells_shape, BF16), payload), [spectrum_scratch],
        exchange(sent), local, cot_cells, inverse_here, forward_here,
    )
    own, pre, signal = lax.optimization_barrier((exchange(sent), pre, signal))
    other = other_core(own)
    layer_out, local, inverse_here = whole_call(
        emit, z, 1200,
        (shape_of(field.shape, BF16), shape_of(cells_shape), shape_of(inverse_back.shape)),
        [pltpu.SemaphoreType.DMA((1,))],
        pre, signal, pointwise_weight, inverse_back, specs=[VMEM, VMEM, VMEM, HBM],
    )
    other, layer_out, local, inverse_here = lax.optimization_barrier((other, layer_out, local, inverse_here))
    back, mixed = whole_call(
        mix_back, z, 1000, (shape_of((z.modes, z.rows, 2 * z.half)), shape_of(spectra_shape)), [spectra_scratch],
        own, other, plane, turned,
    )
    sent = whole_call(plane_cells, z, 1000, payload, [spread_scratch], mixed, other_core(mixed), plane_back)
    sent, back, spectra = lax.optimization_barrier((sent, back, spectra))
    returned = exchange(sent)
    gradient = whole_call(
        grad_weights, z, 5000, shape_of(weight_shape), weight_scratch, spectra, back, out_specs=HBM, room=28
    )
    returned, gradient = lax.optimization_barrier((returned, gradient))
    grad_field = whole_call(
        finish, z, 1000, shape_of(field.shape, BF16), [spectrum_scratch], returned, local, inverse_here
    )
    return (layer_out, grad_field, jnp.transpose(gradient.reshape(native.shape), (0, 1, 2, 5, 3, 4)))


def solution(mesh):
    return jax.shard_map(
        on_device,
        mesh=mesh,
        in_specs=(
            P(None, "gx", "gy", None),
            P(None, "gx", "gy", None),
            P("gx", None, None, None, "gy", None),
            P(),
            P(),
        ),
        out_specs=(
            P(None, "gx", "gy", None),
            P(None, "gx", "gy", None),
            P("gx", None, None, None, "gy", None),
        ),
        check_vma=False,
    )
```

```python
import math

import jax
import jax.numpy as jnp
import ml_dtypes
import numpy as np
from jax import lax
from jax.experimental import pallas as pl
from jax.experimental.pallas import tpu as pltpu
from jax.sharding import PartitionSpec as P

KZ = 16
KT = 4
NT = 16
LANES = 128
EXACT = lax.Precision.HIGHEST
F32 = jnp.float32
BF16 = jnp.bfloat16


def round_up(value, step):
    return -(-value // step) * step


def frequencies(kept):
    index = np.arange(kept)
    return np.where(index < kept // 2, index, index - kept)


def depth_time_table(cells):
    depth_cells = cells // NT
    depth = np.arange(depth_cells)[:, None, None, None] * frequencies(KZ)[None, None, :, None] * NT
    time = np.arange(NT)[None, :, None, None] * np.arange(KT)[None, None, None, :] * depth_cells
    phase = np.mod(depth + time, cells).reshape(cells, KZ * KT)
    angles = phase.astype(np.float32) * np.float32(2.0 * math.pi / cells)
    factor = np.float32(1.0 / math.sqrt(cells))
    return np.stack([np.cos(angles) * factor, -np.sin(angles) * factor], axis=1).astype(np.float32)


def plane_factors(sizes):
    length_x, length_y = sizes.nx * sizes.cells_x, sizes.ny * sizes.cells_y
    lane = np.arange(4 * sizes.half)
    mode = lane % sizes.half
    quarter = lane // sizes.half % 2 - lane // (2 * sizes.half)
    inside = mode < sizes.kept
    kx = np.arange(sizes.ny)[:, None] * sizes.local_x + np.where(inside, mode // sizes.kept_y, 0)
    turn_x = np.mod(np.arange(length_x)[:, None] * frequencies(sizes.kept_x)[kx][:, None, :], length_x) / length_x
    turn_y = np.mod(np.arange(length_y)[:, None] * frequencies(sizes.kept_y)[mode % sizes.kept_y], length_y) / length_y
    angle_x, angle_y = 2.0 * math.pi * turn_x, 2.0 * math.pi * (turn_y + quarter / 4.0)
    scale = inside / math.sqrt(length_x * length_y)
    factors_x = np.concatenate([np.cos(angle_x), -np.sin(angle_x)], -1)
    factors_y = np.concatenate([np.cos(angle_y) * scale, np.sin(angle_y) * scale], -1)
    return factors_x.astype(np.float32), factors_y.astype(np.float32)


class Sizes:
    def __init__(self, field, weight):
        self.nx, self.ny = lax.axis_size("gx"), lax.axis_size("gy")
        self.channels, self.cells_x, self.cells_y, self.depth = field.shape
        self.modes = weight.shape[0]
        self.local_x, self.kept_y = weight.shape[4:]
        self.kept_x = self.local_x * self.ny
        self.cells = self.cells_x * self.cells_y
        self.chips = self.nx * self.ny // 2
        self.kept = self.local_x * self.kept_y
        self.half = round_up(self.kept, LANES // 2)
        self.flat = 2 * self.channels * self.modes
        self.width = round_up(self.flat, LANES)
        self.all_modes = 2 * self.modes * self.nx
        self.rows = round_up(self.channels, 8)


def gather_cells(source, scratch, sizes):
    for w in range(sizes.channels):
        for x in range(sizes.cells_x):
            first = (w * sizes.cells_x + x) * sizes.cells_y
            scratch[first : first + sizes.cells_y, :] = source[w, x].astype(F32)
    return scratch[...]


def scatter_cells(values, target, sizes):
    for w in range(sizes.channels):
        for x in range(sizes.cells_x):
            first = (w * sizes.cells_x + x) * sizes.cells_y
            target[w, x] = values[first : first + sizes.cells_y, :].astype(target.dtype)


def lane_group(sizes):
    return lax.broadcasted_iota(jnp.int32, (sizes.cells, LANES), 1) // sizes.modes


def send_modes(values, target, sizes):
    group = lane_group(sizes)
    tiles = [values[w * sizes.cells : (w + 1) * sizes.cells, :] for w in range(sizes.channels)]
    for i in range(sizes.nx):
        out = [jnp.zeros((sizes.cells, LANES), F32) for _ in range(sizes.width // LANES)]
        for s in range(2):
            have = (i * 2 + s) * sizes.modes
            for w in range(sizes.channels):
                tile, want = divmod((s * sizes.channels + w) * sizes.modes, LANES)
                moved = tiles[w]
                if want != have:
                    moved = pltpu.roll(moved, (want - have) % LANES, 1)
                out[tile] = jnp.where(group == want // sizes.modes, moved, out[tile])
        for t, value in enumerate(out):
            for y in range(sizes.ny // 2):
                target[i * (sizes.ny // 2) + y, :, t * LANES : (t + 1) * LANES] = value


def receive_modes(source, scratch, sizes):
    group = lane_group(sizes)
    tiles = []
    for i in range(sizes.nx):
        row = []
        for t in range(sizes.width // LANES):
            value = None
            for y in range(sizes.ny // 2):
                part = source[i * (sizes.ny // 2) + y, :, t * LANES : (t + 1) * LANES]
                value = part if value is None else value + part
            row.append(value)
        tiles.append(row)
    for w in range(sizes.channels):
        out = jnp.zeros((sizes.cells, LANES), F32)
        for i in range(sizes.nx):
            for s in range(2):
                want = (i * 2 + s) * sizes.modes
                tile, have = divmod((s * sizes.channels + w) * sizes.modes, LANES)
                moved = tiles[i][tile]
                if want != have:
                    moved = pltpu.roll(moved, (want - have) % LANES, 1)
                out = jnp.where(group == want // sizes.modes, moved, out)
        scratch[w * sizes.cells : (w + 1) * sizes.cells, :] = out
    return scratch[...]


def dot(left, right, **kwargs):
    return jnp.dot(left, right, preferred_element_type=F32, **kwargs)


def fetch(sources, targets, semaphores):
    copies = [pltpu.make_async_copy(*pair, semaphores.at[at]) for at, pair in enumerate(zip(sources, targets))]
    for copy in copies:
        copy.start()
    for copy in copies:
        copy.wait()


def depth_forward(sizes, field, table, out, cells, field_here, table_here, semaphores):
    fetch((field, table), (field_here, table_here), semaphores)
    values = gather_cells(field_here, cells, sizes).astype(BF16)
    send_modes(dot(values, table_here[...]), out, sizes)


def one_hot(rows, columns, step, along_rows):
    row = lax.broadcasted_iota(jnp.int32, (rows, columns), 0)
    column = lax.broadcasted_iota(jnp.int32, (rows, columns), 1)
    same = row // step == column if along_rows else row == column // step
    return jnp.where(same, 1.0, 0.0).astype(BF16)


def cell_mixer(weights, across, sizes):
    count = sizes.channels * sizes.cells
    left = one_hot(count, sizes.channels, sizes.cells, True)
    right = one_hot(sizes.channels, count, sizes.cells, False)
    tall = lax.dot_general(left, weights, (((1,), (1 if across else 0,)), ((), ())), preferred_element_type=F32)
    wide = dot(tall.astype(BF16), right)
    row = lax.broadcasted_iota(jnp.int32, (count, count), 0)
    column = lax.broadcasted_iota(jnp.int32, (count, count), 1)
    same = lax.rem(row, sizes.cells) == lax.rem(column, sizes.cells)
    return jnp.where(same, wide, 0.0).astype(BF16)


def prepare(sizes, field, cotangent, weight, bias, inverse, forward, local, cot_cells, inverse_out, forward_out, cells, field_here, cot_here, semaphores):
    fetch((field, cotangent, inverse, forward), (field_here, cot_here, inverse_out, forward_out), semaphores)
    values = gather_cells(field_here, cells, sizes).astype(BF16)
    bypass = dot(cell_mixer(weight[...], True, sizes), values)
    for o in range(sizes.channels):
        rows = slice(o * sizes.cells, (o + 1) * sizes.cells)
        local[rows, :] = bypass[rows, :] + bias[o]
    gather_cells(cot_here, cot_cells, sizes)


def emit(sizes, pre, signal, weight, inverse, layer_out, local, inverse_out, semaphore):
    copy = pltpu.make_async_copy(inverse, inverse_out, semaphore.at[0])
    copy.start()
    scatter_cells(gelu_parts(pre[...])[0], layer_out, sizes)
    local[...] = dot(cell_mixer(weight[...], False, sizes), signal[...])
    copy.wait()


def plane_tables(sizes, place, mine, other, factors_y, table, back):
    half_rows = sizes.chips * sizes.cells
    lanes = 4 * sizes.half

    def chosen(rows, length, index):
        column = lax.broadcasted_iota(jnp.int32, (rows, length), 1)
        return jnp.where(column == index(lax.broadcasted_iota(jnp.int32, (rows, length), 0)), 1.0, 0.0)

    def at_x(row):
        chip = lax.rem(row // sizes.cells, sizes.chips)
        return chip // (sizes.ny // 2) * sizes.cells_x + lax.rem(row // sizes.cells_y, sizes.cells_x)

    def at_y(row):
        chip = lax.rem(row // sizes.cells, sizes.chips)
        core = lax.rem(place + row // half_rows, 2)
        return (lax.rem(chip, sizes.ny // 2) * 2 + core) * sizes.cells_y + lax.rem(row, sizes.cells_y)

    def product(left, right):
        return left[:, :lanes] * right[:, :lanes] + left[:, lanes:] * right[:, lanes:]

    pick_x = chosen(2 * half_rows, sizes.nx * sizes.cells_x, at_x)
    pick_y = chosen(2 * half_rows, sizes.ny * sizes.cells_y, at_y)
    spread_y = dot(pick_y, factors_y[...], precision=EXACT)
    table[...] = product(dot(pick_x, mine[...], precision=EXACT), spread_y)
    back[:, :lanes] = table[:half_rows, :]
    back[:, lanes:] = product(dot(pick_x[:half_rows], other[...], precision=EXACT), spread_y[:half_rows])


def turn_weights(sizes, source, after, place, factors_x, factors_y, target, table, back, here, mine, other, mine_y, semaphores, small):
    del after
    place = place[0]
    pair = place + 1 - 2 * lax.rem(place, 2)
    moves = ((factors_x.at[place], mine), (factors_x.at[pair], other), (factors_y, mine_y))
    tables = [pltpu.make_async_copy(*move, small.at[at]) for at, move in enumerate(moves)]
    copies = [pltpu.make_async_copy(source.at[at], here.at[at], semaphores.at[at]) for at in range(2 * sizes.modes)]
    for copy in tables + copies:
        copy.start()
    for copy in tables:
        copy.wait()
    plane_tables(sizes, place, mine, other, mine_y, table, back)
    if sizes.half > sizes.kept:
        target[...] = jnp.zeros_like(target)
    elif sizes.rows > sizes.channels:
        target[:, :, sizes.channels :, :] = jnp.zeros(
            (sizes.modes, sizes.channels, sizes.rows - sizes.channels, 2 * sizes.half), F32
        )

    def turn(mode, carry):
        for s in range(2):
            at = 2 * mode + s
            pltpu.make_async_copy(source.at[at], here.at[at], semaphores.at[at]).wait()
        for w in range(sizes.channels):
            blocks = [here[2 * mode + s, w].reshape(sizes.kept, sizes.channels) for s in range(2)]
            if sizes.half == sizes.kept:
                target[mode, w, : sizes.channels, :] = jnp.concatenate(blocks, 0).T
            else:
                for s, block in enumerate(blocks):
                    target[mode, w, : sizes.channels, s * sizes.half : s * sizes.half + sizes.kept] = block.T
        return carry

    lax.fori_loop(0, sizes.modes, turn, 0)


def plane_spectra(sizes, own, other, table, target):
    received = jnp.concatenate(
        [ref[...].reshape(sizes.chips * sizes.cells, sizes.width) for ref in (own, other)], 0
    )
    both = dot(received.T, table[...], precision=EXACT)
    count = sizes.channels * sizes.modes
    target[:count, :] = both[:count, : 2 * sizes.half] + both[count : 2 * count, 2 * sizes.half :]


def plane_cells(sizes, own, other, table, out, spread):
    rows, lanes = own.shape
    spread[...] = jnp.zeros_like(spread)
    for at, ref in enumerate((own, other)):
        for s in range(2):
            first = (at * 2 + s) * lanes
            spread[s * rows : (s + 1) * rows, first : first + lanes] = ref[...]
    cells = lax.dot_general(
        table[...], spread[...], (((1,), (1,)), ((), ())), precision=EXACT, preferred_element_type=F32
    )
    out[...] = cells.reshape(out.shape)


def swap_parts(values, sizes):
    return pltpu.roll(values, sizes.half, 1)


def mode_rows(first, sizes):
    return pl.ds(first, sizes.channels, stride=sizes.modes)


def first_lanes(rows, sizes):
    return lax.broadcasted_iota(jnp.int32, (rows, 2 * sizes.half), 1) < sizes.half


def mix_forward(sizes, own, other, table, weight, spectra, mixed):
    plane_spectra(sizes, own, other, table, spectra)
    real = first_lanes(sizes.rows, sizes)
    for m in range(sizes.modes):
        straight = jnp.zeros((sizes.rows, 2 * sizes.half), F32)
        crossed = jnp.zeros((sizes.rows, 2 * sizes.half), F32)
        for w in range(sizes.channels):
            row = spectra[w * sizes.modes + m : w * sizes.modes + m + 1, :]
            block = weight[m, w]
            straight = straight + row * block
            crossed = crossed + swap_parts(row, sizes) * block
        real_part = straight - swap_parts(straight, sizes)
        imag_part = crossed + swap_parts(crossed, sizes)
        result = jnp.where(real, real_part, imag_part)
        mixed[mode_rows(m, sizes), :] = result[: sizes.channels]


def mix_back(sizes, own, other, table, weight, back, mixed, spectra):
    plane_spectra(sizes, own, other, table, spectra)
    real = first_lanes(sizes.channels, sizes)
    for m in range(sizes.modes):
        rows = spectra[mode_rows(m, sizes), :]
        if sizes.rows > sizes.channels:
            rows = jnp.concatenate([rows, jnp.zeros((sizes.rows - sizes.channels, 2 * sizes.half), F32)], 0)
        back[m] = rows
        turned = swap_parts(rows, sizes)
        straight, crossed = [], []
        for w in range(sizes.channels):
            block = weight[m, w]
            straight.append(jnp.sum(block * rows, axis=0, keepdims=True))
            crossed.append(jnp.sum(block * turned, axis=0, keepdims=True))
        straight = jnp.concatenate(straight, 0)
        crossed = jnp.concatenate(crossed, 0)
        real_part = straight + swap_parts(straight, sizes)
        imag_part = swap_parts(crossed, sizes) - crossed
        mixed[mode_rows(m, sizes), :] = jnp.where(real, real_part, imag_part)


def grad_weights(sizes, spectra, back, target, here, semaphores):
    real = first_lanes(1, sizes)

    def copy(at):
        return pltpu.make_async_copy(here.at[at], target.at[at], semaphores.at[at])

    def one_mode(mode, carry):
        rows = back[mode]
        turned = swap_parts(rows, sizes)
        for w in range(sizes.channels):
            row = spectra[pl.ds(w * sizes.modes + mode, 1), :]
            swapped = swap_parts(row, sizes)
            real_part = jnp.where(real, row, swapped)
            imag_part = jnp.where(real, swapped, -row)
            block = (real_part * rows + imag_part * turned).T
            for s in range(2):
                part = block[s * sizes.half : s * sizes.half + sizes.kept, : sizes.channels]
                here[2 * mode + s, w] = part.reshape(sizes.local_x, sizes.kept_y, sizes.channels)
        for s in range(2):
            copy(2 * mode + s).start()
        return carry

    lax.fori_loop(0, sizes.modes, one_mode, 0)
    for at in range(2 * sizes.modes):
        copy(at).wait()


def gelu_parts(pre):
    slope = math.sqrt(2.0 / math.pi)
    squared = pre * pre
    bend = jnp.tanh(slope * (pre + 0.044715 * (squared * pre)))
    value = 0.5 * pre * (1.0 + bend)
    derivative = 0.5 * (1.0 + bend) + 0.5 * pre * (1.0 - bend * bend) * (slope * (1.0 + 3.0 * 0.044715 * squared))
    return value, derivative


def activate(sizes, received, local, cotangent, inverse, forward, pre_out, signal_out, out, spectrum):
    pre = dot(receive_modes(received, spectrum, sizes), inverse[...], precision=EXACT) + local[...]
    pre_out[...] = pre
    signal = (cotangent[...] * gelu_parts(pre)[1]).astype(BF16)
    signal_out[...] = signal
    send_modes(dot(signal, forward[...]), out, sizes)


def finish(sizes, received, local, inverse, grad_field, spectrum):
    spatial = dot(receive_modes(received, spectrum, sizes), inverse[...], precision=EXACT)
    scatter_cells(spatial + local[...], grad_field, sizes)


def shape_of(shape, dtype=F32):
    return jax.ShapeDtypeStruct(shape, dtype)


VMEM = pl.BlockSpec(memory_space=pltpu.VMEM)
SMEM = pl.BlockSpec(memory_space=pltpu.SMEM)
HBM = pl.BlockSpec(memory_space=pltpu.HBM)
ANYWHERE = pl.BlockSpec(memory_space=pl.ANY)


def settings(mebibytes):
    return pltpu.CompilerParams(vmem_limit_bytes=mebibytes * 1024 * 1024)


def cost(nanoseconds):
    return pl.CostEstimate(flops=0, bytes_accessed=3000 * nanoseconds, transcendentals=0)


def whole_call(body, sizes, nanoseconds, out_shape, scratch, *args, specs=None, out_specs=None, room=16):
    def kernel(*refs):
        body(sizes, *refs)

    if specs:
        args = [
            pltpu.with_memory_space_constraint(arg, pltpu.HBM) if spec is HBM else arg for arg, spec in zip(args, specs)
        ]
    return pl.pallas_call(
        kernel,
        out_shape=out_shape,
        in_specs=specs or [VMEM] * len(args),
        out_specs=out_specs or jax.tree.map(lambda _: VMEM, out_shape),
        scratch_shapes=scratch,
        name=body.__name__,
        cost_estimate=cost(nanoseconds),
        compiler_params=settings(room),
    )(*args)


def on_device(field, cotangent, spectral_weight, pointwise_weight, channel_bias):
    z = Sizes(field, spectral_weight)
    depth_table = depth_time_table(z.depth)
    modes = depth_table.shape[2]
    kappa = np.where(np.arange(modes) % KT == 0, 1.0, 2.0).astype(np.float32)
    ordered = depth_table.reshape(z.depth, 2, z.nx, z.modes).transpose(0, 2, 1, 3).reshape(z.depth, z.all_modes)
    doubled = np.repeat(kappa.reshape(z.nx, 1, z.modes), 2, axis=1).reshape(z.all_modes)
    forward_first = jnp.asarray(ordered.astype(ml_dtypes.bfloat16))
    forward_back = jnp.asarray((ordered.astype(ml_dtypes.bfloat16).astype(np.float32) * doubled).astype(ml_dtypes.bfloat16))
    inverse_back = jnp.asarray(np.ascontiguousarray(ordered.T))
    inverse_first = jnp.asarray(np.ascontiguousarray((ordered * doubled).T))
    groups = [[gx * z.ny + 2 * y + c for gx in range(z.nx) for y in range(z.ny // 2)] for c in range(2)]
    pairs = [(s, s ^ 1) for s in range(z.ny)]

    def exchange(payload):
        return lax.all_to_all(
            payload, ("gx", "gy"), split_axis=0, concat_axis=0, tiled=True, axis_index_groups=groups
        )

    def other_core(payload):
        return lax.ppermute(payload, "gy", pairs)

    payload = shape_of((z.chips, z.cells, z.width))
    cell_rows = z.channels * z.cells
    cells_shape = (cell_rows, z.depth)
    cells_scratch = pltpu.VMEM(cells_shape, F32)
    spectrum_scratch = pltpu.VMEM((cell_rows, z.all_modes), F32)
    spectra_shape = (z.channels * z.modes, 2 * z.half)
    spectra_scratch = pltpu.VMEM(spectra_shape, F32)
    spread_scratch = pltpu.VMEM((z.width, 8 * z.half), F32)
    field_scratch = pltpu.VMEM(field.shape, BF16)

    native = jnp.transpose(spectral_weight, (0, 1, 2, 4, 5, 3))
    weight_shape = (2 * z.modes,) + native.shape[2:]
    weight_scratch = [pltpu.VMEM(weight_shape, F32), pltpu.SemaphoreType.DMA((2 * z.modes,))]

    factors_x, factors_y = plane_factors(z)
    half_rows = z.chips * z.cells

    sent = whole_call(
        depth_forward, z, 1500, payload,
        [cells_scratch, field_scratch, pltpu.VMEM(forward_first.shape, BF16), pltpu.SemaphoreType.DMA((2,))],
        field, forward_first, specs=[HBM] * 2,
    )
    own = exchange(sent)
    factor_scratch = pltpu.VMEM(factors_x.shape[1:], F32)
    turned, plane, plane_back = whole_call(
        turn_weights, z, 5000,
        (
            shape_of((z.modes, z.channels, z.rows, 2 * z.half)),
            shape_of((2 * half_rows, 4 * z.half)),
            shape_of((half_rows, 8 * z.half)),
        ),
        [
            weight_scratch[0], factor_scratch, factor_scratch, pltpu.VMEM(factors_y.shape, F32),
            weight_scratch[1], pltpu.SemaphoreType.DMA((3,)),
        ],
        native.reshape(weight_shape), sent, lax.axis_index("gy").reshape(1), jnp.asarray(factors_x), jnp.asarray(factors_y),
        specs=[HBM, ANYWHERE, SMEM, HBM, HBM], room=28,
    )
    own, turned, plane, plane_back, field, cotangent = lax.optimization_barrier(
        (own, turned, plane, plane_back, field, cotangent)
    )
    other = other_core(own)
    local, cot_cells, inverse_here, forward_here = whole_call(
        prepare, z, 1500,
        (shape_of(cells_shape), shape_of(cells_shape), shape_of(inverse_first.shape), shape_of(forward_back.shape, BF16)),
        [cells_scratch, field_scratch, field_scratch, pltpu.SemaphoreType.DMA((4,))],
        field, cotangent, pointwise_weight, channel_bias, inverse_first, forward_back,
        specs=[HBM, HBM, VMEM, SMEM, HBM, HBM],
    )
    other, local, cot_cells, inverse_here, forward_here = lax.optimization_barrier(
        (other, local, cot_cells, inverse_here, forward_here)
    )
    spectra, mixed = whole_call(
        mix_forward, z, 1000, (shape_of(spectra_shape), shape_of(spectra_shape)), [], own, other, plane, turned
    )
    sent = whole_call(plane_cells, z, 1000, payload, [spread_scratch], mixed, other_core(mixed), plane_back)
    pre, signal, sent = whole_call(
        activate, z, 2000,
        (shape_of(cells_shape), shape_of(cells_shape, BF16), payload), [spectrum_scratch],
        exchange(sent), local, cot_cells, inverse_here, forward_here,
    )
    own, pre, signal = lax.optimization_barrier((exchange(sent), pre, signal))
    other = other_core(own)
    layer_out, local, inverse_here = whole_call(
        emit, z, 1200,
        (shape_of(field.shape, BF16), shape_of(cells_shape), shape_of(inverse_back.shape)),
        [pltpu.SemaphoreType.DMA((1,))],
        pre, signal, pointwise_weight, inverse_back, specs=[VMEM, VMEM, VMEM, HBM],
    )
    other, layer_out, local, inverse_here = lax.optimization_barrier((other, layer_out, local, inverse_here))
    back, mixed = whole_call(
        mix_back, z, 1000, (shape_of((z.modes, z.rows, 2 * z.half)), shape_of(spectra_shape)), [spectra_scratch],
        own, other, plane, turned,
    )
    sent = whole_call(plane_cells, z, 1000, payload, [spread_scratch], mixed, other_core(mixed), plane_back)
    sent, back, spectra = lax.optimization_barrier((sent, back, spectra))
    returned = exchange(sent)
    gradient = whole_call(
        grad_weights, z, 5000, shape_of(weight_shape), weight_scratch, spectra, back, out_specs=HBM, room=28
    )
    returned, gradient = lax.optimization_barrier((returned, gradient))
    grad_field = whole_call(
        finish, z, 1000, shape_of(field.shape, BF16), [spectrum_scratch], returned, local, inverse_here
    )
    return (layer_out, grad_field, jnp.transpose(gradient.reshape(native.shape), (0, 1, 2, 5, 3, 4)))


def solution(mesh):
    return jax.shard_map(
        on_device,
        mesh=mesh,
        in_specs=(
            P(None, "gx", "gy", None),
            P(None, "gx", "gy", None),
            P("gx", None, None, None, "gy", None),
            P(),
            P(),
        ),
        out_specs=(
            P(None, "gx", "gy", None),
            P(None, "gx", "gy", None),
            P("gx", None, None, None, "gy", None),
        ),
        check_vma=False,
    )
```

```python
import math

import jax
import jax.numpy as jnp
import ml_dtypes
import numpy as np
from jax import lax
from jax.experimental import pallas as pl
from jax.experimental.pallas import tpu as pltpu
from jax.sharding import PartitionSpec as P

KZ = 16
KT = 4
NT = 16
LANES = 128
EXACT = lax.Precision.HIGHEST
F32 = jnp.float32
BF16 = jnp.bfloat16


def round_up(value, step):
    return -(-value // step) * step


def frequencies(kept):
    index = np.arange(kept)
    return np.where(index < kept // 2, index, index - kept)


def depth_time_table(cells):
    depth_cells = cells // NT
    depth = np.arange(depth_cells)[:, None, None, None] * frequencies(KZ)[None, None, :, None] * NT
    time = np.arange(NT)[None, :, None, None] * np.arange(KT)[None, None, None, :] * depth_cells
    phase = np.mod(depth + time, cells).reshape(cells, KZ * KT)
    angles = phase.astype(np.float32) * np.float32(2.0 * math.pi / cells)
    factor = np.float32(1.0 / math.sqrt(cells))
    return np.stack([np.cos(angles) * factor, -np.sin(angles) * factor], axis=1).astype(np.float32)


def plane_tables(sizes):
    length_x, length_y = sizes.nx * sizes.cells_x, sizes.ny * sizes.cells_y
    phase_x = np.mod(np.arange(length_x)[:, None] * frequencies(sizes.kept_x), length_x) / length_x
    phase_y = np.mod(np.arange(length_y)[:, None] * frequencies(sizes.kept_y), length_y) / length_y
    angle = 2.0 * math.pi * (phase_x[:, None, :, None] + phase_y[None, :, None, :])
    scale = 1.0 / math.sqrt(length_x * length_y)
    cosine, sine = np.cos(angle) * scale, np.sin(angle) * scale
    parts = np.stack([np.stack([cosine, -sine]), np.stack([sine, cosine])])
    parts = parts.reshape(
        2, 2, sizes.nx, sizes.cells_x, sizes.ny // 2, 2, sizes.cells_y, sizes.ny, sizes.kept
    ).transpose(7, 5, 2, 4, 3, 6, 0, 1, 8)
    padded = np.zeros(parts.shape[:-1] + (sizes.half,), np.float32)
    padded[..., : sizes.kept] = parts
    ordered = np.stack([padded[j][[j % 2, 1 - j % 2]] for j in range(sizes.ny)])
    return ordered.reshape(sizes.ny, 2 * sizes.chips * sizes.cells, 4 * sizes.half)


class Sizes:
    def __init__(self, field, weight):
        self.nx, self.ny = lax.axis_size("gx"), lax.axis_size("gy")
        self.channels, self.cells_x, self.cells_y, self.depth = field.shape
        self.modes = weight.shape[0]
        self.local_x, self.kept_y = weight.shape[4:]
        self.kept_x = self.local_x * self.ny
        self.cells = self.cells_x * self.cells_y
        self.chips = self.nx * self.ny // 2
        self.kept = self.local_x * self.kept_y
        self.half = round_up(self.kept, LANES // 2)
        self.flat = 2 * self.channels * self.modes
        self.width = round_up(self.flat, LANES)
        self.all_modes = 2 * self.modes * self.nx
        self.rows = round_up(self.channels, 8)


def gather_cells(source, scratch, sizes):
    for w in range(sizes.channels):
        for x in range(sizes.cells_x):
            first = (w * sizes.cells_x + x) * sizes.cells_y
            scratch[first : first + sizes.cells_y, :] = source[w, x].astype(F32)
    return scratch[...]


def scatter_cells(values, target, sizes):
    for w in range(sizes.channels):
        for x in range(sizes.cells_x):
            first = (w * sizes.cells_x + x) * sizes.cells_y
            target[w, x] = values[first : first + sizes.cells_y, :].astype(target.dtype)


def lane_group(sizes):
    return lax.broadcasted_iota(jnp.int32, (sizes.cells, LANES), 1) // sizes.modes


def send_modes(values, target, sizes):
    group = lane_group(sizes)
    tiles = [values[w * sizes.cells : (w + 1) * sizes.cells, :] for w in range(sizes.channels)]
    for i in range(sizes.nx):
        out = [jnp.zeros((sizes.cells, LANES), F32) for _ in range(sizes.width // LANES)]
        for s in range(2):
            have = (i * 2 + s) * sizes.modes
            for w in range(sizes.channels):
                tile, want = divmod((s * sizes.channels + w) * sizes.modes, LANES)
                moved = tiles[w]
                if want != have:
                    moved = pltpu.roll(moved, (want - have) % LANES, 1)
                out[tile] = jnp.where(group == want // sizes.modes, moved, out[tile])
        for t, value in enumerate(out):
            for y in range(sizes.ny // 2):
                target[i * (sizes.ny // 2) + y, :, t * LANES : (t + 1) * LANES] = value


def receive_modes(source, scratch, sizes):
    group = lane_group(sizes)
    tiles = []
    for i in range(sizes.nx):
        row = []
        for t in range(sizes.width // LANES):
            value = None
            for y in range(sizes.ny // 2):
                part = source[i * (sizes.ny // 2) + y, :, t * LANES : (t + 1) * LANES]
                value = part if value is None else value + part
            row.append(value)
        tiles.append(row)
    for w in range(sizes.channels):
        out = jnp.zeros((sizes.cells, LANES), F32)
        for i in range(sizes.nx):
            for s in range(2):
                want = (i * 2 + s) * sizes.modes
                tile, have = divmod((s * sizes.channels + w) * sizes.modes, LANES)
                moved = tiles[i][tile]
                if want != have:
                    moved = pltpu.roll(moved, (want - have) % LANES, 1)
                out = jnp.where(group == want // sizes.modes, moved, out)
        scratch[w * sizes.cells : (w + 1) * sizes.cells, :] = out
    return scratch[...]


def dot(left, right, **kwargs):
    return jnp.dot(left, right, preferred_element_type=F32, **kwargs)


def fetch(sources, targets, semaphores):
    copies = [pltpu.make_async_copy(*pair, semaphores.at[at]) for at, pair in enumerate(zip(sources, targets))]
    for copy in copies:
        copy.start()
    for copy in copies:
        copy.wait()


def depth_forward(sizes, field, table, out, cells, field_here, table_here, semaphores):
    fetch((field, table), (field_here, table_here), semaphores)
    values = gather_cells(field_here, cells, sizes).astype(BF16)
    send_modes(dot(values, table_here[...]), out, sizes)


def one_hot(rows, columns, step, along_rows):
    row = lax.broadcasted_iota(jnp.int32, (rows, columns), 0)
    column = lax.broadcasted_iota(jnp.int32, (rows, columns), 1)
    same = row // step == column if along_rows else row == column // step
    return jnp.where(same, 1.0, 0.0).astype(BF16)


def cell_mixer(weights, across, sizes):
    count = sizes.channels * sizes.cells
    left = one_hot(count, sizes.channels, sizes.cells, True)
    right = one_hot(sizes.channels, count, sizes.cells, False)
    tall = lax.dot_general(left, weights, (((1,), (1 if across else 0,)), ((), ())), preferred_element_type=F32)
    wide = dot(tall.astype(BF16), right)
    row = lax.broadcasted_iota(jnp.int32, (count, count), 0)
    column = lax.broadcasted_iota(jnp.int32, (count, count), 1)
    same = lax.rem(row, sizes.cells) == lax.rem(column, sizes.cells)
    return jnp.where(same, wide, 0.0).astype(BF16)


def emit(sizes, pre, signal, weight, inverse, layer_out, local, inverse_out, semaphore):
    copy = pltpu.make_async_copy(inverse, inverse_out, semaphore.at[0])
    copy.start()
    scatter_cells(gelu_parts(pre[...])[0], layer_out, sizes)
    local[...] = dot(cell_mixer(weight[...], False, sizes), signal[...])
    copy.wait()


def prepare(
    sizes, source, after, place, tables, field, cotangent, weight, bias, inverse, forward,
    target, table, back, local, cot_cells, inverse_out, forward_out,
    here, cells, field_here, cot_here, semaphores, small,
):
    del after
    place = place[0]
    pair = place + 1 - 2 * lax.rem(place, 2)
    half_rows, lanes = back.shape[0], table.shape[1]
    moves = (
        (field, field_here),
        (cotangent, cot_here),
        (tables.at[place], table),
        (tables.at[place, pl.ds(0, half_rows)], back.at[:, pl.ds(0, lanes)]),
        (tables.at[pair, pl.ds(half_rows, half_rows)], back.at[:, pl.ds(lanes, lanes)]),
        (inverse, inverse_out),
        (forward, forward_out),
    )
    few = [pltpu.make_async_copy(*move, small.at[at]) for at, move in enumerate(moves)]
    copies = [pltpu.make_async_copy(source.at[at], here.at[at], semaphores.at[at]) for at in range(2 * sizes.modes)]
    for copy in few + copies:
        copy.start()
    few[0].wait()
    values = gather_cells(field_here, cells, sizes).astype(BF16)
    bypass = dot(cell_mixer(weight[...], True, sizes), values)
    for o in range(sizes.channels):
        rows = slice(o * sizes.cells, (o + 1) * sizes.cells)
        local[rows, :] = bypass[rows, :] + bias[o]
    few[1].wait()
    gather_cells(cot_here, cot_cells, sizes)
    if sizes.half > sizes.kept:
        target[...] = jnp.zeros_like(target)
    elif sizes.rows > sizes.channels:
        target[:, :, sizes.channels :, :] = jnp.zeros(
            (sizes.modes, sizes.channels, sizes.rows - sizes.channels, 2 * sizes.half), F32
        )

    def turn(mode, carry):
        for s in range(2):
            at = 2 * mode + s
            pltpu.make_async_copy(source.at[at], here.at[at], semaphores.at[at]).wait()
        for w in range(sizes.channels):
            blocks = [here[2 * mode + s, w].reshape(sizes.kept, sizes.channels) for s in range(2)]
            if sizes.half == sizes.kept:
                target[mode, w, : sizes.channels, :] = jnp.concatenate(blocks, 0).T
            else:
                for s, block in enumerate(blocks):
                    target[mode, w, : sizes.channels, s * sizes.half : s * sizes.half + sizes.kept] = block.T
        return carry

    lax.fori_loop(0, sizes.modes, turn, 0)
    for copy in few[2:]:
        copy.wait()


def plane_spectra(sizes, own, other, table, target):
    received = jnp.concatenate(
        [ref[...].reshape(sizes.chips * sizes.cells, sizes.width) for ref in (own, other)], 0
    )
    both = dot(received.T, table[...], precision=EXACT)
    count = sizes.channels * sizes.modes
    target[:count, :] = both[:count, : 2 * sizes.half] + both[count : 2 * count, 2 * sizes.half :]


def plane_cells(sizes, own, other, table, out, spread):
    rows, lanes = own.shape
    spread[...] = jnp.zeros_like(spread)
    for at, ref in enumerate((own, other)):
        for s in range(2):
            first = (at * 2 + s) * lanes
            spread[s * rows : (s + 1) * rows, first : first + lanes] = ref[...]
    cells = lax.dot_general(
        table[...], spread[...], (((1,), (1,)), ((), ())), precision=EXACT, preferred_element_type=F32
    )
    out[...] = cells.reshape(out.shape)


def swap_parts(values, sizes):
    return pltpu.roll(values, sizes.half, 1)


def mode_rows(first, sizes):
    return pl.ds(first, sizes.channels, stride=sizes.modes)


def first_lanes(rows, sizes):
    return lax.broadcasted_iota(jnp.int32, (rows, 2 * sizes.half), 1) < sizes.half


def mix_forward(sizes, own, other, table, weight, spectra, mixed):
    plane_spectra(sizes, own, other, table, spectra)
    real = first_lanes(sizes.rows, sizes)
    for m in range(sizes.modes):
        straight = jnp.zeros((sizes.rows, 2 * sizes.half), F32)
        crossed = jnp.zeros((sizes.rows, 2 * sizes.half), F32)
        for w in range(sizes.channels):
            row = spectra[w * sizes.modes + m : w * sizes.modes + m + 1, :]
            block = weight[m, w]
            straight = straight + row * block
            crossed = crossed + swap_parts(row, sizes) * block
        real_part = straight - swap_parts(straight, sizes)
        imag_part = crossed + swap_parts(crossed, sizes)
        result = jnp.where(real, real_part, imag_part)
        mixed[mode_rows(m, sizes), :] = result[: sizes.channels]


def mix_back(sizes, own, other, table, weight, back, mixed, spectra):
    plane_spectra(sizes, own, other, table, spectra)
    real = first_lanes(sizes.channels, sizes)
    for m in range(sizes.modes):
        rows = spectra[mode_rows(m, sizes), :]
        if sizes.rows > sizes.channels:
            rows = jnp.concatenate([rows, jnp.zeros((sizes.rows - sizes.channels, 2 * sizes.half), F32)], 0)
        back[m] = rows
        turned = swap_parts(rows, sizes)
        straight, crossed = [], []
        for w in range(sizes.channels):
            block = weight[m, w]
            straight.append(jnp.sum(block * rows, axis=0, keepdims=True))
            crossed.append(jnp.sum(block * turned, axis=0, keepdims=True))
        straight = jnp.concatenate(straight, 0)
        crossed = jnp.concatenate(crossed, 0)
        real_part = straight + swap_parts(straight, sizes)
        imag_part = swap_parts(crossed, sizes) - crossed
        mixed[mode_rows(m, sizes), :] = jnp.where(real, real_part, imag_part)


def grad_weights(sizes, spectra, back, target, here, straight, crossed, semaphores):
    values = spectra[...]
    turned = swap_parts(values, sizes)
    real = first_lanes(values.shape[0], sizes)
    straight[...] = jnp.where(real, values, turned)
    crossed[...] = jnp.where(real, turned, -values)
    copies = [pltpu.make_async_copy(here.at[at], target.at[at], semaphores.at[at]) for at in range(2 * sizes.modes)]
    for mode in range(sizes.modes):
        rows = back[mode]
        turned = swap_parts(rows, sizes)
        for w in range(sizes.channels):
            at = slice(w * sizes.modes + mode, w * sizes.modes + mode + 1)
            block = (straight[at, :] * rows + crossed[at, :] * turned).T
            for s in range(2):
                part = block[s * sizes.half : s * sizes.half + sizes.kept, : sizes.channels]
                here[2 * mode + s, w] = part.reshape(sizes.local_x, sizes.kept_y, sizes.channels)
        for s in range(2):
            copies[2 * mode + s].start()
    for copy in copies:
        copy.wait()


def gelu_parts(pre):
    slope = math.sqrt(2.0 / math.pi)
    squared = pre * pre
    bend = jnp.tanh(slope * (pre + 0.044715 * (squared * pre)))
    value = 0.5 * pre * (1.0 + bend)
    derivative = 0.5 * (1.0 + bend) + 0.5 * pre * (1.0 - bend * bend) * (slope * (1.0 + 3.0 * 0.044715 * squared))
    return value, derivative


def activate(sizes, received, local, cotangent, inverse, forward, pre_out, signal_out, out, spectrum):
    pre = dot(receive_modes(received, spectrum, sizes), inverse[...], precision=EXACT) + local[...]
    pre_out[...] = pre
    signal = (cotangent[...] * gelu_parts(pre)[1]).astype(BF16)
    signal_out[...] = signal
    send_modes(dot(signal, forward[...]), out, sizes)


def finish(sizes, received, local, inverse, grad_field, spectrum):
    spatial = dot(receive_modes(received, spectrum, sizes), inverse[...], precision=EXACT)
    scatter_cells(spatial + local[...], grad_field, sizes)


def shape_of(shape, dtype=F32):
    return jax.ShapeDtypeStruct(shape, dtype)


VMEM = pl.BlockSpec(memory_space=pltpu.VMEM)
SMEM = pl.BlockSpec(memory_space=pltpu.SMEM)
HBM = pl.BlockSpec(memory_space=pltpu.HBM)
ANYWHERE = pl.BlockSpec(memory_space=pl.ANY)


def settings(mebibytes):
    return pltpu.CompilerParams(vmem_limit_bytes=mebibytes * 1024 * 1024)


def cost(nanoseconds):
    return pl.CostEstimate(flops=0, bytes_accessed=3000 * nanoseconds, transcendentals=0)


def whole_call(body, sizes, nanoseconds, out_shape, scratch, *args, specs=None, out_specs=None, room=16):
    def kernel(*refs):
        body(sizes, *refs)

    if specs:
        args = [
            pltpu.with_memory_space_constraint(arg, pltpu.HBM) if spec is HBM else arg for arg, spec in zip(args, specs)
        ]
    return pl.pallas_call(
        kernel,
        out_shape=out_shape,
        in_specs=specs or [VMEM] * len(args),
        out_specs=out_specs or jax.tree.map(lambda _: VMEM, out_shape),
        scratch_shapes=scratch,
        name=body.__name__,
        cost_estimate=cost(nanoseconds),
        compiler_params=settings(room),
    )(*args)


def on_device(field, cotangent, spectral_weight, pointwise_weight, channel_bias):
    z = Sizes(field, spectral_weight)
    depth_table = depth_time_table(z.depth)
    modes = depth_table.shape[2]
    kappa = np.where(np.arange(modes) % KT == 0, 1.0, 2.0).astype(np.float32)
    ordered = depth_table.reshape(z.depth, 2, z.nx, z.modes).transpose(0, 2, 1, 3).reshape(z.depth, z.all_modes)
    doubled = np.repeat(kappa.reshape(z.nx, 1, z.modes), 2, axis=1).reshape(z.all_modes)
    forward_first = jnp.asarray(ordered.astype(ml_dtypes.bfloat16))
    forward_back = jnp.asarray((ordered.astype(ml_dtypes.bfloat16).astype(np.float32) * doubled).astype(ml_dtypes.bfloat16))
    inverse_back = jnp.asarray(np.ascontiguousarray(ordered.T))
    inverse_first = jnp.asarray(np.ascontiguousarray((ordered * doubled).T))
    groups = [[gx * z.ny + 2 * y + c for gx in range(z.nx) for y in range(z.ny // 2)] for c in range(2)]
    pairs = [(s, s ^ 1) for s in range(z.ny)]

    def exchange(payload):
        return lax.all_to_all(
            payload, ("gx", "gy"), split_axis=0, concat_axis=0, tiled=True, axis_index_groups=groups
        )

    def other_core(payload):
        return lax.ppermute(payload, "gy", pairs)

    payload = shape_of((z.chips, z.cells, z.width))
    cell_rows = z.channels * z.cells
    cells_shape = (cell_rows, z.depth)
    cells_scratch = pltpu.VMEM(cells_shape, F32)
    spectrum_scratch = pltpu.VMEM((cell_rows, z.all_modes), F32)
    spectra_shape = (z.channels * z.modes, 2 * z.half)
    spectra_scratch = pltpu.VMEM(spectra_shape, F32)
    spread_scratch = pltpu.VMEM((z.width, 8 * z.half), F32)
    field_scratch = pltpu.VMEM(field.shape, BF16)

    native = jnp.transpose(spectral_weight, (0, 1, 2, 4, 5, 3))
    weight_shape = (2 * z.modes,) + native.shape[2:]
    weight_scratch = [pltpu.VMEM(weight_shape, F32), pltpu.SemaphoreType.DMA((2 * z.modes,))]

    half_rows = z.chips * z.cells

    sent = whole_call(
        depth_forward, z, 1500, payload,
        [cells_scratch, field_scratch, pltpu.VMEM(forward_first.shape, BF16), pltpu.SemaphoreType.DMA((2,))],
        field, forward_first, specs=[HBM] * 2,
    )
    own = exchange(sent)
    turned, plane, plane_back, local, cot_cells, inverse_here, forward_here = whole_call(
        prepare, z, 5000,
        (
            shape_of((z.modes, z.channels, z.rows, 2 * z.half)),
            shape_of((2 * half_rows, 4 * z.half)),
            shape_of((half_rows, 8 * z.half)),
            shape_of(cells_shape),
            shape_of(cells_shape),
            shape_of(inverse_first.shape),
            shape_of(forward_back.shape, BF16),
        ),
        [weight_scratch[0], cells_scratch, field_scratch, field_scratch, weight_scratch[1], pltpu.SemaphoreType.DMA((7,))],
        native.reshape(weight_shape), sent, lax.axis_index("gy").reshape(1), jnp.asarray(plane_tables(z)),
        field, cotangent, pointwise_weight, channel_bias, inverse_first, forward_back,
        specs=[HBM, ANYWHERE, SMEM, HBM, HBM, HBM, VMEM, SMEM, HBM, HBM], room=28,
    )
    own, turned, plane, plane_back, local, cot_cells, inverse_here, forward_here = lax.optimization_barrier(
        (own, turned, plane, plane_back, local, cot_cells, inverse_here, forward_here)
    )
    other = other_core(own)
    spectra, mixed = whole_call(
        mix_forward, z, 1000, (shape_of(spectra_shape), shape_of(spectra_shape)), [], own, other, plane, turned
    )
    sent = whole_call(plane_cells, z, 1000, payload, [spread_scratch], mixed, other_core(mixed), plane_back)
    pre, signal, sent = whole_call(
        activate, z, 2000,
        (shape_of(cells_shape), shape_of(cells_shape, BF16), payload), [spectrum_scratch],
        exchange(sent), local, cot_cells, inverse_here, forward_here,
    )
    own, pre, signal = lax.optimization_barrier((exchange(sent), pre, signal))
    other = other_core(own)
    layer_out, local, inverse_here = whole_call(
        emit, z, 1200,
        (shape_of(field.shape, BF16), shape_of(cells_shape), shape_of(inverse_back.shape)),
        [pltpu.SemaphoreType.DMA((1,))],
        pre, signal, pointwise_weight, inverse_back, specs=[VMEM, VMEM, VMEM, HBM],
    )
    other, layer_out, local, inverse_here = lax.optimization_barrier((other, layer_out, local, inverse_here))
    back, mixed = whole_call(
        mix_back, z, 1000, (shape_of((z.modes, z.rows, 2 * z.half)), shape_of(spectra_shape)), [spectra_scratch],
        own, other, plane, turned,
    )
    sent = whole_call(plane_cells, z, 1000, payload, [spread_scratch], mixed, other_core(mixed), plane_back)
    sent, back, spectra = lax.optimization_barrier((sent, back, spectra))
    returned = exchange(sent)
    gradient = whole_call(
        grad_weights, z, 5000, shape_of(weight_shape),
        [weight_scratch[0], spectra_scratch, spectra_scratch, weight_scratch[1]],
        spectra, back, out_specs=HBM, room=28,
    )
    returned, gradient = lax.optimization_barrier((returned, gradient))
    grad_field = whole_call(
        finish, z, 1000, shape_of(field.shape, BF16), [spectrum_scratch], returned, local, inverse_here
    )
    return (layer_out, grad_field, jnp.transpose(gradient.reshape(native.shape), (0, 1, 2, 5, 3, 4)))


def solution(mesh):
    return jax.shard_map(
        on_device,
        mesh=mesh,
        in_specs=(
            P(None, "gx", "gy", None),
            P(None, "gx", "gy", None),
            P("gx", None, None, None, "gy", None),
            P(),
            P(),
        ),
        out_specs=(
            P(None, "gx", "gy", None),
            P(None, "gx", "gy", None),
            P("gx", None, None, None, "gy", None),
        ),
        check_vma=False,
    )
```

```python
import math

import jax
import jax.numpy as jnp
import ml_dtypes
import numpy as np
from jax import lax
from jax.experimental import pallas as pl
from jax.experimental.pallas import tpu as pltpu
from jax.sharding import PartitionSpec as P

KZ = 16
KT = 4
NT = 16
LANES = 128
EXACT = lax.Precision.HIGHEST
F32 = jnp.float32
BF16 = jnp.bfloat16


def round_up(value, step):
    return -(-value // step) * step


def frequencies(kept):
    index = np.arange(kept)
    return np.where(index < kept // 2, index, index - kept)


def depth_time_table(cells):
    depth_cells = cells // NT
    depth = np.arange(depth_cells)[:, None, None, None] * frequencies(KZ)[None, None, :, None] * NT
    time = np.arange(NT)[None, :, None, None] * np.arange(KT)[None, None, None, :] * depth_cells
    phase = np.mod(depth + time, cells).reshape(cells, KZ * KT)
    angles = phase.astype(np.float32) * np.float32(2.0 * math.pi / cells)
    factor = np.float32(1.0 / math.sqrt(cells))
    return np.stack([np.cos(angles) * factor, -np.sin(angles) * factor], axis=1).astype(np.float32)


def plane_tables(sizes):
    length_x, length_y = sizes.nx * sizes.cells_x, sizes.ny * sizes.cells_y
    phase_x = np.mod(np.arange(length_x)[:, None] * frequencies(sizes.kept_x), length_x) / length_x
    phase_y = np.mod(np.arange(length_y)[:, None] * frequencies(sizes.kept_y), length_y) / length_y
    angle = 2.0 * math.pi * (phase_x[:, None, :, None] + phase_y[None, :, None, :])
    scale = 1.0 / math.sqrt(length_x * length_y)
    cosine, sine = np.cos(angle) * scale, np.sin(angle) * scale
    parts = np.stack([np.stack([cosine, -sine]), np.stack([sine, cosine])])
    parts = parts.reshape(
        2, 2, sizes.nx, sizes.cells_x, sizes.ny // 2, 2, sizes.cells_y, sizes.ny, sizes.kept
    ).transpose(7, 5, 2, 4, 3, 6, 0, 1, 8)
    padded = np.zeros(parts.shape[:-1] + (sizes.half,), np.float32)
    padded[..., : sizes.kept] = parts
    ordered = np.stack([padded[j][[j % 2, 1 - j % 2]] for j in range(sizes.ny)])
    return ordered.reshape(sizes.ny, 2 * sizes.chips * sizes.cells, 4 * sizes.half)


class Sizes:
    def __init__(self, field, weight):
        self.nx, self.ny = lax.axis_size("gx"), lax.axis_size("gy")
        self.channels, self.cells_x, self.cells_y, self.depth = field.shape
        self.modes = weight.shape[0]
        self.local_x, self.kept_y = weight.shape[4:]
        self.kept_x = self.local_x * self.ny
        self.cells = self.cells_x * self.cells_y
        self.chips = self.nx * self.ny // 2
        self.kept = self.local_x * self.kept_y
        self.half = round_up(self.kept, LANES // 2)
        self.flat = 2 * self.channels * self.modes
        self.width = round_up(self.flat, LANES)
        self.all_modes = 2 * self.modes * self.nx
        self.rows = round_up(self.channels, 8)


def gather_cells(source, scratch, sizes):
    for w in range(sizes.channels):
        for x in range(sizes.cells_x):
            first = (w * sizes.cells_x + x) * sizes.cells_y
            scratch[first : first + sizes.cells_y, :] = source[w, x].astype(F32)
    return scratch[...]


def scatter_cells(values, target, sizes):
    for w in range(sizes.channels):
        for x in range(sizes.cells_x):
            first = (w * sizes.cells_x + x) * sizes.cells_y
            target[w, x] = values[first : first + sizes.cells_y, :].astype(target.dtype)


def lane_group(sizes):
    return lax.broadcasted_iota(jnp.int32, (sizes.cells, LANES), 1) // sizes.modes


def send_modes(values, target, sizes):
    group = lane_group(sizes)
    tiles = [values[w * sizes.cells : (w + 1) * sizes.cells, :] for w in range(sizes.channels)]
    for i in range(sizes.nx):
        out = [jnp.zeros((sizes.cells, LANES), F32) for _ in range(sizes.width // LANES)]
        for s in range(2):
            have = (i * 2 + s) * sizes.modes
            for w in range(sizes.channels):
                tile, want = divmod((s * sizes.channels + w) * sizes.modes, LANES)
                moved = tiles[w]
                if want != have:
                    moved = pltpu.roll(moved, (want - have) % LANES, 1)
                out[tile] = jnp.where(group == want // sizes.modes, moved, out[tile])
        for t, value in enumerate(out):
            for y in range(sizes.ny // 2):
                target[i * (sizes.ny // 2) + y, :, t * LANES : (t + 1) * LANES] = value


def receive_modes(source, scratch, sizes):
    group = lane_group(sizes)
    tiles = []
    for i in range(sizes.nx):
        row = []
        for t in range(sizes.width // LANES):
            value = None
            for y in range(sizes.ny // 2):
                part = source[i * (sizes.ny // 2) + y, :, t * LANES : (t + 1) * LANES]
                value = part if value is None else value + part
            row.append(value)
        tiles.append(row)
    for w in range(sizes.channels):
        out = jnp.zeros((sizes.cells, LANES), F32)
        for i in range(sizes.nx):
            for s in range(2):
                want = (i * 2 + s) * sizes.modes
                tile, have = divmod((s * sizes.channels + w) * sizes.modes, LANES)
                moved = tiles[i][tile]
                if want != have:
                    moved = pltpu.roll(moved, (want - have) % LANES, 1)
                out = jnp.where(group == want // sizes.modes, moved, out)
        scratch[w * sizes.cells : (w + 1) * sizes.cells, :] = out
    return scratch[...]


def dot(left, right, **kwargs):
    return jnp.dot(left, right, preferred_element_type=F32, **kwargs)


def fetch(sources, targets, semaphores):
    copies = [pltpu.make_async_copy(*pair, semaphores.at[at]) for at, pair in enumerate(zip(sources, targets))]
    for copy in copies:
        copy.start()
    for copy in copies:
        copy.wait()


def depth_forward(sizes, field, table, out, cells, field_here, table_here, semaphores):
    fetch((field, table), (field_here, table_here), semaphores)
    values = gather_cells(field_here, cells, sizes).astype(BF16)
    send_modes(dot(values, table_here[...]), out, sizes)


def one_hot(rows, columns, step, along_rows):
    row = lax.broadcasted_iota(jnp.int32, (rows, columns), 0)
    column = lax.broadcasted_iota(jnp.int32, (rows, columns), 1)
    same = row // step == column if along_rows else row == column // step
    return jnp.where(same, 1.0, 0.0).astype(BF16)


def cell_mixer(weights, across, sizes):
    count = sizes.channels * sizes.cells
    left = one_hot(count, sizes.channels, sizes.cells, True)
    right = one_hot(sizes.channels, count, sizes.cells, False)
    tall = lax.dot_general(left, weights, (((1,), (1 if across else 0,)), ((), ())), preferred_element_type=F32)
    wide = dot(tall.astype(BF16), right)
    row = lax.broadcasted_iota(jnp.int32, (count, count), 0)
    column = lax.broadcasted_iota(jnp.int32, (count, count), 1)
    same = lax.rem(row, sizes.cells) == lax.rem(column, sizes.cells)
    return jnp.where(same, wide, 0.0).astype(BF16)


def emit(sizes, pre, signal, weight, inverse, layer_out, local, inverse_out, weight_here, semaphores):
    copies = [
        pltpu.make_async_copy(weight, weight_here, semaphores.at[0]),
        pltpu.make_async_copy(inverse, inverse_out, semaphores.at[1]),
    ]
    for copy in copies:
        copy.start()
    scatter_cells(gelu_parts(pre[...])[0], layer_out, sizes)
    copies[0].wait()
    local[...] = dot(cell_mixer(weight_here[...], False, sizes), signal[...])
    copies[1].wait()


def fetch_tables(sizes, inverse, forward, after, inverse_out, forward_out, semaphores):
    del after
    fetch((inverse, forward), (inverse_out, forward_out), semaphores)


def prepare(
    sizes, source, after, tables, field, cotangent, weight, bias,
    target, table, back, local, cot_cells,
    here, cells, field_here, cot_here, weight_here, bias_here, semaphores, small,
):
    del after
    place = lax.axis_index("gy")
    pair = place + 1 - 2 * lax.rem(place, 2)
    half_rows, lanes = back.shape[0], table.shape[1]
    moves = (
        (field, field_here),
        (cotangent, cot_here),
        (weight, weight_here),
        (bias, bias_here),
        (tables.at[place], table),
        (tables.at[place, pl.ds(0, half_rows)], back.at[:, pl.ds(0, lanes)]),
        (tables.at[pair, pl.ds(half_rows, half_rows)], back.at[:, pl.ds(lanes, lanes)]),
    )
    few = [pltpu.make_async_copy(*move, small.at[at]) for at, move in enumerate(moves)]
    copies = [pltpu.make_async_copy(source.at[at], here.at[at], semaphores.at[at]) for at in range(2 * sizes.modes)]
    for copy in few + copies:
        copy.start()
    if sizes.half > sizes.kept:
        target[...] = jnp.zeros_like(target)
    elif sizes.rows > sizes.channels:
        target[:, :, sizes.channels :, :] = jnp.zeros(
            (sizes.modes, sizes.channels, sizes.rows - sizes.channels, 2 * sizes.half), F32
        )
    for mode in range(sizes.modes):
        for s in range(2):
            copies[2 * mode + s].wait()
        for w in range(sizes.channels):
            blocks = [here[2 * mode + s, w].reshape(sizes.kept, sizes.channels) for s in range(2)]
            if sizes.half == sizes.kept:
                target[mode, w, : sizes.channels, :] = jnp.concatenate(blocks, 0).T
            else:
                for s, block in enumerate(blocks):
                    target[mode, w, : sizes.channels, s * sizes.half : s * sizes.half + sizes.kept] = block.T
        if mode == 1:
            for copy in few:
                copy.wait()
            values = gather_cells(field_here, cells, sizes).astype(BF16)
            spread = one_hot(sizes.channels * sizes.cells, sizes.channels, sizes.cells, True).astype(F32)
            offset = jnp.sum(spread * bias_here[...].reshape(1, sizes.channels), axis=1, keepdims=True)
            local[...] = dot(cell_mixer(weight_here[...], True, sizes), values) + offset
            gather_cells(cot_here, cot_cells, sizes)


def plane_spectra(sizes, own, other, table, target):
    received = jnp.concatenate(
        [ref[...].reshape(sizes.chips * sizes.cells, sizes.width) for ref in (own, other)], 0
    )
    both = dot(received.T, table[...], precision=EXACT)
    count = sizes.channels * sizes.modes
    target[:count, :] = both[:count, : 2 * sizes.half] + both[count : 2 * count, 2 * sizes.half :]


def plane_cells(sizes, own, other, table, out, spread):
    rows, lanes = own.shape
    spread[...] = jnp.zeros_like(spread)
    for at, ref in enumerate((own, other)):
        for s in range(2):
            first = (at * 2 + s) * lanes
            spread[s * rows : (s + 1) * rows, first : first + lanes] = ref[...]
    cells = lax.dot_general(
        table[...], spread[...], (((1,), (1,)), ((), ())), precision=EXACT, preferred_element_type=F32
    )
    out[...] = cells.reshape(out.shape)


def swap_parts(values, sizes):
    return pltpu.roll(values, sizes.half, 1)


def mode_rows(first, sizes):
    return pl.ds(first, sizes.channels, stride=sizes.modes)


def first_lanes(rows, sizes):
    return lax.broadcasted_iota(jnp.int32, (rows, 2 * sizes.half), 1) < sizes.half


def mix_forward(sizes, own, other, table, weight, spectra, mixed):
    plane_spectra(sizes, own, other, table, spectra)
    real = first_lanes(sizes.rows, sizes)
    for m in range(sizes.modes):
        straight = jnp.zeros((sizes.rows, 2 * sizes.half), F32)
        crossed = jnp.zeros((sizes.rows, 2 * sizes.half), F32)
        for w in range(sizes.channels):
            row = spectra[w * sizes.modes + m : w * sizes.modes + m + 1, :]
            block = weight[m, w]
            straight = straight + row * block
            crossed = crossed + swap_parts(row, sizes) * block
        real_part = straight - swap_parts(straight, sizes)
        imag_part = crossed + swap_parts(crossed, sizes)
        result = jnp.where(real, real_part, imag_part)
        mixed[mode_rows(m, sizes), :] = result[: sizes.channels]


def mix_back(sizes, own, other, table, weight, back, mixed, spectra):
    plane_spectra(sizes, own, other, table, spectra)
    real = first_lanes(sizes.channels, sizes)
    for m in range(sizes.modes):
        rows = spectra[mode_rows(m, sizes), :]
        if sizes.rows > sizes.channels:
            rows = jnp.concatenate([rows, jnp.zeros((sizes.rows - sizes.channels, 2 * sizes.half), F32)], 0)
        back[m] = rows
        turned = swap_parts(rows, sizes)
        straight, crossed = [], []
        for w in range(sizes.channels):
            block = weight[m, w]
            straight.append(jnp.sum(block * rows, axis=0, keepdims=True))
            crossed.append(jnp.sum(block * turned, axis=0, keepdims=True))
        straight = jnp.concatenate(straight, 0)
        crossed = jnp.concatenate(crossed, 0)
        real_part = straight + swap_parts(straight, sizes)
        imag_part = swap_parts(crossed, sizes) - crossed
        mixed[mode_rows(m, sizes), :] = jnp.where(real, real_part, imag_part)


def grad_weights(sizes, spectra, back, target, here, straight, crossed, semaphores):
    values = spectra[...]
    turned = swap_parts(values, sizes)
    real = first_lanes(values.shape[0], sizes)
    straight[...] = jnp.where(real, values, turned)
    crossed[...] = jnp.where(real, turned, -values)
    copies = [pltpu.make_async_copy(here.at[at], target.at[at], semaphores.at[at]) for at in range(2 * sizes.modes)]
    for mode in range(sizes.modes):
        rows = back[mode]
        turned = swap_parts(rows, sizes)
        for w in range(sizes.channels):
            at = slice(w * sizes.modes + mode, w * sizes.modes + mode + 1)
            block = (straight[at, :] * rows + crossed[at, :] * turned).T
            for s in range(2):
                part = block[s * sizes.half : s * sizes.half + sizes.kept, : sizes.channels]
                here[2 * mode + s, w] = part.reshape(sizes.local_x, sizes.kept_y, sizes.channels)
        for s in range(2):
            copies[2 * mode + s].start()
    for copy in copies:
        copy.wait()


def gelu_parts(pre):
    slope = math.sqrt(2.0 / math.pi)
    squared = pre * pre
    bend = jnp.tanh(slope * (pre + 0.044715 * (squared * pre)))
    value = 0.5 * pre * (1.0 + bend)
    derivative = 0.5 * (1.0 + bend) + 0.5 * pre * (1.0 - bend * bend) * (slope * (1.0 + 3.0 * 0.044715 * squared))
    return value, derivative


def activate(sizes, received, local, cotangent, inverse, forward, pre_out, signal_out, out, spectrum):
    pre = dot(receive_modes(received, spectrum, sizes), inverse[...], precision=EXACT) + local[...]
    pre_out[...] = pre
    signal = (cotangent[...] * gelu_parts(pre)[1]).astype(BF16)
    signal_out[...] = signal
    send_modes(dot(signal, forward[...]), out, sizes)


def finish(sizes, received, local, inverse, grad_field, spectrum):
    spatial = dot(receive_modes(received, spectrum, sizes), inverse[...], precision=EXACT)
    scatter_cells(spatial + local[...], grad_field, sizes)


def shape_of(shape, dtype=F32):
    return jax.ShapeDtypeStruct(shape, dtype)


VMEM = pl.BlockSpec(memory_space=pltpu.VMEM)
HBM = pl.BlockSpec(memory_space=pltpu.HBM)
ANYWHERE = pl.BlockSpec(memory_space=pl.ANY)


def settings(mebibytes):
    return pltpu.CompilerParams(vmem_limit_bytes=mebibytes * 1024 * 1024)


def cost(nanoseconds):
    return pl.CostEstimate(flops=0, bytes_accessed=3000 * nanoseconds, transcendentals=0)


def whole_call(body, sizes, nanoseconds, out_shape, scratch, *args, specs=None, out_specs=None, room=16):
    def kernel(*refs):
        body(sizes, *refs)

    if specs:
        args = [
            pltpu.with_memory_space_constraint(arg, pltpu.HBM) if spec is HBM else arg for arg, spec in zip(args, specs)
        ]
    return pl.pallas_call(
        kernel,
        out_shape=out_shape,
        in_specs=specs or [VMEM] * len(args),
        out_specs=out_specs or jax.tree.map(lambda _: VMEM, out_shape),
        scratch_shapes=scratch,
        name=body.__name__,
        cost_estimate=cost(nanoseconds),
        compiler_params=settings(room),
    )(*args)


def on_device(field, cotangent, spectral_weight, pointwise_weight, channel_bias):
    z = Sizes(field, spectral_weight)
    depth_table = depth_time_table(z.depth)
    modes = depth_table.shape[2]
    kappa = np.where(np.arange(modes) % KT == 0, 1.0, 2.0).astype(np.float32)
    ordered = depth_table.reshape(z.depth, 2, z.nx, z.modes).transpose(0, 2, 1, 3).reshape(z.depth, z.all_modes)
    doubled = np.repeat(kappa.reshape(z.nx, 1, z.modes), 2, axis=1).reshape(z.all_modes)
    forward_first = jnp.asarray(ordered.astype(ml_dtypes.bfloat16))
    forward_back = jnp.asarray((ordered.astype(ml_dtypes.bfloat16).astype(np.float32) * doubled).astype(ml_dtypes.bfloat16))
    inverse_back = jnp.asarray(np.ascontiguousarray(ordered.T))
    inverse_first = jnp.asarray(np.ascontiguousarray((ordered * doubled).T))
    groups = [[gx * z.ny + 2 * y + c for gx in range(z.nx) for y in range(z.ny // 2)] for c in range(2)]
    pairs = [(s, s ^ 1) for s in range(z.ny)]

    def exchange(payload):
        return lax.all_to_all(
            payload, ("gx", "gy"), split_axis=0, concat_axis=0, tiled=True, axis_index_groups=groups
        )

    def other_core(payload):
        return lax.ppermute(payload, "gy", pairs)

    payload = shape_of((z.chips, z.cells, z.width))
    cell_rows = z.channels * z.cells
    cells_shape = (cell_rows, z.depth)
    cells_scratch = pltpu.VMEM(cells_shape, F32)
    spectrum_scratch = pltpu.VMEM((cell_rows, z.all_modes), F32)
    spectra_shape = (z.channels * z.modes, 2 * z.half)
    spectra_scratch = pltpu.VMEM(spectra_shape, F32)
    spread_scratch = pltpu.VMEM((z.width, 8 * z.half), F32)
    field_scratch = pltpu.VMEM(field.shape, BF16)

    native = jnp.transpose(spectral_weight, (0, 1, 2, 4, 5, 3))
    weight_shape = (2 * z.modes,) + native.shape[2:]
    weight_scratch = [pltpu.VMEM(weight_shape, F32), pltpu.SemaphoreType.DMA((2 * z.modes,))]

    half_rows = z.chips * z.cells

    sent = whole_call(
        depth_forward, z, 1500, payload,
        [cells_scratch, field_scratch, pltpu.VMEM(forward_first.shape, BF16), pltpu.SemaphoreType.DMA((2,))],
        field, forward_first, specs=[HBM] * 2,
    )
    own = exchange(sent)
    weight_here = pltpu.VMEM(pointwise_weight.shape, BF16)
    turned, plane, plane_back, local, cot_cells = whole_call(
        prepare, z, 5000,
        (
            shape_of((z.modes, z.channels, z.rows, 2 * z.half)),
            shape_of((2 * half_rows, 4 * z.half)),
            shape_of((half_rows, 8 * z.half)),
            shape_of(cells_shape),
            shape_of(cells_shape),
        ),
        [
            weight_scratch[0], cells_scratch, field_scratch, field_scratch, weight_here,
            pltpu.VMEM(channel_bias.shape, F32), weight_scratch[1], pltpu.SemaphoreType.DMA((7,)),
        ],
        native.reshape(weight_shape), sent, jnp.asarray(plane_tables(z)), field, cotangent, pointwise_weight, channel_bias,
        specs=[HBM, ANYWHERE] + [HBM] * 5, room=24,
    )
    own, turned, plane, plane_back, local, cot_cells = lax.optimization_barrier(
        (own, turned, plane, plane_back, local, cot_cells)
    )
    other = other_core(own)
    inverse_here, forward_here = whole_call(
        fetch_tables, z, 1000, (shape_of(inverse_first.shape), shape_of(forward_back.shape, BF16)),
        [pltpu.SemaphoreType.DMA((2,))],
        inverse_first, forward_back, own, specs=[HBM, HBM, ANYWHERE],
    )
    other, inverse_here, forward_here = lax.optimization_barrier((other, inverse_here, forward_here))
    spectra, mixed = whole_call(
        mix_forward, z, 1000, (shape_of(spectra_shape), shape_of(spectra_shape)), [], own, other, plane, turned
    )
    sent = whole_call(plane_cells, z, 1000, payload, [spread_scratch], mixed, other_core(mixed), plane_back)
    pre, signal, sent = whole_call(
        activate, z, 2000,
        (shape_of(cells_shape), shape_of(cells_shape, BF16), payload), [spectrum_scratch],
        exchange(sent), local, cot_cells, inverse_here, forward_here,
    )
    own = exchange(sent)
    back, mixed = whole_call(
        mix_back, z, 1000, (shape_of((z.modes, z.rows, 2 * z.half)), shape_of(spectra_shape)), [spectra_scratch],
        own, other_core(own), plane, turned,
    )
    sent = whole_call(plane_cells, z, 1000, payload, [spread_scratch], mixed, other_core(mixed), plane_back)
    sent, back, spectra, pre, signal = lax.optimization_barrier((sent, back, spectra, pre, signal))
    returned = exchange(sent)
    gradient = whole_call(
        grad_weights, z, 5000, shape_of(weight_shape),
        [weight_scratch[0], spectra_scratch, spectra_scratch, weight_scratch[1]],
        spectra, back, out_specs=HBM, room=28,
    )
    layer_out, local, inverse_here = whole_call(
        emit, z, 1500,
        (shape_of(field.shape, BF16), shape_of(cells_shape), shape_of(inverse_back.shape)),
        [weight_here, pltpu.SemaphoreType.DMA((2,))],
        pre, signal, pointwise_weight, inverse_back, specs=[VMEM, VMEM, HBM, HBM],
    )
    returned, gradient, layer_out, local, inverse_here = lax.optimization_barrier(
        (returned, gradient, layer_out, local, inverse_here)
    )
    grad_field = whole_call(
        finish, z, 1000, shape_of(field.shape, BF16), [spectrum_scratch], returned, local, inverse_here
    )
    return (layer_out, grad_field, jnp.transpose(gradient.reshape(native.shape), (0, 1, 2, 5, 3, 4)))


def solution(mesh):
    return jax.shard_map(
        on_device,
        mesh=mesh,
        in_specs=(
            P(None, "gx", "gy", None),
            P(None, "gx", "gy", None),
            P("gx", None, None, None, "gy", None),
            P(),
            P(),
        ),
        out_specs=(
            P(None, "gx", "gy", None),
            P(None, "gx", "gy", None),
            P("gx", None, None, None, "gy", None),
        ),
        check_vma=False,
    )
```

```python
import math

import jax
import jax.numpy as jnp
import ml_dtypes
import numpy as np
from jax import lax
from jax.experimental import pallas as pl
from jax.experimental.pallas import tpu as pltpu
from jax.sharding import PartitionSpec as P

KZ = 16
KT = 4
NT = 16
LANES = 128
EXACT = lax.Precision.HIGHEST
F32 = jnp.float32
BF16 = jnp.bfloat16


def round_up(value, step):
    return -(-value // step) * step


def frequencies(kept):
    index = np.arange(kept)
    return np.where(index < kept // 2, index, index - kept)


def depth_time_table(cells):
    depth_cells = cells // NT
    depth = np.arange(depth_cells)[:, None, None, None] * frequencies(KZ)[None, None, :, None] * NT
    time = np.arange(NT)[None, :, None, None] * np.arange(KT)[None, None, None, :] * depth_cells
    phase = np.mod(depth + time, cells).reshape(cells, KZ * KT)
    angles = phase.astype(np.float32) * np.float32(2.0 * math.pi / cells)
    factor = np.float32(1.0 / math.sqrt(cells))
    return np.stack([np.cos(angles) * factor, -np.sin(angles) * factor], axis=1).astype(np.float32)


def plane_tables(sizes):
    length_x, length_y = sizes.nx * sizes.cells_x, sizes.ny * sizes.cells_y
    phase_x = np.mod(np.arange(length_x)[:, None] * frequencies(sizes.kept_x), length_x) / length_x
    phase_y = np.mod(np.arange(length_y)[:, None] * frequencies(sizes.kept_y), length_y) / length_y
    angle = 2.0 * math.pi * (phase_x[:, None, :, None] + phase_y[None, :, None, :])
    scale = 1.0 / math.sqrt(length_x * length_y)
    cosine, sine = np.cos(angle) * scale, np.sin(angle) * scale
    parts = np.stack([np.stack([cosine, -sine]), np.stack([sine, cosine])])
    parts = parts.reshape(
        2, 2, sizes.nx, sizes.cells_x, sizes.ny // 2, 2, sizes.cells_y, sizes.ny, sizes.kept
    ).transpose(7, 5, 2, 4, 3, 6, 0, 1, 8)
    padded = np.zeros(parts.shape[:-1] + (sizes.half,), np.float32)
    padded[..., : sizes.kept] = parts
    ordered = np.stack([padded[j][[j % 2, 1 - j % 2]] for j in range(sizes.ny)])
    return ordered.reshape(sizes.ny, 2 * sizes.chips * sizes.cells, 4 * sizes.half)


class Sizes:
    def __init__(self, field, weight):
        self.nx, self.ny = lax.axis_size("gx"), lax.axis_size("gy")
        self.channels, self.cells_x, self.cells_y, self.depth = field.shape
        self.modes = weight.shape[0]
        self.local_x, self.kept_y = weight.shape[4:]
        self.kept_x = self.local_x * self.ny
        self.cells = self.cells_x * self.cells_y
        self.chips = self.nx * self.ny // 2
        self.kept = self.local_x * self.kept_y
        self.half = round_up(self.kept, LANES // 2)
        self.flat = 2 * self.channels * self.modes
        self.width = round_up(self.flat, LANES)
        self.all_modes = 2 * self.modes * self.nx
        self.rows = round_up(self.channels, 8)


def gather_cells(source, scratch, sizes):
    for w in range(sizes.channels):
        for x in range(sizes.cells_x):
            first = (w * sizes.cells_x + x) * sizes.cells_y
            scratch[first : first + sizes.cells_y, :] = source[w, x].astype(F32)
    return scratch[...]


def scatter_cells(values, target, sizes):
    for w in range(sizes.channels):
        for x in range(sizes.cells_x):
            first = (w * sizes.cells_x + x) * sizes.cells_y
            target[w, x] = values[first : first + sizes.cells_y, :].astype(target.dtype)


def lane_group(sizes):
    return lax.broadcasted_iota(jnp.int32, (sizes.cells, LANES), 1) // sizes.modes


def send_modes(values, target, sizes):
    group = lane_group(sizes)
    tiles = [values[w * sizes.cells : (w + 1) * sizes.cells, :] for w in range(sizes.channels)]
    for i in range(sizes.nx):
        out = [jnp.zeros((sizes.cells, LANES), F32) for _ in range(sizes.width // LANES)]
        for s in range(2):
            have = (i * 2 + s) * sizes.modes
            for w in range(sizes.channels):
                tile, want = divmod((s * sizes.channels + w) * sizes.modes, LANES)
                moved = tiles[w]
                if want != have:
                    moved = pltpu.roll(moved, (want - have) % LANES, 1)
                out[tile] = jnp.where(group == want // sizes.modes, moved, out[tile])
        for t, value in enumerate(out):
            for y in range(sizes.ny // 2):
                target[i * (sizes.ny // 2) + y, :, t * LANES : (t + 1) * LANES] = value


def receive_modes(source, scratch, sizes):
    group = lane_group(sizes)
    tiles = []
    for i in range(sizes.nx):
        row = []
        for t in range(sizes.width // LANES):
            value = None
            for y in range(sizes.ny // 2):
                part = source[i * (sizes.ny // 2) + y, :, t * LANES : (t + 1) * LANES]
                value = part if value is None else value + part
            row.append(value)
        tiles.append(row)
    for w in range(sizes.channels):
        out = jnp.zeros((sizes.cells, LANES), F32)
        for i in range(sizes.nx):
            for s in range(2):
                want = (i * 2 + s) * sizes.modes
                tile, have = divmod((s * sizes.channels + w) * sizes.modes, LANES)
                moved = tiles[i][tile]
                if want != have:
                    moved = pltpu.roll(moved, (want - have) % LANES, 1)
                out = jnp.where(group == want // sizes.modes, moved, out)
        scratch[w * sizes.cells : (w + 1) * sizes.cells, :] = out
    return scratch[...]


def dot(left, right, **kwargs):
    return jnp.dot(left, right, preferred_element_type=F32, **kwargs)


def fetch(sources, targets, semaphores):
    copies = [pltpu.make_async_copy(*pair, semaphores.at[at]) for at, pair in enumerate(zip(sources, targets))]
    for copy in copies:
        copy.start()
    for copy in copies:
        copy.wait()


def depth_forward(sizes, field, table, out, cells, field_here, table_here, semaphores):
    fetch((field, table), (field_here, table_here), semaphores)
    values = gather_cells(field_here, cells, sizes).astype(BF16)
    send_modes(dot(values, table_here[...]), out, sizes)


def one_hot(rows, columns, step, along_rows):
    row = lax.broadcasted_iota(jnp.int32, (rows, columns), 0)
    column = lax.broadcasted_iota(jnp.int32, (rows, columns), 1)
    same = row // step == column if along_rows else row == column // step
    return jnp.where(same, 1.0, 0.0).astype(BF16)


def cell_mixer(weights, across, sizes):
    count = sizes.channels * sizes.cells
    left = one_hot(count, sizes.channels, sizes.cells, True)
    right = one_hot(sizes.channels, count, sizes.cells, False)
    tall = lax.dot_general(left, weights, (((1,), (1 if across else 0,)), ((), ())), preferred_element_type=F32)
    wide = dot(tall.astype(BF16), right)
    row = lax.broadcasted_iota(jnp.int32, (count, count), 0)
    column = lax.broadcasted_iota(jnp.int32, (count, count), 1)
    same = lax.rem(row, sizes.cells) == lax.rem(column, sizes.cells)
    return jnp.where(same, wide, 0.0).astype(BF16)


def emit(sizes, pre, signal, weight, inverse, layer_out, local, inverse_out, weight_here, semaphores):
    copies = [
        pltpu.make_async_copy(weight, weight_here, semaphores.at[0]),
        pltpu.make_async_copy(inverse, inverse_out, semaphores.at[1]),
    ]
    for copy in copies:
        copy.start()
    scatter_cells(gelu_parts(pre[...])[0], layer_out, sizes)
    copies[0].wait()
    local[...] = dot(cell_mixer(weight_here[...], False, sizes), signal[...])
    copies[1].wait()


def fetch_tables(sizes, inverse, forward, after, inverse_out, forward_out, semaphores):
    del after
    fetch((inverse, forward), (inverse_out, forward_out), semaphores)


def prepare(
    sizes, source, after, tables, field, weight, bias,
    target, table, back, local,
    here, cells, field_here, weight_here, bias_here, semaphores, small,
):
    del after
    place = lax.axis_index("gy")
    pair = place + 1 - 2 * lax.rem(place, 2)
    half_rows, lanes = back.shape[0], table.shape[1]
    moves = (
        (field, field_here),
        (weight, weight_here),
        (bias, bias_here),
        (tables.at[place], table),
        (tables.at[place, pl.ds(0, half_rows)], back.at[:, pl.ds(0, lanes)]),
        (tables.at[pair, pl.ds(half_rows, half_rows)], back.at[:, pl.ds(lanes, lanes)]),
    )
    few = [pltpu.make_async_copy(*move, small.at[at]) for at, move in enumerate(moves)]
    copies = [pltpu.make_async_copy(source.at[at], here.at[at], semaphores.at[at]) for at in range(2 * sizes.modes)]
    for copy in few + copies:
        copy.start()
    if sizes.half > sizes.kept:
        target[...] = jnp.zeros_like(target)
    elif sizes.rows > sizes.channels:
        target[:, :, sizes.channels :, :] = jnp.zeros(
            (sizes.modes, sizes.channels, sizes.rows - sizes.channels, 2 * sizes.half), F32
        )
    for mode in range(sizes.modes):
        for s in range(2):
            copies[2 * mode + s].wait()
        for w in range(sizes.channels):
            blocks = [here[2 * mode + s, w].reshape(sizes.kept, sizes.channels) for s in range(2)]
            if sizes.half == sizes.kept:
                target[mode, w, : sizes.channels, :] = jnp.concatenate(blocks, 0).T
            else:
                for s, block in enumerate(blocks):
                    target[mode, w, : sizes.channels, s * sizes.half : s * sizes.half + sizes.kept] = block.T
    for copy in few:
        copy.wait()
    values = gather_cells(field_here, cells, sizes).astype(BF16)
    spread = one_hot(sizes.channels * sizes.cells, sizes.channels, sizes.cells, True).astype(F32)
    offset = jnp.sum(spread * bias_here[...].reshape(1, sizes.channels), axis=1, keepdims=True)
    local[...] = dot(cell_mixer(weight_here[...], True, sizes), values) + offset


def plane_spectra(sizes, own, other, table, target):
    received = jnp.concatenate(
        [ref[...].reshape(sizes.chips * sizes.cells, sizes.width) for ref in (own, other)], 0
    )
    both = dot(received.T, table[...], precision=EXACT)
    count = sizes.channels * sizes.modes
    target[:count, :] = both[:count, : 2 * sizes.half] + both[count : 2 * count, 2 * sizes.half :]


def plane_cells(sizes, own, other, table, out, spread):
    rows, lanes = own.shape
    spread[...] = jnp.zeros_like(spread)
    for at, ref in enumerate((own, other)):
        for s in range(2):
            first = (at * 2 + s) * lanes
            spread[s * rows : (s + 1) * rows, first : first + lanes] = ref[...]
    cells = lax.dot_general(
        table[...], spread[...], (((1,), (1,)), ((), ())), precision=EXACT, preferred_element_type=F32
    )
    out[...] = cells.reshape(out.shape)


def swap_parts(values, sizes):
    return pltpu.roll(values, sizes.half, 1)


def mode_rows(first, sizes):
    return pl.ds(first, sizes.channels, stride=sizes.modes)


def first_lanes(rows, sizes):
    return lax.broadcasted_iota(jnp.int32, (rows, 2 * sizes.half), 1) < sizes.half


def mix_forward(sizes, own, other, table, weight, spectra, mixed):
    plane_spectra(sizes, own, other, table, spectra)
    real = first_lanes(sizes.rows, sizes)
    for m in range(sizes.modes):
        straight = jnp.zeros((sizes.rows, 2 * sizes.half), F32)
        crossed = jnp.zeros((sizes.rows, 2 * sizes.half), F32)
        for w in range(sizes.channels):
            row = spectra[w * sizes.modes + m : w * sizes.modes + m + 1, :]
            block = weight[m, w]
            straight = straight + row * block
            crossed = crossed + swap_parts(row, sizes) * block
        real_part = straight - swap_parts(straight, sizes)
        imag_part = crossed + swap_parts(crossed, sizes)
        result = jnp.where(real, real_part, imag_part)
        mixed[mode_rows(m, sizes), :] = result[: sizes.channels]


def mix_back(sizes, own, other, table, weight, back, mixed, spectra):
    plane_spectra(sizes, own, other, table, spectra)
    real = first_lanes(sizes.channels, sizes)
    for m in range(sizes.modes):
        rows = spectra[mode_rows(m, sizes), :]
        if sizes.rows > sizes.channels:
            rows = jnp.concatenate([rows, jnp.zeros((sizes.rows - sizes.channels, 2 * sizes.half), F32)], 0)
        back[m] = rows
        turned = swap_parts(rows, sizes)
        straight, crossed = [], []
        for w in range(sizes.channels):
            block = weight[m, w]
            straight.append(jnp.sum(block * rows, axis=0, keepdims=True))
            crossed.append(jnp.sum(block * turned, axis=0, keepdims=True))
        straight = jnp.concatenate(straight, 0)
        crossed = jnp.concatenate(crossed, 0)
        real_part = straight + swap_parts(straight, sizes)
        imag_part = swap_parts(crossed, sizes) - crossed
        mixed[mode_rows(m, sizes), :] = jnp.where(real, real_part, imag_part)


def grad_weights(sizes, spectra, back, target, here, straight, crossed, semaphores):
    values = spectra[...]
    turned = swap_parts(values, sizes)
    real = first_lanes(values.shape[0], sizes)
    straight[...] = jnp.where(real, values, turned)
    crossed[...] = jnp.where(real, turned, -values)
    copies = [pltpu.make_async_copy(here.at[at], target.at[at], semaphores.at[at]) for at in range(2 * sizes.modes)]
    for mode in range(sizes.modes):
        rows = back[mode]
        turned = swap_parts(rows, sizes)
        for w in range(sizes.channels):
            at = slice(w * sizes.modes + mode, w * sizes.modes + mode + 1)
            block = (straight[at, :] * rows + crossed[at, :] * turned).T
            for s in range(2):
                part = block[s * sizes.half : s * sizes.half + sizes.kept, : sizes.channels]
                here[2 * mode + s, w] = part.reshape(sizes.local_x, sizes.kept_y, sizes.channels)
        for s in range(2):
            copies[2 * mode + s].start()
    for copy in copies:
        copy.wait()


def gelu_parts(pre):
    slope = math.sqrt(2.0 / math.pi)
    squared = pre * pre
    bend = jnp.tanh(slope * (pre + 0.044715 * (squared * pre)))
    value = 0.5 * pre * (1.0 + bend)
    derivative = 0.5 * (1.0 + bend) + 0.5 * pre * (1.0 - bend * bend) * (slope * (1.0 + 3.0 * 0.044715 * squared))
    return value, derivative


def activate(sizes, received, local, cotangent, inverse, forward, pre_out, signal_out, out, spectrum, cells, cot_here, semaphore):
    copy = pltpu.make_async_copy(cotangent, cot_here, semaphore.at[0])
    copy.start()
    pre = dot(receive_modes(received, spectrum, sizes), inverse[...], precision=EXACT) + local[...]
    pre_out[...] = pre
    derivative = gelu_parts(pre)[1]
    copy.wait()
    signal = (gather_cells(cot_here, cells, sizes) * derivative).astype(BF16)
    signal_out[...] = signal
    send_modes(dot(signal, forward[...]), out, sizes)


def finish(sizes, received, local, inverse, grad_field, spectrum):
    spatial = dot(receive_modes(received, spectrum, sizes), inverse[...], precision=EXACT)
    scatter_cells(spatial + local[...], grad_field, sizes)


def shape_of(shape, dtype=F32):
    return jax.ShapeDtypeStruct(shape, dtype)


VMEM = pl.BlockSpec(memory_space=pltpu.VMEM)
HBM = pl.BlockSpec(memory_space=pltpu.HBM)
ANYWHERE = pl.BlockSpec(memory_space=pl.ANY)


def settings(mebibytes):
    return pltpu.CompilerParams(vmem_limit_bytes=mebibytes * 1024 * 1024)


def cost(nanoseconds):
    return pl.CostEstimate(flops=0, bytes_accessed=3000 * nanoseconds, transcendentals=0)


def whole_call(body, sizes, nanoseconds, out_shape, scratch, *args, specs=None, out_specs=None, room=16):
    def kernel(*refs):
        body(sizes, *refs)

    if specs:
        args = [
            pltpu.with_memory_space_constraint(arg, pltpu.HBM) if spec is HBM else arg for arg, spec in zip(args, specs)
        ]
    return pl.pallas_call(
        kernel,
        out_shape=out_shape,
        in_specs=specs or [VMEM] * len(args),
        out_specs=out_specs or jax.tree.map(lambda _: VMEM, out_shape),
        scratch_shapes=scratch,
        name=body.__name__,
        cost_estimate=cost(nanoseconds),
        compiler_params=settings(room),
    )(*args)


def on_device(field, cotangent, spectral_weight, pointwise_weight, channel_bias):
    z = Sizes(field, spectral_weight)
    depth_table = depth_time_table(z.depth)
    modes = depth_table.shape[2]
    kappa = np.where(np.arange(modes) % KT == 0, 1.0, 2.0).astype(np.float32)
    ordered = depth_table.reshape(z.depth, 2, z.nx, z.modes).transpose(0, 2, 1, 3).reshape(z.depth, z.all_modes)
    doubled = np.repeat(kappa.reshape(z.nx, 1, z.modes), 2, axis=1).reshape(z.all_modes)
    forward_first = jnp.asarray(ordered.astype(ml_dtypes.bfloat16))
    forward_back = jnp.asarray((ordered.astype(ml_dtypes.bfloat16).astype(np.float32) * doubled).astype(ml_dtypes.bfloat16))
    inverse_back = jnp.asarray(np.ascontiguousarray(ordered.T))
    inverse_first = jnp.asarray(np.ascontiguousarray((ordered * doubled).T))
    groups = [[gx * z.ny + 2 * y + c for gx in range(z.nx) for y in range(z.ny // 2)] for c in range(2)]
    pairs = [(s, s ^ 1) for s in range(z.ny)]

    def exchange(payload):
        return lax.all_to_all(
            payload, ("gx", "gy"), split_axis=0, concat_axis=0, tiled=True, axis_index_groups=groups
        )

    def other_core(payload):
        return lax.ppermute(payload, "gy", pairs)

    payload = shape_of((z.chips, z.cells, z.width))
    cell_rows = z.channels * z.cells
    cells_shape = (cell_rows, z.depth)
    cells_scratch = pltpu.VMEM(cells_shape, F32)
    spectrum_scratch = pltpu.VMEM((cell_rows, z.all_modes), F32)
    spectra_shape = (z.channels * z.modes, 2 * z.half)
    spectra_scratch = pltpu.VMEM(spectra_shape, F32)
    spread_scratch = pltpu.VMEM((z.width, 8 * z.half), F32)
    field_scratch = pltpu.VMEM(field.shape, BF16)

    native = jnp.transpose(spectral_weight, (0, 1, 2, 4, 5, 3))
    weight_shape = (2 * z.modes,) + native.shape[2:]
    weight_scratch = [pltpu.VMEM(weight_shape, F32), pltpu.SemaphoreType.DMA((2 * z.modes,))]

    half_rows = z.chips * z.cells

    sent = whole_call(
        depth_forward, z, 1500, payload,
        [cells_scratch, field_scratch, pltpu.VMEM(forward_first.shape, BF16), pltpu.SemaphoreType.DMA((2,))],
        field, forward_first, specs=[HBM] * 2,
    )
    own = exchange(sent)
    weight_here = pltpu.VMEM(pointwise_weight.shape, BF16)
    turned, plane, plane_back, local = whole_call(
        prepare, z, 5000,
        (
            shape_of((z.modes, z.channels, z.rows, 2 * z.half)),
            shape_of((2 * half_rows, 4 * z.half)),
            shape_of((half_rows, 8 * z.half)),
            shape_of(cells_shape),
        ),
        [
            weight_scratch[0], cells_scratch, field_scratch, weight_here,
            pltpu.VMEM(channel_bias.shape, F32), weight_scratch[1], pltpu.SemaphoreType.DMA((6,)),
        ],
        native.reshape(weight_shape), sent, jnp.asarray(plane_tables(z)), field, pointwise_weight, channel_bias,
        specs=[HBM, ANYWHERE] + [HBM] * 4, room=16,
    )
    own, turned, plane, plane_back, local = lax.optimization_barrier((own, turned, plane, plane_back, local))
    other = other_core(own)
    inverse_here, forward_here = whole_call(
        fetch_tables, z, 1000, (shape_of(inverse_first.shape), shape_of(forward_back.shape, BF16)),
        [pltpu.SemaphoreType.DMA((2,))],
        inverse_first, forward_back, own, specs=[HBM, HBM, ANYWHERE],
    )
    other, inverse_here, forward_here = lax.optimization_barrier((other, inverse_here, forward_here))
    spectra, mixed = whole_call(
        mix_forward, z, 1000, (shape_of(spectra_shape), shape_of(spectra_shape)), [], own, other, plane, turned
    )
    sent = whole_call(plane_cells, z, 1000, payload, [spread_scratch], mixed, other_core(mixed), plane_back)
    pre, signal, sent = whole_call(
        activate, z, 2000,
        (shape_of(cells_shape), shape_of(cells_shape, BF16), payload),
        [spectrum_scratch, cells_scratch, field_scratch, pltpu.SemaphoreType.DMA((1,))],
        exchange(sent), local, cotangent, inverse_here, forward_here, specs=[VMEM, VMEM, HBM, VMEM, VMEM],
    )
    own = exchange(sent)
    back, mixed = whole_call(
        mix_back, z, 1000, (shape_of((z.modes, z.rows, 2 * z.half)), shape_of(spectra_shape)), [spectra_scratch],
        own, other_core(own), plane, turned,
    )
    sent = whole_call(plane_cells, z, 1000, payload, [spread_scratch], mixed, other_core(mixed), plane_back)
    sent, back, spectra, pre, signal = lax.optimization_barrier((sent, back, spectra, pre, signal))
    returned = exchange(sent)
    gradient = whole_call(
        grad_weights, z, 5000, shape_of(weight_shape),
        [weight_scratch[0], spectra_scratch, spectra_scratch, weight_scratch[1]],
        spectra, back, out_specs=HBM, room=28,
    )
    layer_out, local, inverse_here = whole_call(
        emit, z, 1500,
        (shape_of(field.shape, BF16), shape_of(cells_shape), shape_of(inverse_back.shape)),
        [weight_here, pltpu.SemaphoreType.DMA((2,))],
        pre, signal, pointwise_weight, inverse_back, specs=[VMEM, VMEM, HBM, HBM],
    )
    returned, gradient, layer_out, local, inverse_here = lax.optimization_barrier(
        (returned, gradient, layer_out, local, inverse_here)
    )
    grad_field = whole_call(
        finish, z, 1000, shape_of(field.shape, BF16), [spectrum_scratch], returned, local, inverse_here
    )
    return (layer_out, grad_field, jnp.transpose(gradient.reshape(native.shape), (0, 1, 2, 5, 3, 4)))


def solution(mesh):
    return jax.shard_map(
        on_device,
        mesh=mesh,
        in_specs=(
            P(None, "gx", "gy", None),
            P(None, "gx", "gy", None),
            P("gx", None, None, None, "gy", None),
            P(),
            P(),
        ),
        out_specs=(
            P(None, "gx", "gy", None),
            P(None, "gx", "gy", None),
            P("gx", None, None, None, "gy", None),
        ),
        check_vma=False,
    )
```

```python
import math

import jax
import jax.numpy as jnp
import ml_dtypes
import numpy as np
from jax import lax
from jax.experimental import pallas as pl
from jax.experimental.pallas import tpu as pltpu
from jax.sharding import PartitionSpec as P

KZ = 16
KT = 4
NT = 16
LANES = 128
F32 = jnp.float32
BF16 = jnp.bfloat16


def round_up(value, step):
    return -(-value // step) * step


def frequencies(kept):
    index = np.arange(kept)
    return np.where(index < kept // 2, index, index - kept)


def depth_time_table(cells):
    depth_cells = cells // NT
    depth = np.arange(depth_cells)[:, None, None, None] * frequencies(KZ)[None, None, :, None] * NT
    time = np.arange(NT)[None, :, None, None] * np.arange(KT)[None, None, None, :] * depth_cells
    phase = np.mod(depth + time, cells).reshape(cells, KZ * KT)
    angles = phase.astype(np.float32) * np.float32(2.0 * math.pi / cells)
    factor = np.float32(1.0 / math.sqrt(cells))
    return np.stack([np.cos(angles) * factor, -np.sin(angles) * factor], axis=1).astype(np.float32)


def plane_tables(sizes):
    length_x, length_y = sizes.nx * sizes.cells_x, sizes.ny * sizes.cells_y
    phase_x = np.mod(np.arange(length_x)[:, None] * frequencies(sizes.kept_x), length_x) / length_x
    phase_y = np.mod(np.arange(length_y)[:, None] * frequencies(sizes.kept_y), length_y) / length_y
    angle = 2.0 * math.pi * (phase_x[:, None, :, None] + phase_y[None, :, None, :])
    scale = 1.0 / math.sqrt(length_x * length_y)
    cosine, sine = np.cos(angle) * scale, np.sin(angle) * scale
    parts = np.stack([np.stack([cosine, -sine]), np.stack([sine, cosine])])
    parts = parts.reshape(
        2, 2, sizes.nx, sizes.cells_x, sizes.ny // 2, 2, sizes.cells_y, sizes.ny, sizes.kept
    ).transpose(7, 5, 2, 4, 3, 6, 0, 1, 8)
    padded = np.zeros(parts.shape[:-1] + (sizes.half,), np.float32)
    padded[..., : sizes.kept] = parts
    ordered = np.stack([padded[j][[j % 2, 1 - j % 2]] for j in range(sizes.ny)])
    return ordered.reshape(sizes.ny, 2 * sizes.chips * sizes.cells, 4 * sizes.half)


class Sizes:
    def __init__(self, field, weight):
        self.nx, self.ny = lax.axis_size("gx"), lax.axis_size("gy")
        self.channels, self.cells_x, self.cells_y, self.depth = field.shape
        self.modes = weight.shape[0]
        self.local_x, self.kept_y = weight.shape[4:]
        self.kept_x = self.local_x * self.ny
        self.cells = self.cells_x * self.cells_y
        self.chips = self.nx * self.ny // 2
        self.kept = self.local_x * self.kept_y
        self.half = round_up(self.kept, LANES // 2)
        self.all_modes = 2 * self.modes * self.nx
        self.groups = LANES // self.modes
        self.main = self.channels // self.groups * self.groups if self.all_modes == LANES else 0
        self.rest = self.channels - self.main
        self.width = 2 * self.main * self.modes + round_up(2 * self.rest * self.modes, LANES)
        self.rows = round_up(self.channels, 8)


def gather_cells(source, scratch, sizes):
    for w in range(sizes.channels):
        for x in range(sizes.cells_x):
            first = (w * sizes.cells_x + x) * sizes.cells_y
            scratch[first : first + sizes.cells_y, :] = source[w, x].astype(F32)
    return scratch[...]


def scatter_cells(values, target, sizes):
    for w in range(sizes.channels):
        for x in range(sizes.cells_x):
            first = (w * sizes.cells_x + x) * sizes.cells_y
            target[w, x] = values[first : first + sizes.cells_y, :].astype(target.dtype)


def lane_group(sizes):
    return lax.broadcasted_iota(jnp.int32, (sizes.cells, LANES), 1) // sizes.modes


def turn_groups(tiles, group, sizes):
    tiles = list(tiles)
    step = 1
    while step < sizes.groups:
        low = group // step % 2 == 0
        for first in range(sizes.groups):
            if first // step % 2 == 0:
                one, two = tiles[first], tiles[first + step]
                tiles[first] = jnp.where(low, one, pltpu.roll(two, step * sizes.modes, 1))
                tiles[first + step] = jnp.where(low, pltpu.roll(one, LANES - step * sizes.modes, 1), two)
        step *= 2
    return tiles


def put_group(target, source, have, want, group, sizes):
    if have != want:
        source = pltpu.roll(source, (want - have) % sizes.groups * sizes.modes, 1)
    return jnp.where(group == want, source, target)


def send_modes(values, target, sizes):
    group = lane_group(sizes)
    tiles = [values[w * sizes.cells : (w + 1) * sizes.cells, :] for w in range(sizes.channels)]
    blocks = sizes.main // sizes.groups
    turned = [turn_groups(tiles[k * sizes.groups : (k + 1) * sizes.groups], group, sizes) for k in range(blocks)]
    for i in range(sizes.nx):
        out = [turned[k][2 * i + s] for s in range(2) for k in range(blocks)]
        rest = [jnp.zeros((sizes.cells, LANES), F32) for _ in range(sizes.width // LANES - len(out))]
        for s in range(2):
            for r in range(sizes.rest):
                tile, want = divmod(s * sizes.rest + r, sizes.groups)
                rest[tile] = put_group(rest[tile], tiles[sizes.main + r], 2 * i + s, want, group, sizes)
        for t, value in enumerate(out + rest):
            for y in range(sizes.ny // 2):
                target[i * (sizes.ny // 2) + y, :, t * LANES : (t + 1) * LANES] = value


def receive_modes(source, scratch, sizes):
    group = lane_group(sizes)
    tiles = []
    for i in range(sizes.nx):
        row = []
        for t in range(sizes.width // LANES):
            value = None
            for y in range(sizes.ny // 2):
                part = source[i * (sizes.ny // 2) + y, :, t * LANES : (t + 1) * LANES]
                value = part if value is None else value + part
            row.append(value)
        tiles.append(row)
    blocks = sizes.main // sizes.groups
    out = []
    for k in range(blocks):
        out += turn_groups([tiles[i][s * blocks + k] for i in range(sizes.nx) for s in range(2)], group, sizes)
    for r in range(sizes.rest):
        value = jnp.zeros((sizes.cells, LANES), F32)
        for i in range(sizes.nx):
            for s in range(2):
                tile, have = divmod(s * sizes.rest + r, sizes.groups)
                value = put_group(value, tiles[i][2 * blocks + tile], have, 2 * i + s, group, sizes)
        out.append(value)
    for w, value in enumerate(out):
        scratch[w * sizes.cells : (w + 1) * sizes.cells, :] = value
    return scratch[...]


def dot(left, right, contract=((1,), (0,))):
    return lax.dot_general(left, right, (contract, ((), ())), preferred_element_type=F32)


def halves(values):
    high = values.astype(BF16)
    return high, (values - high.astype(F32)).astype(BF16)


def fine_dot(left, right, contract=((1,), (0,))):
    left_high, left_low = halves(left)
    right_high, right_low = halves(right)
    small = dot(left_high, right_low, contract) + dot(left_low, right_high, contract)
    return dot(left_high, right_high, contract) + small


def fetch(sources, targets, semaphores):
    copies = [pltpu.make_async_copy(*pair, semaphores.at[at]) for at, pair in enumerate(zip(sources, targets))]
    for copy in copies:
        copy.start()
    for copy in copies:
        copy.wait()


def depth_forward(sizes, field, table, out, cells, field_here, table_here, semaphores):
    fetch((field, table), (field_here, table_here), semaphores)
    values = gather_cells(field_here, cells, sizes).astype(BF16)
    send_modes(dot(values, table_here[...]), out, sizes)


def one_hot(rows, columns, step, along_rows):
    row = lax.broadcasted_iota(jnp.int32, (rows, columns), 0)
    column = lax.broadcasted_iota(jnp.int32, (rows, columns), 1)
    same = row // step == column if along_rows else row == column // step
    return jnp.where(same, 1.0, 0.0).astype(BF16)


def cell_mixer(weights, across, sizes):
    count = sizes.channels * sizes.cells
    left = one_hot(count, sizes.channels, sizes.cells, True)
    right = one_hot(sizes.channels, count, sizes.cells, False)
    tall = dot(left, weights, ((1,), (1 if across else 0,)))
    wide = dot(tall.astype(BF16), right)
    row = lax.broadcasted_iota(jnp.int32, (count, count), 0)
    column = lax.broadcasted_iota(jnp.int32, (count, count), 1)
    same = lax.rem(row, sizes.cells) == lax.rem(column, sizes.cells)
    return jnp.where(same, wide, 0.0).astype(BF16)


def emit(sizes, pre, signal, weight, inverse, layer_out, local, inverse_out, weight_here, semaphores):
    copies = [
        pltpu.make_async_copy(weight, weight_here, semaphores.at[0]),
        pltpu.make_async_copy(inverse, inverse_out, semaphores.at[1]),
    ]
    for copy in copies:
        copy.start()
    scatter_cells(gelu_parts(pre[...])[0], layer_out, sizes)
    copies[0].wait()
    local[...] = dot(cell_mixer(weight_here[...], False, sizes), signal[...])
    copies[1].wait()


def fetch_tables(sizes, inverse, forward, after, inverse_out, forward_out, semaphores):
    del after
    fetch((inverse, forward), (inverse_out, forward_out), semaphores)


def prepare(
    sizes, source, after, tables, field, weight, bias,
    target, table, back, local,
    here, cells, field_here, weight_here, bias_here, semaphores, small,
):
    del after
    place = lax.axis_index("gy")
    pair = place + 1 - 2 * lax.rem(place, 2)
    half_rows, lanes = back.shape[0] // 2, table.shape[1] // 2
    moves = (
        (field, field_here),
        (weight, weight_here),
        (bias, bias_here),
        (tables.at[place], table),
    )
    for s in range(2):
        for owner, first in ((place, 0), (pair, 1)):
            source_lanes, rows = pl.ds(s * lanes, lanes), pl.ds(first * half_rows, half_rows)
            moves += (
                (
                    tables.at[owner, rows, source_lanes],
                    back.at[pl.ds(s * half_rows, half_rows), pl.ds(first * lanes, lanes)],
                ),
            )
    few = [pltpu.make_async_copy(*move, small.at[at]) for at, move in enumerate(moves)]
    copies = [pltpu.make_async_copy(source.at[at], here.at[at], semaphores.at[at]) for at in range(2 * sizes.modes)]
    for copy in few + copies:
        copy.start()
    if sizes.half > sizes.kept:
        target[...] = jnp.zeros_like(target)
    elif sizes.rows > sizes.channels:
        target[:, :, sizes.channels :, :] = jnp.zeros(
            (sizes.modes, sizes.channels, sizes.rows - sizes.channels, 2 * sizes.half), F32
        )
    for mode in range(sizes.modes):
        for s in range(2):
            copies[2 * mode + s].wait()
        for w in range(sizes.channels):
            blocks = [here[2 * mode + s, w].reshape(sizes.kept, sizes.channels) for s in range(2)]
            if sizes.half == sizes.kept:
                target[mode, w, : sizes.channels, :] = jnp.concatenate(blocks, 0).T
            else:
                for s, block in enumerate(blocks):
                    target[mode, w, : sizes.channels, s * sizes.half : s * sizes.half + sizes.kept] = block.T
    for copy in few:
        copy.wait()
    values = gather_cells(field_here, cells, sizes).astype(BF16)
    spread = one_hot(sizes.channels * sizes.cells, sizes.channels, sizes.cells, True).astype(F32)
    offset = jnp.sum(spread * bias_here[...].reshape(1, sizes.channels), axis=1, keepdims=True)
    local[...] = dot(cell_mixer(weight_here[...], True, sizes), values) + offset


def plane_spectra(sizes, own, other, table, target):
    received = jnp.concatenate(
        [ref[...].reshape(sizes.chips * sizes.cells, sizes.width) for ref in (own, other)], 0
    )
    both = fine_dot(received.T, table[...])
    lanes = 2 * sizes.half
    first, to = 0, 0
    for count in (sizes.main * sizes.modes, sizes.rest * sizes.modes):
        if count:
            middle = first + count
            target[to : to + count, :] = both[first:middle, :lanes] + both[middle : middle + count, lanes:]
            first, to = middle + count, to + count


def plane_cells(sizes, own, other, table, out):
    modes = jnp.concatenate([own[...], other[...]], 1)
    cells = fine_dot(table[...], modes, ((1,), (1,)))
    count = sizes.chips * sizes.cells
    parts = [cells[:count], cells[count:]]
    main = sizes.main * sizes.modes
    if main:
        for s, part in enumerate(parts):
            out[:, :, s * main : (s + 1) * main] = part[:, :main].reshape(sizes.chips, sizes.cells, main)
    if sizes.rest:
        filler = jnp.zeros((count, sizes.width - 2 * sizes.channels * sizes.modes), F32)
        rest = jnp.concatenate([part[:, main:] for part in parts] + [filler], 1)
        out[:, :, 2 * main :] = rest.reshape(sizes.chips, sizes.cells, sizes.width - 2 * main)


def swap_parts(values, sizes):
    return pltpu.roll(values, sizes.half, 1)


def mode_rows(first, sizes):
    return pl.ds(first, sizes.channels, stride=sizes.modes)


def first_lanes(rows, sizes):
    return lax.broadcasted_iota(jnp.int32, (rows, 2 * sizes.half), 1) < sizes.half


def mix_forward(sizes, own, other, table, weight, spectra, mixed, swapped):
    plane_spectra(sizes, own, other, table, spectra)
    swapped[...] = swap_parts(spectra[...], sizes)
    real = first_lanes(sizes.rows, sizes)
    for m in range(sizes.modes):
        straight = jnp.zeros((sizes.rows, 2 * sizes.half), F32)
        crossed = jnp.zeros((sizes.rows, 2 * sizes.half), F32)
        for w in range(sizes.channels):
            at = slice(w * sizes.modes + m, w * sizes.modes + m + 1)
            block = weight[m, w]
            straight = straight + spectra[at, :] * block
            crossed = crossed + swapped[at, :] * block
        real_part = straight - swap_parts(straight, sizes)
        imag_part = crossed + swap_parts(crossed, sizes)
        result = jnp.where(real, real_part, imag_part)
        mixed[mode_rows(m, sizes), :] = result[: sizes.channels]


def mix_back(sizes, own, other, table, weight, back, mixed, spectra):
    plane_spectra(sizes, own, other, table, spectra)
    real = first_lanes(sizes.channels, sizes)
    for m in range(sizes.modes):
        rows = spectra[mode_rows(m, sizes), :]
        if sizes.rows > sizes.channels:
            rows = jnp.concatenate([rows, jnp.zeros((sizes.rows - sizes.channels, 2 * sizes.half), F32)], 0)
        back[m] = rows
        turned = swap_parts(rows, sizes)
        straight, crossed = [], []
        for w in range(sizes.channels):
            block = weight[m, w]
            straight.append(jnp.sum(block * rows, axis=0, keepdims=True))
            crossed.append(jnp.sum(block * turned, axis=0, keepdims=True))
        straight = jnp.concatenate(straight, 0)
        crossed = jnp.concatenate(crossed, 0)
        real_part = straight + swap_parts(straight, sizes)
        imag_part = swap_parts(crossed, sizes) - crossed
        mixed[mode_rows(m, sizes), :] = jnp.where(real, real_part, imag_part)


def grad_weights(sizes, spectra, back, target, here, straight, crossed, semaphores):
    values = spectra[...]
    turned = swap_parts(values, sizes)
    real = first_lanes(values.shape[0], sizes)
    straight[...] = jnp.where(real, values, turned)
    crossed[...] = jnp.where(real, turned, -values)
    copies = [pltpu.make_async_copy(here.at[at], target.at[at], semaphores.at[at]) for at in range(2 * sizes.modes)]
    for mode in range(sizes.modes):
        rows = back[mode]
        turned = swap_parts(rows, sizes)
        for w in range(sizes.channels):
            at = slice(w * sizes.modes + mode, w * sizes.modes + mode + 1)
            block = (straight[at, :] * rows + crossed[at, :] * turned).T
            for s in range(2):
                part = block[s * sizes.half : s * sizes.half + sizes.kept, : sizes.channels]
                here[2 * mode + s, w] = part.reshape(sizes.local_x, sizes.kept_y, sizes.channels)
        for s in range(2):
            copies[2 * mode + s].start()
    for copy in copies:
        copy.wait()


def gelu_parts(pre):
    slope = math.sqrt(2.0 / math.pi)
    squared = pre * pre
    bend = jnp.tanh(slope * (pre + 0.044715 * (squared * pre)))
    value = 0.5 * pre * (1.0 + bend)
    derivative = 0.5 * (1.0 + bend) + 0.5 * pre * (1.0 - bend * bend) * (slope * (1.0 + 3.0 * 0.044715 * squared))
    return value, derivative


def activate(sizes, received, local, cotangent, inverse, forward, pre_out, signal_out, out, spectrum, cells, cot_here, semaphore):
    copy = pltpu.make_async_copy(cotangent, cot_here, semaphore.at[0])
    copy.start()
    pre = fine_dot(receive_modes(received, spectrum, sizes), inverse[...]) + local[...]
    pre_out[...] = pre
    derivative = gelu_parts(pre)[1]
    copy.wait()
    signal = (gather_cells(cot_here, cells, sizes) * derivative).astype(BF16)
    signal_out[...] = signal
    send_modes(dot(signal, forward[...]), out, sizes)


def finish(sizes, received, local, inverse, grad_field, spectrum):
    spatial = fine_dot(receive_modes(received, spectrum, sizes), inverse[...])
    scatter_cells(spatial + local[...], grad_field, sizes)


def shape_of(shape, dtype=F32):
    return jax.ShapeDtypeStruct(shape, dtype)


VMEM = pl.BlockSpec(memory_space=pltpu.VMEM)
HBM = pl.BlockSpec(memory_space=pltpu.HBM)
ANYWHERE = pl.BlockSpec(memory_space=pl.ANY)


def settings(mebibytes):
    return pltpu.CompilerParams(vmem_limit_bytes=mebibytes * 1024 * 1024)


def cost(nanoseconds):
    return pl.CostEstimate(flops=0, bytes_accessed=3000 * nanoseconds, transcendentals=0)


def whole_call(body, sizes, nanoseconds, out_shape, scratch, *args, specs=None, out_specs=None, room=16):
    def kernel(*refs):
        body(sizes, *refs)

    if specs:
        args = [
            pltpu.with_memory_space_constraint(arg, pltpu.HBM) if spec is HBM else arg for arg, spec in zip(args, specs)
        ]
    return pl.pallas_call(
        kernel,
        out_shape=out_shape,
        in_specs=specs or [VMEM] * len(args),
        out_specs=out_specs or jax.tree.map(lambda _: VMEM, out_shape),
        scratch_shapes=scratch,
        name=body.__name__,
        cost_estimate=cost(nanoseconds),
        compiler_params=settings(room),
    )(*args)


def on_device(field, cotangent, spectral_weight, pointwise_weight, channel_bias):
    z = Sizes(field, spectral_weight)
    depth_table = depth_time_table(z.depth)
    modes = depth_table.shape[2]
    kappa = np.where(np.arange(modes) % KT == 0, 1.0, 2.0).astype(np.float32)
    ordered = depth_table.reshape(z.depth, 2, z.nx, z.modes).transpose(0, 2, 1, 3).reshape(z.depth, z.all_modes)
    doubled = np.repeat(kappa.reshape(z.nx, 1, z.modes), 2, axis=1).reshape(z.all_modes)
    forward_first = jnp.asarray(ordered.astype(ml_dtypes.bfloat16))
    forward_back = jnp.asarray((ordered.astype(ml_dtypes.bfloat16).astype(np.float32) * doubled).astype(ml_dtypes.bfloat16))
    inverse_back = jnp.asarray(np.ascontiguousarray(ordered.T))
    inverse_first = jnp.asarray(np.ascontiguousarray((ordered * doubled).T))
    groups = [[gx * z.ny + 2 * y + c for gx in range(z.nx) for y in range(z.ny // 2)] for c in range(2)]
    pairs = [(s, s ^ 1) for s in range(z.ny)]

    def exchange(payload):
        return lax.all_to_all(
            payload, ("gx", "gy"), split_axis=0, concat_axis=0, tiled=True, axis_index_groups=groups
        )

    def other_core(payload):
        return lax.ppermute(payload, "gy", pairs)

    payload = shape_of((z.chips, z.cells, z.width))
    cell_rows = z.channels * z.cells
    cells_shape = (cell_rows, z.depth)
    cells_scratch = pltpu.VMEM(cells_shape, F32)
    spectrum_scratch = pltpu.VMEM((cell_rows, z.all_modes), F32)
    spectra_shape = (z.channels * z.modes, 2 * z.half)
    spectra_scratch = pltpu.VMEM(spectra_shape, F32)
    field_scratch = pltpu.VMEM(field.shape, BF16)

    native = jnp.transpose(spectral_weight, (0, 1, 2, 4, 5, 3))
    weight_shape = (2 * z.modes,) + native.shape[2:]
    weight_scratch = [pltpu.VMEM(weight_shape, F32), pltpu.SemaphoreType.DMA((2 * z.modes,))]

    half_rows = z.chips * z.cells

    sent = whole_call(
        depth_forward, z, 1500, payload,
        [cells_scratch, field_scratch, pltpu.VMEM(forward_first.shape, BF16), pltpu.SemaphoreType.DMA((2,))],
        field, forward_first, specs=[HBM] * 2,
    )
    own = exchange(sent)
    weight_here = pltpu.VMEM(pointwise_weight.shape, BF16)
    turned, plane, plane_back, local = whole_call(
        prepare, z, 5000,
        (
            shape_of((z.modes, z.channels, z.rows, 2 * z.half)),
            shape_of((2 * half_rows, 4 * z.half)),
            shape_of((2 * half_rows, 4 * z.half)),
            shape_of(cells_shape),
        ),
        [
            weight_scratch[0], cells_scratch, field_scratch, weight_here,
            pltpu.VMEM(channel_bias.shape, F32), weight_scratch[1], pltpu.SemaphoreType.DMA((8,)),
        ],
        native.reshape(weight_shape), sent, jnp.asarray(plane_tables(z)), field, pointwise_weight, channel_bias,
        specs=[HBM, ANYWHERE] + [HBM] * 4, room=16,
    )
    own, turned, plane, plane_back, local = lax.optimization_barrier((own, turned, plane, plane_back, local))
    other = other_core(own)
    inverse_here, forward_here = whole_call(
        fetch_tables, z, 1000, (shape_of(inverse_first.shape), shape_of(forward_back.shape, BF16)),
        [pltpu.SemaphoreType.DMA((2,))],
        inverse_first, forward_back, own, specs=[HBM, HBM, ANYWHERE],
    )
    other, inverse_here, forward_here = lax.optimization_barrier((other, inverse_here, forward_here))
    spectra, mixed = whole_call(
        mix_forward, z, 1000, (shape_of(spectra_shape), shape_of(spectra_shape)), [spectra_scratch], own, other, plane, turned
    )
    sent = whole_call(plane_cells, z, 1000, payload, [], mixed, other_core(mixed), plane_back)
    pre, signal, sent = whole_call(
        activate, z, 2000,
        (shape_of(cells_shape), shape_of(cells_shape, BF16), payload),
        [spectrum_scratch, cells_scratch, field_scratch, pltpu.SemaphoreType.DMA((1,))],
        exchange(sent), local, cotangent, inverse_here, forward_here, specs=[VMEM, VMEM, HBM, VMEM, VMEM],
    )
    own = exchange(sent)
    back, mixed = whole_call(
        mix_back, z, 1000, (shape_of((z.modes, z.rows, 2 * z.half)), shape_of(spectra_shape)), [spectra_scratch],
        own, other_core(own), plane, turned,
    )
    sent = whole_call(plane_cells, z, 1000, payload, [], mixed, other_core(mixed), plane_back)
    sent, back, spectra, pre, signal = lax.optimization_barrier((sent, back, spectra, pre, signal))
    returned = exchange(sent)
    gradient = whole_call(
        grad_weights, z, 5000, shape_of(weight_shape),
        [weight_scratch[0], spectra_scratch, spectra_scratch, weight_scratch[1]],
        spectra, back, out_specs=HBM, room=28,
    )
    layer_out, local, inverse_here = whole_call(
        emit, z, 1500,
        (shape_of(field.shape, BF16), shape_of(cells_shape), shape_of(inverse_back.shape)),
        [weight_here, pltpu.SemaphoreType.DMA((2,))],
        pre, signal, pointwise_weight, inverse_back, specs=[VMEM, VMEM, HBM, HBM],
    )
    returned, gradient, layer_out, local, inverse_here = lax.optimization_barrier(
        (returned, gradient, layer_out, local, inverse_here)
    )
    grad_field = whole_call(
        finish, z, 1000, shape_of(field.shape, BF16), [spectrum_scratch], returned, local, inverse_here
    )
    return (layer_out, grad_field, jnp.transpose(gradient.reshape(native.shape), (0, 1, 2, 5, 3, 4)))


def solution(mesh):
    return jax.shard_map(
        on_device,
        mesh=mesh,
        in_specs=(
            P(None, "gx", "gy", None),
            P(None, "gx", "gy", None),
            P("gx", None, None, None, "gy", None),
            P(),
            P(),
        ),
        out_specs=(
            P(None, "gx", "gy", None),
            P(None, "gx", "gy", None),
            P("gx", None, None, None, "gy", None),
        ),
        check_vma=False,
    )
```

```python
import math

import jax
import jax.numpy as jnp
import ml_dtypes
import numpy as np
from jax import lax
from jax.experimental import pallas as pl
from jax.experimental.pallas import tpu as pltpu
from jax.sharding import PartitionSpec as P

KZ = 16
KT = 4
NT = 16
LANES = 128
F32 = jnp.float32
BF16 = jnp.bfloat16


def round_up(value, step):
    return -(-value // step) * step


def frequencies(kept):
    index = np.arange(kept)
    return np.where(index < kept // 2, index, index - kept)


def depth_time_table(cells):
    depth_cells = cells // NT
    depth = np.arange(depth_cells)[:, None, None, None] * frequencies(KZ)[None, None, :, None] * NT
    time = np.arange(NT)[None, :, None, None] * np.arange(KT)[None, None, None, :] * depth_cells
    phase = np.mod(depth + time, cells).reshape(cells, KZ * KT)
    angles = phase.astype(np.float32) * np.float32(2.0 * math.pi / cells)
    factor = np.float32(1.0 / math.sqrt(cells))
    return np.stack([np.cos(angles) * factor, -np.sin(angles) * factor], axis=1).astype(np.float32)


def plane_tables(sizes):
    length_x, length_y = sizes.nx * sizes.cells_x, sizes.ny * sizes.cells_y
    phase_x = np.mod(np.arange(length_x)[:, None] * frequencies(sizes.kept_x), length_x) / length_x
    phase_y = np.mod(np.arange(length_y)[:, None] * frequencies(sizes.kept_y), length_y) / length_y
    angle = 2.0 * math.pi * (phase_x[:, None, :, None] + phase_y[None, :, None, :])
    scale = 1.0 / math.sqrt(length_x * length_y)
    cosine, sine = np.cos(angle) * scale, np.sin(angle) * scale
    parts = np.stack([np.stack([cosine, -sine]), np.stack([sine, cosine])])
    parts = parts.reshape(
        2, 2, sizes.nx, sizes.cells_x, sizes.ny, sizes.cells_y, sizes.ny, sizes.kept
    ).transpose(6, 3, 2, 4, 5, 0, 1, 7)
    padded = np.zeros(parts.shape[:-1] + (sizes.half,), np.float32)
    padded[..., : sizes.kept] = parts
    return padded.reshape(sizes.ny, sizes.devices * sizes.cells, 4 * sizes.half)


class Sizes:
    def __init__(self, field, weight):
        self.nx, self.ny = lax.axis_size("gx"), lax.axis_size("gy")
        self.channels, self.cells_x, self.cells_y, self.depth = field.shape
        self.modes = weight.shape[0]
        self.local_x, self.kept_y = weight.shape[4:]
        self.kept_x = self.local_x * self.ny
        self.cells = self.cells_x * self.cells_y
        self.devices = self.nx * self.ny
        self.share = self.modes // 2
        self.kept = self.local_x * self.kept_y
        self.half = round_up(self.kept, LANES // 2)
        self.all_modes = 2 * self.modes * self.nx
        self.groups = LANES // self.modes
        self.main = self.channels // self.groups * self.groups if self.all_modes == LANES else 0
        self.rest = self.channels - self.main
        self.main_lanes = self.main * self.modes
        self.rest_lanes = self.rest * self.modes
        self.rest_tiles = round_up(self.rest_lanes, LANES) // LANES
        self.rest_first = self.cells_x * self.main_lanes
        self.width = self.rest_first + round_up(self.cells_x * self.rest_lanes, LANES)
        self.rows = round_up(self.channels, 8)


def gather_cells(source, scratch, sizes):
    for w in range(sizes.channels):
        for x in range(sizes.cells_x):
            first = (w * sizes.cells_x + x) * sizes.cells_y
            scratch[first : first + sizes.cells_y, :] = source[w, x].astype(F32)
    return scratch[...]


def scatter_cells(values, target, sizes):
    for w in range(sizes.channels):
        for x in range(sizes.cells_x):
            first = (w * sizes.cells_x + x) * sizes.cells_y
            target[w, x] = values[first : first + sizes.cells_y, :].astype(target.dtype)


def lane_group(sizes):
    return lax.broadcasted_iota(jnp.int32, (sizes.cells, LANES), 1) // sizes.modes


def turn_groups(tiles, group, sizes):
    tiles = list(tiles)
    step = 1
    while step < sizes.groups:
        low = group // step % 2 == 0
        for first in range(sizes.groups):
            if first // step % 2 == 0:
                one, two = tiles[first], tiles[first + step]
                tiles[first] = jnp.where(low, one, pltpu.roll(two, step * sizes.modes, 1))
                tiles[first + step] = jnp.where(low, pltpu.roll(one, LANES - step * sizes.modes, 1), two)
        step *= 2
    return tiles


def put_group(target, source, have, want, group, sizes):
    if have != want:
        source = pltpu.roll(source, (want - have) % sizes.groups * sizes.modes, 1)
    return jnp.where(group == want, source, target)


def send_modes(values, target, sizes):
    group = lane_group(sizes)
    tiles = [values[w * sizes.cells : (w + 1) * sizes.cells, :] for w in range(sizes.channels)]
    turned = []
    for first in range(0, sizes.main, sizes.groups):
        turned.append(turn_groups(tiles[first : first + sizes.groups], group, sizes))
    for at in range(2 * sizes.nx):
        main = [block[at] for block in turned]
        rest = [jnp.zeros((sizes.cells, LANES), F32) for _ in range(sizes.rest_tiles)]
        for r in range(sizes.rest):
            tile, want = divmod(r, sizes.groups)
            rest[tile] = put_group(rest[tile], tiles[sizes.main + r], at, want, group, sizes)
        last = []
        for x in range(sizes.cells_x):
            rows = slice(x * sizes.cells_y, (x + 1) * sizes.cells_y)
            for k, value in enumerate(main):
                lanes = slice(x * sizes.main_lanes + k * LANES, x * sizes.main_lanes + (k + 1) * LANES)
                for y in range(sizes.ny // 2):
                    target[at // 2 * sizes.ny + 2 * y + at % 2, :, lanes] = value[rows]
            if rest:
                last.append(jnp.concatenate([value[rows] for value in rest], 1)[:, : sizes.rest_lanes])
        if rest:
            used = sizes.rest_first + sizes.cells_x * sizes.rest_lanes
            if sizes.width > used:
                last.append(jnp.zeros((sizes.cells_y, sizes.width - used), F32))
            last = jnp.concatenate(last, 1)
            for y in range(sizes.ny // 2):
                target[at // 2 * sizes.ny + 2 * y + at % 2, :, sizes.rest_first :] = last


def receive_modes(source, scratch, sizes):
    group = lane_group(sizes)
    parts = source[...].reshape(sizes.nx, sizes.ny // 2, 2, sizes.cells_y, sizes.width)
    values = parts[:, 0]
    for y in range(1, sizes.ny // 2):
        values = values + parts[:, y]
    values = values.reshape(2 * sizes.nx, sizes.cells_y, sizes.width)
    out = []
    for k in range(sizes.main // sizes.groups):
        firsts = [x * sizes.main_lanes + k * LANES for x in range(sizes.cells_x)]
        tall = jnp.concatenate([values[:, :, first : first + LANES] for first in firsts], 1)
        out += turn_groups([tall[at] for at in range(2 * sizes.nx)], group, sizes)
    if sizes.rest:
        firsts = [sizes.rest_first + x * sizes.rest_lanes for x in range(sizes.cells_x)]
        tall = jnp.concatenate([values[:, :, first : first + sizes.rest_lanes] for first in firsts], 1)
        filler = sizes.rest_tiles * LANES - sizes.rest_lanes
        if filler:
            tall = jnp.concatenate([tall, jnp.zeros(tall.shape[:2] + (filler,), F32)], 2)
        for r in range(sizes.rest):
            value = jnp.zeros((sizes.cells, LANES), F32)
            tile, have = divmod(r, sizes.groups)
            for at in range(2 * sizes.nx):
                source_tile = tall[at, :, tile * LANES : (tile + 1) * LANES]
                value = put_group(value, source_tile, have, at, group, sizes)
            out.append(value)
    for w, value in enumerate(out):
        scratch[w * sizes.cells : (w + 1) * sizes.cells, :] = value
    return scratch[...]


def dot(left, right, contract=((1,), (0,))):
    return lax.dot_general(left, right, (contract, ((), ())), preferred_element_type=F32)


def halves(values):
    high = values.astype(BF16)
    return high, (values - high.astype(F32)).astype(BF16)


def fine_dot(left, right, contract=((1,), (0,))):
    left_high, left_low = halves(left)
    right_high, right_low = halves(right)
    small = dot(left_high, right_low, contract) + dot(left_low, right_high, contract)
    return dot(left_high, right_high, contract) + small


def fetch(sources, targets, semaphores):
    copies = [pltpu.make_async_copy(*pair, semaphores.at[at]) for at, pair in enumerate(zip(sources, targets))]
    for copy in copies:
        copy.start()
    for copy in copies:
        copy.wait()


def depth_forward(sizes, field, table, out, cells, field_here, table_here, semaphores):
    fetch((field, table), (field_here, table_here), semaphores)
    values = gather_cells(field_here, cells, sizes).astype(BF16)
    send_modes(dot(values, table_here[...]), out, sizes)


def one_hot(rows, columns, step, along_rows):
    row = lax.broadcasted_iota(jnp.int32, (rows, columns), 0)
    column = lax.broadcasted_iota(jnp.int32, (rows, columns), 1)
    same = row // step == column if along_rows else row == column // step
    return jnp.where(same, 1.0, 0.0).astype(BF16)


def cell_mixer(weights, across, sizes):
    count = sizes.channels * sizes.cells
    left = one_hot(count, sizes.channels, sizes.cells, True)
    right = one_hot(sizes.channels, count, sizes.cells, False)
    tall = dot(left, weights, ((1,), (1 if across else 0,)))
    wide = dot(tall.astype(BF16), right)
    row = lax.broadcasted_iota(jnp.int32, (count, count), 0)
    column = lax.broadcasted_iota(jnp.int32, (count, count), 1)
    same = lax.rem(row, sizes.cells) == lax.rem(column, sizes.cells)
    return jnp.where(same, wide, 0.0).astype(BF16)


def emit(sizes, pre, signal, weight, inverse, layer_out, local, inverse_out, weight_here, semaphores):
    copies = [
        pltpu.make_async_copy(weight, weight_here, semaphores.at[0]),
        pltpu.make_async_copy(inverse, inverse_out, semaphores.at[1]),
    ]
    for copy in copies:
        copy.start()
    scatter_cells(gelu_parts(pre[...])[0], layer_out, sizes)
    copies[0].wait()
    local[...] = dot(cell_mixer(weight_here[...], False, sizes), signal[...])
    copies[1].wait()


def core_of():
    return lax.rem(lax.axis_index("gy"), 2)


def start_weights(sizes, source, half, here, semaphores):
    copies = []
    for at in range(2 * sizes.share):
        copies.append(pltpu.make_async_copy(source.at[2 * sizes.share * half + at], here.at[at], semaphores.at[at]))
        copies[-1].start()
    return copies


def turn_weights(sizes, copies, here, target):
    if sizes.half > sizes.kept:
        target[...] = jnp.zeros_like(target)
    elif sizes.rows > sizes.channels:
        target[:, :, sizes.channels :, :] = jnp.zeros(
            (sizes.share, sizes.channels, sizes.rows - sizes.channels, 2 * sizes.half), F32
        )
    for mode in range(sizes.share):
        for s in range(2):
            copies[2 * mode + s].wait()
        for w in range(sizes.channels):
            blocks = [here[2 * mode + s, w].reshape(sizes.kept, sizes.channels) for s in range(2)]
            if sizes.half == sizes.kept:
                target[mode, w, : sizes.channels, :] = jnp.concatenate(blocks, 0).T
            else:
                for s, block in enumerate(blocks):
                    target[mode, w, : sizes.channels, s * sizes.half : s * sizes.half + sizes.kept] = block.T


def turn_other(sizes, source, after, target, here, semaphores):
    del after
    turn_weights(sizes, start_weights(sizes, source, 1 - core_of(), here, semaphores), here, target)


def prepare(
    sizes, source, after, tables, field, weight, bias, inverse, forward,
    target, table, local, inverse_out, forward_out,
    here, cells, field_here, weight_here, bias_here, semaphores, small,
):
    del after
    place = lax.axis_index("gy")
    lanes = 2 * sizes.half
    moves = [(field, field_here), (weight, weight_here), (bias, bias_here)]
    for s in range(2):
        for at, owner in enumerate((place, place + 1 - 2 * core_of())):
            moves.append(
                (tables.at[owner, :, pl.ds(s * lanes, lanes)], table.at[:, pl.ds((2 * s + at) * lanes, lanes)])
            )
    moves += [(inverse, inverse_out), (forward, forward_out)]
    few = [pltpu.make_async_copy(*move, small.at[at]) for at, move in enumerate(moves)]
    copies = start_weights(sizes, source, core_of(), here, semaphores)
    for copy in few:
        copy.start()
    turn_weights(sizes, copies, here, target)
    for copy in few:
        copy.wait()
    values = gather_cells(field_here, cells, sizes).astype(BF16)
    spread = one_hot(sizes.channels * sizes.cells, sizes.channels, sizes.cells, True).astype(F32)
    offset = jnp.sum(spread * bias_here[...].reshape(1, sizes.channels), axis=1, keepdims=True)
    local[...] = dot(cell_mixer(weight_here[...], True, sizes), values) + offset


def plane_spectra(sizes, received, table, targets, flat):
    for at in range(sizes.devices):
        flat[at * sizes.cells_y : (at + 1) * sizes.cells_y, :] = received[at]
    turned = flat[...].T
    blocks = []
    for first, count in ((0, sizes.main_lanes), (sizes.rest_first, sizes.rest_lanes)):
        if count:
            firsts = [first + x * count for x in range(sizes.cells_x)]
            blocks.append(jnp.concatenate([turned[at : at + count] for at in firsts], 1))
    both = fine_dot(jnp.concatenate(blocks, 0), table[...])
    rows, lanes = both.shape[0], 2 * sizes.half
    total = both[:, : 2 * lanes] + pltpu.roll(both[:, 2 * lanes :], rows - sizes.share, 0)
    for at, target in enumerate(targets):
        target[...] = total[:, at * lanes : (at + 1) * lanes]


def plane_cells(sizes, spread, table, out):
    modes = jnp.concatenate([spread[at] for at in range(4)], 1)
    cells = fine_dot(table[...], modes, ((1,), (1,)))
    count = sizes.devices * sizes.cells_y
    parts = [cells[x * count : (x + 1) * count] for x in range(sizes.cells_x)]
    pieces = [part[:, : sizes.main_lanes] for part in parts] if sizes.main else []
    if sizes.rest:
        pieces += [part[:, sizes.main_lanes :] for part in parts]
    used = sizes.rest_first + sizes.cells_x * sizes.rest_lanes
    if sizes.width > used:
        pieces.append(jnp.zeros((count, sizes.width - used), F32))
    wide = jnp.concatenate(pieces, 1)
    for at in range(sizes.devices):
        out[at] = wide[at * sizes.cells_y : (at + 1) * sizes.cells_y, :]


def swap_parts(values, sizes):
    return pltpu.roll(values, sizes.half, 1)


def mode_rows(first, sizes):
    return pl.ds(first, sizes.channels, stride=sizes.modes)


def put_mixed(spread, at, mode, values, sizes):
    for s in range(2):
        spread[2 * s + at, mode_rows(s * sizes.share + mode, sizes), :] = values


def first_lanes(rows, sizes):
    return lax.broadcasted_iota(jnp.int32, (rows, 2 * sizes.half), 1) < sizes.half


def mix_forward(sizes, received, table, weight, other_weight, spectra, other_spectra, out, spread, swapped, flat):
    plane_spectra(sizes, received, table, (spectra, other_spectra), flat)
    spread[...] = jnp.zeros_like(spread)
    real = first_lanes(sizes.rows, sizes)
    for at, (rows, block) in enumerate(((spectra, weight), (other_spectra, other_weight))):
        swapped[...] = swap_parts(rows[...], sizes)
        for m in range(sizes.share):
            straight = jnp.zeros((sizes.rows, 2 * sizes.half), F32)
            crossed = jnp.zeros((sizes.rows, 2 * sizes.half), F32)
            for w in range(sizes.channels):
                row = slice(w * sizes.modes + m, w * sizes.modes + m + 1)
                straight = straight + rows[row, :] * block[m, w]
                crossed = crossed + swapped[row, :] * block[m, w]
            real_part = straight - swap_parts(straight, sizes)
            imag_part = crossed + swap_parts(crossed, sizes)
            put_mixed(spread, at, m, jnp.where(real, real_part, imag_part)[: sizes.channels], sizes)
    plane_cells(sizes, spread, table, out)


def mix_back(sizes, received, table, weight, other_weight, back, other_back, out, spread, flat):
    plane_spectra(sizes, received, table, (back, other_back), flat)
    spread[...] = jnp.zeros_like(spread)
    real = first_lanes(sizes.channels, sizes)
    for at, (source, block) in enumerate(((back, weight), (other_back, other_weight))):
        for m in range(sizes.share):
            rows = source[mode_rows(m, sizes), :]
            if sizes.rows > sizes.channels:
                rows = jnp.concatenate([rows, jnp.zeros((sizes.rows - sizes.channels, 2 * sizes.half), F32)], 0)
            turned = swap_parts(rows, sizes)
            straight, crossed = [], []
            for w in range(sizes.channels):
                straight.append(jnp.sum(block[m, w] * rows, axis=0, keepdims=True))
                crossed.append(jnp.sum(block[m, w] * turned, axis=0, keepdims=True))
            straight = jnp.concatenate(straight, 0)
            crossed = jnp.concatenate(crossed, 0)
            real_part = straight + swap_parts(straight, sizes)
            imag_part = swap_parts(crossed, sizes) - crossed
            put_mixed(spread, at, m, jnp.where(real, real_part, imag_part), sizes)
    plane_cells(sizes, spread, table, out)


def grad_weights(
    sizes, spectra, back, given_spectra, given_back, target, here, straight, crossed, semaphores
):
    copies = []
    for which, (source, backward) in enumerate(((spectra, back), (given_spectra, given_back))):
        half = core_of() if which == 0 else 1 - core_of()
        values = source[...]
        turned = swap_parts(values, sizes)
        real = first_lanes(values.shape[0], sizes)
        straight[...] = jnp.where(real, values, turned)
        crossed[...] = jnp.where(real, turned, -values)
        for mode in range(sizes.share):
            rows = backward[mode_rows(mode, sizes), :]
            if sizes.rows > sizes.channels:
                rows = jnp.concatenate([rows, jnp.zeros((sizes.rows - sizes.channels, 2 * sizes.half), F32)], 0)
            turned = swap_parts(rows, sizes)
            local = 2 * (which * sizes.share + mode)
            for w in range(sizes.channels):
                at = slice(w * sizes.modes + mode, w * sizes.modes + mode + 1)
                block = (straight[at, :] * rows + crossed[at, :] * turned).T
                for s in range(2):
                    part = block[s * sizes.half : s * sizes.half + sizes.kept, : sizes.channels]
                    here[local + s, w] = part.reshape(sizes.local_x, sizes.kept_y, sizes.channels)
            for s in range(2):
                to = 2 * (half * sizes.share + mode) + s
                copies.append(pltpu.make_async_copy(here.at[local + s], target.at[to], semaphores.at[local + s]))
                copies[-1].start()
    for copy in copies:
        copy.wait()


def gelu_parts(pre):
    slope = math.sqrt(2.0 / math.pi)
    squared = pre * pre
    bend = jnp.tanh(slope * (pre + 0.044715 * (squared * pre)))
    value = 0.5 * pre * (1.0 + bend)
    derivative = 0.5 * (1.0 + bend) + 0.5 * pre * (1.0 - bend * bend) * (slope * (1.0 + 3.0 * 0.044715 * squared))
    return value, derivative


def activate(sizes, received, local, cotangent, inverse, forward, pre_out, signal_out, out, spectrum, cells, cot_here, semaphore):
    copy = pltpu.make_async_copy(cotangent, cot_here, semaphore.at[0])
    copy.start()
    pre = fine_dot(receive_modes(received, spectrum, sizes), inverse[...]) + local[...]
    pre_out[...] = pre
    derivative = gelu_parts(pre)[1]
    copy.wait()
    signal = (gather_cells(cot_here, cells, sizes) * derivative).astype(BF16)
    signal_out[...] = signal
    send_modes(dot(signal, forward[...]), out, sizes)


def finish(sizes, received, local, inverse, grad_field, spectrum):
    spatial = fine_dot(receive_modes(received, spectrum, sizes), inverse[...])
    scatter_cells(spatial + local[...], grad_field, sizes)


def shape_of(shape, dtype=F32):
    return jax.ShapeDtypeStruct(shape, dtype)


VMEM = pl.BlockSpec(memory_space=pltpu.VMEM)
HBM = pl.BlockSpec(memory_space=pltpu.HBM)
ANYWHERE = pl.BlockSpec(memory_space=pl.ANY)


def settings(mebibytes):
    return pltpu.CompilerParams(vmem_limit_bytes=mebibytes * 1024 * 1024)


def cost(nanoseconds):
    return pl.CostEstimate(flops=0, bytes_accessed=3000 * nanoseconds, transcendentals=0)


def whole_call(body, sizes, nanoseconds, out_shape, scratch, *args, specs=None, out_specs=None, room=16):
    def kernel(*refs):
        body(sizes, *refs)

    if specs:
        args = [
            pltpu.with_memory_space_constraint(arg, pltpu.HBM) if spec is HBM else arg for arg, spec in zip(args, specs)
        ]
    return pl.pallas_call(
        kernel,
        out_shape=out_shape,
        in_specs=specs or [VMEM] * len(args),
        out_specs=out_specs or jax.tree.map(lambda _: VMEM, out_shape),
        scratch_shapes=scratch,
        name=body.__name__,
        cost_estimate=cost(nanoseconds),
        compiler_params=settings(room),
    )(*args)


def on_device(field, cotangent, spectral_weight, pointwise_weight, channel_bias):
    z = Sizes(field, spectral_weight)
    depth_table = depth_time_table(z.depth)
    modes = depth_table.shape[2]
    kappa = np.where(np.arange(modes) % KT == 0, 1.0, 2.0).astype(np.float32)
    shares = (z.nx, 2, z.share)
    ordered = depth_table.reshape((z.depth, 2) + shares).transpose(0, 2, 3, 1, 4).reshape(z.depth, z.all_modes)
    doubled = np.repeat(kappa.reshape(z.nx, 2, 1, z.share), 2, axis=2).reshape(z.all_modes)
    forward_first = jnp.asarray(ordered.astype(ml_dtypes.bfloat16))
    forward_back = jnp.asarray((ordered.astype(ml_dtypes.bfloat16).astype(np.float32) * doubled).astype(ml_dtypes.bfloat16))
    inverse_back = jnp.asarray(np.ascontiguousarray(ordered.T))
    inverse_first = jnp.asarray(np.ascontiguousarray((ordered * doubled).T))
    pairs = [(s, s ^ 1) for s in range(z.ny)]

    def exchange(payload):
        return lax.all_to_all(payload, ("gx", "gy"), split_axis=0, concat_axis=0, tiled=True)

    def other_core(values):
        return lax.ppermute(values, "gy", pairs)

    payload = shape_of((z.devices, z.cells_y, z.width))
    cell_rows = z.channels * z.cells
    cells_shape = (cell_rows, z.depth)
    cells_scratch = pltpu.VMEM(cells_shape, F32)
    spectrum_scratch = pltpu.VMEM((cell_rows, z.all_modes), F32)
    spectra_shape = (z.channels * z.modes, 2 * z.half)
    spectra_scratch = pltpu.VMEM(spectra_shape, F32)
    flat_scratch = pltpu.VMEM((z.devices * z.cells_y, z.width), F32)
    spread_scratch = pltpu.VMEM((4,) + spectra_shape, F32)
    field_scratch = pltpu.VMEM(field.shape, BF16)
    weight_here = pltpu.VMEM(pointwise_weight.shape, BF16)
    native = jnp.transpose(spectral_weight, (0, 1, 2, 4, 5, 3))
    weight_shape = (2 * z.modes,) + native.shape[2:]
    half_scratch = pltpu.VMEM((z.modes,) + native.shape[2:], F32)
    turned_shape = shape_of((z.share, z.channels, z.rows, 2 * z.half))

    def flags(count):
        return pltpu.SemaphoreType.DMA((count,))

    sent = whole_call(
        depth_forward, z, 1500, payload,
        [cells_scratch, field_scratch, pltpu.VMEM(forward_first.shape, BF16), flags(2)],
        field, forward_first, specs=[HBM] * 2,
    )
    received = exchange(sent)
    weights = native.reshape(weight_shape)
    turned_away = whole_call(
        turn_other, z, 2700, turned_shape, [half_scratch, flags(z.modes)], weights, sent, specs=[HBM, ANYWHERE]
    )
    other_turned = other_core(turned_away)
    turned, plane, local, inverse_here, forward_here = whole_call(
        prepare, z, 3500,
        (
            turned_shape,
            shape_of((z.devices * z.cells, 8 * z.half)),
            shape_of(cells_shape),
            shape_of(inverse_first.shape),
            shape_of(forward_back.shape, BF16),
        ),
        [
            half_scratch, cells_scratch, field_scratch, weight_here, pltpu.VMEM(channel_bias.shape, F32),
            flags(z.modes), flags(9),
        ],
        weights, turned_away, jnp.asarray(plane_tables(z)), field, pointwise_weight, channel_bias,
        inverse_first, forward_back, specs=[HBM, ANYWHERE] + [HBM] * 6,
    )
    received, other_turned, turned, plane, local, inverse_here, forward_here = lax.optimization_barrier(
        (received, other_turned, turned, plane, local, inverse_here, forward_here)
    )
    spectra, other_spectra, sent = whole_call(
        mix_forward, z, 1000, (shape_of(spectra_shape), shape_of(spectra_shape), payload),
        [spread_scratch, spectra_scratch, flat_scratch], received, plane, turned, other_turned,
    )
    pre, signal, sent = whole_call(
        activate, z, 2000,
        (shape_of(cells_shape), shape_of(cells_shape, BF16), payload),
        [spectrum_scratch, cells_scratch, field_scratch, flags(1)],
        exchange(sent), local, cotangent, inverse_here, forward_here, specs=[VMEM, VMEM, HBM, VMEM, VMEM],
    )
    back, other_back, sent = whole_call(
        mix_back, z, 1000, (shape_of(spectra_shape), shape_of(spectra_shape), payload),
        [spread_scratch, flat_scratch], exchange(sent), plane, turned, other_turned,
    )
    sent, spectra, other_spectra, back, other_back, pre, signal = lax.optimization_barrier(
        (sent, spectra, other_spectra, back, other_back, pre, signal)
    )
    returned = exchange(sent)
    given_spectra, given_back = other_core(other_spectra), other_core(other_back)
    layer_out, local, inverse_here = whole_call(
        emit, z, 1500,
        (shape_of(field.shape, BF16), shape_of(cells_shape), shape_of(inverse_back.shape)),
        [weight_here, flags(2)],
        pre, signal, pointwise_weight, inverse_back, specs=[VMEM, VMEM, HBM, HBM],
    )
    gradient = whole_call(
        grad_weights, z, 5000, shape_of(weight_shape),
        [pltpu.VMEM(weight_shape, F32), spectra_scratch, spectra_scratch, flags(2 * z.modes)],
        spectra, back, given_spectra, given_back, out_specs=HBM, room=28,
    )
    returned, gradient, layer_out, local, inverse_here = lax.optimization_barrier(
        (returned, gradient, layer_out, local, inverse_here)
    )
    grad_field = whole_call(
        finish, z, 1000, shape_of(field.shape, BF16), [spectrum_scratch], returned, local, inverse_here
    )
    return (layer_out, grad_field, jnp.transpose(gradient.reshape(native.shape), (0, 1, 2, 5, 3, 4)))


def solution(mesh):
    return jax.shard_map(
        on_device,
        mesh=mesh,
        in_specs=(
            P(None, "gx", "gy", None),
            P(None, "gx", "gy", None),
            P("gx", None, None, None, "gy", None),
            P(),
            P(),
        ),
        out_specs=(
            P(None, "gx", "gy", None),
            P(None, "gx", "gy", None),
            P("gx", None, None, None, "gy", None),
        ),
        check_vma=False,
    )
```

```python
import math

import jax
import jax.numpy as jnp
import ml_dtypes
import numpy as np
from jax import lax
from jax.experimental import pallas as pl
from jax.experimental.pallas import tpu as pltpu
from jax.sharding import PartitionSpec as P

KZ = 16
KT = 4
NT = 16
LANES = 128
F32 = jnp.float32
BF16 = jnp.bfloat16


def round_up(value, step):
    return -(-value // step) * step


def frequencies(kept):
    index = np.arange(kept)
    return np.where(index < kept // 2, index, index - kept)


def depth_time_table(cells):
    depth_cells = cells // NT
    depth = np.arange(depth_cells)[:, None, None, None] * frequencies(KZ)[None, None, :, None] * NT
    time = np.arange(NT)[None, :, None, None] * np.arange(KT)[None, None, None, :] * depth_cells
    phase = np.mod(depth + time, cells).reshape(cells, KZ * KT)
    angles = phase.astype(np.float32) * np.float32(2.0 * math.pi / cells)
    factor = np.float32(1.0 / math.sqrt(cells))
    return np.stack([np.cos(angles) * factor, -np.sin(angles) * factor], axis=1).astype(np.float32)


def plane_tables(sizes):
    length_x, length_y = sizes.nx * sizes.cells_x, sizes.ny * sizes.cells_y
    phase_x = np.mod(np.arange(length_x)[:, None] * frequencies(sizes.kept_x), length_x) / length_x
    phase_y = np.mod(np.arange(length_y)[:, None] * frequencies(sizes.kept_y), length_y) / length_y
    angle = 2.0 * math.pi * (phase_x[:, None, :, None] + phase_y[None, :, None, :])
    scale = 1.0 / math.sqrt(length_x * length_y)
    cosine, sine = np.cos(angle) * scale, np.sin(angle) * scale
    parts = np.stack([np.stack([cosine, -sine]), np.stack([sine, cosine])])
    parts = parts.reshape(
        2, 2, sizes.nx, sizes.cells_x, sizes.ny, sizes.cells_y, sizes.ny, sizes.kept
    ).transpose(6, 3, 2, 4, 5, 0, 1, 7)
    padded = np.zeros(parts.shape[:-1] + (sizes.half,), np.float32)
    padded[..., : sizes.kept] = parts
    return padded.reshape(sizes.ny, sizes.devices * sizes.cells, 4 * sizes.half)


class Sizes:
    def __init__(self, field, weight):
        self.nx, self.ny = lax.axis_size("gx"), lax.axis_size("gy")
        self.channels, self.cells_x, self.cells_y, self.depth = field.shape
        self.modes = weight.shape[0]
        self.local_x, self.kept_y = weight.shape[4:]
        self.kept_x = self.local_x * self.ny
        self.cells = self.cells_x * self.cells_y
        self.devices = self.nx * self.ny
        self.share = self.modes // 2
        self.kept = self.local_x * self.kept_y
        self.half = round_up(self.kept, LANES // 2)
        self.all_modes = 2 * self.modes * self.nx
        self.groups = LANES // self.modes
        self.main = self.channels // self.groups * self.groups if self.all_modes == LANES else 0
        self.rest = self.channels - self.main
        self.main_lanes = self.main * self.modes
        self.rest_lanes = self.rest * self.modes
        self.rest_tiles = round_up(self.rest_lanes, LANES) // LANES
        self.rest_first = self.cells_x * self.main_lanes
        self.width = self.rest_first + round_up(self.cells_x * self.rest_lanes, LANES)
        self.rows = round_up(self.channels, 8)


def gather_cells(source, scratch, sizes):
    for w in range(sizes.channels):
        for x in range(sizes.cells_x):
            first = (w * sizes.cells_x + x) * sizes.cells_y
            scratch[first : first + sizes.cells_y, :] = source[w, x].astype(F32)
    return scratch[...]


def scatter_cells(values, target, sizes):
    for w in range(sizes.channels):
        for x in range(sizes.cells_x):
            first = (w * sizes.cells_x + x) * sizes.cells_y
            target[w, x] = values[first : first + sizes.cells_y, :].astype(target.dtype)


def lane_group(sizes):
    return lax.broadcasted_iota(jnp.int32, (sizes.cells, LANES), 1) // sizes.modes


def turn_groups(tiles, group, sizes):
    tiles = list(tiles)
    step = 1
    while step < sizes.groups:
        low = group // step % 2 == 0
        for first in range(sizes.groups):
            if first // step % 2 == 0:
                one, two = tiles[first], tiles[first + step]
                tiles[first] = jnp.where(low, one, pltpu.roll(two, step * sizes.modes, 1))
                tiles[first + step] = jnp.where(low, pltpu.roll(one, LANES - step * sizes.modes, 1), two)
        step *= 2
    return tiles


def put_group(target, source, have, want, group, sizes):
    if have != want:
        source = pltpu.roll(source, (want - have) % sizes.groups * sizes.modes, 1)
    return jnp.where(group == want, source, target)


def send_modes(values, target, sizes):
    group = lane_group(sizes)
    tiles = [values[w * sizes.cells : (w + 1) * sizes.cells, :] for w in range(sizes.channels)]
    turned = []
    for first in range(0, sizes.main, sizes.groups):
        turned.append(turn_groups(tiles[first : first + sizes.groups], group, sizes))
    for at in range(2 * sizes.nx):
        main = [block[at] for block in turned]
        rest = [jnp.zeros((sizes.cells, LANES), F32) for _ in range(sizes.rest_tiles)]
        for r in range(sizes.rest):
            tile, want = divmod(r, sizes.groups)
            rest[tile] = put_group(rest[tile], tiles[sizes.main + r], at, want, group, sizes)
        last = []
        for x in range(sizes.cells_x):
            rows = slice(x * sizes.cells_y, (x + 1) * sizes.cells_y)
            for k, value in enumerate(main):
                lanes = slice(x * sizes.main_lanes + k * LANES, x * sizes.main_lanes + (k + 1) * LANES)
                for y in range(sizes.ny // 2):
                    target[at // 2 * sizes.ny + 2 * y + at % 2, :, lanes] = value[rows]
            if rest:
                last.append(jnp.concatenate([value[rows] for value in rest], 1)[:, : sizes.rest_lanes])
        if rest:
            used = sizes.rest_first + sizes.cells_x * sizes.rest_lanes
            if sizes.width > used:
                last.append(jnp.zeros((sizes.cells_y, sizes.width - used), F32))
            last = jnp.concatenate(last, 1)
            for y in range(sizes.ny // 2):
                target[at // 2 * sizes.ny + 2 * y + at % 2, :, sizes.rest_first :] = last


def receive_modes(source, scratch, sizes):
    group = lane_group(sizes)
    parts = source[...].reshape(sizes.nx, sizes.ny // 2, 2, sizes.cells_y, sizes.width)
    values = parts[:, 0]
    for y in range(1, sizes.ny // 2):
        values = values + parts[:, y]
    values = values.reshape(2 * sizes.nx, sizes.cells_y, sizes.width)
    out = []
    for k in range(sizes.main // sizes.groups):
        firsts = [x * sizes.main_lanes + k * LANES for x in range(sizes.cells_x)]
        tall = jnp.concatenate([values[:, :, first : first + LANES] for first in firsts], 1)
        out += turn_groups([tall[at] for at in range(2 * sizes.nx)], group, sizes)
    if sizes.rest:
        firsts = [sizes.rest_first + x * sizes.rest_lanes for x in range(sizes.cells_x)]
        tall = jnp.concatenate([values[:, :, first : first + sizes.rest_lanes] for first in firsts], 1)
        filler = sizes.rest_tiles * LANES - sizes.rest_lanes
        if filler:
            tall = jnp.concatenate([tall, jnp.zeros(tall.shape[:2] + (filler,), F32)], 2)
        for r in range(sizes.rest):
            value = jnp.zeros((sizes.cells, LANES), F32)
            tile, have = divmod(r, sizes.groups)
            for at in range(2 * sizes.nx):
                source_tile = tall[at, :, tile * LANES : (tile + 1) * LANES]
                value = put_group(value, source_tile, have, at, group, sizes)
            out.append(value)
    for w, value in enumerate(out):
        scratch[w * sizes.cells : (w + 1) * sizes.cells, :] = value
    return scratch[...]


def dot(left, right, contract=((1,), (0,))):
    return lax.dot_general(left, right, (contract, ((), ())), preferred_element_type=F32)


def halves(values):
    high = values.astype(BF16)
    return high, (values - high.astype(F32)).astype(BF16)


def fine_dot(left, right, contract=((1,), (0,))):
    left_high, left_low = halves(left)
    right_high, right_low = halves(right)
    small = dot(left_high, right_low, contract) + dot(left_low, right_high, contract)
    return dot(left_high, right_high, contract) + small


def fetch(sources, targets, semaphores):
    copies = [pltpu.make_async_copy(*pair, semaphores.at[at]) for at, pair in enumerate(zip(sources, targets))]
    for copy in copies:
        copy.start()
    for copy in copies:
        copy.wait()


def depth_forward(sizes, field, table, out, cells, field_here, table_here, semaphores):
    fetch((field, table), (field_here, table_here), semaphores)
    values = gather_cells(field_here, cells, sizes).astype(BF16)
    send_modes(dot(values, table_here[...]), out, sizes)


def one_hot(rows, columns, step, along_rows):
    row = lax.broadcasted_iota(jnp.int32, (rows, columns), 0)
    column = lax.broadcasted_iota(jnp.int32, (rows, columns), 1)
    same = row // step == column if along_rows else row == column // step
    return jnp.where(same, 1.0, 0.0).astype(BF16)


def cell_mixer(weights, across, sizes):
    count = sizes.channels * sizes.cells
    left = one_hot(count, sizes.channels, sizes.cells, True)
    right = one_hot(sizes.channels, count, sizes.cells, False)
    tall = dot(left, weights, ((1,), (1 if across else 0,)))
    wide = dot(tall.astype(BF16), right)
    row = lax.broadcasted_iota(jnp.int32, (count, count), 0)
    column = lax.broadcasted_iota(jnp.int32, (count, count), 1)
    same = lax.rem(row, sizes.cells) == lax.rem(column, sizes.cells)
    return jnp.where(same, wide, 0.0).astype(BF16)


def emit(sizes, pre, signal, weight, inverse, layer_out, local, inverse_out, weight_here, semaphores):
    copies = [
        pltpu.make_async_copy(weight, weight_here, semaphores.at[0]),
        pltpu.make_async_copy(inverse, inverse_out, semaphores.at[1]),
    ]
    for copy in copies:
        copy.start()
    scatter_cells(gelu_parts(pre[...])[0], layer_out, sizes)
    copies[0].wait()
    local[...] = dot(cell_mixer(weight_here[...], False, sizes), signal[...])
    copies[1].wait()


def core_of():
    return lax.rem(lax.axis_index("gy"), 2)


def start_weights(sizes, source, half, here, semaphores):
    copies = []
    for at in range(2 * sizes.share):
        copies.append(pltpu.make_async_copy(source.at[2 * sizes.share * half + at], here.at[at], semaphores.at[at]))
        copies[-1].start()
    return copies


def turn_weights(sizes, copies, here, target):
    if sizes.half > sizes.kept:
        target[...] = jnp.zeros_like(target)
    elif sizes.rows > sizes.channels:
        target[:, :, sizes.channels :, :] = jnp.zeros(
            (sizes.share, sizes.channels, sizes.rows - sizes.channels, 2 * sizes.half), F32
        )
    for mode in range(sizes.share):
        for s in range(2):
            copies[2 * mode + s].wait()
        for w in range(sizes.channels):
            blocks = [here[2 * mode + s, w].reshape(sizes.kept, sizes.channels) for s in range(2)]
            if sizes.half == sizes.kept:
                target[mode, w, : sizes.channels, :] = jnp.concatenate(blocks, 0).T
            else:
                for s, block in enumerate(blocks):
                    target[mode, w, : sizes.channels, s * sizes.half : s * sizes.half + sizes.kept] = block.T


def turn_other(sizes, source, after, target, here, semaphores):
    del after
    turn_weights(sizes, start_weights(sizes, source, 1 - core_of(), here, semaphores), here, target)


def prepare(
    sizes, source, after, tables, field, weight, bias,
    target, table, local,
    here, cells, field_here, weight_here, bias_here, local_here, semaphores, small,
):
    del after
    place = lax.axis_index("gy")
    lanes = 2 * sizes.half
    moves = [(field, field_here), (weight, weight_here), (bias, bias_here)]
    for s in range(2):
        for at, owner in enumerate((place, place + 1 - 2 * core_of())):
            moves.append(
                (tables.at[owner, :, pl.ds(s * lanes, lanes)], table.at[:, pl.ds((2 * s + at) * lanes, lanes)])
            )
    few = [pltpu.make_async_copy(*move, small.at[at]) for at, move in enumerate(moves)]
    copies = start_weights(sizes, source, core_of(), here, semaphores)
    for copy in few:
        copy.start()
    turn_weights(sizes, copies, here, target)
    for copy in few:
        copy.wait()
    values = gather_cells(field_here, cells, sizes).astype(BF16)
    spread = one_hot(sizes.channels * sizes.cells, sizes.channels, sizes.cells, True).astype(F32)
    offset = jnp.sum(spread * bias_here[...].reshape(1, sizes.channels), axis=1, keepdims=True)
    local_here[...] = dot(cell_mixer(weight_here[...], True, sizes), values) + offset
    copy = pltpu.make_async_copy(local_here, local, small.at[0])
    copy.start()
    copy.wait()


def plane_spectra(sizes, received, table, targets, flat):
    for at in range(sizes.devices):
        flat[at * sizes.cells_y : (at + 1) * sizes.cells_y, :] = received[at]
    turned = flat[...].T
    blocks = []
    for first, count in ((0, sizes.main_lanes), (sizes.rest_first, sizes.rest_lanes)):
        if count:
            firsts = [first + x * count for x in range(sizes.cells_x)]
            blocks.append(jnp.concatenate([turned[at : at + count] for at in firsts], 1))
    both = fine_dot(jnp.concatenate(blocks, 0), table[...])
    rows, lanes = both.shape[0], 2 * sizes.half
    total = both[:, : 2 * lanes] + pltpu.roll(both[:, 2 * lanes :], rows - sizes.share, 0)
    for at, target in enumerate(targets):
        target[...] = total[:, at * lanes : (at + 1) * lanes]


def plane_cells(sizes, spread, table, out):
    modes = jnp.concatenate([spread[at] for at in range(4)], 1)
    cells = fine_dot(table[...], modes, ((1,), (1,)))
    count = sizes.devices * sizes.cells_y
    parts = [cells[x * count : (x + 1) * count] for x in range(sizes.cells_x)]
    pieces = [part[:, : sizes.main_lanes] for part in parts] if sizes.main else []
    if sizes.rest:
        pieces += [part[:, sizes.main_lanes :] for part in parts]
    used = sizes.rest_first + sizes.cells_x * sizes.rest_lanes
    if sizes.width > used:
        pieces.append(jnp.zeros((count, sizes.width - used), F32))
    wide = jnp.concatenate(pieces, 1)
    for at in range(sizes.devices):
        out[at] = wide[at * sizes.cells_y : (at + 1) * sizes.cells_y, :]


def swap_parts(values, sizes):
    return pltpu.roll(values, sizes.half, 1)


def mode_rows(first, sizes):
    return pl.ds(first, sizes.channels, stride=sizes.modes)


def put_mixed(spread, at, mode, values, sizes):
    for s in range(2):
        spread[2 * s + at, mode_rows(s * sizes.share + mode, sizes), :] = values


def first_lanes(rows, sizes):
    return lax.broadcasted_iota(jnp.int32, (rows, 2 * sizes.half), 1) < sizes.half


def mix_forward(sizes, received, table, weight, other_weight, spectra, other_spectra, out, spread, swapped, flat):
    plane_spectra(sizes, received, table, (spectra, other_spectra), flat)
    spread[...] = jnp.zeros_like(spread)
    real = first_lanes(sizes.rows, sizes)
    for at, (rows, block) in enumerate(((spectra, weight), (other_spectra, other_weight))):
        swapped[...] = swap_parts(rows[...], sizes)
        for m in range(sizes.share):
            straight = jnp.zeros((sizes.rows, 2 * sizes.half), F32)
            crossed = jnp.zeros((sizes.rows, 2 * sizes.half), F32)
            for w in range(sizes.channels):
                row = slice(w * sizes.modes + m, w * sizes.modes + m + 1)
                straight = straight + rows[row, :] * block[m, w]
                crossed = crossed + swapped[row, :] * block[m, w]
            real_part = straight - swap_parts(straight, sizes)
            imag_part = crossed + swap_parts(crossed, sizes)
            put_mixed(spread, at, m, jnp.where(real, real_part, imag_part)[: sizes.channels], sizes)
    plane_cells(sizes, spread, table, out)


def mix_back(sizes, received, table, weight, other_weight, back, other_back, out, spread, flat):
    plane_spectra(sizes, received, table, (back, other_back), flat)
    spread[...] = jnp.zeros_like(spread)
    real = first_lanes(sizes.channels, sizes)
    for at, (source, block) in enumerate(((back, weight), (other_back, other_weight))):
        for m in range(sizes.share):
            rows = source[mode_rows(m, sizes), :]
            if sizes.rows > sizes.channels:
                rows = jnp.concatenate([rows, jnp.zeros((sizes.rows - sizes.channels, 2 * sizes.half), F32)], 0)
            turned = swap_parts(rows, sizes)
            straight, crossed = [], []
            for w in range(sizes.channels):
                straight.append(jnp.sum(block[m, w] * rows, axis=0, keepdims=True))
                crossed.append(jnp.sum(block[m, w] * turned, axis=0, keepdims=True))
            straight = jnp.concatenate(straight, 0)
            crossed = jnp.concatenate(crossed, 0)
            real_part = straight + swap_parts(straight, sizes)
            imag_part = swap_parts(crossed, sizes) - crossed
            put_mixed(spread, at, m, jnp.where(real, real_part, imag_part), sizes)
    plane_cells(sizes, spread, table, out)


def grad_weights(
    sizes, spectra, back, given_spectra, given_back, target, here, straight, crossed, semaphores
):
    copies = []
    for which, (source, backward) in enumerate(((spectra, back), (given_spectra, given_back))):
        half = core_of() if which == 0 else 1 - core_of()
        values = source[...]
        turned = swap_parts(values, sizes)
        real = first_lanes(values.shape[0], sizes)
        straight[...] = jnp.where(real, values, turned)
        crossed[...] = jnp.where(real, turned, -values)
        for mode in range(sizes.share):
            rows = backward[mode_rows(mode, sizes), :]
            if sizes.rows > sizes.channels:
                rows = jnp.concatenate([rows, jnp.zeros((sizes.rows - sizes.channels, 2 * sizes.half), F32)], 0)
            turned = swap_parts(rows, sizes)
            local = 2 * (which * sizes.share + mode)
            for w in range(sizes.channels):
                at = slice(w * sizes.modes + mode, w * sizes.modes + mode + 1)
                block = (straight[at, :] * rows + crossed[at, :] * turned).T
                for s in range(2):
                    part = block[s * sizes.half : s * sizes.half + sizes.kept, : sizes.channels]
                    here[local + s, w] = part.reshape(sizes.local_x, sizes.kept_y, sizes.channels)
            for s in range(2):
                to = 2 * (half * sizes.share + mode) + s
                copies.append(pltpu.make_async_copy(here.at[local + s], target.at[to], semaphores.at[local + s]))
                copies[-1].start()
    for copy in copies:
        copy.wait()


def gelu_parts(pre):
    slope = math.sqrt(2.0 / math.pi)
    squared = pre * pre
    bend = jnp.tanh(slope * (pre + 0.044715 * (squared * pre)))
    value = 0.5 * pre * (1.0 + bend)
    derivative = 0.5 * (1.0 + bend) + 0.5 * pre * (1.0 - bend * bend) * (slope * (1.0 + 3.0 * 0.044715 * squared))
    return value, derivative


def activate(
    sizes, received, local, cotangent, inverse, forward, pre_out, signal_out, out,
    spectrum, cells, inverse_here, local_here, cot_here, forward_here, semaphores,
):
    moves = ((inverse, inverse_here), (local, local_here), (cotangent, cot_here), (forward, forward_here))
    copies = [pltpu.make_async_copy(*move, semaphores.at[at]) for at, move in enumerate(moves)]
    for copy in copies:
        copy.start()
    values = receive_modes(received, spectrum, sizes)
    copies[0].wait()
    copies[1].wait()
    pre = fine_dot(values, inverse_here[...]) + local_here[...]
    pre_out[...] = pre
    derivative = gelu_parts(pre)[1]
    copies[2].wait()
    signal = (gather_cells(cot_here, cells, sizes) * derivative).astype(BF16)
    signal_out[...] = signal
    copies[3].wait()
    send_modes(dot(signal, forward_here[...]), out, sizes)


def finish(sizes, received, local, inverse, grad_field, spectrum):
    spatial = fine_dot(receive_modes(received, spectrum, sizes), inverse[...])
    scatter_cells(spatial + local[...], grad_field, sizes)


def shape_of(shape, dtype=F32):
    return jax.ShapeDtypeStruct(shape, dtype)


VMEM = pl.BlockSpec(memory_space=pltpu.VMEM)
HBM = pl.BlockSpec(memory_space=pltpu.HBM)
ANYWHERE = pl.BlockSpec(memory_space=pl.ANY)


def settings(mebibytes):
    return pltpu.CompilerParams(vmem_limit_bytes=mebibytes * 1024 * 1024)


def cost(nanoseconds):
    return pl.CostEstimate(flops=0, bytes_accessed=3000 * nanoseconds, transcendentals=0)


def whole_call(body, sizes, nanoseconds, out_shape, scratch, *args, specs=None, out_specs=None, room=16):
    def kernel(*refs):
        body(sizes, *refs)

    if specs:
        args = [
            pltpu.with_memory_space_constraint(arg, pltpu.HBM) if spec is HBM else arg for arg, spec in zip(args, specs)
        ]
    return pl.pallas_call(
        kernel,
        out_shape=out_shape,
        in_specs=specs or [VMEM] * len(args),
        out_specs=out_specs or jax.tree.map(lambda _: VMEM, out_shape),
        scratch_shapes=scratch,
        name=body.__name__,
        cost_estimate=cost(nanoseconds),
        compiler_params=settings(room),
    )(*args)


def on_device(field, cotangent, spectral_weight, pointwise_weight, channel_bias):
    z = Sizes(field, spectral_weight)
    depth_table = depth_time_table(z.depth)
    modes = depth_table.shape[2]
    kappa = np.where(np.arange(modes) % KT == 0, 1.0, 2.0).astype(np.float32)
    shares = (z.nx, 2, z.share)
    ordered = depth_table.reshape((z.depth, 2) + shares).transpose(0, 2, 3, 1, 4).reshape(z.depth, z.all_modes)
    doubled = np.repeat(kappa.reshape(z.nx, 2, 1, z.share), 2, axis=2).reshape(z.all_modes)
    forward_first = jnp.asarray(ordered.astype(ml_dtypes.bfloat16))
    forward_back = jnp.asarray((ordered.astype(ml_dtypes.bfloat16).astype(np.float32) * doubled).astype(ml_dtypes.bfloat16))
    inverse_back = jnp.asarray(np.ascontiguousarray(ordered.T))
    inverse_first = jnp.asarray(np.ascontiguousarray((ordered * doubled).T))
    pairs = [(s, s ^ 1) for s in range(z.ny)]

    def exchange(payload):
        return lax.all_to_all(payload, ("gx", "gy"), split_axis=0, concat_axis=0, tiled=True)

    def other_core(values):
        return lax.ppermute(values, "gy", pairs)

    payload = shape_of((z.devices, z.cells_y, z.width))
    cell_rows = z.channels * z.cells
    cells_shape = (cell_rows, z.depth)
    cells_scratch = pltpu.VMEM(cells_shape, F32)
    spectrum_scratch = pltpu.VMEM((cell_rows, z.all_modes), F32)
    spectra_shape = (z.channels * z.modes, 2 * z.half)
    spectra_scratch = pltpu.VMEM(spectra_shape, F32)
    flat_scratch = pltpu.VMEM((z.devices * z.cells_y, z.width), F32)
    spread_scratch = pltpu.VMEM((4,) + spectra_shape, F32)
    field_scratch = pltpu.VMEM(field.shape, BF16)
    weight_here = pltpu.VMEM(pointwise_weight.shape, BF16)
    native = jnp.transpose(spectral_weight, (0, 1, 2, 4, 5, 3))
    weight_shape = (2 * z.modes,) + native.shape[2:]
    half_scratch = pltpu.VMEM((z.modes,) + native.shape[2:], F32)
    turned_shape = shape_of((z.share, z.channels, z.rows, 2 * z.half))

    def flags(count):
        return pltpu.SemaphoreType.DMA((count,))

    sent = whole_call(
        depth_forward, z, 1500, payload,
        [cells_scratch, field_scratch, pltpu.VMEM(forward_first.shape, BF16), flags(2)],
        field, forward_first, specs=[HBM] * 2,
    )
    received = exchange(sent)
    weights = native.reshape(weight_shape)
    turned_away = whole_call(
        turn_other, z, 100, turned_shape, [half_scratch, flags(z.modes)], weights, sent, specs=[HBM, ANYWHERE]
    )
    other_turned = other_core(turned_away)
    turned, plane, local = whole_call(
        prepare, z, 100,
        (turned_shape, shape_of((z.devices * z.cells, 8 * z.half)), shape_of(cells_shape)),
        [
            half_scratch, cells_scratch, field_scratch, weight_here, pltpu.VMEM(channel_bias.shape, F32),
            cells_scratch, flags(z.modes), flags(7),
        ],
        weights, turned_away, jnp.asarray(plane_tables(z)), field, pointwise_weight, channel_bias,
        specs=[HBM, ANYWHERE] + [HBM] * 4, out_specs=(VMEM, VMEM, HBM),
    )
    received, other_turned, turned, plane, local = lax.optimization_barrier(
        (received, other_turned, turned, plane, local)
    )
    spectra, other_spectra, sent = whole_call(
        mix_forward, z, 1000, (shape_of(spectra_shape), shape_of(spectra_shape), payload),
        [spread_scratch, spectra_scratch, flat_scratch], received, plane, turned, other_turned,
    )
    pre, signal, sent = whole_call(
        activate, z, 2000,
        (shape_of(cells_shape), shape_of(cells_shape, BF16), payload),
        [
            spectrum_scratch, cells_scratch, pltpu.VMEM(inverse_first.shape, F32), cells_scratch, field_scratch,
            pltpu.VMEM(forward_back.shape, BF16), flags(4),
        ],
        exchange(sent), local, cotangent, inverse_first, forward_back, specs=[VMEM] + [HBM] * 4,
    )
    back, other_back, sent = whole_call(
        mix_back, z, 1000, (shape_of(spectra_shape), shape_of(spectra_shape), payload),
        [spread_scratch, flat_scratch], exchange(sent), plane, turned, other_turned,
    )
    sent, spectra, other_spectra, back, other_back, pre, signal = lax.optimization_barrier(
        (sent, spectra, other_spectra, back, other_back, pre, signal)
    )
    returned = exchange(sent)
    given_spectra, given_back = other_core(other_spectra), other_core(other_back)
    layer_out, local, inverse_here = whole_call(
        emit, z, 1500,
        (shape_of(field.shape, BF16), shape_of(cells_shape), shape_of(inverse_back.shape)),
        [weight_here, flags(2)],
        pre, signal, pointwise_weight, inverse_back, specs=[VMEM, VMEM, HBM, HBM],
    )
    gradient = whole_call(
        grad_weights, z, 5000, shape_of(weight_shape),
        [pltpu.VMEM(weight_shape, F32), spectra_scratch, spectra_scratch, flags(2 * z.modes)],
        spectra, back, given_spectra, given_back, out_specs=HBM, room=28,
    )
    returned, gradient, layer_out, local, inverse_here = lax.optimization_barrier(
        (returned, gradient, layer_out, local, inverse_here)
    )
    grad_field = whole_call(
        finish, z, 1000, shape_of(field.shape, BF16), [spectrum_scratch], returned, local, inverse_here
    )
    return (layer_out, grad_field, jnp.transpose(gradient.reshape(native.shape), (0, 1, 2, 5, 3, 4)))


def solution(mesh):
    return jax.shard_map(
        on_device,
        mesh=mesh,
        in_specs=(
            P(None, "gx", "gy", None),
            P(None, "gx", "gy", None),
            P("gx", None, None, None, "gy", None),
            P(),
            P(),
        ),
        out_specs=(
            P(None, "gx", "gy", None),
            P(None, "gx", "gy", None),
            P("gx", None, None, None, "gy", None),
        ),
        check_vma=False,
    )
```

```python
import math

import jax
import jax.numpy as jnp
import ml_dtypes
import numpy as np
from jax import lax
from jax.experimental import pallas as pl
from jax.experimental.pallas import tpu as pltpu
from jax.sharding import PartitionSpec as P

KZ = 16
KT = 4
NT = 16
LANES = 128
F32 = jnp.float32
BF16 = jnp.bfloat16


def round_up(value, step):
    return -(-value // step) * step


def frequencies(kept):
    index = np.arange(kept)
    return np.where(index < kept // 2, index, index - kept)


def depth_time_table(cells):
    depth_cells = cells // NT
    depth = np.arange(depth_cells)[:, None, None, None] * frequencies(KZ)[None, None, :, None] * NT
    time = np.arange(NT)[None, :, None, None] * np.arange(KT)[None, None, None, :] * depth_cells
    phase = np.mod(depth + time, cells).reshape(cells, KZ * KT)
    angles = phase.astype(np.float32) * np.float32(2.0 * math.pi / cells)
    factor = np.float32(1.0 / math.sqrt(cells))
    return np.stack([np.cos(angles) * factor, -np.sin(angles) * factor], axis=1).astype(np.float32)


def plane_tables(sizes):
    length_x, length_y = sizes.nx * sizes.cells_x, sizes.ny * sizes.cells_y
    phase_x = np.mod(np.arange(length_x)[:, None] * frequencies(sizes.kept_x), length_x) / length_x
    phase_y = np.mod(np.arange(length_y)[:, None] * frequencies(sizes.kept_y), length_y) / length_y
    angle = 2.0 * math.pi * (phase_x[:, None, :, None] + phase_y[None, :, None, :])
    scale = 1.0 / math.sqrt(length_x * length_y)
    cosine, sine = np.cos(angle) * scale, np.sin(angle) * scale
    parts = np.stack([np.stack([cosine, -sine]), np.stack([sine, cosine])])
    parts = parts.reshape(
        2, 2, sizes.nx, sizes.cells_x, sizes.ny, sizes.cells_y, sizes.ny, sizes.kept
    ).transpose(6, 3, 2, 4, 5, 0, 1, 7)
    padded = np.zeros(parts.shape[:-1] + (sizes.half,), np.float32)
    padded[..., : sizes.kept] = parts
    return padded.reshape(sizes.ny, sizes.devices * sizes.cells, 4 * sizes.half)


class Sizes:
    def __init__(self, field, weight):
        self.nx, self.ny = lax.axis_size("gx"), lax.axis_size("gy")
        self.channels, self.cells_x, self.cells_y, self.depth = field.shape
        self.modes = weight.shape[0]
        self.local_x, self.kept_y = weight.shape[4:]
        self.kept_x = self.local_x * self.ny
        self.cells = self.cells_x * self.cells_y
        self.devices = self.nx * self.ny
        self.share = self.modes // 2
        self.kept = self.local_x * self.kept_y
        self.half = round_up(self.kept, LANES // 2)
        self.all_modes = 2 * self.modes * self.nx
        self.groups = LANES // self.modes
        self.main = self.channels // self.groups * self.groups if self.all_modes == LANES else 0
        self.rest = self.channels - self.main
        self.main_lanes = self.main * self.modes
        self.rest_lanes = self.rest * self.modes
        self.rest_tiles = round_up(self.rest_lanes, LANES) // LANES
        self.rest_first = self.cells_x * self.main_lanes
        self.width = self.rest_first + round_up(self.cells_x * self.rest_lanes, LANES)
        self.rows = round_up(self.channels, 8)


def gather_cells(source, scratch, sizes):
    for w in range(sizes.channels):
        for x in range(sizes.cells_x):
            first = (w * sizes.cells_x + x) * sizes.cells_y
            scratch[first : first + sizes.cells_y, :] = source[w, x].astype(F32)
    return scratch[...]


def scatter_cells(values, target, sizes):
    for w in range(sizes.channels):
        for x in range(sizes.cells_x):
            first = (w * sizes.cells_x + x) * sizes.cells_y
            target[w, x] = values[first : first + sizes.cells_y, :].astype(target.dtype)


def lane_group(sizes):
    return lax.broadcasted_iota(jnp.int32, (sizes.cells, LANES), 1) // sizes.modes


def turn_groups(tiles, group, sizes):
    tiles = list(tiles)
    step = 1
    while step < sizes.groups:
        low = group // step % 2 == 0
        for first in range(sizes.groups):
            if first // step % 2 == 0:
                one, two = tiles[first], tiles[first + step]
                tiles[first] = jnp.where(low, one, pltpu.roll(two, step * sizes.modes, 1))
                tiles[first + step] = jnp.where(low, pltpu.roll(one, LANES - step * sizes.modes, 1), two)
        step *= 2
    return tiles


def put_group(target, source, have, want, group, sizes):
    if have != want:
        source = pltpu.roll(source, (want - have) % sizes.groups * sizes.modes, 1)
    return jnp.where(group == want, source, target)


def send_modes(values, target, sizes):
    group = lane_group(sizes)
    tiles = [values[w * sizes.cells : (w + 1) * sizes.cells, :] for w in range(sizes.channels)]
    turned = []
    for first in range(0, sizes.main, sizes.groups):
        turned.append(turn_groups(tiles[first : first + sizes.groups], group, sizes))
    for at in range(2 * sizes.nx):
        main = [block[at] for block in turned]
        rest = [jnp.zeros((sizes.cells, LANES), F32) for _ in range(sizes.rest_tiles)]
        for r in range(sizes.rest):
            tile, want = divmod(r, sizes.groups)
            rest[tile] = put_group(rest[tile], tiles[sizes.main + r], at, want, group, sizes)
        last = []
        for x in range(sizes.cells_x):
            rows = slice(x * sizes.cells_y, (x + 1) * sizes.cells_y)
            for k, value in enumerate(main):
                lanes = slice(x * sizes.main_lanes + k * LANES, x * sizes.main_lanes + (k + 1) * LANES)
                for y in range(sizes.ny // 2):
                    target[at // 2 * sizes.ny + 2 * y + at % 2, :, lanes] = value[rows]
            if rest:
                last.append(jnp.concatenate([value[rows] for value in rest], 1)[:, : sizes.rest_lanes])
        if rest:
            used = sizes.rest_first + sizes.cells_x * sizes.rest_lanes
            if sizes.width > used:
                last.append(jnp.zeros((sizes.cells_y, sizes.width - used), F32))
            last = jnp.concatenate(last, 1)
            for y in range(sizes.ny // 2):
                target[at // 2 * sizes.ny + 2 * y + at % 2, :, sizes.rest_first :] = last


def receive_modes(source, scratch, sizes):
    group = lane_group(sizes)
    parts = source[...].reshape(sizes.nx, sizes.ny // 2, 2, sizes.cells_y, sizes.width)
    values = parts[:, 0]
    for y in range(1, sizes.ny // 2):
        values = values + parts[:, y]
    values = values.reshape(2 * sizes.nx, sizes.cells_y, sizes.width)
    out = []
    for k in range(sizes.main // sizes.groups):
        firsts = [x * sizes.main_lanes + k * LANES for x in range(sizes.cells_x)]
        tall = jnp.concatenate([values[:, :, first : first + LANES] for first in firsts], 1)
        out += turn_groups([tall[at] for at in range(2 * sizes.nx)], group, sizes)
    if sizes.rest:
        firsts = [sizes.rest_first + x * sizes.rest_lanes for x in range(sizes.cells_x)]
        tall = jnp.concatenate([values[:, :, first : first + sizes.rest_lanes] for first in firsts], 1)
        filler = sizes.rest_tiles * LANES - sizes.rest_lanes
        if filler:
            tall = jnp.concatenate([tall, jnp.zeros(tall.shape[:2] + (filler,), F32)], 2)
        for r in range(sizes.rest):
            value = jnp.zeros((sizes.cells, LANES), F32)
            tile, have = divmod(r, sizes.groups)
            for at in range(2 * sizes.nx):
                source_tile = tall[at, :, tile * LANES : (tile + 1) * LANES]
                value = put_group(value, source_tile, have, at, group, sizes)
            out.append(value)
    for w, value in enumerate(out):
        scratch[w * sizes.cells : (w + 1) * sizes.cells, :] = value
    return scratch[...]


def dot(left, right, contract=((1,), (0,))):
    return lax.dot_general(left, right, (contract, ((), ())), preferred_element_type=F32)


def halves(values):
    high = values.astype(BF16)
    return high, (values - high.astype(F32)).astype(BF16)


def fine_dot(left, right, contract=((1,), (0,))):
    left_high, left_low = halves(left)
    right_high, right_low = halves(right)
    small = dot(left_high, right_low, contract) + dot(left_low, right_high, contract)
    return dot(left_high, right_high, contract) + small


def fetch(sources, targets, semaphores):
    copies = [pltpu.make_async_copy(*pair, semaphores.at[at]) for at, pair in enumerate(zip(sources, targets))]
    for copy in copies:
        copy.start()
    for copy in copies:
        copy.wait()


def depth_forward(
    sizes, field, table, source, out, target,
    cells, field_here, table_here, out_here, here, semaphores, weight_semaphores,
):
    few = [
        pltpu.make_async_copy(field, field_here, semaphores.at[0]),
        pltpu.make_async_copy(table, table_here, semaphores.at[1]),
    ]
    for copy in few:
        copy.start()
    copies = start_weights(sizes, source, 1 - core_of(), here, weight_semaphores)
    clear_weights(sizes, target)
    for copy in few:
        copy.wait()
    values = gather_cells(field_here, cells, sizes).astype(BF16)
    send_modes(dot(values, table_here[...]), out_here, sizes)
    copy = pltpu.make_async_copy(out_here, out, semaphores.at[2])
    copy.start()
    turn_weights(sizes, copies, here, target)
    copy.wait()


def one_hot(rows, columns, step, along_rows):
    row = lax.broadcasted_iota(jnp.int32, (rows, columns), 0)
    column = lax.broadcasted_iota(jnp.int32, (rows, columns), 1)
    same = row // step == column if along_rows else row == column // step
    return jnp.where(same, 1.0, 0.0).astype(BF16)


def cell_mixer(weights, across, sizes):
    count = sizes.channels * sizes.cells
    left = one_hot(count, sizes.channels, sizes.cells, True)
    right = one_hot(sizes.channels, count, sizes.cells, False)
    tall = dot(left, weights, ((1,), (1 if across else 0,)))
    wide = dot(tall.astype(BF16), right)
    row = lax.broadcasted_iota(jnp.int32, (count, count), 0)
    column = lax.broadcasted_iota(jnp.int32, (count, count), 1)
    same = lax.rem(row, sizes.cells) == lax.rem(column, sizes.cells)
    return jnp.where(same, wide, 0.0).astype(BF16)


def emit(sizes, pre, signal, weight, inverse, layer_out, local, inverse_out, weight_here, semaphores):
    copies = [
        pltpu.make_async_copy(weight, weight_here, semaphores.at[0]),
        pltpu.make_async_copy(inverse, inverse_out, semaphores.at[1]),
    ]
    for copy in copies:
        copy.start()
    scatter_cells(gelu_parts(pre[...])[0], layer_out, sizes)
    copies[0].wait()
    local[...] = dot(cell_mixer(weight_here[...], False, sizes), signal[...])
    copies[1].wait()


def core_of():
    return lax.rem(lax.axis_index("gy"), 2)


def start_weights(sizes, source, half, here, semaphores):
    copies = []
    for at in range(2 * sizes.share):
        copies.append(pltpu.make_async_copy(source.at[2 * sizes.share * half + at], here.at[at], semaphores.at[at]))
        copies[-1].start()
    return copies


def clear_weights(sizes, target):
    if sizes.half > sizes.kept:
        target[...] = jnp.zeros_like(target)
    elif sizes.rows > sizes.channels:
        target[:, :, sizes.channels :, :] = jnp.zeros(
            (sizes.share, sizes.channels, sizes.rows - sizes.channels, 2 * sizes.half), F32
        )


def turn_weights(sizes, copies, here, target):
    for mode in range(sizes.share):
        for s in range(2):
            copies[2 * mode + s].wait()
        for w in range(sizes.channels):
            blocks = [here[2 * mode + s, w].reshape(sizes.kept, sizes.channels) for s in range(2)]
            if sizes.half == sizes.kept:
                target[mode, w, : sizes.channels, :] = jnp.concatenate(blocks, 0).T
            else:
                for s, block in enumerate(blocks):
                    target[mode, w, : sizes.channels, s * sizes.half : s * sizes.half + sizes.kept] = block.T


def prepare(
    sizes, source, after, tables, field, weight, bias,
    target, table, local,
    here, cells, field_here, weight_here, bias_here, local_here, semaphores, small,
):
    del after
    place = lax.axis_index("gy")
    lanes = 2 * sizes.half
    moves = [(field, field_here), (weight, weight_here), (bias, bias_here)]
    for s in range(2):
        for at, owner in enumerate((place, place + 1 - 2 * core_of())):
            moves.append(
                (tables.at[owner, :, pl.ds(s * lanes, lanes)], table.at[:, pl.ds((2 * s + at) * lanes, lanes)])
            )
    few = [pltpu.make_async_copy(*move, small.at[at]) for at, move in enumerate(moves)]
    copies = start_weights(sizes, source, core_of(), here, semaphores)
    for copy in few:
        copy.start()
    clear_weights(sizes, target)
    turn_weights(sizes, copies, here, target)
    for copy in few:
        copy.wait()
    values = gather_cells(field_here, cells, sizes).astype(BF16)
    spread = one_hot(sizes.channels * sizes.cells, sizes.channels, sizes.cells, True).astype(F32)
    offset = jnp.sum(spread * bias_here[...].reshape(1, sizes.channels), axis=1, keepdims=True)
    local_here[...] = dot(cell_mixer(weight_here[...], True, sizes), values) + offset
    copy = pltpu.make_async_copy(local_here, local, small.at[0])
    copy.start()
    copy.wait()


def plane_spectra(sizes, received, table, targets, flat):
    for at in range(sizes.devices):
        flat[at * sizes.cells_y : (at + 1) * sizes.cells_y, :] = received[at]
    turned = flat[...].T
    blocks = []
    for first, count in ((0, sizes.main_lanes), (sizes.rest_first, sizes.rest_lanes)):
        if count:
            firsts = [first + x * count for x in range(sizes.cells_x)]
            blocks.append(jnp.concatenate([turned[at : at + count] for at in firsts], 1))
    both = fine_dot(jnp.concatenate(blocks, 0), table[...])
    rows, lanes = both.shape[0], 2 * sizes.half
    total = both[:, : 2 * lanes] + pltpu.roll(both[:, 2 * lanes :], rows - sizes.share, 0)
    for at, target in enumerate(targets):
        target[...] = total[:, at * lanes : (at + 1) * lanes]


def plane_cells(sizes, spread, table, out):
    modes = jnp.concatenate([spread[at] for at in range(4)], 1)
    cells = fine_dot(table[...], modes, ((1,), (1,)))
    count = sizes.devices * sizes.cells_y
    parts = [cells[x * count : (x + 1) * count] for x in range(sizes.cells_x)]
    pieces = [part[:, : sizes.main_lanes] for part in parts] if sizes.main else []
    if sizes.rest:
        pieces += [part[:, sizes.main_lanes :] for part in parts]
    used = sizes.rest_first + sizes.cells_x * sizes.rest_lanes
    if sizes.width > used:
        pieces.append(jnp.zeros((count, sizes.width - used), F32))
    wide = jnp.concatenate(pieces, 1)
    for at in range(sizes.devices):
        out[at] = wide[at * sizes.cells_y : (at + 1) * sizes.cells_y, :]


def swap_parts(values, sizes):
    return pltpu.roll(values, sizes.half, 1)


def mode_rows(first, sizes):
    return pl.ds(first, sizes.channels, stride=sizes.modes)


def put_mixed(spread, at, mode, values, sizes):
    for s in range(2):
        spread[2 * s + at, mode_rows(s * sizes.share + mode, sizes), :] = values


def first_lanes(rows, sizes):
    return lax.broadcasted_iota(jnp.int32, (rows, 2 * sizes.half), 1) < sizes.half


def mix_forward(sizes, received, table, weight, other_weight, spectra, other_spectra, out, spread, swapped, flat):
    plane_spectra(sizes, received, table, (spectra, other_spectra), flat)
    spread[...] = jnp.zeros_like(spread)
    real = first_lanes(sizes.rows, sizes)
    for at, (rows, block) in enumerate(((spectra, weight), (other_spectra, other_weight))):
        swapped[...] = swap_parts(rows[...], sizes)
        for m in range(sizes.share):
            straight = jnp.zeros((sizes.rows, 2 * sizes.half), F32)
            crossed = jnp.zeros((sizes.rows, 2 * sizes.half), F32)
            for w in range(sizes.channels):
                row = slice(w * sizes.modes + m, w * sizes.modes + m + 1)
                straight = straight + rows[row, :] * block[m, w]
                crossed = crossed + swapped[row, :] * block[m, w]
            real_part = straight - swap_parts(straight, sizes)
            imag_part = crossed + swap_parts(crossed, sizes)
            put_mixed(spread, at, m, jnp.where(real, real_part, imag_part)[: sizes.channels], sizes)
    plane_cells(sizes, spread, table, out)


def mix_back(sizes, received, table, weight, other_weight, back, other_back, out, spread, flat):
    plane_spectra(sizes, received, table, (back, other_back), flat)
    spread[...] = jnp.zeros_like(spread)
    real = first_lanes(sizes.channels, sizes)
    for at, (source, block) in enumerate(((back, weight), (other_back, other_weight))):
        for m in range(sizes.share):
            rows = source[mode_rows(m, sizes), :]
            if sizes.rows > sizes.channels:
                rows = jnp.concatenate([rows, jnp.zeros((sizes.rows - sizes.channels, 2 * sizes.half), F32)], 0)
            turned = swap_parts(rows, sizes)
            straight, crossed = [], []
            for w in range(sizes.channels):
                straight.append(jnp.sum(block[m, w] * rows, axis=0, keepdims=True))
                crossed.append(jnp.sum(block[m, w] * turned, axis=0, keepdims=True))
            straight = jnp.concatenate(straight, 0)
            crossed = jnp.concatenate(crossed, 0)
            real_part = straight + swap_parts(straight, sizes)
            imag_part = swap_parts(crossed, sizes) - crossed
            put_mixed(spread, at, m, jnp.where(real, real_part, imag_part), sizes)
    plane_cells(sizes, spread, table, out)


def grad_weights(
    sizes, spectra, back, given_spectra, given_back, target, here, straight, crossed, semaphores
):
    copies = []
    for which, (source, backward) in enumerate(((spectra, back), (given_spectra, given_back))):
        half = core_of() if which == 0 else 1 - core_of()
        values = source[...]
        turned = swap_parts(values, sizes)
        real = first_lanes(values.shape[0], sizes)
        straight[...] = jnp.where(real, values, turned)
        crossed[...] = jnp.where(real, turned, -values)
        for mode in range(sizes.share):
            rows = backward[mode_rows(mode, sizes), :]
            if sizes.rows > sizes.channels:
                rows = jnp.concatenate([rows, jnp.zeros((sizes.rows - sizes.channels, 2 * sizes.half), F32)], 0)
            turned = swap_parts(rows, sizes)
            local = 2 * (which * sizes.share + mode)
            for w in range(sizes.channels):
                at = slice(w * sizes.modes + mode, w * sizes.modes + mode + 1)
                block = (straight[at, :] * rows + crossed[at, :] * turned).T
                for s in range(2):
                    part = block[s * sizes.half : s * sizes.half + sizes.kept, : sizes.channels]
                    here[local + s, w] = part.reshape(sizes.local_x, sizes.kept_y, sizes.channels)
            for s in range(2):
                to = 2 * (half * sizes.share + mode) + s
                copies.append(pltpu.make_async_copy(here.at[local + s], target.at[to], semaphores.at[local + s]))
                copies[-1].start()
    for copy in copies:
        copy.wait()


def gelu_parts(pre):
    slope = math.sqrt(2.0 / math.pi)
    squared = pre * pre
    bend = jnp.tanh(slope * (pre + 0.044715 * (squared * pre)))
    value = 0.5 * pre * (1.0 + bend)
    derivative = 0.5 * (1.0 + bend) + 0.5 * pre * (1.0 - bend * bend) * (slope * (1.0 + 3.0 * 0.044715 * squared))
    return value, derivative


def activate(
    sizes, received, local, cotangent, inverse, forward, pre_out, signal_out, out,
    spectrum, cells, inverse_here, local_here, cot_here, forward_here, semaphores,
):
    moves = ((inverse, inverse_here), (local, local_here), (cotangent, cot_here), (forward, forward_here))
    copies = [pltpu.make_async_copy(*move, semaphores.at[at]) for at, move in enumerate(moves)]
    for copy in copies:
        copy.start()
    values = receive_modes(received, spectrum, sizes)
    copies[0].wait()
    copies[1].wait()
    pre = fine_dot(values, inverse_here[...]) + local_here[...]
    pre_out[...] = pre
    derivative = gelu_parts(pre)[1]
    copies[2].wait()
    signal = (gather_cells(cot_here, cells, sizes) * derivative).astype(BF16)
    signal_out[...] = signal
    copies[3].wait()
    send_modes(dot(signal, forward_here[...]), out, sizes)


def finish(sizes, received, local, inverse, grad_field, spectrum):
    spatial = fine_dot(receive_modes(received, spectrum, sizes), inverse[...])
    scatter_cells(spatial + local[...], grad_field, sizes)


def shape_of(shape, dtype=F32):
    return jax.ShapeDtypeStruct(shape, dtype)


VMEM = pl.BlockSpec(memory_space=pltpu.VMEM)
HBM = pl.BlockSpec(memory_space=pltpu.HBM)
ANYWHERE = pl.BlockSpec(memory_space=pl.ANY)


def settings(mebibytes):
    return pltpu.CompilerParams(vmem_limit_bytes=mebibytes * 1024 * 1024)


def cost(nanoseconds):
    return pl.CostEstimate(flops=0, bytes_accessed=3000 * nanoseconds, transcendentals=0)


def whole_call(body, sizes, nanoseconds, out_shape, scratch, *args, specs=None, out_specs=None, room=16):
    def kernel(*refs):
        body(sizes, *refs)

    if specs:
        args = [
            pltpu.with_memory_space_constraint(arg, pltpu.HBM) if spec is HBM else arg for arg, spec in zip(args, specs)
        ]
    return pl.pallas_call(
        kernel,
        out_shape=out_shape,
        in_specs=specs or [VMEM] * len(args),
        out_specs=out_specs or jax.tree.map(lambda _: VMEM, out_shape),
        scratch_shapes=scratch,
        name=body.__name__,
        cost_estimate=cost(nanoseconds),
        compiler_params=settings(room),
    )(*args)


def on_device(field, cotangent, spectral_weight, pointwise_weight, channel_bias):
    z = Sizes(field, spectral_weight)
    depth_table = depth_time_table(z.depth)
    modes = depth_table.shape[2]
    kappa = np.where(np.arange(modes) % KT == 0, 1.0, 2.0).astype(np.float32)
    shares = (z.nx, 2, z.share)
    ordered = depth_table.reshape((z.depth, 2) + shares).transpose(0, 2, 3, 1, 4).reshape(z.depth, z.all_modes)
    doubled = np.repeat(kappa.reshape(z.nx, 2, 1, z.share), 2, axis=2).reshape(z.all_modes)
    forward_first = jnp.asarray(ordered.astype(ml_dtypes.bfloat16))
    forward_back = jnp.asarray((ordered.astype(ml_dtypes.bfloat16).astype(np.float32) * doubled).astype(ml_dtypes.bfloat16))
    inverse_back = jnp.asarray(np.ascontiguousarray(ordered.T))
    inverse_first = jnp.asarray(np.ascontiguousarray((ordered * doubled).T))
    pairs = [(s, s ^ 1) for s in range(z.ny)]

    def exchange(payload):
        return lax.all_to_all(payload, ("gx", "gy"), split_axis=0, concat_axis=0, tiled=True)

    def other_core(values):
        return lax.ppermute(values, "gy", pairs)

    payload = shape_of((z.devices, z.cells_y, z.width))
    cell_rows = z.channels * z.cells
    cells_shape = (cell_rows, z.depth)
    cells_scratch = pltpu.VMEM(cells_shape, F32)
    spectrum_scratch = pltpu.VMEM((cell_rows, z.all_modes), F32)
    spectra_shape = (z.channels * z.modes, 2 * z.half)
    spectra_scratch = pltpu.VMEM(spectra_shape, F32)
    flat_scratch = pltpu.VMEM((z.devices * z.cells_y, z.width), F32)
    spread_scratch = pltpu.VMEM((4,) + spectra_shape, F32)
    field_scratch = pltpu.VMEM(field.shape, BF16)
    weight_here = pltpu.VMEM(pointwise_weight.shape, BF16)
    native = jnp.transpose(spectral_weight, (0, 1, 2, 4, 5, 3))
    weight_shape = (2 * z.modes,) + native.shape[2:]
    half_scratch = pltpu.VMEM((z.modes,) + native.shape[2:], F32)
    turned_shape = shape_of((z.share, z.channels, z.rows, 2 * z.half))

    def flags(count):
        return pltpu.SemaphoreType.DMA((count,))

    weights = native.reshape(weight_shape)
    sent, turned_away = whole_call(
        depth_forward, z, 1500, (payload, turned_shape),
        [
            cells_scratch, field_scratch, pltpu.VMEM(forward_first.shape, BF16), pltpu.VMEM(payload.shape, F32),
            half_scratch, flags(3), flags(z.modes),
        ],
        field, forward_first, weights, specs=[HBM] * 3, out_specs=(HBM, VMEM),
    )
    received = exchange(sent)
    other_turned = other_core(turned_away)
    turned, plane, local = whole_call(
        prepare, z, 100,
        (turned_shape, shape_of((z.devices * z.cells, 8 * z.half)), shape_of(cells_shape)),
        [
            half_scratch, cells_scratch, field_scratch, weight_here, pltpu.VMEM(channel_bias.shape, F32),
            cells_scratch, flags(z.modes), flags(7),
        ],
        weights, turned_away, jnp.asarray(plane_tables(z)), field, pointwise_weight, channel_bias,
        specs=[HBM, ANYWHERE] + [HBM] * 4, out_specs=(VMEM, VMEM, HBM),
    )
    received, other_turned, turned, plane, local = lax.optimization_barrier(
        (received, other_turned, turned, plane, local)
    )
    spectra, other_spectra, sent = whole_call(
        mix_forward, z, 1000, (shape_of(spectra_shape), shape_of(spectra_shape), payload),
        [spread_scratch, spectra_scratch, flat_scratch], received, plane, turned, other_turned,
    )
    pre, signal, sent = whole_call(
        activate, z, 2000,
        (shape_of(cells_shape), shape_of(cells_shape, BF16), payload),
        [
            spectrum_scratch, cells_scratch, pltpu.VMEM(inverse_first.shape, F32), cells_scratch, field_scratch,
            pltpu.VMEM(forward_back.shape, BF16), flags(4),
        ],
        exchange(sent), local, cotangent, inverse_first, forward_back, specs=[VMEM] + [HBM] * 4,
    )
    back, other_back, sent = whole_call(
        mix_back, z, 1000, (shape_of(spectra_shape), shape_of(spectra_shape), payload),
        [spread_scratch, flat_scratch], exchange(sent), plane, turned, other_turned,
    )
    sent, spectra, other_spectra, back, other_back, pre, signal = lax.optimization_barrier(
        (sent, spectra, other_spectra, back, other_back, pre, signal)
    )
    returned = exchange(sent)
    given_spectra, given_back = other_core(other_spectra), other_core(other_back)
    layer_out, local, inverse_here = whole_call(
        emit, z, 1500,
        (shape_of(field.shape, BF16), shape_of(cells_shape), shape_of(inverse_back.shape)),
        [weight_here, flags(2)],
        pre, signal, pointwise_weight, inverse_back, specs=[VMEM, VMEM, HBM, HBM],
    )
    gradient = whole_call(
        grad_weights, z, 5000, shape_of(weight_shape),
        [pltpu.VMEM(weight_shape, F32), spectra_scratch, spectra_scratch, flags(2 * z.modes)],
        spectra, back, given_spectra, given_back, out_specs=HBM, room=28,
    )
    returned, gradient, layer_out, local, inverse_here = lax.optimization_barrier(
        (returned, gradient, layer_out, local, inverse_here)
    )
    grad_field = whole_call(
        finish, z, 1000, shape_of(field.shape, BF16), [spectrum_scratch], returned, local, inverse_here
    )
    return (layer_out, grad_field, jnp.transpose(gradient.reshape(native.shape), (0, 1, 2, 5, 3, 4)))


def solution(mesh):
    return jax.shard_map(
        on_device,
        mesh=mesh,
        in_specs=(
            P(None, "gx", "gy", None),
            P(None, "gx", "gy", None),
            P("gx", None, None, None, "gy", None),
            P(),
            P(),
        ),
        out_specs=(
            P(None, "gx", "gy", None),
            P(None, "gx", "gy", None),
            P("gx", None, None, None, "gy", None),
        ),
        check_vma=False,
    )
```

```python
import math

import jax
import jax.numpy as jnp
import ml_dtypes
import numpy as np
from jax import lax
from jax.experimental import pallas as pl
from jax.experimental.pallas import tpu as pltpu
from jax.sharding import PartitionSpec as P

KZ = 16
KT = 4
NT = 16
LANES = 128
F32 = jnp.float32
BF16 = jnp.bfloat16


def round_up(value, step):
    return -(-value // step) * step


def frequencies(kept):
    index = np.arange(kept)
    return np.where(index < kept // 2, index, index - kept)


def depth_time_table(cells):
    depth_cells = cells // NT
    depth = np.arange(depth_cells)[:, None, None, None] * frequencies(KZ)[None, None, :, None] * NT
    time = np.arange(NT)[None, :, None, None] * np.arange(KT)[None, None, None, :] * depth_cells
    phase = np.mod(depth + time, cells).reshape(cells, KZ * KT)
    angles = phase.astype(np.float32) * np.float32(2.0 * math.pi / cells)
    factor = np.float32(1.0 / math.sqrt(cells))
    return np.stack([np.cos(angles) * factor, -np.sin(angles) * factor], axis=1).astype(np.float32)


def plane_tables(sizes):
    length_x, length_y = sizes.nx * sizes.cells_x, sizes.ny * sizes.cells_y
    phase_x = np.mod(np.arange(length_x)[:, None] * frequencies(sizes.kept_x), length_x) / length_x
    phase_y = np.mod(np.arange(length_y)[:, None] * frequencies(sizes.kept_y), length_y) / length_y
    angle = 2.0 * math.pi * (phase_x[:, None, :, None] + phase_y[None, :, None, :])
    scale = 1.0 / math.sqrt(length_x * length_y)
    cosine, sine = np.cos(angle) * scale, np.sin(angle) * scale
    parts = np.stack([np.stack([cosine, -sine]), np.stack([sine, cosine])])
    pairs = sizes.cells_y // sizes.pair
    parts = parts.reshape(
        2, 2, sizes.nx, sizes.cells_x, sizes.ny, pairs, sizes.pair, sizes.ny, sizes.kept
    ).transpose(7, 3, 5, 2, 4, 6, 0, 1, 8)
    padded = np.zeros(parts.shape[:-1] + (sizes.half,), np.float32)
    padded[..., : sizes.kept] = parts
    return padded.reshape(sizes.ny, sizes.devices * sizes.cells, 4 * sizes.half)


class Sizes:
    def __init__(self, field, weight):
        self.nx, self.ny = lax.axis_size("gx"), lax.axis_size("gy")
        self.channels, self.cells_x, self.cells_y, self.depth = field.shape
        self.modes = weight.shape[0]
        self.local_x, self.kept_y = weight.shape[4:]
        self.kept_x = self.local_x * self.ny
        self.cells = self.cells_x * self.cells_y
        self.devices = self.nx * self.ny
        self.share = self.modes // 2
        self.kept = self.local_x * self.kept_y
        self.half = round_up(self.kept, LANES // 2)
        self.all_modes = 2 * self.modes * self.nx
        self.groups = LANES // self.modes
        self.main = self.channels // self.groups * self.groups if self.all_modes == LANES else 0
        self.rest = self.channels - self.main
        self.main_lanes = self.main * self.modes
        self.rest_lanes = self.rest * self.modes
        self.rest_tiles = round_up(self.rest_lanes, LANES) // LANES
        self.pair = math.gcd(self.cells_y, 2)
        self.pieces = self.cells // self.pair
        self.rest_first = self.pieces * self.main_lanes
        self.rest_width = round_up(self.pieces * self.rest_lanes, LANES)
        self.width = self.rest_first + self.rest_width
        self.spread_rows = self.main_lanes + self.rest_width
        self.rows = round_up(self.channels, 8)


def gather_cells(source, scratch, sizes):
    for w in range(sizes.channels):
        for x in range(sizes.cells_x):
            first = (w * sizes.cells_x + x) * sizes.cells_y
            scratch[first : first + sizes.cells_y, :] = source[w, x].astype(F32)
    return scratch[...]


def scatter_cells(values, target, sizes):
    for w in range(sizes.channels):
        for x in range(sizes.cells_x):
            first = (w * sizes.cells_x + x) * sizes.cells_y
            target[w, x] = values[first : first + sizes.cells_y, :].astype(target.dtype)


def lane_group(sizes):
    return lax.broadcasted_iota(jnp.int32, (sizes.cells, LANES), 1) // sizes.modes


def turn_groups(tiles, group, sizes):
    tiles = list(tiles)
    step = 1
    while step < sizes.groups:
        low = group // step % 2 == 0
        for first in range(sizes.groups):
            if first // step % 2 == 0:
                one, two = tiles[first], tiles[first + step]
                tiles[first] = jnp.where(low, one, pltpu.roll(two, step * sizes.modes, 1))
                tiles[first + step] = jnp.where(low, pltpu.roll(one, LANES - step * sizes.modes, 1), two)
        step *= 2
    return tiles


def put_group(target, source, have, want, group, sizes):
    if have != want:
        source = pltpu.roll(source, (want - have) % sizes.groups * sizes.modes, 1)
    return jnp.where(group == want, source, target)


def send_modes(values, target, sizes):
    group = lane_group(sizes)
    tiles = [values[w * sizes.cells : (w + 1) * sizes.cells, :] for w in range(sizes.channels)]
    turned = []
    for first in range(0, sizes.main, sizes.groups):
        turned.append(turn_groups(tiles[first : first + sizes.groups], group, sizes))
    for at in range(2 * sizes.nx):
        main = [block[at] for block in turned]
        last = [jnp.zeros((sizes.cells, LANES), F32) for _ in range(sizes.rest_width // LANES)]
        for r in range(sizes.rest):
            tile, want = divmod(r, sizes.groups)
            last[tile] = put_group(last[tile], tiles[sizes.main + r], at, want, group, sizes)
        if last:
            last = side_by_side(jnp.concatenate(last, 1), sizes.pair, sizes)
        for y in range(sizes.ny // 2):
            device = at // 2 * sizes.ny + 2 * y + at % 2
            for piece in range(sizes.pieces):
                rows = slice(piece * sizes.pair, (piece + 1) * sizes.pair)
                for k, value in enumerate(main):
                    first = piece * sizes.main_lanes + k * LANES
                    target[device, :, first : first + LANES] = value[rows]
            if sizes.rest:
                target[device, :, sizes.rest_first :] = last


def side_by_side(values, rows, sizes):
    total = values[:rows]
    for piece in range(1, sizes.pieces):
        moved = pltpu.roll(values, piece * sizes.rest_lanes, 1)
        total = total + moved[piece * rows : (piece + 1) * rows]
    return total


def receive_modes(source, scratch, tall, sizes):
    group = lane_group(sizes)
    parts = source[...].reshape(sizes.nx, sizes.ny // 2, 2, sizes.pair, sizes.width)
    values = parts[:, 0]
    for y in range(1, sizes.ny // 2):
        values = values + parts[:, y]
    values = values.reshape(2 * sizes.nx, sizes.pair, sizes.width)
    for piece in range(sizes.pieces):
        rows = slice(piece * sizes.pair, (piece + 1) * sizes.pair)
        if sizes.main:
            first = piece * sizes.main_lanes
            tall[:, rows, : sizes.main_lanes] = values[:, :, first : first + sizes.main_lanes]
        if sizes.rest:
            last = values[:, :, sizes.rest_first :]
            if piece:
                last = pltpu.roll(last, sizes.rest_width - piece * sizes.rest_lanes, 2)
            tall[:, rows, sizes.main_lanes :] = last
    out = []
    for first in range(0, sizes.main_lanes, LANES):
        tiles = [tall[at, :, first : first + LANES] for at in range(2 * sizes.nx)]
        out += turn_groups(tiles, group, sizes)
    for r in range(sizes.rest):
        value = jnp.zeros((sizes.cells, LANES), F32)
        tile, have = divmod(r, sizes.groups)
        first = sizes.main_lanes + tile * LANES
        for at in range(2 * sizes.nx):
            value = put_group(value, tall[at, :, first : first + LANES], have, at, group, sizes)
        out.append(value)
    for w, value in enumerate(out):
        scratch[w * sizes.cells : (w + 1) * sizes.cells, :] = value
    return scratch[...]


def dot(left, right, contract=((1,), (0,))):
    return lax.dot_general(left, right, (contract, ((), ())), preferred_element_type=F32)


def halves(values):
    high = values.astype(BF16)
    return high, (values - high.astype(F32)).astype(BF16)


def fine_dot(left, right, contract=((1,), (0,))):
    left_high, left_low = halves(left)
    right_high, right_low = halves(right)
    small = dot(left_high, right_low, contract) + dot(left_low, right_high, contract)
    return dot(left_high, right_high, contract) + small


def fetch(sources, targets, semaphores):
    copies = [pltpu.make_async_copy(*pair, semaphores.at[at]) for at, pair in enumerate(zip(sources, targets))]
    for copy in copies:
        copy.start()
    for copy in copies:
        copy.wait()


def depth_forward(
    sizes, field, table, source, out, target,
    cells, field_here, table_here, out_here, here, semaphores, weight_semaphores,
):
    few = [
        pltpu.make_async_copy(field, field_here, semaphores.at[0]),
        pltpu.make_async_copy(table, table_here, semaphores.at[1]),
    ]
    for copy in few:
        copy.start()
    copies = start_weights(sizes, source, 1 - core_of(), here, weight_semaphores)
    clear_weights(sizes, target)
    for copy in few:
        copy.wait()
    values = gather_cells(field_here, cells, sizes).astype(BF16)
    send_modes(dot(values, table_here[...]), out_here, sizes)
    copy = pltpu.make_async_copy(out_here, out, semaphores.at[2])
    copy.start()
    turn_weights(sizes, copies, here, target)
    copy.wait()


def one_hot(rows, columns, step, along_rows):
    row = lax.broadcasted_iota(jnp.int32, (rows, columns), 0)
    column = lax.broadcasted_iota(jnp.int32, (rows, columns), 1)
    same = row // step == column if along_rows else row == column // step
    return jnp.where(same, 1.0, 0.0).astype(BF16)


def cell_mixer(weights, across, sizes):
    count = sizes.channels * sizes.cells
    left = one_hot(count, sizes.channels, sizes.cells, True)
    right = one_hot(sizes.channels, count, sizes.cells, False)
    tall = dot(left, weights, ((1,), (1 if across else 0,)))
    wide = dot(tall.astype(BF16), right)
    row = lax.broadcasted_iota(jnp.int32, (count, count), 0)
    column = lax.broadcasted_iota(jnp.int32, (count, count), 1)
    same = lax.rem(row, sizes.cells) == lax.rem(column, sizes.cells)
    return jnp.where(same, wide, 0.0).astype(BF16)


def emit(sizes, pre, signal, weight, inverse, layer_out, local, inverse_out, weight_here, semaphores):
    copies = [
        pltpu.make_async_copy(weight, weight_here, semaphores.at[0]),
        pltpu.make_async_copy(inverse, inverse_out, semaphores.at[1]),
    ]
    for copy in copies:
        copy.start()
    scatter_cells(gelu_parts(pre[...])[0], layer_out, sizes)
    copies[0].wait()
    local[...] = dot(cell_mixer(weight_here[...], False, sizes), signal[...])
    copies[1].wait()


def core_of():
    return lax.rem(lax.axis_index("gy"), 2)


def start_weights(sizes, source, half, here, semaphores):
    copies = []
    for at in range(2 * sizes.share):
        copies.append(pltpu.make_async_copy(source.at[2 * sizes.share * half + at], here.at[at], semaphores.at[at]))
        copies[-1].start()
    return copies


def clear_weights(sizes, target):
    if sizes.half > sizes.kept:
        target[...] = jnp.zeros_like(target)
    elif sizes.rows > sizes.channels:
        target[:, :, sizes.channels :, :] = jnp.zeros(
            (sizes.share, sizes.channels, sizes.rows - sizes.channels, 2 * sizes.half), F32
        )


def turn_weights(sizes, copies, here, target):
    for mode in range(sizes.share):
        for s in range(2):
            copies[2 * mode + s].wait()
        for w in range(sizes.channels):
            blocks = [here[2 * mode + s, w].reshape(sizes.kept, sizes.channels) for s in range(2)]
            if sizes.half == sizes.kept:
                target[mode, w, : sizes.channels, :] = jnp.concatenate(blocks, 0).T
            else:
                for s, block in enumerate(blocks):
                    target[mode, w, : sizes.channels, s * sizes.half : s * sizes.half + sizes.kept] = block.T


def prepare(
    sizes, source, after, tables, field, cotangent, weight, bias,
    target, table, local, cotangent_out,
    here, cells, field_here, cot_here, cot_cells, weight_here, bias_here, local_here, semaphores, small,
):
    del after
    place = lax.axis_index("gy")
    lanes = 2 * sizes.half
    moves = [(field, field_here), (cotangent, cot_here), (weight, weight_here), (bias, bias_here)]
    for s in range(2):
        for at, owner in enumerate((place, place + 1 - 2 * core_of())):
            moves.append(
                (tables.at[owner, :, pl.ds(s * lanes, lanes)], table.at[:, pl.ds((2 * s + at) * lanes, lanes)])
            )
    few = [pltpu.make_async_copy(*move, small.at[at]) for at, move in enumerate(moves)]
    copies = start_weights(sizes, source, core_of(), here, semaphores)
    for copy in few:
        copy.start()
    clear_weights(sizes, target)
    turn_weights(sizes, copies, here, target)
    for copy in few:
        copy.wait()
    values = gather_cells(field_here, cells, sizes).astype(BF16)
    spread = one_hot(sizes.channels * sizes.cells, sizes.channels, sizes.cells, True).astype(F32)
    offset = jnp.sum(spread * bias_here[...].reshape(1, sizes.channels), axis=1, keepdims=True)
    local_here[...] = dot(cell_mixer(weight_here[...], True, sizes), values) + offset
    gather_cells(cot_here, cot_cells, sizes)
    results = [
        pltpu.make_async_copy(local_here, local, small.at[0]),
        pltpu.make_async_copy(cot_cells, cotangent_out, small.at[1]),
    ]
    for copy in results:
        copy.start()
    for copy in results:
        copy.wait()


def plane_spectra(sizes, received, table, targets, flat):
    count = sizes.devices * sizes.pair
    for at in range(sizes.devices):
        for piece in range(sizes.pieces):
            rows = slice(piece * count + at * sizes.pair, piece * count + (at + 1) * sizes.pair)
            if sizes.main:
                first = piece * sizes.main_lanes
                flat[rows, : sizes.main_lanes] = received[at, :, first : first + sizes.main_lanes]
            if sizes.rest:
                flat[rows, sizes.main_lanes :] = received[at, :, sizes.rest_first :]
    if sizes.rest:
        for piece in range(1, sizes.pieces):
            rows = slice(piece * count, (piece + 1) * count)
            shift = sizes.rest_width - piece * sizes.rest_lanes
            flat[rows, sizes.main_lanes :] = pltpu.roll(flat[rows, sizes.main_lanes :], shift, 1)
    rows, lanes = targets[0].shape
    both = fine_dot(flat[...].T[:rows], table[...])
    total = both[:, : 2 * lanes] + pltpu.roll(both[:, 2 * lanes :], rows - sizes.share, 0)
    for at, target in enumerate(targets):
        target[...] = total[:, at * lanes : (at + 1) * lanes]


def plane_cells(sizes, spread, table, out):
    modes = jnp.concatenate([spread[at] for at in range(4)], 1)
    cells = fine_dot(table[...], modes, ((1,), (1,)))
    count = sizes.devices * sizes.pair
    if sizes.rest:
        last = side_by_side(cells[:, sizes.main_lanes :], count, sizes)
    for at in range(sizes.devices):
        rows = slice(at * sizes.pair, (at + 1) * sizes.pair)
        for piece in range(sizes.pieces):
            if sizes.main:
                first = piece * sizes.main_lanes
                out[at, :, first : first + sizes.main_lanes] = cells[
                    piece * count + at * sizes.pair : piece * count + (at + 1) * sizes.pair, : sizes.main_lanes
                ]
        if sizes.rest:
            out[at, :, sizes.rest_first :] = last[rows]


def swap_parts(values, sizes):
    return pltpu.roll(values, sizes.half, 1)


def mode_rows(first, sizes):
    return pl.ds(first, sizes.channels, stride=sizes.modes)


def put_mixed(spread, at, mode, values, sizes):
    for s in range(2):
        spread[2 * s + at, mode_rows(s * sizes.share + mode, sizes), :] = values


def first_lanes(rows, sizes):
    return lax.broadcasted_iota(jnp.int32, (rows, 2 * sizes.half), 1) < sizes.half


def mix_forward(
    sizes, received, table, weight, other_weight, local, cotangent, inverse, forward,
    spectra, other_spectra, out, local_out, cotangent_out, inverse_out, forward_out,
    spread, swapped, flat, semaphores,
):
    moves = ((local, local_out), (cotangent, cotangent_out), (inverse, inverse_out), (forward, forward_out))
    copies = [pltpu.make_async_copy(*move, semaphores.at[at]) for at, move in enumerate(moves)]
    for copy in copies:
        copy.start()
    plane_spectra(sizes, received, table, (spectra, other_spectra), flat)
    spread[...] = jnp.zeros_like(spread)
    real = first_lanes(sizes.rows, sizes)
    for at, (rows, block) in enumerate(((spectra, weight), (other_spectra, other_weight))):
        swapped[...] = swap_parts(rows[...], sizes)
        for m in range(sizes.share):
            straight = jnp.zeros((sizes.rows, 2 * sizes.half), F32)
            crossed = jnp.zeros((sizes.rows, 2 * sizes.half), F32)
            for w in range(sizes.channels):
                row = slice(w * sizes.modes + m, w * sizes.modes + m + 1)
                straight = straight + rows[row, :] * block[m, w]
                crossed = crossed + swapped[row, :] * block[m, w]
            real_part = straight - swap_parts(straight, sizes)
            imag_part = crossed + swap_parts(crossed, sizes)
            put_mixed(spread, at, m, jnp.where(real, real_part, imag_part)[: sizes.channels], sizes)
    plane_cells(sizes, spread, table, out)
    for copy in copies:
        copy.wait()


def mix_back(sizes, received, table, weight, other_weight, back, other_back, out, spread, flat):
    plane_spectra(sizes, received, table, (back, other_back), flat)
    spread[...] = jnp.zeros_like(spread)
    real = first_lanes(sizes.channels, sizes)
    for at, (source, block) in enumerate(((back, weight), (other_back, other_weight))):
        for m in range(sizes.share):
            rows = source[mode_rows(m, sizes), :]
            if sizes.rows > sizes.channels:
                rows = jnp.concatenate([rows, jnp.zeros((sizes.rows - sizes.channels, 2 * sizes.half), F32)], 0)
            turned = swap_parts(rows, sizes)
            straight, crossed = [], []
            for w in range(sizes.channels):
                straight.append(jnp.sum(block[m, w] * rows, axis=0, keepdims=True))
                crossed.append(jnp.sum(block[m, w] * turned, axis=0, keepdims=True))
            straight = jnp.concatenate(straight, 0)
            crossed = jnp.concatenate(crossed, 0)
            real_part = straight + swap_parts(straight, sizes)
            imag_part = swap_parts(crossed, sizes) - crossed
            put_mixed(spread, at, m, jnp.where(real, real_part, imag_part), sizes)
    plane_cells(sizes, spread, table, out)


def grad_weights(
    sizes, spectra, back, given_spectra, given_back, target, here, straight, crossed, semaphores
):
    copies = []
    for which, (source, backward) in enumerate(((spectra, back), (given_spectra, given_back))):
        half = core_of() if which == 0 else 1 - core_of()
        values = source[...]
        turned = swap_parts(values, sizes)
        real = first_lanes(values.shape[0], sizes)
        straight[...] = jnp.where(real, values, turned)
        crossed[...] = jnp.where(real, turned, -values)
        for mode in range(sizes.share):
            rows = backward[mode_rows(mode, sizes), :]
            if sizes.rows > sizes.channels:
                rows = jnp.concatenate([rows, jnp.zeros((sizes.rows - sizes.channels, 2 * sizes.half), F32)], 0)
            turned = swap_parts(rows, sizes)
            local = 2 * (which * sizes.share + mode)
            for w in range(sizes.channels):
                at = slice(w * sizes.modes + mode, w * sizes.modes + mode + 1)
                block = (straight[at, :] * rows + crossed[at, :] * turned).T
                for s in range(2):
                    part = block[s * sizes.half : s * sizes.half + sizes.kept, : sizes.channels]
                    here[local + s, w] = part.reshape(sizes.local_x, sizes.kept_y, sizes.channels)
            for s in range(2):
                to = 2 * (half * sizes.share + mode) + s
                copies.append(pltpu.make_async_copy(here.at[local + s], target.at[to], semaphores.at[local + s]))
                copies[-1].start()
    for copy in copies:
        copy.wait()


def gelu_parts(pre):
    slope = math.sqrt(2.0 / math.pi)
    squared = pre * pre
    bend = jnp.tanh(slope * (pre + 0.044715 * (squared * pre)))
    value = 0.5 * pre * (1.0 + bend)
    derivative = 0.5 * (1.0 + bend) + 0.5 * pre * (1.0 - bend * bend) * (slope * (1.0 + 3.0 * 0.044715 * squared))
    return value, derivative


def activate(
    sizes, received, local, cotangent, inverse, forward, pre_out, signal_out, out, spectrum, tall
):
    pre = fine_dot(receive_modes(received, spectrum, tall, sizes), inverse[...]) + local[...]
    pre_out[...] = pre
    signal = (cotangent[...] * gelu_parts(pre)[1]).astype(BF16)
    signal_out[...] = signal
    send_modes(dot(signal, forward[...]), out, sizes)


def finish(sizes, received, local, inverse, grad_field, spectrum, tall):
    spatial = fine_dot(receive_modes(received, spectrum, tall, sizes), inverse[...])
    scatter_cells(spatial + local[...], grad_field, sizes)


def shape_of(shape, dtype=F32):
    return jax.ShapeDtypeStruct(shape, dtype)


VMEM = pl.BlockSpec(memory_space=pltpu.VMEM)
HELD = pl.BlockSpec(memory_space=pltpu.VMEM)
HBM = pl.BlockSpec(memory_space=pltpu.HBM)
ANYWHERE = pl.BlockSpec(memory_space=pl.ANY)


def settings(mebibytes):
    return pltpu.CompilerParams(vmem_limit_bytes=mebibytes * 1024 * 1024)


def cost(nanoseconds):
    return pl.CostEstimate(flops=0, bytes_accessed=3000 * nanoseconds, transcendentals=0)


def whole_call(body, sizes, nanoseconds, out_shape, scratch, *args, specs=None, out_specs=None, room=16):
    def kernel(*refs):
        body(sizes, *refs)

    if specs:
        spaces = [pltpu.HBM if spec is HBM else pltpu.VMEM if spec is HELD else None for spec in specs]
        args = [
            pltpu.with_memory_space_constraint(arg, space) if space else arg for arg, space in zip(args, spaces)
        ]
    return pl.pallas_call(
        kernel,
        out_shape=out_shape,
        in_specs=specs or [VMEM] * len(args),
        out_specs=out_specs or jax.tree.map(lambda _: VMEM, out_shape),
        scratch_shapes=scratch,
        name=body.__name__,
        cost_estimate=cost(nanoseconds),
        compiler_params=settings(room),
    )(*args)


def on_device(field, cotangent, spectral_weight, pointwise_weight, channel_bias):
    z = Sizes(field, spectral_weight)
    depth_table = depth_time_table(z.depth)
    modes = depth_table.shape[2]
    kappa = np.where(np.arange(modes) % KT == 0, 1.0, 2.0).astype(np.float32)
    shares = (z.nx, 2, z.share)
    ordered = depth_table.reshape((z.depth, 2) + shares).transpose(0, 2, 3, 1, 4).reshape(z.depth, z.all_modes)
    doubled = np.repeat(kappa.reshape(z.nx, 2, 1, z.share), 2, axis=2).reshape(z.all_modes)
    forward_first = jnp.asarray(ordered.astype(ml_dtypes.bfloat16))
    forward_back = jnp.asarray((ordered.astype(ml_dtypes.bfloat16).astype(np.float32) * doubled).astype(ml_dtypes.bfloat16))
    inverse_back = jnp.asarray(np.ascontiguousarray(ordered.T))
    inverse_first = jnp.asarray(np.ascontiguousarray((ordered * doubled).T))
    pairs = [(s, s ^ 1) for s in range(z.ny)]

    def exchange(payload):
        return lax.all_to_all(payload, ("gx", "gy"), split_axis=0, concat_axis=0, tiled=True)

    def other_core(values):
        return lax.ppermute(values, "gy", pairs)

    payload = shape_of((z.devices, z.pair, z.width))
    cell_rows = z.channels * z.cells
    cells_shape = (cell_rows, z.depth)
    cells_scratch = pltpu.VMEM(cells_shape, F32)
    spectrum_scratch = pltpu.VMEM((cell_rows, z.all_modes), F32)
    spectra_shape = (z.channels * z.modes, 2 * z.half)
    spectra_scratch = pltpu.VMEM(spectra_shape, F32)
    flat_scratch = pltpu.VMEM((z.devices * z.cells, z.spread_rows), F32)
    spread_scratch = pltpu.VMEM((4, z.spread_rows, 2 * z.half), F32)
    tall_scratch = pltpu.VMEM((2 * z.nx, z.cells, z.spread_rows), F32)
    field_scratch = pltpu.VMEM(field.shape, BF16)
    weight_here = pltpu.VMEM(pointwise_weight.shape, BF16)
    native = jnp.transpose(spectral_weight, (0, 1, 2, 4, 5, 3))
    weight_shape = (2 * z.modes,) + native.shape[2:]
    half_scratch = pltpu.VMEM((z.modes,) + native.shape[2:], F32)
    turned_shape = shape_of((z.share, z.channels, z.rows, 2 * z.half))

    def flags(count):
        return pltpu.SemaphoreType.DMA((count,))

    weights = native.reshape(weight_shape)
    sent, turned_away = whole_call(
        depth_forward, z, 1500, (payload, turned_shape),
        [
            cells_scratch, field_scratch, pltpu.VMEM(forward_first.shape, BF16), pltpu.VMEM(payload.shape, F32),
            half_scratch, flags(3), flags(z.modes),
        ],
        field, forward_first, weights, specs=[HBM] * 3, out_specs=(HBM, VMEM),
    )
    received = exchange(sent)
    other_turned = other_core(turned_away)
    turned, plane, local, cot_cells = whole_call(
        prepare, z, 100,
        (turned_shape, shape_of((z.devices * z.cells, 8 * z.half)), shape_of(cells_shape), shape_of(cells_shape)),
        [
            half_scratch, cells_scratch, field_scratch, field_scratch, cells_scratch, weight_here,
            pltpu.VMEM(channel_bias.shape, F32), cells_scratch, flags(z.modes), flags(8),
        ],
        weights, turned_away, jnp.asarray(plane_tables(z)), field, cotangent, pointwise_weight, channel_bias,
        specs=[HBM, ANYWHERE] + [HBM] * 5, out_specs=(VMEM, VMEM, HBM, HBM),
    )
    received, other_turned, turned, plane, local, cot_cells = lax.optimization_barrier(
        (received, other_turned, turned, plane, local, cot_cells)
    )
    spectra, other_spectra, sent, local, cot_cells, inverse_here, forward_here = whole_call(
        mix_forward, z, 1000,
        (
            shape_of(spectra_shape), shape_of(spectra_shape), payload, shape_of(cells_shape), shape_of(cells_shape),
            shape_of(inverse_first.shape), shape_of(forward_back.shape, BF16),
        ),
        [spread_scratch, spectra_scratch, flat_scratch, flags(4)],
        received, plane, turned, other_turned, local, cot_cells, inverse_first, forward_back,
        specs=[HELD] + [VMEM] * 3 + [HBM] * 4,
    )
    pre, signal, sent = whole_call(
        activate, z, 2000,
        (shape_of(cells_shape), shape_of(cells_shape, BF16), payload), [spectrum_scratch, tall_scratch],
        exchange(sent), local, cot_cells, inverse_here, forward_here,
    )
    back, other_back, sent = whole_call(
        mix_back, z, 1000, (shape_of(spectra_shape), shape_of(spectra_shape), payload),
        [spread_scratch, flat_scratch], exchange(sent), plane, turned, other_turned,
    )
    sent, spectra, other_spectra, back, other_back, pre, signal = lax.optimization_barrier(
        (sent, spectra, other_spectra, back, other_back, pre, signal)
    )
    returned = exchange(sent)
    given_spectra, given_back = other_core(other_spectra), other_core(other_back)
    layer_out, local, inverse_here = whole_call(
        emit, z, 1500,
        (shape_of(field.shape, BF16), shape_of(cells_shape), shape_of(inverse_back.shape)),
        [weight_here, flags(2)],
        pre, signal, pointwise_weight, inverse_back, specs=[VMEM, VMEM, HBM, HBM],
    )
    gradient = whole_call(
        grad_weights, z, 5000, shape_of(weight_shape),
        [pltpu.VMEM(weight_shape, F32), spectra_scratch, spectra_scratch, flags(2 * z.modes)],
        spectra, back, given_spectra, given_back, out_specs=HBM, room=28,
    )
    returned, gradient, layer_out, local, inverse_here = lax.optimization_barrier(
        (returned, gradient, layer_out, local, inverse_here)
    )
    grad_field = whole_call(
        finish, z, 1000, shape_of(field.shape, BF16), [spectrum_scratch, tall_scratch], returned, local, inverse_here
    )
    return (layer_out, grad_field, jnp.transpose(gradient.reshape(native.shape), (0, 1, 2, 5, 3, 4)))


def solution(mesh):
    return jax.shard_map(
        on_device,
        mesh=mesh,
        in_specs=(
            P(None, "gx", "gy", None),
            P(None, "gx", "gy", None),
            P("gx", None, None, None, "gy", None),
            P(),
            P(),
        ),
        out_specs=(
            P(None, "gx", "gy", None),
            P(None, "gx", "gy", None),
            P("gx", None, None, None, "gy", None),
        ),
        check_vma=False,
    )
```

```python
import math

import jax
import jax.numpy as jnp
import ml_dtypes
import numpy as np
from jax import lax
from jax.experimental import pallas as pl
from jax.experimental.pallas import tpu as pltpu
from jax.sharding import PartitionSpec as P

KZ = 16
KT = 4
NT = 16
LANES = 128
F32 = jnp.float32
BF16 = jnp.bfloat16


def round_up(value, step):
    return -(-value // step) * step


def frequencies(kept):
    index = np.arange(kept)
    return np.where(index < kept // 2, index, index - kept)


def depth_time_table(cells):
    depth_cells = cells // NT
    depth = np.arange(depth_cells)[:, None, None, None] * frequencies(KZ)[None, None, :, None] * NT
    time = np.arange(NT)[None, :, None, None] * np.arange(KT)[None, None, None, :] * depth_cells
    phase = np.mod(depth + time, cells).reshape(cells, KZ * KT)
    angles = phase.astype(np.float32) * np.float32(2.0 * math.pi / cells)
    factor = np.float32(1.0 / math.sqrt(cells))
    return np.stack([np.cos(angles) * factor, -np.sin(angles) * factor], axis=1).astype(np.float32)


def plane_tables(sizes):
    length_x, length_y = sizes.nx * sizes.cells_x, sizes.ny * sizes.cells_y
    phase_x = np.mod(np.arange(length_x)[:, None] * frequencies(sizes.kept_x), length_x) / length_x
    phase_y = np.mod(np.arange(length_y)[:, None] * frequencies(sizes.kept_y), length_y) / length_y
    angle = 2.0 * math.pi * (phase_x[:, None, :, None] + phase_y[None, :, None, :])
    scale = 1.0 / math.sqrt(length_x * length_y)
    cosine, sine = np.cos(angle) * scale, np.sin(angle) * scale
    parts = np.stack([np.stack([cosine, -sine]), np.stack([sine, cosine])])
    pairs = sizes.cells_y // sizes.pair
    parts = parts.reshape(
        2, 2, sizes.nx, sizes.cells_x, sizes.ny, pairs, sizes.pair, sizes.ny, sizes.kept
    ).transpose(7, 3, 5, 2, 4, 6, 0, 1, 8)
    padded = np.zeros(parts.shape[:-1] + (sizes.half,), np.float32)
    padded[..., : sizes.kept] = parts
    return padded.reshape(sizes.ny, sizes.devices * sizes.cells, 4 * sizes.half)


class Sizes:
    def __init__(self, field, weight):
        self.nx, self.ny = lax.axis_size("gx"), lax.axis_size("gy")
        self.channels, self.cells_x, self.cells_y, self.depth = field.shape
        self.modes = weight.shape[0]
        self.local_x, self.kept_y = weight.shape[4:]
        self.kept_x = self.local_x * self.ny
        self.cells = self.cells_x * self.cells_y
        self.devices = self.nx * self.ny
        self.share = self.modes // 2
        self.kept = self.local_x * self.kept_y
        self.half = round_up(self.kept, LANES // 2)
        self.all_modes = 2 * self.modes * self.nx
        self.groups = LANES // self.modes
        self.main = self.channels // self.groups * self.groups if self.all_modes == LANES else 0
        self.rest = self.channels - self.main
        self.main_lanes = self.main * self.modes
        self.rest_lanes = self.rest * self.modes
        self.rest_tiles = round_up(self.rest_lanes, LANES) // LANES
        self.pair = math.gcd(self.cells_y, 2)
        self.pieces = self.cells // self.pair
        self.rest_first = self.pieces * self.main_lanes
        self.rest_width = round_up(self.pieces * self.rest_lanes, LANES)
        self.width = self.rest_first + self.rest_width
        self.spread_rows = self.main_lanes + self.rest_width
        self.rows = round_up(self.channels, 8)


def gather_cells(source, scratch, sizes):
    for w in range(sizes.channels):
        for x in range(sizes.cells_x):
            first = (w * sizes.cells_x + x) * sizes.cells_y
            scratch[first : first + sizes.cells_y, :] = source[w, x].astype(F32)
    return scratch[...]


def scatter_cells(values, target, sizes):
    for w in range(sizes.channels):
        for x in range(sizes.cells_x):
            first = (w * sizes.cells_x + x) * sizes.cells_y
            target[w, x] = values[first : first + sizes.cells_y, :].astype(target.dtype)


def lane_group(sizes):
    return lax.broadcasted_iota(jnp.int32, (sizes.cells, LANES), 1) // sizes.modes


def turn_groups(tiles, group, sizes):
    tiles = list(tiles)
    step = 1
    while step < sizes.groups:
        low = group // step % 2 == 0
        for first in range(sizes.groups):
            if first // step % 2 == 0:
                one, two = tiles[first], tiles[first + step]
                tiles[first] = jnp.where(low, one, pltpu.roll(two, step * sizes.modes, 1))
                tiles[first + step] = jnp.where(low, pltpu.roll(one, LANES - step * sizes.modes, 1), two)
        step *= 2
    return tiles


def put_group(target, source, have, want, group, sizes):
    if have != want:
        source = pltpu.roll(source, (want - have) % sizes.groups * sizes.modes, 1)
    return jnp.where(group == want, source, target)


def send_modes(values, target, sizes):
    group = lane_group(sizes)
    tiles = [values[w * sizes.cells : (w + 1) * sizes.cells, :] for w in range(sizes.channels)]
    turned = []
    for first in range(0, sizes.main, sizes.groups):
        turned.append(turn_groups(tiles[first : first + sizes.groups], group, sizes))
    for at in range(2 * sizes.nx):
        main = [block[at] for block in turned]
        last = [jnp.zeros((sizes.cells, LANES), F32) for _ in range(sizes.rest_width // LANES)]
        for r in range(sizes.rest):
            tile, want = divmod(r, sizes.groups)
            last[tile] = put_group(last[tile], tiles[sizes.main + r], at, want, group, sizes)
        if last:
            last = side_by_side(jnp.concatenate(last, 1), sizes.pair, sizes)
        for y in range(sizes.ny // 2):
            device = at // 2 * sizes.ny + 2 * y + at % 2
            for piece in range(sizes.pieces):
                rows = slice(piece * sizes.pair, (piece + 1) * sizes.pair)
                for k, value in enumerate(main):
                    first = piece * sizes.main_lanes + k * LANES
                    target[device, :, first : first + LANES] = value[rows]
            if sizes.rest:
                target[device, :, sizes.rest_first :] = last


def side_by_side(values, rows, sizes):
    total = values[:rows]
    for piece in range(1, sizes.pieces):
        moved = pltpu.roll(values, piece * sizes.rest_lanes, 1)
        total = total + moved[piece * rows : (piece + 1) * rows]
    return total


def receive_modes(source, scratch, tall, sizes):
    group = lane_group(sizes)
    parts = source[...].reshape(sizes.nx, sizes.ny // 2, 2, sizes.pair, sizes.width)
    values = parts[:, 0]
    for y in range(1, sizes.ny // 2):
        values = values + parts[:, y]
    values = values.reshape(2 * sizes.nx, sizes.pair, sizes.width)
    for piece in range(sizes.pieces):
        rows = slice(piece * sizes.pair, (piece + 1) * sizes.pair)
        if sizes.main:
            first = piece * sizes.main_lanes
            tall[:, rows, : sizes.main_lanes] = values[:, :, first : first + sizes.main_lanes]
        if sizes.rest:
            last = values[:, :, sizes.rest_first :]
            if piece:
                last = pltpu.roll(last, sizes.rest_width - piece * sizes.rest_lanes, 2)
            tall[:, rows, sizes.main_lanes :] = last
    out = []
    for first in range(0, sizes.main_lanes, LANES):
        tiles = [tall[at, :, first : first + LANES] for at in range(2 * sizes.nx)]
        out += turn_groups(tiles, group, sizes)
    for r in range(sizes.rest):
        value = jnp.zeros((sizes.cells, LANES), F32)
        tile, have = divmod(r, sizes.groups)
        first = sizes.main_lanes + tile * LANES
        for at in range(2 * sizes.nx):
            value = put_group(value, tall[at, :, first : first + LANES], have, at, group, sizes)
        out.append(value)
    for w, value in enumerate(out):
        scratch[w * sizes.cells : (w + 1) * sizes.cells, :] = value
    return scratch[...]


def dot(left, right, contract=((1,), (0,))):
    return lax.dot_general(left, right, (contract, ((), ())), preferred_element_type=F32)


def halves(values):
    high = values.astype(BF16)
    return high, (values - high.astype(F32)).astype(BF16)


def fine_dot(left, right, contract=((1,), (0,))):
    left_high, left_low = halves(left)
    right_high, right_low = halves(right)
    small = dot(left_high, right_low, contract) + dot(left_low, right_high, contract)
    return dot(left_high, right_high, contract) + small


def fetch(sources, targets, semaphores):
    copies = [pltpu.make_async_copy(*pair, semaphores.at[at]) for at, pair in enumerate(zip(sources, targets))]
    for copy in copies:
        copy.start()
    for copy in copies:
        copy.wait()


def depth_forward(
    sizes, field, table, source, out, target,
    cells, field_here, table_here, out_here, here, semaphores, weight_semaphores,
):
    few = [
        pltpu.make_async_copy(field, field_here, semaphores.at[0]),
        pltpu.make_async_copy(table, table_here, semaphores.at[1]),
    ]
    for copy in few:
        copy.start()
    copies = start_weights(sizes, source, 1 - core_of(), here, weight_semaphores)
    clear_weights(sizes, target)
    for copy in few:
        copy.wait()
    values = gather_cells(field_here, cells, sizes).astype(BF16)
    send_modes(dot(values, table_here[...]), out_here, sizes)
    copy = pltpu.make_async_copy(out_here, out, semaphores.at[2])
    copy.start()
    turn_weights(sizes, copies, here, target)
    copy.wait()


def one_hot(rows, columns, step, along_rows):
    row = lax.broadcasted_iota(jnp.int32, (rows, columns), 0)
    column = lax.broadcasted_iota(jnp.int32, (rows, columns), 1)
    same = row // step == column if along_rows else row == column // step
    return jnp.where(same, 1.0, 0.0).astype(BF16)


def cell_mixer(weights, across, sizes):
    count = sizes.channels * sizes.cells
    left = one_hot(count, sizes.channels, sizes.cells, True)
    right = one_hot(sizes.channels, count, sizes.cells, False)
    tall = dot(left, weights, ((1,), (1 if across else 0,)))
    wide = dot(tall.astype(BF16), right)
    row = lax.broadcasted_iota(jnp.int32, (count, count), 0)
    column = lax.broadcasted_iota(jnp.int32, (count, count), 1)
    same = lax.rem(row, sizes.cells) == lax.rem(column, sizes.cells)
    return jnp.where(same, wide, 0.0).astype(BF16)


def emit(sizes, pre, signal, weight, inverse, layer_out, local, inverse_out, weight_here, semaphores):
    copies = [
        pltpu.make_async_copy(weight, weight_here, semaphores.at[0]),
        pltpu.make_async_copy(inverse, inverse_out, semaphores.at[1]),
    ]
    for copy in copies:
        copy.start()
    scatter_cells(gelu_parts(pre[...])[0], layer_out, sizes)
    copies[0].wait()
    local[...] = dot(cell_mixer(weight_here[...], False, sizes), signal[...])
    copies[1].wait()


def core_of():
    return lax.rem(lax.axis_index("gy"), 2)


def start_weights(sizes, source, half, here, semaphores):
    copies = []
    for at in range(2 * sizes.share):
        copies.append(pltpu.make_async_copy(source.at[2 * sizes.share * half + at], here.at[at], semaphores.at[at]))
        copies[-1].start()
    return copies


def clear_weights(sizes, target):
    if sizes.half > sizes.kept:
        target[...] = jnp.zeros_like(target)
    elif sizes.rows > sizes.channels:
        target[:, :, sizes.channels :, :] = jnp.zeros(
            (sizes.share, sizes.channels, sizes.rows - sizes.channels, 2 * sizes.half), F32
        )


def turn_weights(sizes, copies, here, target):
    for mode in range(sizes.share):
        for s in range(2):
            copies[2 * mode + s].wait()
        for w in range(sizes.channels):
            blocks = [here[2 * mode + s, w].reshape(sizes.kept, sizes.channels) for s in range(2)]
            if sizes.half == sizes.kept:
                target[mode, w, : sizes.channels, :] = jnp.concatenate(blocks, 0).T
            else:
                for s, block in enumerate(blocks):
                    target[mode, w, : sizes.channels, s * sizes.half : s * sizes.half + sizes.kept] = block.T


def prepare(
    sizes, source, after, tables, field, cotangent, weight, bias,
    target, table, local, cotangent_out,
    here, cells, field_here, cot_here, cot_cells, weight_here, bias_here, local_here, semaphores, small,
):
    del after
    place = lax.axis_index("gy")
    lanes = 2 * sizes.half
    moves = [(field, field_here), (cotangent, cot_here), (weight, weight_here), (bias, bias_here)]
    for s in range(2):
        for at, owner in enumerate((place, place + 1 - 2 * core_of())):
            moves.append(
                (tables.at[owner, :, pl.ds(s * lanes, lanes)], table.at[:, pl.ds((2 * s + at) * lanes, lanes)])
            )
    few = [pltpu.make_async_copy(*move, small.at[at]) for at, move in enumerate(moves)]
    copies = start_weights(sizes, source, core_of(), here, semaphores)
    for copy in few:
        copy.start()
    clear_weights(sizes, target)
    turn_weights(sizes, copies, here, target)
    for copy in few:
        copy.wait()
    values = gather_cells(field_here, cells, sizes).astype(BF16)
    spread = one_hot(sizes.channels * sizes.cells, sizes.channels, sizes.cells, True).astype(F32)
    offset = jnp.sum(spread * bias_here[...].reshape(1, sizes.channels), axis=1, keepdims=True)
    local_here[...] = dot(cell_mixer(weight_here[...], True, sizes), values) + offset
    gather_cells(cot_here, cot_cells, sizes)
    results = [
        pltpu.make_async_copy(local_here, local, small.at[0]),
        pltpu.make_async_copy(cot_cells, cotangent_out, small.at[1]),
    ]
    for copy in results:
        copy.start()
    for copy in results:
        copy.wait()


def plane_spectra(sizes, received, table, targets, flat):
    count = sizes.devices * sizes.pair
    for at in range(sizes.devices):
        for piece in range(sizes.pieces):
            rows = slice(piece * count + at * sizes.pair, piece * count + (at + 1) * sizes.pair)
            if sizes.main:
                first = piece * sizes.main_lanes
                flat[rows, : sizes.main_lanes] = received[at, :, first : first + sizes.main_lanes]
            if sizes.rest:
                flat[rows, sizes.main_lanes :] = received[at, :, sizes.rest_first :]
    if sizes.rest:
        for piece in range(1, sizes.pieces):
            rows = slice(piece * count, (piece + 1) * count)
            shift = sizes.rest_width - piece * sizes.rest_lanes
            flat[rows, sizes.main_lanes :] = pltpu.roll(flat[rows, sizes.main_lanes :], shift, 1)
    rows, lanes = targets[0].shape
    both = fine_dot(flat[...].T[:rows], table[...])
    total = both[:, : 2 * lanes] + pltpu.roll(both[:, 2 * lanes :], rows - sizes.share, 0)
    for at, target in enumerate(targets):
        target[...] = total[:, at * lanes : (at + 1) * lanes]


def plane_cells(sizes, spread, table, out):
    modes = jnp.concatenate([spread[at] for at in range(4)], 1)
    cells = fine_dot(table[...], modes, ((1,), (1,)))
    count = sizes.devices * sizes.pair
    if sizes.rest:
        last = side_by_side(cells[:, sizes.main_lanes :], count, sizes)
    for at in range(sizes.devices):
        rows = slice(at * sizes.pair, (at + 1) * sizes.pair)
        for piece in range(sizes.pieces):
            if sizes.main:
                first = piece * sizes.main_lanes
                out[at, :, first : first + sizes.main_lanes] = cells[
                    piece * count + at * sizes.pair : piece * count + (at + 1) * sizes.pair, : sizes.main_lanes
                ]
        if sizes.rest:
            out[at, :, sizes.rest_first :] = last[rows]


def swap_parts(values, sizes):
    return pltpu.roll(values, sizes.half, 1)


def mode_rows(first, sizes):
    return pl.ds(first, sizes.channels, stride=sizes.modes)


def put_mixed(spread, at, mode, values, sizes):
    for s in range(2):
        spread[2 * s + at, mode_rows(s * sizes.share + mode, sizes), :] = values


def first_lanes(rows, sizes):
    return lax.broadcasted_iota(jnp.int32, (rows, 2 * sizes.half), 1) < sizes.half


def mix_forward(
    sizes, received, table, weight, other_weight, local, cotangent, inverse, forward,
    spectra, other_spectra, out, local_out, cotangent_out, inverse_out, forward_out,
    spread, swapped, flat, other_here, semaphores,
):
    moves = (
        (other_weight, other_here), (local, local_out), (cotangent, cotangent_out), (inverse, inverse_out),
        (forward, forward_out),
    )
    copies = [pltpu.make_async_copy(*move, semaphores.at[at]) for at, move in enumerate(moves)]
    for copy in copies:
        copy.start()
    plane_spectra(sizes, received, table, (spectra, other_spectra), flat)
    spread[...] = jnp.zeros_like(spread)
    real = first_lanes(sizes.rows, sizes)
    for at, (rows, block) in enumerate(((spectra, weight), (other_spectra, other_here))):
        if at:
            copies[0].wait()
        swapped[...] = swap_parts(rows[...], sizes)
        for m in range(sizes.share):
            straight = jnp.zeros((sizes.rows, 2 * sizes.half), F32)
            crossed = jnp.zeros((sizes.rows, 2 * sizes.half), F32)
            for w in range(sizes.channels):
                row = slice(w * sizes.modes + m, w * sizes.modes + m + 1)
                straight = straight + rows[row, :] * block[m, w]
                crossed = crossed + swapped[row, :] * block[m, w]
            real_part = straight - swap_parts(straight, sizes)
            imag_part = crossed + swap_parts(crossed, sizes)
            put_mixed(spread, at, m, jnp.where(real, real_part, imag_part)[: sizes.channels], sizes)
    plane_cells(sizes, spread, table, out)
    for copy in copies[1:]:
        copy.wait()


def mix_back(sizes, received, table, weight, other_weight, back, other_back, out, spread, flat, other_here, semaphore):
    copy = pltpu.make_async_copy(other_weight, other_here, semaphore.at[0])
    copy.start()
    plane_spectra(sizes, received, table, (back, other_back), flat)
    spread[...] = jnp.zeros_like(spread)
    real = first_lanes(sizes.channels, sizes)
    for at, (source, block) in enumerate(((back, weight), (other_back, other_here))):
        if at:
            copy.wait()
        for m in range(sizes.share):
            rows = source[mode_rows(m, sizes), :]
            if sizes.rows > sizes.channels:
                rows = jnp.concatenate([rows, jnp.zeros((sizes.rows - sizes.channels, 2 * sizes.half), F32)], 0)
            turned = swap_parts(rows, sizes)
            straight, crossed = [], []
            for w in range(sizes.channels):
                straight.append(jnp.sum(block[m, w] * rows, axis=0, keepdims=True))
                crossed.append(jnp.sum(block[m, w] * turned, axis=0, keepdims=True))
            straight = jnp.concatenate(straight, 0)
            crossed = jnp.concatenate(crossed, 0)
            real_part = straight + swap_parts(straight, sizes)
            imag_part = swap_parts(crossed, sizes) - crossed
            put_mixed(spread, at, m, jnp.where(real, real_part, imag_part), sizes)
    plane_cells(sizes, spread, table, out)


def grad_weights(
    sizes, spectra, back, given_spectra, given_back, target, here, straight, crossed, semaphores
):
    copies = []
    for which, (source, backward) in enumerate(((spectra, back), (given_spectra, given_back))):
        half = core_of() if which == 0 else 1 - core_of()
        values = source[...]
        turned = swap_parts(values, sizes)
        real = first_lanes(values.shape[0], sizes)
        straight[...] = jnp.where(real, values, turned)
        crossed[...] = jnp.where(real, turned, -values)
        for mode in range(sizes.share):
            rows = backward[mode_rows(mode, sizes), :]
            if sizes.rows > sizes.channels:
                rows = jnp.concatenate([rows, jnp.zeros((sizes.rows - sizes.channels, 2 * sizes.half), F32)], 0)
            turned = swap_parts(rows, sizes)
            local = 2 * (which * sizes.share + mode)
            for w in range(sizes.channels):
                at = slice(w * sizes.modes + mode, w * sizes.modes + mode + 1)
                block = (straight[at, :] * rows + crossed[at, :] * turned).T
                for s in range(2):
                    part = block[s * sizes.half : s * sizes.half + sizes.kept, : sizes.channels]
                    here[local + s, w] = part.reshape(sizes.local_x, sizes.kept_y, sizes.channels)
            for s in range(2):
                to = 2 * (half * sizes.share + mode) + s
                copies.append(pltpu.make_async_copy(here.at[local + s], target.at[to], semaphores.at[local + s]))
                copies[-1].start()
    for copy in copies:
        copy.wait()


def gelu_parts(pre):
    slope = math.sqrt(2.0 / math.pi)
    squared = pre * pre
    bend = jnp.tanh(slope * (pre + 0.044715 * (squared * pre)))
    value = 0.5 * pre * (1.0 + bend)
    derivative = 0.5 * (1.0 + bend) + 0.5 * pre * (1.0 - bend * bend) * (slope * (1.0 + 3.0 * 0.044715 * squared))
    return value, derivative


def activate(
    sizes, received, local, cotangent, inverse, forward, pre_out, signal_out, out, spectrum, tall
):
    pre = fine_dot(receive_modes(received, spectrum, tall, sizes), inverse[...]) + local[...]
    pre_out[...] = pre
    signal = (cotangent[...] * gelu_parts(pre)[1]).astype(BF16)
    signal_out[...] = signal
    send_modes(dot(signal, forward[...]), out, sizes)


def finish(sizes, received, local, inverse, grad_field, spectrum, tall):
    spatial = fine_dot(receive_modes(received, spectrum, tall, sizes), inverse[...])
    scatter_cells(spatial + local[...], grad_field, sizes)


def shape_of(shape, dtype=F32):
    return jax.ShapeDtypeStruct(shape, dtype)


VMEM = pl.BlockSpec(memory_space=pltpu.VMEM)
HELD = pl.BlockSpec(memory_space=pltpu.VMEM)
HBM = pl.BlockSpec(memory_space=pltpu.HBM)
ANYWHERE = pl.BlockSpec(memory_space=pl.ANY)


def settings(mebibytes):
    return pltpu.CompilerParams(vmem_limit_bytes=mebibytes * 1024 * 1024)


def cost(nanoseconds):
    return pl.CostEstimate(flops=0, bytes_accessed=3000 * nanoseconds, transcendentals=0)


def whole_call(body, sizes, nanoseconds, out_shape, scratch, *args, specs=None, out_specs=None, room=16):
    def kernel(*refs):
        body(sizes, *refs)

    if specs:
        spaces = [pltpu.HBM if spec is HBM else pltpu.VMEM if spec is HELD else None for spec in specs]
        args = [
            pltpu.with_memory_space_constraint(arg, space) if space else arg for arg, space in zip(args, spaces)
        ]
    return pl.pallas_call(
        kernel,
        out_shape=out_shape,
        in_specs=specs or [VMEM] * len(args),
        out_specs=out_specs or jax.tree.map(lambda _: VMEM, out_shape),
        scratch_shapes=scratch,
        name=body.__name__,
        cost_estimate=cost(nanoseconds),
        compiler_params=settings(room),
    )(*args)


def on_device(field, cotangent, spectral_weight, pointwise_weight, channel_bias):
    z = Sizes(field, spectral_weight)
    depth_table = depth_time_table(z.depth)
    modes = depth_table.shape[2]
    kappa = np.where(np.arange(modes) % KT == 0, 1.0, 2.0).astype(np.float32)
    shares = (z.nx, 2, z.share)
    ordered = depth_table.reshape((z.depth, 2) + shares).transpose(0, 2, 3, 1, 4).reshape(z.depth, z.all_modes)
    doubled = np.repeat(kappa.reshape(z.nx, 2, 1, z.share), 2, axis=2).reshape(z.all_modes)
    forward_first = jnp.asarray(ordered.astype(ml_dtypes.bfloat16))
    forward_back = jnp.asarray((ordered.astype(ml_dtypes.bfloat16).astype(np.float32) * doubled).astype(ml_dtypes.bfloat16))
    inverse_back = jnp.asarray(np.ascontiguousarray(ordered.T))
    inverse_first = jnp.asarray(np.ascontiguousarray((ordered * doubled).T))
    pairs = [(s, s ^ 1) for s in range(z.ny)]

    def exchange(payload):
        return lax.all_to_all(payload, ("gx", "gy"), split_axis=0, concat_axis=0, tiled=True)

    def other_core(values):
        return lax.ppermute(values, "gy", pairs)

    payload = shape_of((z.devices, z.pair, z.width))
    cell_rows = z.channels * z.cells
    cells_shape = (cell_rows, z.depth)
    cells_scratch = pltpu.VMEM(cells_shape, F32)
    spectrum_scratch = pltpu.VMEM((cell_rows, z.all_modes), F32)
    spectra_shape = (z.channels * z.modes, 2 * z.half)
    spectra_scratch = pltpu.VMEM(spectra_shape, F32)
    flat_scratch = pltpu.VMEM((z.devices * z.cells, z.spread_rows), F32)
    spread_scratch = pltpu.VMEM((4, z.spread_rows, 2 * z.half), F32)
    tall_scratch = pltpu.VMEM((2 * z.nx, z.cells, z.spread_rows), F32)
    field_scratch = pltpu.VMEM(field.shape, BF16)
    weight_here = pltpu.VMEM(pointwise_weight.shape, BF16)
    native = jnp.transpose(spectral_weight, (0, 1, 2, 4, 5, 3))
    weight_shape = (2 * z.modes,) + native.shape[2:]
    half_scratch = pltpu.VMEM((z.modes,) + native.shape[2:], F32)
    turned_shape = shape_of((z.share, z.channels, z.rows, 2 * z.half))

    def flags(count):
        return pltpu.SemaphoreType.DMA((count,))

    weights = native.reshape(weight_shape)
    sent, turned_away = whole_call(
        depth_forward, z, 1500, (payload, turned_shape),
        [
            cells_scratch, field_scratch, pltpu.VMEM(forward_first.shape, BF16), pltpu.VMEM(payload.shape, F32),
            half_scratch, flags(3), flags(z.modes),
        ],
        field, forward_first, weights, specs=[HBM] * 3, out_specs=(HBM, VMEM),
    )
    received = exchange(sent)
    other_turned = other_core(turned_away)
    turned, plane, local, cot_cells = whole_call(
        prepare, z, 100,
        (turned_shape, shape_of((z.devices * z.cells, 8 * z.half)), pltpu.HBM(cells_shape, F32), pltpu.HBM(cells_shape, F32)),
        [
            half_scratch, cells_scratch, field_scratch, field_scratch, cells_scratch, weight_here,
            pltpu.VMEM(channel_bias.shape, F32), cells_scratch, flags(z.modes), flags(8),
        ],
        weights, turned_away, jnp.asarray(plane_tables(z)), field, cotangent, pointwise_weight, channel_bias,
        specs=[HBM, ANYWHERE] + [HBM] * 5, out_specs=(VMEM, VMEM, HBM, HBM),
    )
    received, other_turned, turned, plane, local, cot_cells = lax.optimization_barrier(
        (received, other_turned, turned, plane, local, cot_cells)
    )
    spectra, other_spectra, sent, local, cot_cells, inverse_here, forward_here = whole_call(
        mix_forward, z, 1000,
        (
            shape_of(spectra_shape), shape_of(spectra_shape), payload, shape_of(cells_shape), shape_of(cells_shape),
            shape_of(inverse_first.shape), shape_of(forward_back.shape, BF16),
        ),
        [spread_scratch, spectra_scratch, flat_scratch, pltpu.VMEM(turned_shape.shape, F32), flags(5)],
        received, plane, turned, other_turned, local, cot_cells, inverse_first, forward_back,
        specs=[HELD] + [VMEM] * 2 + [HBM] * 5,
    )
    pre, signal, sent = whole_call(
        activate, z, 2000,
        (shape_of(cells_shape), shape_of(cells_shape, BF16), payload), [spectrum_scratch, tall_scratch],
        exchange(sent), local, cot_cells, inverse_here, forward_here,
    )
    back, other_back, sent = whole_call(
        mix_back, z, 1000, (shape_of(spectra_shape), shape_of(spectra_shape), payload),
        [spread_scratch, flat_scratch, pltpu.VMEM(turned_shape.shape, F32), flags(1)],
        exchange(sent), plane, turned, other_turned, specs=[VMEM] * 3 + [HBM],
    )
    sent, spectra, other_spectra, back, other_back, pre, signal = lax.optimization_barrier(
        (sent, spectra, other_spectra, back, other_back, pre, signal)
    )
    returned = exchange(sent)
    given_spectra, given_back = other_core(other_spectra), other_core(other_back)
    layer_out, local, inverse_here = whole_call(
        emit, z, 1500,
        (shape_of(field.shape, BF16), shape_of(cells_shape), shape_of(inverse_back.shape)),
        [weight_here, flags(2)],
        pre, signal, pointwise_weight, inverse_back, specs=[VMEM, VMEM, HBM, HBM],
    )
    gradient = whole_call(
        grad_weights, z, 5000, shape_of(weight_shape),
        [pltpu.VMEM(weight_shape, F32), spectra_scratch, spectra_scratch, flags(2 * z.modes)],
        spectra, back, given_spectra, given_back, out_specs=HBM, room=28,
    )
    returned, gradient, layer_out, local, inverse_here = lax.optimization_barrier(
        (returned, gradient, layer_out, local, inverse_here)
    )
    grad_field = whole_call(
        finish, z, 1000, shape_of(field.shape, BF16), [spectrum_scratch, tall_scratch], returned, local, inverse_here
    )
    return (layer_out, grad_field, jnp.transpose(gradient.reshape(native.shape), (0, 1, 2, 5, 3, 4)))


def solution(mesh):
    return jax.shard_map(
        on_device,
        mesh=mesh,
        in_specs=(
            P(None, "gx", "gy", None),
            P(None, "gx", "gy", None),
            P("gx", None, None, None, "gy", None),
            P(),
            P(),
        ),
        out_specs=(
            P(None, "gx", "gy", None),
            P(None, "gx", "gy", None),
            P("gx", None, None, None, "gy", None),
        ),
        check_vma=False,
    )
```

```python
import math

import jax
import jax.numpy as jnp
import ml_dtypes
import numpy as np
from jax import lax
from jax.experimental import pallas as pl
from jax.experimental.pallas import tpu as pltpu
from jax.sharding import PartitionSpec as P

KZ = 16
KT = 4
NT = 16
LANES = 128
F32 = jnp.float32
BF16 = jnp.bfloat16


def round_up(value, step):
    return -(-value // step) * step


def frequencies(kept):
    index = np.arange(kept)
    return np.where(index < kept // 2, index, index - kept)


def depth_time_table(cells):
    depth_cells = cells // NT
    depth = np.arange(depth_cells)[:, None, None, None] * frequencies(KZ)[None, None, :, None] * NT
    time = np.arange(NT)[None, :, None, None] * np.arange(KT)[None, None, None, :] * depth_cells
    phase = np.mod(depth + time, cells).reshape(cells, KZ * KT)
    angles = phase.astype(np.float32) * np.float32(2.0 * math.pi / cells)
    factor = np.float32(1.0 / math.sqrt(cells))
    return np.stack([np.cos(angles) * factor, -np.sin(angles) * factor], axis=1).astype(np.float32)


def plane_tables(sizes):
    length_x, length_y = sizes.nx * sizes.cells_x, sizes.ny * sizes.cells_y
    phase_x = np.mod(np.arange(length_x)[:, None] * frequencies(sizes.kept_x), length_x) / length_x
    phase_y = np.mod(np.arange(length_y)[:, None] * frequencies(sizes.kept_y), length_y) / length_y
    angle = 2.0 * math.pi * (phase_x[:, None, :, None] + phase_y[None, :, None, :])
    scale = 1.0 / math.sqrt(length_x * length_y)
    cosine, sine = np.cos(angle) * scale, np.sin(angle) * scale
    parts = np.stack([np.stack([cosine, -sine]), np.stack([sine, cosine])])
    pairs = sizes.cells_y // sizes.pair
    parts = parts.reshape(
        2, 2, sizes.nx, sizes.cells_x, sizes.ny, pairs, sizes.pair, sizes.ny, sizes.kept
    ).transpose(7, 3, 5, 2, 4, 6, 0, 1, 8)
    padded = np.zeros(parts.shape[:-1] + (sizes.half,), np.float32)
    padded[..., : sizes.kept] = parts
    return padded.reshape(sizes.ny, sizes.devices * sizes.cells, 4 * sizes.half)


class Sizes:
    def __init__(self, field, weight):
        self.nx, self.ny = lax.axis_size("gx"), lax.axis_size("gy")
        self.channels, self.cells_x, self.cells_y, self.depth = field.shape
        self.modes = weight.shape[0]
        self.local_x, self.kept_y = weight.shape[4:]
        self.kept_x = self.local_x * self.ny
        self.cells = self.cells_x * self.cells_y
        self.devices = self.nx * self.ny
        self.share = self.modes // 2
        self.kept = self.local_x * self.kept_y
        self.half = round_up(self.kept, LANES // 2)
        self.all_modes = 2 * self.modes * self.nx
        self.groups = LANES // self.modes
        self.main = self.channels // self.groups * self.groups if self.all_modes == LANES else 0
        self.rest = self.channels - self.main
        self.main_lanes = self.main * self.modes
        self.rest_lanes = self.rest * self.modes
        self.rest_tiles = round_up(self.rest_lanes, LANES) // LANES
        self.pair = math.gcd(self.cells_y, 2)
        self.pieces = self.cells // self.pair
        self.rest_first = self.pieces * self.main_lanes
        self.rest_width = round_up(self.pieces * self.rest_lanes, LANES)
        self.width = self.rest_first + self.rest_width
        self.spread_rows = self.main_lanes + self.rest_width
        self.rows = round_up(self.channels, 8)


def gather_cells(source, scratch, sizes):
    for w in range(sizes.channels):
        for x in range(sizes.cells_x):
            first = (w * sizes.cells_x + x) * sizes.cells_y
            scratch[first : first + sizes.cells_y, :] = source[w, x].astype(F32)
    return scratch[...]


def scatter_cells(values, target, sizes):
    for w in range(sizes.channels):
        for x in range(sizes.cells_x):
            first = (w * sizes.cells_x + x) * sizes.cells_y
            target[w, x] = values[first : first + sizes.cells_y, :].astype(target.dtype)


def lane_group(sizes):
    return lax.broadcasted_iota(jnp.int32, (sizes.cells, LANES), 1) // sizes.modes


def turn_groups(tiles, group, sizes):
    tiles = list(tiles)
    step = 1
    while step < sizes.groups:
        low = group // step % 2 == 0
        for first in range(sizes.groups):
            if first // step % 2 == 0:
                one, two = tiles[first], tiles[first + step]
                tiles[first] = jnp.where(low, one, pltpu.roll(two, step * sizes.modes, 1))
                tiles[first + step] = jnp.where(low, pltpu.roll(one, LANES - step * sizes.modes, 1), two)
        step *= 2
    return tiles


def put_group(target, source, have, want, group, sizes):
    if have != want:
        source = pltpu.roll(source, (want - have) % sizes.groups * sizes.modes, 1)
    return jnp.where(group == want, source, target)


def send_modes(values, target, sizes):
    group = lane_group(sizes)
    tiles = [values[w * sizes.cells : (w + 1) * sizes.cells, :] for w in range(sizes.channels)]
    turned = []
    for first in range(0, sizes.main, sizes.groups):
        turned.append(turn_groups(tiles[first : first + sizes.groups], group, sizes))
    for at in range(2 * sizes.nx):
        main = [block[at] for block in turned]
        last = [jnp.zeros((sizes.cells, LANES), F32) for _ in range(sizes.rest_width // LANES)]
        for r in range(sizes.rest):
            tile, want = divmod(r, sizes.groups)
            last[tile] = put_group(last[tile], tiles[sizes.main + r], at, want, group, sizes)
        if last:
            last = side_by_side(jnp.concatenate(last, 1), sizes.pair, sizes)
        for y in range(sizes.ny // 2):
            device = at // 2 * sizes.ny + 2 * y + at % 2
            for piece in range(sizes.pieces):
                rows = slice(piece * sizes.pair, (piece + 1) * sizes.pair)
                for k, value in enumerate(main):
                    first = piece * sizes.main_lanes + k * LANES
                    target[device, :, first : first + LANES] = value[rows]
            if sizes.rest:
                target[device, :, sizes.rest_first :] = last


def side_by_side(values, rows, sizes):
    total = values[:rows]
    for piece in range(1, sizes.pieces):
        moved = pltpu.roll(values, piece * sizes.rest_lanes, 1)
        total = total + moved[piece * rows : (piece + 1) * rows]
    return total


def receive_modes(source, scratch, tall, sizes):
    group = lane_group(sizes)
    parts = source[...].reshape(sizes.nx, sizes.ny // 2, 2, sizes.pair, sizes.width)
    values = parts[:, 0]
    for y in range(1, sizes.ny // 2):
        values = values + parts[:, y]
    values = values.reshape(2 * sizes.nx, sizes.pair, sizes.width)
    for piece in range(sizes.pieces):
        rows = slice(piece * sizes.pair, (piece + 1) * sizes.pair)
        if sizes.main:
            first = piece * sizes.main_lanes
            tall[:, rows, : sizes.main_lanes] = values[:, :, first : first + sizes.main_lanes]
        if sizes.rest:
            last = values[:, :, sizes.rest_first :]
            if piece:
                last = pltpu.roll(last, sizes.rest_width - piece * sizes.rest_lanes, 2)
            tall[:, rows, sizes.main_lanes :] = last
    out = []
    for first in range(0, sizes.main_lanes, LANES):
        tiles = [tall[at, :, first : first + LANES] for at in range(2 * sizes.nx)]
        out += turn_groups(tiles, group, sizes)
    for r in range(sizes.rest):
        value = jnp.zeros((sizes.cells, LANES), F32)
        tile, have = divmod(r, sizes.groups)
        first = sizes.main_lanes + tile * LANES
        for at in range(2 * sizes.nx):
            value = put_group(value, tall[at, :, first : first + LANES], have, at, group, sizes)
        out.append(value)
    for w, value in enumerate(out):
        scratch[w * sizes.cells : (w + 1) * sizes.cells, :] = value
    return scratch[...]


def dot(left, right, contract=((1,), (0,))):
    return lax.dot_general(left, right, (contract, ((), ())), preferred_element_type=F32)


def halves(values):
    high = values.astype(BF16)
    return high, (values - high.astype(F32)).astype(BF16)


def fine_dot(left, right, contract=((1,), (0,))):
    left_high, left_low = halves(left)
    right_high, right_low = halves(right)
    small = dot(left_high, right_low, contract) + dot(left_low, right_high, contract)
    return dot(left_high, right_high, contract) + small


def fetch(sources, targets, semaphores):
    copies = [pltpu.make_async_copy(*pair, semaphores.at[at]) for at, pair in enumerate(zip(sources, targets))]
    for copy in copies:
        copy.start()
    for copy in copies:
        copy.wait()


def depth_forward(
    sizes, field, table, source, out, target,
    cells, field_here, table_here, out_here, here, semaphores, weight_semaphores,
):
    few = [
        pltpu.make_async_copy(field, field_here, semaphores.at[0]),
        pltpu.make_async_copy(table, table_here, semaphores.at[1]),
    ]
    for copy in few:
        copy.start()
    copies = start_weights(sizes, source, 1 - core_of(), here, weight_semaphores)
    clear_weights(sizes, target)
    for copy in few:
        copy.wait()
    values = gather_cells(field_here, cells, sizes).astype(BF16)
    send_modes(dot(values, table_here[...]), out_here, sizes)
    copy = pltpu.make_async_copy(out_here, out, semaphores.at[2])
    copy.start()
    turn_weights(sizes, copies, here, target)
    copy.wait()


def one_hot(rows, columns, step, along_rows):
    row = lax.broadcasted_iota(jnp.int32, (rows, columns), 0)
    column = lax.broadcasted_iota(jnp.int32, (rows, columns), 1)
    same = row // step == column if along_rows else row == column // step
    return jnp.where(same, 1.0, 0.0).astype(BF16)


def cell_mixer(weights, across, sizes):
    count = sizes.channels * sizes.cells
    left = one_hot(count, sizes.channels, sizes.cells, True)
    right = one_hot(sizes.channels, count, sizes.cells, False)
    tall = dot(left, weights, ((1,), (1 if across else 0,)))
    wide = dot(tall.astype(BF16), right)
    row = lax.broadcasted_iota(jnp.int32, (count, count), 0)
    column = lax.broadcasted_iota(jnp.int32, (count, count), 1)
    same = lax.rem(row, sizes.cells) == lax.rem(column, sizes.cells)
    return jnp.where(same, wide, 0.0).astype(BF16)


def emit(sizes, pre, signal, weight, inverse, layer_out, local, inverse_out, weight_here, semaphores):
    copies = [
        pltpu.make_async_copy(weight, weight_here, semaphores.at[0]),
        pltpu.make_async_copy(inverse, inverse_out, semaphores.at[1]),
    ]
    for copy in copies:
        copy.start()
    scatter_cells(gelu_parts(pre[...])[0], layer_out, sizes)
    copies[0].wait()
    local[...] = dot(cell_mixer(weight_here[...], False, sizes), signal[...])
    copies[1].wait()


def core_of():
    return lax.rem(lax.axis_index("gy"), 2)


def start_weights(sizes, source, half, here, semaphores):
    copies = []
    for at in range(2 * sizes.share):
        copies.append(pltpu.make_async_copy(source.at[2 * sizes.share * half + at], here.at[at], semaphores.at[at]))
        copies[-1].start()
    return copies


def clear_weights(sizes, target):
    if sizes.half > sizes.kept:
        target[...] = jnp.zeros_like(target)
    elif sizes.rows > sizes.channels:
        target[:, :, sizes.channels :, :] = jnp.zeros(
            (sizes.share, sizes.channels, sizes.rows - sizes.channels, 2 * sizes.half), F32
        )


def turn_weights(sizes, copies, here, target):
    for mode in range(sizes.share):
        for s in range(2):
            copies[2 * mode + s].wait()
        for w in range(sizes.channels):
            blocks = [here[2 * mode + s, w].reshape(sizes.kept, sizes.channels) for s in range(2)]
            if sizes.half == sizes.kept:
                target[mode, w, : sizes.channels, :] = jnp.concatenate(blocks, 0).T
            else:
                for s, block in enumerate(blocks):
                    target[mode, w, : sizes.channels, s * sizes.half : s * sizes.half + sizes.kept] = block.T


def prepare(
    sizes, source, after, tables, field, cotangent, weight, bias,
    target, table, local, cotangent_out,
    here, cells, field_here, cot_here, cot_cells, weight_here, bias_here, local_here, semaphores, small,
):
    del after
    place = lax.axis_index("gy")
    lanes = 2 * sizes.half
    moves = [(field, field_here), (cotangent, cot_here), (weight, weight_here), (bias, bias_here)]
    for s in range(2):
        for at, owner in enumerate((place, place + 1 - 2 * core_of())):
            moves.append(
                (tables.at[owner, :, pl.ds(s * lanes, lanes)], table.at[:, pl.ds((2 * s + at) * lanes, lanes)])
            )
    few = [pltpu.make_async_copy(*move, small.at[at]) for at, move in enumerate(moves)]
    copies = start_weights(sizes, source, core_of(), here, semaphores)
    for copy in few:
        copy.start()
    clear_weights(sizes, target)
    turn_weights(sizes, copies, here, target)
    for copy in few:
        copy.wait()
    values = gather_cells(field_here, cells, sizes).astype(BF16)
    spread = one_hot(sizes.channels * sizes.cells, sizes.channels, sizes.cells, True).astype(F32)
    offset = jnp.sum(spread * bias_here[...].reshape(1, sizes.channels), axis=1, keepdims=True)
    local_here[...] = dot(cell_mixer(weight_here[...], True, sizes), values) + offset
    gather_cells(cot_here, cot_cells, sizes)
    results = [
        pltpu.make_async_copy(local_here, local, small.at[0]),
        pltpu.make_async_copy(cot_cells, cotangent_out, small.at[1]),
    ]
    for copy in results:
        copy.start()
    for copy in results:
        copy.wait()


def plane_spectra(sizes, received, table, targets, flat):
    count = sizes.devices * sizes.pair
    for at in range(sizes.devices):
        for piece in range(sizes.pieces):
            rows = slice(piece * count + at * sizes.pair, piece * count + (at + 1) * sizes.pair)
            if sizes.main:
                first = piece * sizes.main_lanes
                flat[rows, : sizes.main_lanes] = received[at, :, first : first + sizes.main_lanes]
            if sizes.rest:
                flat[rows, sizes.main_lanes :] = received[at, :, sizes.rest_first :]
    if sizes.rest:
        for piece in range(1, sizes.pieces):
            rows = slice(piece * count, (piece + 1) * count)
            shift = sizes.rest_width - piece * sizes.rest_lanes
            flat[rows, sizes.main_lanes :] = pltpu.roll(flat[rows, sizes.main_lanes :], shift, 1)
    rows, lanes = targets[0].shape
    both = fine_dot(flat[...].T[:rows], table[...])
    total = both[:, : 2 * lanes] + pltpu.roll(both[:, 2 * lanes :], rows - sizes.share, 0)
    for at, target in enumerate(targets):
        target[...] = total[:, at * lanes : (at + 1) * lanes]


def plane_cells(sizes, spread, table, out):
    modes = jnp.concatenate([spread[at] for at in range(4)], 1)
    cells = fine_dot(table[...], modes, ((1,), (1,)))
    count = sizes.devices * sizes.pair
    if sizes.rest:
        last = side_by_side(cells[:, sizes.main_lanes :], count, sizes)
    for at in range(sizes.devices):
        rows = slice(at * sizes.pair, (at + 1) * sizes.pair)
        for piece in range(sizes.pieces):
            if sizes.main:
                first = piece * sizes.main_lanes
                out[at, :, first : first + sizes.main_lanes] = cells[
                    piece * count + at * sizes.pair : piece * count + (at + 1) * sizes.pair, : sizes.main_lanes
                ]
        if sizes.rest:
            out[at, :, sizes.rest_first :] = last[rows]


def swap_parts(values, sizes):
    return pltpu.roll(values, sizes.half, 1)


def mode_rows(first, sizes):
    return pl.ds(first, sizes.channels, stride=sizes.modes)


def put_mixed(spread, at, mode, values, sizes):
    for s in range(2):
        spread[2 * s + at, mode_rows(s * sizes.share + mode, sizes), :] = values


def first_lanes(rows, sizes):
    return lax.broadcasted_iota(jnp.int32, (rows, 2 * sizes.half), 1) < sizes.half


def mix_forward(
    sizes, received, table, weight, other_weight, local, cotangent, inverse, forward,
    spectra, other_spectra, out, local_out, cotangent_out, inverse_out, forward_out, other_here,
    spread, swapped, flat, semaphores,
):
    moves = (
        (other_weight, other_here), (local, local_out), (cotangent, cotangent_out), (inverse, inverse_out),
        (forward, forward_out),
    )
    copies = [pltpu.make_async_copy(*move, semaphores.at[at]) for at, move in enumerate(moves)]
    for copy in copies:
        copy.start()
    plane_spectra(sizes, received, table, (spectra, other_spectra), flat)
    spread[...] = jnp.zeros_like(spread)
    real = first_lanes(sizes.rows, sizes)
    for at, (rows, block) in enumerate(((spectra, weight), (other_spectra, other_here))):
        if at:
            copies[0].wait()
        swapped[...] = swap_parts(rows[...], sizes)
        for m in range(sizes.share):
            straight = jnp.zeros((sizes.rows, 2 * sizes.half), F32)
            crossed = jnp.zeros((sizes.rows, 2 * sizes.half), F32)
            for w in range(sizes.channels):
                row = slice(w * sizes.modes + m, w * sizes.modes + m + 1)
                straight = straight + rows[row, :] * block[m, w]
                crossed = crossed + swapped[row, :] * block[m, w]
            real_part = straight - swap_parts(straight, sizes)
            imag_part = crossed + swap_parts(crossed, sizes)
            put_mixed(spread, at, m, jnp.where(real, real_part, imag_part)[: sizes.channels], sizes)
    plane_cells(sizes, spread, table, out)
    for copy in copies[1:]:
        copy.wait()


def mix_back(sizes, received, table, weight, other_weight, back, other_back, out, spread, flat):
    plane_spectra(sizes, received, table, (back, other_back), flat)
    spread[...] = jnp.zeros_like(spread)
    real = first_lanes(sizes.channels, sizes)
    for at, (source, block) in enumerate(((back, weight), (other_back, other_weight))):
        for m in range(sizes.share):
            rows = source[mode_rows(m, sizes), :]
            if sizes.rows > sizes.channels:
                rows = jnp.concatenate([rows, jnp.zeros((sizes.rows - sizes.channels, 2 * sizes.half), F32)], 0)
            turned = swap_parts(rows, sizes)
            straight, crossed = [], []
            for w in range(sizes.channels):
                straight.append(jnp.sum(block[m, w] * rows, axis=0, keepdims=True))
                crossed.append(jnp.sum(block[m, w] * turned, axis=0, keepdims=True))
            straight = jnp.concatenate(straight, 0)
            crossed = jnp.concatenate(crossed, 0)
            real_part = straight + swap_parts(straight, sizes)
            imag_part = swap_parts(crossed, sizes) - crossed
            put_mixed(spread, at, m, jnp.where(real, real_part, imag_part), sizes)
    plane_cells(sizes, spread, table, out)


def grad_weights(
    sizes, spectra, back, given_spectra, given_back, target, here, straight, crossed, semaphores
):
    copies = []
    for which, (source, backward) in enumerate(((spectra, back), (given_spectra, given_back))):
        half = core_of() if which == 0 else 1 - core_of()
        values = source[...]
        turned = swap_parts(values, sizes)
        real = first_lanes(values.shape[0], sizes)
        straight[...] = jnp.where(real, values, turned)
        crossed[...] = jnp.where(real, turned, -values)
        for mode in range(sizes.share):
            rows = backward[mode_rows(mode, sizes), :]
            if sizes.rows > sizes.channels:
                rows = jnp.concatenate([rows, jnp.zeros((sizes.rows - sizes.channels, 2 * sizes.half), F32)], 0)
            turned = swap_parts(rows, sizes)
            local = 2 * (which * sizes.share + mode)
            for w in range(sizes.channels):
                at = slice(w * sizes.modes + mode, w * sizes.modes + mode + 1)
                block = (straight[at, :] * rows + crossed[at, :] * turned).T
                for s in range(2):
                    part = block[s * sizes.half : s * sizes.half + sizes.kept, : sizes.channels]
                    here[local + s, w] = part.reshape(sizes.local_x, sizes.kept_y, sizes.channels)
            for s in range(2):
                to = 2 * (half * sizes.share + mode) + s
                copies.append(pltpu.make_async_copy(here.at[local + s], target.at[to], semaphores.at[local + s]))
                copies[-1].start()
    for copy in copies:
        copy.wait()


def gelu_parts(pre):
    slope = math.sqrt(2.0 / math.pi)
    squared = pre * pre
    bend = jnp.tanh(slope * (pre + 0.044715 * (squared * pre)))
    value = 0.5 * pre * (1.0 + bend)
    derivative = 0.5 * (1.0 + bend) + 0.5 * pre * (1.0 - bend * bend) * (slope * (1.0 + 3.0 * 0.044715 * squared))
    return value, derivative


def activate(
    sizes, received, local, cotangent, inverse, forward, pre_out, signal_out, out, spectrum, tall
):
    pre = fine_dot(receive_modes(received, spectrum, tall, sizes), inverse[...]) + local[...]
    pre_out[...] = pre
    signal = (cotangent[...] * gelu_parts(pre)[1]).astype(BF16)
    signal_out[...] = signal
    send_modes(dot(signal, forward[...]), out, sizes)


def finish(sizes, received, local, inverse, grad_field, spectrum, tall):
    spatial = fine_dot(receive_modes(received, spectrum, tall, sizes), inverse[...])
    scatter_cells(spatial + local[...], grad_field, sizes)


def shape_of(shape, dtype=F32):
    return jax.ShapeDtypeStruct(shape, dtype)


VMEM = pl.BlockSpec(memory_space=pltpu.VMEM)
HELD = pl.BlockSpec(memory_space=pltpu.VMEM)
HBM = pl.BlockSpec(memory_space=pltpu.HBM)
ANYWHERE = pl.BlockSpec(memory_space=pl.ANY)


def settings(mebibytes):
    return pltpu.CompilerParams(vmem_limit_bytes=mebibytes * 1024 * 1024)


def cost(nanoseconds):
    return pl.CostEstimate(flops=0, bytes_accessed=3000 * nanoseconds, transcendentals=0)


def whole_call(body, sizes, nanoseconds, out_shape, scratch, *args, specs=None, out_specs=None, room=16):
    def kernel(*refs):
        body(sizes, *refs)

    if specs:
        spaces = [pltpu.HBM if spec is HBM else pltpu.VMEM if spec is HELD else None for spec in specs]
        args = [
            pltpu.with_memory_space_constraint(arg, space) if space else arg for arg, space in zip(args, spaces)
        ]
    return pl.pallas_call(
        kernel,
        out_shape=out_shape,
        in_specs=specs or [VMEM] * len(args),
        out_specs=out_specs or jax.tree.map(lambda _: VMEM, out_shape),
        scratch_shapes=scratch,
        name=body.__name__,
        cost_estimate=cost(nanoseconds),
        compiler_params=settings(room),
    )(*args)


def on_device(field, cotangent, spectral_weight, pointwise_weight, channel_bias):
    z = Sizes(field, spectral_weight)
    depth_table = depth_time_table(z.depth)
    modes = depth_table.shape[2]
    kappa = np.where(np.arange(modes) % KT == 0, 1.0, 2.0).astype(np.float32)
    shares = (z.nx, 2, z.share)
    ordered = depth_table.reshape((z.depth, 2) + shares).transpose(0, 2, 3, 1, 4).reshape(z.depth, z.all_modes)
    doubled = np.repeat(kappa.reshape(z.nx, 2, 1, z.share), 2, axis=2).reshape(z.all_modes)
    forward_first = jnp.asarray(ordered.astype(ml_dtypes.bfloat16))
    forward_back = jnp.asarray((ordered.astype(ml_dtypes.bfloat16).astype(np.float32) * doubled).astype(ml_dtypes.bfloat16))
    inverse_back = jnp.asarray(np.ascontiguousarray(ordered.T))
    inverse_first = jnp.asarray(np.ascontiguousarray((ordered * doubled).T))
    pairs = [(s, s ^ 1) for s in range(z.ny)]

    def exchange(payload):
        return lax.all_to_all(payload, ("gx", "gy"), split_axis=0, concat_axis=0, tiled=True)

    def other_core(values):
        return lax.ppermute(values, "gy", pairs)

    payload = shape_of((z.devices, z.pair, z.width))
    cell_rows = z.channels * z.cells
    cells_shape = (cell_rows, z.depth)
    cells_scratch = pltpu.VMEM(cells_shape, F32)
    spectrum_scratch = pltpu.VMEM((cell_rows, z.all_modes), F32)
    spectra_shape = (z.channels * z.modes, 2 * z.half)
    spectra_scratch = pltpu.VMEM(spectra_shape, F32)
    flat_scratch = pltpu.VMEM((z.devices * z.cells, z.spread_rows), F32)
    spread_scratch = pltpu.VMEM((4, z.spread_rows, 2 * z.half), F32)
    tall_scratch = pltpu.VMEM((2 * z.nx, z.cells, z.spread_rows), F32)
    field_scratch = pltpu.VMEM(field.shape, BF16)
    weight_here = pltpu.VMEM(pointwise_weight.shape, BF16)
    native = jnp.transpose(spectral_weight, (0, 1, 2, 4, 5, 3))
    weight_shape = (2 * z.modes,) + native.shape[2:]
    half_scratch = pltpu.VMEM((z.modes,) + native.shape[2:], F32)
    turned_shape = shape_of((z.share, z.channels, z.rows, 2 * z.half))

    def flags(count):
        return pltpu.SemaphoreType.DMA((count,))

    weights = native.reshape(weight_shape)
    sent, turned_away = whole_call(
        depth_forward, z, 1500, (payload, turned_shape),
        [
            cells_scratch, field_scratch, pltpu.VMEM(forward_first.shape, BF16), pltpu.VMEM(payload.shape, F32),
            half_scratch, flags(3), flags(z.modes),
        ],
        field, forward_first, weights, specs=[HBM] * 3, out_specs=(HBM, VMEM),
    )
    received = exchange(sent)
    other_turned = other_core(turned_away)
    turned, plane, local, cot_cells = whole_call(
        prepare, z, 100,
        (turned_shape, shape_of((z.devices * z.cells, 8 * z.half)), pltpu.HBM(cells_shape, F32), pltpu.HBM(cells_shape, F32)),
        [
            half_scratch, cells_scratch, field_scratch, field_scratch, cells_scratch, weight_here,
            pltpu.VMEM(channel_bias.shape, F32), cells_scratch, flags(z.modes), flags(8),
        ],
        weights, turned_away, jnp.asarray(plane_tables(z)), field, cotangent, pointwise_weight, channel_bias,
        specs=[HBM, ANYWHERE] + [HBM] * 5, out_specs=(VMEM, VMEM, HBM, HBM),
    )
    received, other_turned, turned, plane, local, cot_cells = lax.optimization_barrier(
        (received, other_turned, turned, plane, local, cot_cells)
    )
    spectra, other_spectra, sent, local, cot_cells, inverse_here, forward_here, other_turned = whole_call(
        mix_forward, z, 1000,
        (
            shape_of(spectra_shape), shape_of(spectra_shape), payload, shape_of(cells_shape), shape_of(cells_shape),
            shape_of(inverse_first.shape), shape_of(forward_back.shape, BF16), turned_shape,
        ),
        [spread_scratch, spectra_scratch, flat_scratch, flags(5)],
        received, plane, turned, other_turned, local, cot_cells, inverse_first, forward_back,
        specs=[HELD] + [VMEM] * 2 + [HBM] * 5,
    )
    pre, signal, sent = whole_call(
        activate, z, 2000,
        (shape_of(cells_shape), shape_of(cells_shape, BF16), payload), [spectrum_scratch, tall_scratch],
        exchange(sent), local, cot_cells, inverse_here, forward_here,
    )
    back, other_back, sent = whole_call(
        mix_back, z, 1000, (shape_of(spectra_shape), shape_of(spectra_shape), payload),
        [spread_scratch, flat_scratch], exchange(sent), plane, turned, other_turned,
    )
    sent, spectra, other_spectra, back, other_back, pre, signal = lax.optimization_barrier(
        (sent, spectra, other_spectra, back, other_back, pre, signal)
    )
    returned = exchange(sent)
    given_spectra, given_back = other_core(other_spectra), other_core(other_back)
    layer_out, local, inverse_here = whole_call(
        emit, z, 1500,
        (shape_of(field.shape, BF16), shape_of(cells_shape), shape_of(inverse_back.shape)),
        [weight_here, flags(2)],
        pre, signal, pointwise_weight, inverse_back, specs=[VMEM, VMEM, HBM, HBM],
    )
    gradient = whole_call(
        grad_weights, z, 5000, shape_of(weight_shape),
        [pltpu.VMEM(weight_shape, F32), spectra_scratch, spectra_scratch, flags(2 * z.modes)],
        spectra, back, given_spectra, given_back, out_specs=HBM, room=28,
    )
    returned, gradient, layer_out, local, inverse_here = lax.optimization_barrier(
        (returned, gradient, layer_out, local, inverse_here)
    )
    grad_field = whole_call(
        finish, z, 1000, shape_of(field.shape, BF16), [spectrum_scratch, tall_scratch], returned, local, inverse_here
    )
    return (layer_out, grad_field, jnp.transpose(gradient.reshape(native.shape), (0, 1, 2, 5, 3, 4)))


def solution(mesh):
    return jax.shard_map(
        on_device,
        mesh=mesh,
        in_specs=(
            P(None, "gx", "gy", None),
            P(None, "gx", "gy", None),
            P("gx", None, None, None, "gy", None),
            P(),
            P(),
        ),
        out_specs=(
            P(None, "gx", "gy", None),
            P(None, "gx", "gy", None),
            P("gx", None, None, None, "gy", None),
        ),
        check_vma=False,
    )
```

```python
import math

import jax
import jax.numpy as jnp
import ml_dtypes
import numpy as np
from jax import lax
from jax.experimental import pallas as pl
from jax.experimental.pallas import tpu as pltpu
from jax.sharding import PartitionSpec as P

KZ = 16
KT = 4
NT = 16
LANES = 128
F32 = jnp.float32
BF16 = jnp.bfloat16


def round_up(value, step):
    return -(-value // step) * step


def frequencies(kept):
    index = np.arange(kept)
    return np.where(index < kept // 2, index, index - kept)


def depth_time_table(cells):
    depth_cells = cells // NT
    depth = np.arange(depth_cells)[:, None, None, None] * frequencies(KZ)[None, None, :, None] * NT
    time = np.arange(NT)[None, :, None, None] * np.arange(KT)[None, None, None, :] * depth_cells
    phase = np.mod(depth + time, cells).reshape(cells, KZ * KT)
    angles = phase.astype(np.float32) * np.float32(2.0 * math.pi / cells)
    factor = np.float32(1.0 / math.sqrt(cells))
    return np.stack([np.cos(angles) * factor, -np.sin(angles) * factor], axis=1).astype(np.float32)


def plane_tables(sizes):
    length_x, length_y = sizes.nx * sizes.cells_x, sizes.ny * sizes.cells_y
    phase_x = np.mod(np.arange(length_x)[:, None] * frequencies(sizes.kept_x), length_x) / length_x
    phase_y = np.mod(np.arange(length_y)[:, None] * frequencies(sizes.kept_y), length_y) / length_y
    angle = 2.0 * math.pi * (phase_x[:, None, :, None] + phase_y[None, :, None, :])
    scale = 1.0 / math.sqrt(length_x * length_y)
    cosine, sine = np.cos(angle) * scale, np.sin(angle) * scale
    parts = np.stack([np.stack([cosine, -sine]), np.stack([sine, cosine])])
    pairs = sizes.cells_y // sizes.pair
    parts = parts.reshape(
        2, 2, sizes.nx, sizes.cells_x, sizes.ny, pairs, sizes.pair, sizes.ny, sizes.kept
    ).transpose(7, 3, 5, 2, 4, 6, 0, 1, 8)
    padded = np.zeros(parts.shape[:-1] + (sizes.half,), np.float32)
    padded[..., : sizes.kept] = parts
    return padded.reshape(sizes.ny, sizes.devices * sizes.cells, 4 * sizes.half)


class Sizes:
    def __init__(self, field, weight):
        self.nx, self.ny = lax.axis_size("gx"), lax.axis_size("gy")
        self.channels, self.cells_x, self.cells_y, self.depth = field.shape
        self.modes = weight.shape[0]
        self.local_x, self.kept_y = weight.shape[4:]
        self.kept_x = self.local_x * self.ny
        self.cells = self.cells_x * self.cells_y
        self.devices = self.nx * self.ny
        self.share = self.modes // 2
        self.kept = self.local_x * self.kept_y
        self.half = round_up(self.kept, LANES // 2)
        self.all_modes = 2 * self.modes * self.nx
        self.groups = LANES // self.modes
        self.main = self.channels // self.groups * self.groups if self.all_modes == LANES else 0
        self.rest = self.channels - self.main
        self.main_lanes = self.main * self.modes
        self.rest_lanes = self.rest * self.modes
        self.rest_tiles = round_up(self.rest_lanes, LANES) // LANES
        self.pair = math.gcd(self.cells_y, 2)
        self.pieces = self.cells // self.pair
        self.rest_first = self.pieces * self.main_lanes
        self.rest_width = round_up(self.pieces * self.rest_lanes, LANES)
        self.width = self.rest_first + self.rest_width
        self.spread_rows = self.main_lanes + self.rest_width
        self.rows = round_up(self.channels, 8)


def gather_cells(source, scratch, sizes):
    for w in range(sizes.channels):
        for x in range(sizes.cells_x):
            first = (w * sizes.cells_x + x) * sizes.cells_y
            scratch[first : first + sizes.cells_y, :] = source[w, x].astype(F32)
    return scratch[...]


def scatter_cells(values, target, sizes):
    for w in range(sizes.channels):
        for x in range(sizes.cells_x):
            first = (w * sizes.cells_x + x) * sizes.cells_y
            target[w, x] = values[first : first + sizes.cells_y, :].astype(target.dtype)


def lane_group(sizes):
    return lax.broadcasted_iota(jnp.int32, (sizes.cells, LANES), 1) // sizes.modes


def turn_groups(tiles, group, sizes):
    tiles = list(tiles)
    step = 1
    while step < sizes.groups:
        low = group // step % 2 == 0
        for first in range(sizes.groups):
            if first // step % 2 == 0:
                one, two = tiles[first], tiles[first + step]
                tiles[first] = jnp.where(low, one, pltpu.roll(two, step * sizes.modes, 1))
                tiles[first + step] = jnp.where(low, pltpu.roll(one, LANES - step * sizes.modes, 1), two)
        step *= 2
    return tiles


def put_group(target, source, have, want, group, sizes):
    if have != want:
        source = pltpu.roll(source, (want - have) % sizes.groups * sizes.modes, 1)
    return jnp.where(group == want, source, target)


def send_modes(values, target, sizes):
    group = lane_group(sizes)
    tiles = [values[w * sizes.cells : (w + 1) * sizes.cells, :] for w in range(sizes.channels)]
    turned = []
    for first in range(0, sizes.main, sizes.groups):
        turned.append(turn_groups(tiles[first : first + sizes.groups], group, sizes))
    for at in range(2 * sizes.nx):
        main = [block[at] for block in turned]
        last = [jnp.zeros((sizes.cells, LANES), F32) for _ in range(sizes.rest_width // LANES)]
        for r in range(sizes.rest):
            tile, want = divmod(r, sizes.groups)
            last[tile] = put_group(last[tile], tiles[sizes.main + r], at, want, group, sizes)
        if last:
            last = side_by_side(jnp.concatenate(last, 1), sizes.pair, sizes)
        for y in range(sizes.ny // 2):
            device = at // 2 * sizes.ny + 2 * y + at % 2
            for piece in range(sizes.pieces):
                rows = slice(piece * sizes.pair, (piece + 1) * sizes.pair)
                for k, value in enumerate(main):
                    first = piece * sizes.main_lanes + k * LANES
                    target[device, :, first : first + LANES] = value[rows]
            if sizes.rest:
                target[device, :, sizes.rest_first :] = last


def side_by_side(values, rows, sizes):
    total = values[:rows]
    for piece in range(1, sizes.pieces):
        moved = pltpu.roll(values, piece * sizes.rest_lanes, 1)
        total = total + moved[piece * rows : (piece + 1) * rows]
    return total


def receive_modes(source, scratch, tall, sizes):
    group = lane_group(sizes)
    parts = source[...].reshape(sizes.nx, sizes.ny // 2, 2, sizes.pair, sizes.width)
    values = parts[:, 0]
    for y in range(1, sizes.ny // 2):
        values = values + parts[:, y]
    values = values.reshape(2 * sizes.nx, sizes.pair, sizes.width)
    for piece in range(sizes.pieces):
        rows = slice(piece * sizes.pair, (piece + 1) * sizes.pair)
        if sizes.main:
            first = piece * sizes.main_lanes
            tall[:, rows, : sizes.main_lanes] = values[:, :, first : first + sizes.main_lanes]
        if sizes.rest:
            last = values[:, :, sizes.rest_first :]
            if piece:
                last = pltpu.roll(last, sizes.rest_width - piece * sizes.rest_lanes, 2)
            tall[:, rows, sizes.main_lanes :] = last
    out = []
    for first in range(0, sizes.main_lanes, LANES):
        tiles = [tall[at, :, first : first + LANES] for at in range(2 * sizes.nx)]
        out += turn_groups(tiles, group, sizes)
    for r in range(sizes.rest):
        value = jnp.zeros((sizes.cells, LANES), F32)
        tile, have = divmod(r, sizes.groups)
        first = sizes.main_lanes + tile * LANES
        for at in range(2 * sizes.nx):
            value = put_group(value, tall[at, :, first : first + LANES], have, at, group, sizes)
        out.append(value)
    for w, value in enumerate(out):
        scratch[w * sizes.cells : (w + 1) * sizes.cells, :] = value
    return scratch[...]


def dot(left, right, contract=((1,), (0,))):
    return lax.dot_general(left, right, (contract, ((), ())), preferred_element_type=F32)


def halves(values):
    high = values.astype(BF16)
    return high, (values - high.astype(F32)).astype(BF16)


def fine_dot(left, right, contract=((1,), (0,))):
    left_high, left_low = halves(left)
    right_high, right_low = halves(right)
    small = dot(left_high, right_low, contract) + dot(left_low, right_high, contract)
    return dot(left_high, right_high, contract) + small


def fetch(sources, targets, semaphores):
    copies = [pltpu.make_async_copy(*pair, semaphores.at[at]) for at, pair in enumerate(zip(sources, targets))]
    for copy in copies:
        copy.start()
    for copy in copies:
        copy.wait()


def depth_forward(
    sizes, field, table, source, out, target,
    cells, field_here, table_here, out_here, here, semaphores, weight_semaphores,
):
    few = [
        pltpu.make_async_copy(field, field_here, semaphores.at[0]),
        pltpu.make_async_copy(table, table_here, semaphores.at[1]),
    ]
    for copy in few:
        copy.start()
    clear_weights(sizes, target)
    for copy in few:
        copy.wait()
    copies = start_weights(sizes, source, 1 - core_of(), here, weight_semaphores)
    values = gather_cells(field_here, cells, sizes).astype(BF16)
    send_modes(dot(values, table_here[...]), out_here, sizes)
    copy = pltpu.make_async_copy(out_here, out, semaphores.at[2])
    copy.start()
    turn_weights(sizes, copies, here, target)
    copy.wait()


def one_hot(rows, columns, step, along_rows):
    row = lax.broadcasted_iota(jnp.int32, (rows, columns), 0)
    column = lax.broadcasted_iota(jnp.int32, (rows, columns), 1)
    same = row // step == column if along_rows else row == column // step
    return jnp.where(same, 1.0, 0.0).astype(BF16)


def cell_mixer(weights, across, sizes):
    count = sizes.channels * sizes.cells
    left = one_hot(count, sizes.channels, sizes.cells, True)
    right = one_hot(sizes.channels, count, sizes.cells, False)
    tall = dot(left, weights, ((1,), (1 if across else 0,)))
    wide = dot(tall.astype(BF16), right)
    row = lax.broadcasted_iota(jnp.int32, (count, count), 0)
    column = lax.broadcasted_iota(jnp.int32, (count, count), 1)
    same = lax.rem(row, sizes.cells) == lax.rem(column, sizes.cells)
    return jnp.where(same, wide, 0.0).astype(BF16)


def emit(sizes, pre, signal, weight, inverse, layer_out, local, inverse_out, weight_here, semaphores):
    copies = [
        pltpu.make_async_copy(weight, weight_here, semaphores.at[0]),
        pltpu.make_async_copy(inverse, inverse_out, semaphores.at[1]),
    ]
    for copy in copies:
        copy.start()
    scatter_cells(gelu_parts(pre[...])[0], layer_out, sizes)
    copies[0].wait()
    local[...] = dot(cell_mixer(weight_here[...], False, sizes), signal[...])
    copies[1].wait()


def core_of():
    return lax.rem(lax.axis_index("gy"), 2)


def start_weights(sizes, source, half, here, semaphores):
    copies = []
    for at in range(2 * sizes.share):
        copies.append(pltpu.make_async_copy(source.at[2 * sizes.share * half + at], here.at[at], semaphores.at[at]))
        copies[-1].start()
    return copies


def clear_weights(sizes, target):
    if sizes.half > sizes.kept:
        target[...] = jnp.zeros_like(target)
    elif sizes.rows > sizes.channels:
        target[:, :, sizes.channels :, :] = jnp.zeros(
            (sizes.share, sizes.channels, sizes.rows - sizes.channels, 2 * sizes.half), F32
        )


def turn_weights(sizes, copies, here, target):
    for mode in range(sizes.share):
        for s in range(2):
            copies[2 * mode + s].wait()
        for w in range(sizes.channels):
            blocks = [here[2 * mode + s, w].reshape(sizes.kept, sizes.channels) for s in range(2)]
            if sizes.half == sizes.kept:
                target[mode, w, : sizes.channels, :] = jnp.concatenate(blocks, 0).T
            else:
                for s, block in enumerate(blocks):
                    target[mode, w, : sizes.channels, s * sizes.half : s * sizes.half + sizes.kept] = block.T


def prepare(
    sizes, source, after, tables, field, cotangent, weight, bias,
    target, table, local, cotangent_out,
    here, cells, field_here, cot_here, cot_cells, weight_here, bias_here, local_here, semaphores, small,
):
    del after
    place = lax.axis_index("gy")
    lanes = 4 * sizes.half
    moves = [(field, field_here), (cotangent, cot_here), (weight, weight_here), (bias, bias_here)]
    for at, owner in enumerate((place, place + 1 - 2 * core_of())):
        moves.append((tables.at[owner], table.at[:, pl.ds(at * lanes, lanes)]))
    few = [pltpu.make_async_copy(*move, small.at[at]) for at, move in enumerate(moves)]
    copies = start_weights(sizes, source, core_of(), here, semaphores)
    for copy in few:
        copy.start()
    clear_weights(sizes, target)
    turn_weights(sizes, copies, here, target)
    for copy in few:
        copy.wait()
    values = gather_cells(field_here, cells, sizes).astype(BF16)
    spread = one_hot(sizes.channels * sizes.cells, sizes.channels, sizes.cells, True).astype(F32)
    offset = jnp.sum(spread * bias_here[...].reshape(1, sizes.channels), axis=1, keepdims=True)
    local_here[...] = dot(cell_mixer(weight_here[...], True, sizes), values) + offset
    gather_cells(cot_here, cot_cells, sizes)
    results = [
        pltpu.make_async_copy(local_here, local, small.at[0]),
        pltpu.make_async_copy(cot_cells, cotangent_out, small.at[1]),
    ]
    for copy in results:
        copy.start()
    for copy in results:
        copy.wait()


def spread_received(sizes, received, flat):
    count = sizes.devices * sizes.pair
    for at in range(sizes.devices):
        for piece in range(sizes.pieces):
            rows = slice(piece * count + at * sizes.pair, piece * count + (at + 1) * sizes.pair)
            if sizes.main:
                first = piece * sizes.main_lanes
                flat[rows, : sizes.main_lanes] = received[at, :, first : first + sizes.main_lanes]
            if sizes.rest:
                flat[rows, sizes.main_lanes :] = received[at, :, sizes.rest_first :]
    if sizes.rest:
        for piece in range(1, sizes.pieces):
            rows = slice(piece * count, (piece + 1) * count)
            shift = sizes.rest_width - piece * sizes.rest_lanes
            flat[rows, sizes.main_lanes :] = pltpu.roll(flat[rows, sizes.main_lanes :], shift, 1)
    return flat[...].T[: sizes.channels * sizes.modes]


def owner_lanes(at, sizes):
    return slice(at * 4 * sizes.half, (at + 1) * 4 * sizes.half)


def plane_spectra(sizes, values, table, at, target):
    both = fine_dot(values, table[:, owner_lanes(at, sizes)])
    rows, lanes = target.shape
    target[...] = both[:, :lanes] + pltpu.roll(both[:, lanes:], rows - sizes.share, 0)


def plane_cells(sizes, spread, table, at):
    modes = jnp.concatenate([spread[2 * at + s] for s in range(2)], 1)
    return fine_dot(table[:, owner_lanes(at, sizes)], modes, ((1,), (1,)))


def send_cells(sizes, cells, out):
    count = sizes.devices * sizes.pair
    if sizes.rest:
        last = side_by_side(cells[:, sizes.main_lanes :], count, sizes)
    for at in range(sizes.devices):
        rows = slice(at * sizes.pair, (at + 1) * sizes.pair)
        for piece in range(sizes.pieces):
            if sizes.main:
                first = piece * sizes.main_lanes
                out[at, :, first : first + sizes.main_lanes] = cells[
                    piece * count + at * sizes.pair : piece * count + (at + 1) * sizes.pair, : sizes.main_lanes
                ]
        if sizes.rest:
            out[at, :, sizes.rest_first :] = last[rows]


def swap_parts(values, sizes):
    return pltpu.roll(values, sizes.half, 1)


def mode_rows(first, sizes):
    return pl.ds(first, sizes.channels, stride=sizes.modes)


def put_mixed(spread, at, mode, values, sizes):
    for s in range(2):
        spread[2 * at + s, mode_rows(s * sizes.share + mode, sizes), :] = values


def first_lanes(rows, sizes):
    return lax.broadcasted_iota(jnp.int32, (rows, 2 * sizes.half), 1) < sizes.half


def mix_forward(
    sizes, received, table, weight, other_weight, local, cotangent, inverse, forward,
    spectra, other_spectra, out, local_out, cotangent_out, inverse_out, forward_out, other_here,
    spread, swapped, flat, semaphores,
):
    moves = (
        (other_weight, other_here), (local, local_out), (cotangent, cotangent_out), (inverse, inverse_out),
        (forward, forward_out),
    )
    copies = [pltpu.make_async_copy(*move, semaphores.at[at]) for at, move in enumerate(moves)]
    for copy in copies:
        copy.start()
    spread[...] = jnp.zeros_like(spread)
    values = spread_received(sizes, received, flat)
    real = first_lanes(sizes.rows, sizes)
    cells = None
    for at, (rows, block) in enumerate(((spectra, weight), (other_spectra, other_here))):
        plane_spectra(sizes, values, table, at, rows)
        if at:
            cells = plane_cells(sizes, spread, table, 0)
            copies[0].wait()
        swapped[...] = swap_parts(rows[...], sizes)
        for m in range(sizes.share):
            straight = jnp.zeros((sizes.rows, 2 * sizes.half), F32)
            crossed = jnp.zeros((sizes.rows, 2 * sizes.half), F32)
            for w in range(sizes.channels):
                row = slice(w * sizes.modes + m, w * sizes.modes + m + 1)
                straight = straight + rows[row, :] * block[m, w]
                crossed = crossed + swapped[row, :] * block[m, w]
            real_part = straight - swap_parts(straight, sizes)
            imag_part = crossed + swap_parts(crossed, sizes)
            put_mixed(spread, at, m, jnp.where(real, real_part, imag_part)[: sizes.channels], sizes)
    send_cells(sizes, cells + plane_cells(sizes, spread, table, 1), out)
    for copy in copies[1:]:
        copy.wait()


def mix_back(sizes, received, table, weight, other_weight, back, other_back, out, spread, flat):
    spread[...] = jnp.zeros_like(spread)
    values = spread_received(sizes, received, flat)
    real = first_lanes(sizes.channels, sizes)
    cells = 0.0
    for at, (source, block) in enumerate(((back, weight), (other_back, other_weight))):
        plane_spectra(sizes, values, table, at, source)
        for m in range(sizes.share):
            rows = source[mode_rows(m, sizes), :]
            if sizes.rows > sizes.channels:
                rows = jnp.concatenate([rows, jnp.zeros((sizes.rows - sizes.channels, 2 * sizes.half), F32)], 0)
            turned = swap_parts(rows, sizes)
            straight, crossed = [], []
            for w in range(sizes.channels):
                straight.append(jnp.sum(block[m, w] * rows, axis=0, keepdims=True))
                crossed.append(jnp.sum(block[m, w] * turned, axis=0, keepdims=True))
            straight = jnp.concatenate(straight, 0)
            crossed = jnp.concatenate(crossed, 0)
            real_part = straight + swap_parts(straight, sizes)
            imag_part = swap_parts(crossed, sizes) - crossed
            put_mixed(spread, at, m, jnp.where(real, real_part, imag_part), sizes)
        cells = cells + plane_cells(sizes, spread, table, at)
    send_cells(sizes, cells, out)


def grad_weights(
    sizes, spectra, back, given_spectra, given_back, target, here, straight, crossed, semaphores
):
    copies = []
    for which, (source, backward) in enumerate(((spectra, back), (given_spectra, given_back))):
        half = core_of() if which == 0 else 1 - core_of()
        values = source[...]
        turned = swap_parts(values, sizes)
        real = first_lanes(values.shape[0], sizes)
        straight[...] = jnp.where(real, values, turned)
        crossed[...] = jnp.where(real, turned, -values)
        for mode in range(sizes.share):
            rows = backward[mode_rows(mode, sizes), :]
            if sizes.rows > sizes.channels:
                rows = jnp.concatenate([rows, jnp.zeros((sizes.rows - sizes.channels, 2 * sizes.half), F32)], 0)
            turned = swap_parts(rows, sizes)
            local = 2 * (which * sizes.share + mode)
            for w in range(sizes.channels):
                at = slice(w * sizes.modes + mode, w * sizes.modes + mode + 1)
                block = (straight[at, :] * rows + crossed[at, :] * turned).T
                for s in range(2):
                    part = block[s * sizes.half : s * sizes.half + sizes.kept, : sizes.channels]
                    here[local + s, w] = part.reshape(sizes.local_x, sizes.kept_y, sizes.channels)
            for s in range(2):
                to = 2 * (half * sizes.share + mode) + s
                copies.append(pltpu.make_async_copy(here.at[local + s], target.at[to], semaphores.at[local + s]))
                copies[-1].start()
    for copy in copies:
        copy.wait()


def gelu_parts(pre):
    slope = math.sqrt(2.0 / math.pi)
    squared = pre * pre
    bend = jnp.tanh(slope * (pre + 0.044715 * (squared * pre)))
    value = 0.5 * pre * (1.0 + bend)
    derivative = 0.5 * (1.0 + bend) + 0.5 * pre * (1.0 - bend * bend) * (slope * (1.0 + 3.0 * 0.044715 * squared))
    return value, derivative


def activate(
    sizes, received, local, cotangent, inverse, forward, pre_out, signal_out, out, spectrum, tall
):
    pre = fine_dot(receive_modes(received, spectrum, tall, sizes), inverse[...]) + local[...]
    pre_out[...] = pre
    signal = (cotangent[...] * gelu_parts(pre)[1]).astype(BF16)
    signal_out[...] = signal
    send_modes(dot(signal, forward[...]), out, sizes)


def finish(sizes, received, local, inverse, grad_field, spectrum, tall):
    spatial = fine_dot(receive_modes(received, spectrum, tall, sizes), inverse[...])
    scatter_cells(spatial + local[...], grad_field, sizes)


def shape_of(shape, dtype=F32):
    return jax.ShapeDtypeStruct(shape, dtype)


VMEM = pl.BlockSpec(memory_space=pltpu.VMEM)
HELD = pl.BlockSpec(memory_space=pltpu.VMEM)
HBM = pl.BlockSpec(memory_space=pltpu.HBM)
ANYWHERE = pl.BlockSpec(memory_space=pl.ANY)


def settings(mebibytes):
    return pltpu.CompilerParams(vmem_limit_bytes=mebibytes * 1024 * 1024)


def cost(nanoseconds):
    return pl.CostEstimate(flops=0, bytes_accessed=3000 * nanoseconds, transcendentals=0)


def whole_call(body, sizes, nanoseconds, out_shape, scratch, *args, specs=None, out_specs=None, room=16):
    def kernel(*refs):
        body(sizes, *refs)

    if specs:
        spaces = [pltpu.HBM if spec is HBM else pltpu.VMEM if spec is HELD else None for spec in specs]
        args = [
            pltpu.with_memory_space_constraint(arg, space) if space else arg for arg, space in zip(args, spaces)
        ]
    return pl.pallas_call(
        kernel,
        out_shape=out_shape,
        in_specs=specs or [VMEM] * len(args),
        out_specs=out_specs or jax.tree.map(lambda _: VMEM, out_shape),
        scratch_shapes=scratch,
        name=body.__name__,
        cost_estimate=cost(nanoseconds),
        compiler_params=settings(room),
    )(*args)


def on_device(field, cotangent, spectral_weight, pointwise_weight, channel_bias):
    z = Sizes(field, spectral_weight)
    depth_table = depth_time_table(z.depth)
    modes = depth_table.shape[2]
    kappa = np.where(np.arange(modes) % KT == 0, 1.0, 2.0).astype(np.float32)
    shares = (z.nx, 2, z.share)
    ordered = depth_table.reshape((z.depth, 2) + shares).transpose(0, 2, 3, 1, 4).reshape(z.depth, z.all_modes)
    doubled = np.repeat(kappa.reshape(z.nx, 2, 1, z.share), 2, axis=2).reshape(z.all_modes)
    forward_first = jnp.asarray(ordered.astype(ml_dtypes.bfloat16))
    forward_back = jnp.asarray((ordered.astype(ml_dtypes.bfloat16).astype(np.float32) * doubled).astype(ml_dtypes.bfloat16))
    inverse_back = jnp.asarray(np.ascontiguousarray(ordered.T))
    inverse_first = jnp.asarray(np.ascontiguousarray((ordered * doubled).T))
    pairs = [(s, s ^ 1) for s in range(z.ny)]

    def exchange(payload):
        return lax.all_to_all(payload, ("gx", "gy"), split_axis=0, concat_axis=0, tiled=True)

    def other_core(values):
        return lax.ppermute(values, "gy", pairs)

    payload = shape_of((z.devices, z.pair, z.width))
    cell_rows = z.channels * z.cells
    cells_shape = (cell_rows, z.depth)
    cells_scratch = pltpu.VMEM(cells_shape, F32)
    spectrum_scratch = pltpu.VMEM((cell_rows, z.all_modes), F32)
    spectra_shape = (z.channels * z.modes, 2 * z.half)
    spectra_scratch = pltpu.VMEM(spectra_shape, F32)
    flat_scratch = pltpu.VMEM((z.devices * z.cells, z.spread_rows), F32)
    spread_scratch = pltpu.VMEM((4, z.spread_rows, 2 * z.half), F32)
    tall_scratch = pltpu.VMEM((2 * z.nx, z.cells, z.spread_rows), F32)
    field_scratch = pltpu.VMEM(field.shape, BF16)
    weight_here = pltpu.VMEM(pointwise_weight.shape, BF16)
    native = jnp.transpose(spectral_weight, (0, 1, 2, 4, 5, 3))
    weight_shape = (2 * z.modes,) + native.shape[2:]
    half_scratch = pltpu.VMEM((z.modes,) + native.shape[2:], F32)
    turned_shape = shape_of((z.share, z.channels, z.rows, 2 * z.half))

    def flags(count):
        return pltpu.SemaphoreType.DMA((count,))

    weights = native.reshape(weight_shape)
    sent, turned_away = whole_call(
        depth_forward, z, 1500, (payload, turned_shape),
        [
            cells_scratch, field_scratch, pltpu.VMEM(forward_first.shape, BF16), pltpu.VMEM(payload.shape, F32),
            half_scratch, flags(3), flags(z.modes),
        ],
        field, forward_first, weights, specs=[HBM] * 3, out_specs=(HBM, VMEM),
    )
    received = exchange(sent)
    other_turned = other_core(turned_away)
    turned, plane, local, cot_cells = whole_call(
        prepare, z, 100,
        (turned_shape, shape_of((z.devices * z.cells, 8 * z.half)), pltpu.HBM(cells_shape, F32), pltpu.HBM(cells_shape, F32)),
        [
            half_scratch, cells_scratch, field_scratch, field_scratch, cells_scratch, weight_here,
            pltpu.VMEM(channel_bias.shape, F32), cells_scratch, flags(z.modes), flags(6),
        ],
        weights, turned_away, jnp.asarray(plane_tables(z)), field, cotangent, pointwise_weight, channel_bias,
        specs=[HBM, ANYWHERE] + [HBM] * 5, out_specs=(VMEM, VMEM, HBM, HBM),
    )
    received, other_turned, turned, plane, local, cot_cells = lax.optimization_barrier(
        (received, other_turned, turned, plane, local, cot_cells)
    )
    spectra, other_spectra, sent, local, cot_cells, inverse_here, forward_here, other_turned = whole_call(
        mix_forward, z, 1000,
        (
            shape_of(spectra_shape), shape_of(spectra_shape), payload, shape_of(cells_shape), shape_of(cells_shape),
            shape_of(inverse_first.shape), shape_of(forward_back.shape, BF16), turned_shape,
        ),
        [spread_scratch, spectra_scratch, flat_scratch, flags(5)],
        received, plane, turned, other_turned, local, cot_cells, inverse_first, forward_back,
        specs=[HELD] + [VMEM] * 2 + [HBM] * 5,
    )
    pre, signal, sent = whole_call(
        activate, z, 2000,
        (shape_of(cells_shape), shape_of(cells_shape, BF16), payload), [spectrum_scratch, tall_scratch],
        exchange(sent), local, cot_cells, inverse_here, forward_here,
    )
    back, other_back, sent = whole_call(
        mix_back, z, 1000, (shape_of(spectra_shape), shape_of(spectra_shape), payload),
        [spread_scratch, flat_scratch], exchange(sent), plane, turned, other_turned,
    )
    sent, spectra, other_spectra, back, other_back, pre, signal = lax.optimization_barrier(
        (sent, spectra, other_spectra, back, other_back, pre, signal)
    )
    returned = exchange(sent)
    given_spectra, given_back = other_core(other_spectra), other_core(other_back)
    layer_out, local, inverse_here = whole_call(
        emit, z, 1500,
        (shape_of(field.shape, BF16), shape_of(cells_shape), shape_of(inverse_back.shape)),
        [weight_here, flags(2)],
        pre, signal, pointwise_weight, inverse_back, specs=[VMEM, VMEM, HBM, HBM],
    )
    gradient = whole_call(
        grad_weights, z, 5000, shape_of(weight_shape),
        [pltpu.VMEM(weight_shape, F32), spectra_scratch, spectra_scratch, flags(2 * z.modes)],
        spectra, back, given_spectra, given_back, out_specs=HBM, room=28,
    )
    returned, gradient, layer_out, local, inverse_here = lax.optimization_barrier(
        (returned, gradient, layer_out, local, inverse_here)
    )
    grad_field = whole_call(
        finish, z, 1000, shape_of(field.shape, BF16), [spectrum_scratch, tall_scratch], returned, local, inverse_here
    )
    return (layer_out, grad_field, jnp.transpose(gradient.reshape(native.shape), (0, 1, 2, 5, 3, 4)))


def solution(mesh):
    return jax.shard_map(
        on_device,
        mesh=mesh,
        in_specs=(
            P(None, "gx", "gy", None),
            P(None, "gx", "gy", None),
            P("gx", None, None, None, "gy", None),
            P(),
            P(),
        ),
        out_specs=(
            P(None, "gx", "gy", None),
            P(None, "gx", "gy", None),
            P("gx", None, None, None, "gy", None),
        ),
        check_vma=False,
    )
```

```python
import math

import jax
import jax.numpy as jnp
import ml_dtypes
import numpy as np
from jax import lax
from jax.experimental import pallas as pl
from jax.experimental.pallas import tpu as pltpu
from jax.sharding import PartitionSpec as P

KZ = 16
KT = 4
NT = 16
LANES = 128
F32 = jnp.float32
BF16 = jnp.bfloat16


def round_up(value, step):
    return -(-value // step) * step


def frequencies(kept):
    index = np.arange(kept)
    return np.where(index < kept // 2, index, index - kept)


def depth_time_table(cells):
    depth_cells = cells // NT
    depth = np.arange(depth_cells)[:, None, None, None] * frequencies(KZ)[None, None, :, None] * NT
    time = np.arange(NT)[None, :, None, None] * np.arange(KT)[None, None, None, :] * depth_cells
    phase = np.mod(depth + time, cells).reshape(cells, KZ * KT)
    angles = phase.astype(np.float32) * np.float32(2.0 * math.pi / cells)
    factor = np.float32(1.0 / math.sqrt(cells))
    return np.stack([np.cos(angles) * factor, -np.sin(angles) * factor], axis=1).astype(np.float32)


def plane_tables(sizes):
    length_x, length_y = sizes.nx * sizes.cells_x, sizes.ny * sizes.cells_y
    phase_x = np.mod(np.arange(length_x)[:, None] * frequencies(sizes.kept_x), length_x) / length_x
    phase_y = np.mod(np.arange(length_y)[:, None] * frequencies(sizes.kept_y), length_y) / length_y
    angle = 2.0 * math.pi * (phase_x[:, None, :, None] + phase_y[None, :, None, :])
    scale = 1.0 / math.sqrt(length_x * length_y)
    cosine, sine = np.cos(angle) * scale, np.sin(angle) * scale
    parts = np.stack([np.stack([cosine, -sine]), np.stack([sine, cosine])])
    pairs = sizes.cells_y // sizes.pair
    parts = parts.reshape(
        2, 2, sizes.nx, sizes.cells_x, sizes.ny, pairs, sizes.pair, sizes.ny, sizes.kept
    ).transpose(7, 3, 5, 2, 4, 6, 0, 1, 8)
    padded = np.zeros(parts.shape[:-1] + (sizes.half,), np.float32)
    padded[..., : sizes.kept] = parts
    return padded.reshape(sizes.ny, sizes.devices * sizes.cells, 4 * sizes.half)


class Sizes:
    def __init__(self, field, weight):
        self.nx, self.ny = lax.axis_size("gx"), lax.axis_size("gy")
        self.channels, self.cells_x, self.cells_y, self.depth = field.shape
        self.modes = weight.shape[0]
        self.local_x, self.kept_y = weight.shape[4:]
        self.kept_x = self.local_x * self.ny
        self.cells = self.cells_x * self.cells_y
        self.devices = self.nx * self.ny
        self.share = self.modes // 2
        self.kept = self.local_x * self.kept_y
        self.half = round_up(self.kept, LANES // 2)
        self.all_modes = 2 * self.modes * self.nx
        self.groups = LANES // self.modes
        self.main = self.channels // self.groups * self.groups if self.all_modes == LANES else 0
        self.rest = self.channels - self.main
        self.main_lanes = self.main * self.modes
        self.rest_lanes = self.rest * self.modes
        self.rest_tiles = round_up(self.rest_lanes, LANES) // LANES
        self.pair = math.gcd(self.cells_y, 2)
        self.pieces = self.cells // self.pair
        self.rest_first = self.pieces * self.main_lanes
        self.rest_width = round_up(self.pieces * self.rest_lanes, LANES)
        self.width = self.rest_first + self.rest_width
        self.spread_rows = self.main_lanes + self.rest_width
        self.rows = round_up(self.channels, 8)


def gather_cells(source, scratch, sizes):
    for w in range(sizes.channels):
        for x in range(sizes.cells_x):
            first = (w * sizes.cells_x + x) * sizes.cells_y
            scratch[first : first + sizes.cells_y, :] = source[w, x].astype(F32)
    return scratch[...]


def scatter_cells(values, target, sizes):
    for w in range(sizes.channels):
        for x in range(sizes.cells_x):
            first = (w * sizes.cells_x + x) * sizes.cells_y
            target[w, x] = values[first : first + sizes.cells_y, :].astype(target.dtype)


def lane_group(sizes):
    return lax.broadcasted_iota(jnp.int32, (sizes.cells, LANES), 1) // sizes.modes


def turn_groups(tiles, group, sizes):
    tiles = list(tiles)
    step = 1
    while step < sizes.groups:
        low = group // step % 2 == 0
        for first in range(sizes.groups):
            if first // step % 2 == 0:
                one, two = tiles[first], tiles[first + step]
                tiles[first] = jnp.where(low, one, pltpu.roll(two, step * sizes.modes, 1))
                tiles[first + step] = jnp.where(low, pltpu.roll(one, LANES - step * sizes.modes, 1), two)
        step *= 2
    return tiles


def put_group(target, source, have, want, group, sizes):
    if have != want:
        source = pltpu.roll(source, (want - have) % sizes.groups * sizes.modes, 1)
    return jnp.where(group == want, source, target)


def send_modes(values, target, sizes):
    group = lane_group(sizes)
    tiles = [values[w * sizes.cells : (w + 1) * sizes.cells, :] for w in range(sizes.channels)]
    turned = []
    for first in range(0, sizes.main, sizes.groups):
        turned.append(turn_groups(tiles[first : first + sizes.groups], group, sizes))
    for at in range(2 * sizes.nx):
        main = [block[at] for block in turned]
        last = [jnp.zeros((sizes.cells, LANES), F32) for _ in range(sizes.rest_width // LANES)]
        for r in range(sizes.rest):
            tile, want = divmod(r, sizes.groups)
            last[tile] = put_group(last[tile], tiles[sizes.main + r], at, want, group, sizes)
        if last:
            last = side_by_side(jnp.concatenate(last, 1), sizes.pair, sizes)
        for y in range(sizes.ny // 2):
            device = at // 2 * sizes.ny + 2 * y + at % 2
            for piece in range(sizes.pieces):
                rows = slice(piece * sizes.pair, (piece + 1) * sizes.pair)
                for k, value in enumerate(main):
                    first = piece * sizes.main_lanes + k * LANES
                    target[device, :, first : first + LANES] = value[rows]
            if sizes.rest:
                target[device, :, sizes.rest_first :] = last


def side_by_side(values, rows, sizes):
    total = values[:rows]
    for piece in range(1, sizes.pieces):
        moved = pltpu.roll(values, piece * sizes.rest_lanes, 1)
        total = total + moved[piece * rows : (piece + 1) * rows]
    return total


def receive_modes(source, scratch, tall, sizes):
    group = lane_group(sizes)
    parts = source[...].reshape(sizes.nx, sizes.ny // 2, 2, sizes.pair, sizes.width)
    values = parts[:, 0]
    for y in range(1, sizes.ny // 2):
        values = values + parts[:, y]
    values = values.reshape(2 * sizes.nx, sizes.pair, sizes.width)
    for piece in range(sizes.pieces):
        rows = slice(piece * sizes.pair, (piece + 1) * sizes.pair)
        if sizes.main:
            first = piece * sizes.main_lanes
            tall[:, rows, : sizes.main_lanes] = values[:, :, first : first + sizes.main_lanes]
        if sizes.rest:
            last = values[:, :, sizes.rest_first :]
            if piece:
                last = pltpu.roll(last, sizes.rest_width - piece * sizes.rest_lanes, 2)
            tall[:, rows, sizes.main_lanes :] = last
    out = []
    for first in range(0, sizes.main_lanes, LANES):
        tiles = [tall[at, :, first : first + LANES] for at in range(2 * sizes.nx)]
        out += turn_groups(tiles, group, sizes)
    for r in range(sizes.rest):
        value = jnp.zeros((sizes.cells, LANES), F32)
        tile, have = divmod(r, sizes.groups)
        first = sizes.main_lanes + tile * LANES
        for at in range(2 * sizes.nx):
            value = put_group(value, tall[at, :, first : first + LANES], have, at, group, sizes)
        out.append(value)
    for w, value in enumerate(out):
        scratch[w * sizes.cells : (w + 1) * sizes.cells, :] = value
    return scratch[...]


def dot(left, right, contract=((1,), (0,))):
    return lax.dot_general(left, right, (contract, ((), ())), preferred_element_type=F32)


def halves(values):
    high = values.astype(BF16)
    return high, (values - high.astype(F32)).astype(BF16)


def fine_dot(left, right, contract=((1,), (0,))):
    left_high, left_low = halves(left)
    right_high, right_low = halves(right)
    small = dot(left_high, right_low, contract) + dot(left_low, right_high, contract)
    return dot(left_high, right_high, contract) + small


def fetch(sources, targets, semaphores):
    copies = [pltpu.make_async_copy(*pair, semaphores.at[at]) for at, pair in enumerate(zip(sources, targets))]
    for copy in copies:
        copy.start()
    for copy in copies:
        copy.wait()


def depth_forward(
    sizes, field, table, source, out, target,
    cells, field_here, table_here, out_here, here, semaphores, weight_semaphores,
):
    few = [
        pltpu.make_async_copy(field, field_here, semaphores.at[0]),
        pltpu.make_async_copy(table, table_here, semaphores.at[1]),
    ]
    for copy in few:
        copy.start()
    clear_weights(sizes, target)
    for copy in few:
        copy.wait()
    copies = start_weights(sizes, source, 1 - core_of(), here, weight_semaphores)
    values = gather_cells(field_here, cells, sizes).astype(BF16)
    send_modes(dot(values, table_here[...]), out_here, sizes)
    copy = pltpu.make_async_copy(out_here, out, semaphores.at[2])
    copy.start()
    turn_weights(sizes, copies, here, target)
    copy.wait()


def one_hot(rows, columns, step, along_rows):
    row = lax.broadcasted_iota(jnp.int32, (rows, columns), 0)
    column = lax.broadcasted_iota(jnp.int32, (rows, columns), 1)
    same = row // step == column if along_rows else row == column // step
    return jnp.where(same, 1.0, 0.0).astype(BF16)


def cell_mixer(weights, across, sizes):
    count = sizes.channels * sizes.cells
    left = one_hot(count, sizes.channels, sizes.cells, True)
    right = one_hot(sizes.channels, count, sizes.cells, False)
    tall = dot(left, weights, ((1,), (1 if across else 0,)))
    wide = dot(tall.astype(BF16), right)
    row = lax.broadcasted_iota(jnp.int32, (count, count), 0)
    column = lax.broadcasted_iota(jnp.int32, (count, count), 1)
    same = lax.rem(row, sizes.cells) == lax.rem(column, sizes.cells)
    return jnp.where(same, wide, 0.0).astype(BF16)


def emit(sizes, pre, signal, weight, inverse, layer_out, local, inverse_out, weight_here, semaphores):
    copies = [
        pltpu.make_async_copy(weight, weight_here, semaphores.at[0]),
        pltpu.make_async_copy(inverse, inverse_out, semaphores.at[1]),
    ]
    for copy in copies:
        copy.start()
    scatter_cells(gelu_parts(pre[...])[0], layer_out, sizes)
    copies[0].wait()
    local[...] = dot(cell_mixer(weight_here[...], False, sizes), signal[...])
    copies[1].wait()


def core_of():
    return lax.rem(lax.axis_index("gy"), 2)


def start_weights(sizes, source, half, here, semaphores):
    copies = []
    for at in range(2 * sizes.share):
        copies.append(pltpu.make_async_copy(source.at[2 * sizes.share * half + at], here.at[at], semaphores.at[at]))
        copies[-1].start()
    return copies


def clear_weights(sizes, target):
    if sizes.half > sizes.kept:
        target[...] = jnp.zeros_like(target)
    elif sizes.rows > sizes.channels:
        target[:, :, sizes.channels :, :] = jnp.zeros(
            (sizes.share, sizes.channels, sizes.rows - sizes.channels, 2 * sizes.half), F32
        )


def turn_weights(sizes, copies, here, target):
    for mode in range(sizes.share):
        for s in range(2):
            copies[2 * mode + s].wait()
        for w in range(sizes.channels):
            blocks = [here[2 * mode + s, w].reshape(sizes.kept, sizes.channels) for s in range(2)]
            if sizes.half == sizes.kept:
                target[mode, w, : sizes.channels, :] = jnp.concatenate(blocks, 0).T
            else:
                for s, block in enumerate(blocks):
                    target[mode, w, : sizes.channels, s * sizes.half : s * sizes.half + sizes.kept] = block.T


def prepare(
    sizes, source, after, tables, field, cotangent, weight, bias,
    target, table, local, cotangent_out,
    here, cells, field_here, cot_here, cot_cells, weight_here, bias_here, local_here, semaphores, small,
):
    del after
    place = lax.axis_index("gy")
    lanes = 2 * sizes.half
    moves = [(field, field_here), (cotangent, cot_here), (weight, weight_here), (bias, bias_here)]
    for s in range(2):
        for at, owner in enumerate((place, place + 1 - 2 * core_of())):
            moves.append(
                (tables.at[owner, :, pl.ds(s * lanes, lanes)], table.at[:, pl.ds((2 * s + at) * lanes, lanes)])
            )
    few = [pltpu.make_async_copy(*move, small.at[at]) for at, move in enumerate(moves)]
    copies = start_weights(sizes, source, core_of(), here, semaphores)
    for copy in few:
        copy.start()
    clear_weights(sizes, target)
    turn_weights(sizes, copies, here, target)
    for copy in few:
        copy.wait()
    values = gather_cells(field_here, cells, sizes).astype(BF16)
    spread = one_hot(sizes.channels * sizes.cells, sizes.channels, sizes.cells, True).astype(F32)
    offset = jnp.sum(spread * bias_here[...].reshape(1, sizes.channels), axis=1, keepdims=True)
    local_here[...] = dot(cell_mixer(weight_here[...], True, sizes), values) + offset
    gather_cells(cot_here, cot_cells, sizes)
    results = [
        pltpu.make_async_copy(local_here, local, small.at[0]),
        pltpu.make_async_copy(cot_cells, cotangent_out, small.at[1]),
    ]
    for copy in results:
        copy.start()
    for copy in results:
        copy.wait()


def fetch_weights(sizes, source, after, target, semaphore):
    del after
    copy = pltpu.make_async_copy(source, target, semaphore.at[0])
    copy.start()
    copy.wait()


def plane_spectra(sizes, received, table, targets, flat):
    count = sizes.devices * sizes.pair
    for at in range(sizes.devices):
        for piece in range(sizes.pieces):
            rows = slice(piece * count + at * sizes.pair, piece * count + (at + 1) * sizes.pair)
            if sizes.main:
                first = piece * sizes.main_lanes
                flat[rows, : sizes.main_lanes] = received[at, :, first : first + sizes.main_lanes]
            if sizes.rest:
                flat[rows, sizes.main_lanes :] = received[at, :, sizes.rest_first :]
    if sizes.rest:
        for piece in range(1, sizes.pieces):
            rows = slice(piece * count, (piece + 1) * count)
            shift = sizes.rest_width - piece * sizes.rest_lanes
            flat[rows, sizes.main_lanes :] = pltpu.roll(flat[rows, sizes.main_lanes :], shift, 1)
    rows, lanes = targets[0].shape
    both = fine_dot(flat[...].T[:rows], table[...])
    total = both[:, : 2 * lanes] + pltpu.roll(both[:, 2 * lanes :], rows - sizes.share, 0)
    for at, target in enumerate(targets):
        target[...] = total[:, at * lanes : (at + 1) * lanes]


def plane_cells(sizes, spread, table, out):
    modes = jnp.concatenate([spread[at] for at in range(4)], 1)
    cells = fine_dot(table[...], modes, ((1,), (1,)))
    count = sizes.devices * sizes.pair
    if sizes.rest:
        last = side_by_side(cells[:, sizes.main_lanes :], count, sizes)
    for at in range(sizes.devices):
        rows = slice(at * sizes.pair, (at + 1) * sizes.pair)
        for piece in range(sizes.pieces):
            if sizes.main:
                first = piece * sizes.main_lanes
                out[at, :, first : first + sizes.main_lanes] = cells[
                    piece * count + at * sizes.pair : piece * count + (at + 1) * sizes.pair, : sizes.main_lanes
                ]
        if sizes.rest:
            out[at, :, sizes.rest_first :] = last[rows]


def swap_parts(values, sizes):
    return pltpu.roll(values, sizes.half, 1)


def mode_rows(first, sizes):
    return pl.ds(first, sizes.channels, stride=sizes.modes)


def put_mixed(spread, at, mode, values, sizes):
    for s in range(2):
        spread[2 * s + at, mode_rows(s * sizes.share + mode, sizes), :] = values


def first_lanes(rows, sizes):
    return lax.broadcasted_iota(jnp.int32, (rows, 2 * sizes.half), 1) < sizes.half


def mix_forward(
    sizes, received, table, weight, other_weight, local, cotangent, inverse, forward,
    spectra, other_spectra, out, local_out, cotangent_out, inverse_out, forward_out,
    spread, swapped, flat, semaphores,
):
    moves = ((local, local_out), (cotangent, cotangent_out), (inverse, inverse_out), (forward, forward_out))
    copies = [pltpu.make_async_copy(*move, semaphores.at[at]) for at, move in enumerate(moves)]
    for copy in copies:
        copy.start()
    plane_spectra(sizes, received, table, (spectra, other_spectra), flat)
    spread[...] = jnp.zeros_like(spread)
    real = first_lanes(sizes.rows, sizes)
    for at, (rows, block) in enumerate(((spectra, weight), (other_spectra, other_weight))):
        swapped[...] = swap_parts(rows[...], sizes)
        for m in range(sizes.share):
            straight = jnp.zeros((sizes.rows, 2 * sizes.half), F32)
            crossed = jnp.zeros((sizes.rows, 2 * sizes.half), F32)
            for w in range(sizes.channels):
                row = slice(w * sizes.modes + m, w * sizes.modes + m + 1)
                straight = straight + rows[row, :] * block[m, w]
                crossed = crossed + swapped[row, :] * block[m, w]
            real_part = straight - swap_parts(straight, sizes)
            imag_part = crossed + swap_parts(crossed, sizes)
            put_mixed(spread, at, m, jnp.where(real, real_part, imag_part)[: sizes.channels], sizes)
    plane_cells(sizes, spread, table, out)
    for copy in copies:
        copy.wait()


def mix_back(sizes, received, table, weight, other_weight, back, other_back, out, spread, flat):
    plane_spectra(sizes, received, table, (back, other_back), flat)
    spread[...] = jnp.zeros_like(spread)
    real = first_lanes(sizes.channels, sizes)
    for at, (source, block) in enumerate(((back, weight), (other_back, other_weight))):
        for m in range(sizes.share):
            rows = source[mode_rows(m, sizes), :]
            if sizes.rows > sizes.channels:
                rows = jnp.concatenate([rows, jnp.zeros((sizes.rows - sizes.channels, 2 * sizes.half), F32)], 0)
            turned = swap_parts(rows, sizes)
            straight, crossed = [], []
            for w in range(sizes.channels):
                straight.append(jnp.sum(block[m, w] * rows, axis=0, keepdims=True))
                crossed.append(jnp.sum(block[m, w] * turned, axis=0, keepdims=True))
            straight = jnp.concatenate(straight, 0)
            crossed = jnp.concatenate(crossed, 0)
            real_part = straight + swap_parts(straight, sizes)
            imag_part = swap_parts(crossed, sizes) - crossed
            put_mixed(spread, at, m, jnp.where(real, real_part, imag_part), sizes)
    plane_cells(sizes, spread, table, out)


def grad_weights(
    sizes, spectra, back, given_spectra, given_back, target, here, straight, crossed, semaphores
):
    copies = []
    for which, (source, backward) in enumerate(((spectra, back), (given_spectra, given_back))):
        half = core_of() if which == 0 else 1 - core_of()
        values = source[...]
        turned = swap_parts(values, sizes)
        real = first_lanes(values.shape[0], sizes)
        straight[...] = jnp.where(real, values, turned)
        crossed[...] = jnp.where(real, turned, -values)
        for mode in range(sizes.share):
            rows = backward[mode_rows(mode, sizes), :]
            if sizes.rows > sizes.channels:
                rows = jnp.concatenate([rows, jnp.zeros((sizes.rows - sizes.channels, 2 * sizes.half), F32)], 0)
            turned = swap_parts(rows, sizes)
            local = 2 * (which * sizes.share + mode)
            for w in range(sizes.channels):
                at = slice(w * sizes.modes + mode, w * sizes.modes + mode + 1)
                block = (straight[at, :] * rows + crossed[at, :] * turned).T
                for s in range(2):
                    part = block[s * sizes.half : s * sizes.half + sizes.kept, : sizes.channels]
                    here[local + s, w] = part.reshape(sizes.local_x, sizes.kept_y, sizes.channels)
            for s in range(2):
                to = 2 * (half * sizes.share + mode) + s
                copies.append(pltpu.make_async_copy(here.at[local + s], target.at[to], semaphores.at[local + s]))
                copies[-1].start()
    for copy in copies:
        copy.wait()


def gelu_parts(pre):
    slope = math.sqrt(2.0 / math.pi)
    squared = pre * pre
    bend = jnp.tanh(slope * (pre + 0.044715 * (squared * pre)))
    value = 0.5 * pre * (1.0 + bend)
    derivative = 0.5 * (1.0 + bend) + 0.5 * pre * (1.0 - bend * bend) * (slope * (1.0 + 3.0 * 0.044715 * squared))
    return value, derivative


def activate(
    sizes, received, local, cotangent, inverse, forward, pre_out, signal_out, out, spectrum, tall
):
    pre = fine_dot(receive_modes(received, spectrum, tall, sizes), inverse[...]) + local[...]
    pre_out[...] = pre
    signal = (cotangent[...] * gelu_parts(pre)[1]).astype(BF16)
    signal_out[...] = signal
    send_modes(dot(signal, forward[...]), out, sizes)


def finish(sizes, received, local, inverse, grad_field, spectrum, tall):
    spatial = fine_dot(receive_modes(received, spectrum, tall, sizes), inverse[...])
    scatter_cells(spatial + local[...], grad_field, sizes)


def shape_of(shape, dtype=F32):
    return jax.ShapeDtypeStruct(shape, dtype)


VMEM = pl.BlockSpec(memory_space=pltpu.VMEM)
HELD = pl.BlockSpec(memory_space=pltpu.VMEM)
HBM = pl.BlockSpec(memory_space=pltpu.HBM)
ANYWHERE = pl.BlockSpec(memory_space=pl.ANY)


def settings(mebibytes):
    return pltpu.CompilerParams(vmem_limit_bytes=mebibytes * 1024 * 1024)


def cost(nanoseconds):
    return pl.CostEstimate(flops=0, bytes_accessed=3000 * nanoseconds, transcendentals=0)


def whole_call(body, sizes, nanoseconds, out_shape, scratch, *args, specs=None, out_specs=None, room=16):
    def kernel(*refs):
        body(sizes, *refs)

    if specs:
        spaces = [pltpu.HBM if spec is HBM else pltpu.VMEM if spec is HELD else None for spec in specs]
        args = [
            pltpu.with_memory_space_constraint(arg, space) if space else arg for arg, space in zip(args, spaces)
        ]
    return pl.pallas_call(
        kernel,
        out_shape=out_shape,
        in_specs=specs or [VMEM] * len(args),
        out_specs=out_specs or jax.tree.map(lambda _: VMEM, out_shape),
        scratch_shapes=scratch,
        name=body.__name__,
        cost_estimate=cost(nanoseconds),
        compiler_params=settings(room),
    )(*args)


def on_device(field, cotangent, spectral_weight, pointwise_weight, channel_bias):
    z = Sizes(field, spectral_weight)
    depth_table = depth_time_table(z.depth)
    modes = depth_table.shape[2]
    kappa = np.where(np.arange(modes) % KT == 0, 1.0, 2.0).astype(np.float32)
    shares = (z.nx, 2, z.share)
    ordered = depth_table.reshape((z.depth, 2) + shares).transpose(0, 2, 3, 1, 4).reshape(z.depth, z.all_modes)
    doubled = np.repeat(kappa.reshape(z.nx, 2, 1, z.share), 2, axis=2).reshape(z.all_modes)
    forward_first = jnp.asarray(ordered.astype(ml_dtypes.bfloat16))
    forward_back = jnp.asarray((ordered.astype(ml_dtypes.bfloat16).astype(np.float32) * doubled).astype(ml_dtypes.bfloat16))
    inverse_back = jnp.asarray(np.ascontiguousarray(ordered.T))
    inverse_first = jnp.asarray(np.ascontiguousarray((ordered * doubled).T))
    pairs = [(s, s ^ 1) for s in range(z.ny)]

    def exchange(payload):
        return lax.all_to_all(payload, ("gx", "gy"), split_axis=0, concat_axis=0, tiled=True)

    def other_core(values):
        return lax.ppermute(values, "gy", pairs)

    payload = shape_of((z.devices, z.pair, z.width))
    cell_rows = z.channels * z.cells
    cells_shape = (cell_rows, z.depth)
    cells_scratch = pltpu.VMEM(cells_shape, F32)
    spectrum_scratch = pltpu.VMEM((cell_rows, z.all_modes), F32)
    spectra_shape = (z.channels * z.modes, 2 * z.half)
    spectra_scratch = pltpu.VMEM(spectra_shape, F32)
    flat_scratch = pltpu.VMEM((z.devices * z.cells, z.spread_rows), F32)
    spread_scratch = pltpu.VMEM((4, z.spread_rows, 2 * z.half), F32)
    tall_scratch = pltpu.VMEM((2 * z.nx, z.cells, z.spread_rows), F32)
    field_scratch = pltpu.VMEM(field.shape, BF16)
    weight_here = pltpu.VMEM(pointwise_weight.shape, BF16)
    native = jnp.transpose(spectral_weight, (0, 1, 2, 4, 5, 3))
    weight_shape = (2 * z.modes,) + native.shape[2:]
    half_scratch = pltpu.VMEM((z.modes,) + native.shape[2:], F32)
    turned_shape = shape_of((z.share, z.channels, z.rows, 2 * z.half))

    def flags(count):
        return pltpu.SemaphoreType.DMA((count,))

    weights = native.reshape(weight_shape)
    sent, turned_away = whole_call(
        depth_forward, z, 1500, (payload, turned_shape),
        [
            cells_scratch, field_scratch, pltpu.VMEM(forward_first.shape, BF16), pltpu.VMEM(payload.shape, F32),
            half_scratch, flags(3), flags(z.modes),
        ],
        field, forward_first, weights, specs=[HBM] * 3, out_specs=(HBM, VMEM),
    )
    received = exchange(sent)
    other_turned = other_core(turned_away)
    turned, plane, local, cot_cells = whole_call(
        prepare, z, 100,
        (turned_shape, shape_of((z.devices * z.cells, 8 * z.half)), pltpu.HBM(cells_shape, F32), pltpu.HBM(cells_shape, F32)),
        [
            half_scratch, cells_scratch, field_scratch, field_scratch, cells_scratch, weight_here,
            pltpu.VMEM(channel_bias.shape, F32), cells_scratch, flags(z.modes), flags(8),
        ],
        weights, turned_away, jnp.asarray(plane_tables(z)), field, cotangent, pointwise_weight, channel_bias,
        specs=[HBM, ANYWHERE] + [HBM] * 5, out_specs=(VMEM, VMEM, HBM, HBM),
    )
    other_turned = whole_call(
        fetch_weights, z, 100, turned_shape, [flags(1)], other_turned, turned, specs=[HBM, ANYWHERE]
    )
    received, other_turned, turned, plane, local, cot_cells = lax.optimization_barrier(
        (received, other_turned, turned, plane, local, cot_cells)
    )
    spectra, other_spectra, sent, local, cot_cells, inverse_here, forward_here = whole_call(
        mix_forward, z, 1000,
        (
            shape_of(spectra_shape), shape_of(spectra_shape), payload, shape_of(cells_shape), shape_of(cells_shape),
            shape_of(inverse_first.shape), shape_of(forward_back.shape, BF16),
        ),
        [spread_scratch, spectra_scratch, flat_scratch, flags(4)],
        received, plane, turned, other_turned, local, cot_cells, inverse_first, forward_back,
        specs=[HELD] + [VMEM] * 3 + [HBM] * 4,
    )
    pre, signal, sent = whole_call(
        activate, z, 2000,
        (shape_of(cells_shape), shape_of(cells_shape, BF16), payload), [spectrum_scratch, tall_scratch],
        exchange(sent), local, cot_cells, inverse_here, forward_here,
    )
    back, other_back, sent = whole_call(
        mix_back, z, 1000, (shape_of(spectra_shape), shape_of(spectra_shape), payload),
        [spread_scratch, flat_scratch], exchange(sent), plane, turned, other_turned,
    )
    sent, spectra, other_spectra, back, other_back, pre, signal = lax.optimization_barrier(
        (sent, spectra, other_spectra, back, other_back, pre, signal)
    )
    returned = exchange(sent)
    given_spectra, given_back = other_core(other_spectra), other_core(other_back)
    layer_out, local, inverse_here = whole_call(
        emit, z, 1500,
        (shape_of(field.shape, BF16), shape_of(cells_shape), shape_of(inverse_back.shape)),
        [weight_here, flags(2)],
        pre, signal, pointwise_weight, inverse_back, specs=[VMEM, VMEM, HBM, HBM],
    )
    gradient = whole_call(
        grad_weights, z, 5000, shape_of(weight_shape),
        [pltpu.VMEM(weight_shape, F32), spectra_scratch, spectra_scratch, flags(2 * z.modes)],
        spectra, back, given_spectra, given_back, out_specs=HBM, room=28,
    )
    returned, gradient, layer_out, local, inverse_here = lax.optimization_barrier(
        (returned, gradient, layer_out, local, inverse_here)
    )
    grad_field = whole_call(
        finish, z, 1000, shape_of(field.shape, BF16), [spectrum_scratch, tall_scratch], returned, local, inverse_here
    )
    return (layer_out, grad_field, jnp.transpose(gradient.reshape(native.shape), (0, 1, 2, 5, 3, 4)))


def solution(mesh):
    return jax.shard_map(
        on_device,
        mesh=mesh,
        in_specs=(
            P(None, "gx", "gy", None),
            P(None, "gx", "gy", None),
            P("gx", None, None, None, "gy", None),
            P(),
            P(),
        ),
        out_specs=(
            P(None, "gx", "gy", None),
            P(None, "gx", "gy", None),
            P("gx", None, None, None, "gy", None),
        ),
        check_vma=False,
    )
```

```python
import math

import jax
import jax.numpy as jnp
import ml_dtypes
import numpy as np
from jax import lax
from jax.experimental import pallas as pl
from jax.experimental.pallas import tpu as pltpu
from jax.sharding import PartitionSpec as P

KZ = 16
KT = 4
NT = 16
LANES = 128
F32 = jnp.float32
BF16 = jnp.bfloat16


def round_up(value, step):
    return -(-value // step) * step


def frequencies(kept):
    index = np.arange(kept)
    return np.where(index < kept // 2, index, index - kept)


def depth_time_table(cells):
    depth_cells = cells // NT
    depth = np.arange(depth_cells)[:, None, None, None] * frequencies(KZ)[None, None, :, None] * NT
    time = np.arange(NT)[None, :, None, None] * np.arange(KT)[None, None, None, :] * depth_cells
    phase = np.mod(depth + time, cells).reshape(cells, KZ * KT)
    angles = phase.astype(np.float32) * np.float32(2.0 * math.pi / cells)
    factor = np.float32(1.0 / math.sqrt(cells))
    return np.stack([np.cos(angles) * factor, -np.sin(angles) * factor], axis=1).astype(np.float32)


def plane_tables(sizes):
    length_x, length_y = sizes.nx * sizes.cells_x, sizes.ny * sizes.cells_y
    phase_x = np.mod(np.arange(length_x)[:, None] * frequencies(sizes.kept_x), length_x) / length_x
    phase_y = np.mod(np.arange(length_y)[:, None] * frequencies(sizes.kept_y), length_y) / length_y
    angle = 2.0 * math.pi * (phase_x[:, None, :, None] + phase_y[None, :, None, :])
    scale = 1.0 / math.sqrt(length_x * length_y)
    cosine, sine = np.cos(angle) * scale, np.sin(angle) * scale
    parts = np.stack([np.stack([cosine, -sine]), np.stack([sine, cosine])])
    pairs = sizes.cells_y // sizes.pair
    parts = parts.reshape(
        2, 2, sizes.nx, sizes.cells_x, sizes.ny, pairs, sizes.pair, sizes.ny, sizes.kept
    ).transpose(7, 3, 5, 2, 4, 6, 0, 1, 8)
    padded = np.zeros(parts.shape[:-1] + (sizes.half,), np.float32)
    padded[..., : sizes.kept] = parts
    return padded.reshape(sizes.ny, sizes.devices * sizes.cells, 4 * sizes.half)


class Sizes:
    def __init__(self, field, weight):
        self.nx, self.ny = lax.axis_size("gx"), lax.axis_size("gy")
        self.channels, self.cells_x, self.cells_y, self.depth = field.shape
        self.modes = weight.shape[0]
        self.local_x, self.kept_y = weight.shape[4:]
        self.kept_x = self.local_x * self.ny
        self.cells = self.cells_x * self.cells_y
        self.devices = self.nx * self.ny
        self.share = self.modes // 2
        self.kept = self.local_x * self.kept_y
        self.half = round_up(self.kept, LANES // 2)
        self.all_modes = 2 * self.modes * self.nx
        self.groups = LANES // self.modes
        self.main = self.channels // self.groups * self.groups if self.all_modes == LANES else 0
        self.rest = self.channels - self.main
        self.main_lanes = self.main * self.modes
        self.rest_lanes = self.rest * self.modes
        self.rest_tiles = round_up(self.rest_lanes, LANES) // LANES
        self.pair = math.gcd(self.cells_y, 2)
        self.pieces = self.cells // self.pair
        self.rest_first = self.pieces * self.main_lanes
        self.rest_width = round_up(self.pieces * self.rest_lanes, LANES)
        self.width = self.rest_first + self.rest_width
        self.spread_rows = self.main_lanes + self.rest_width
        self.rows = round_up(self.channels, 8)


def gather_cells(source, scratch, sizes):
    for w in range(sizes.channels):
        for x in range(sizes.cells_x):
            first = (w * sizes.cells_x + x) * sizes.cells_y
            scratch[first : first + sizes.cells_y, :] = source[w, x].astype(F32)
    return scratch[...]


def scatter_cells(values, target, sizes):
    for w in range(sizes.channels):
        for x in range(sizes.cells_x):
            first = (w * sizes.cells_x + x) * sizes.cells_y
            target[w, x] = values[first : first + sizes.cells_y, :].astype(target.dtype)


def lane_group(sizes):
    return lax.broadcasted_iota(jnp.int32, (sizes.cells, LANES), 1) // sizes.modes


def turn_groups(tiles, group, sizes):
    tiles = list(tiles)
    step = 1
    while step < sizes.groups:
        low = group // step % 2 == 0
        for first in range(sizes.groups):
            if first // step % 2 == 0:
                one, two = tiles[first], tiles[first + step]
                tiles[first] = jnp.where(low, one, pltpu.roll(two, step * sizes.modes, 1))
                tiles[first + step] = jnp.where(low, pltpu.roll(one, LANES - step * sizes.modes, 1), two)
        step *= 2
    return tiles


def put_group(target, source, have, want, group, sizes):
    if have != want:
        source = pltpu.roll(source, (want - have) % sizes.groups * sizes.modes, 1)
    return jnp.where(group == want, source, target)


def send_modes(values, target, sizes):
    group = lane_group(sizes)
    tiles = [values[w * sizes.cells : (w + 1) * sizes.cells, :] for w in range(sizes.channels)]
    turned = []
    for first in range(0, sizes.main, sizes.groups):
        turned.append(turn_groups(tiles[first : first + sizes.groups], group, sizes))
    for at in range(2 * sizes.nx):
        main = [block[at] for block in turned]
        last = [jnp.zeros((sizes.cells, LANES), F32) for _ in range(sizes.rest_width // LANES)]
        for r in range(sizes.rest):
            tile, want = divmod(r, sizes.groups)
            last[tile] = put_group(last[tile], tiles[sizes.main + r], at, want, group, sizes)
        if last:
            last = side_by_side(jnp.concatenate(last, 1), sizes.pair, sizes)
        for y in range(sizes.ny // 2):
            device = at // 2 * sizes.ny + 2 * y + at % 2
            for piece in range(sizes.pieces):
                rows = slice(piece * sizes.pair, (piece + 1) * sizes.pair)
                for k, value in enumerate(main):
                    first = piece * sizes.main_lanes + k * LANES
                    target[device, :, first : first + LANES] = value[rows]
            if sizes.rest:
                target[device, :, sizes.rest_first :] = last


def side_by_side(values, rows, sizes):
    total = values[:rows]
    for piece in range(1, sizes.pieces):
        moved = pltpu.roll(values, piece * sizes.rest_lanes, 1)
        total = total + moved[piece * rows : (piece + 1) * rows]
    return total


def receive_modes(source, scratch, tall, sizes):
    group = lane_group(sizes)
    parts = source[...].reshape(sizes.nx, sizes.ny // 2, 2, sizes.pair, sizes.width)
    values = parts[:, 0]
    for y in range(1, sizes.ny // 2):
        values = values + parts[:, y]
    values = values.reshape(2 * sizes.nx, sizes.pair, sizes.width)
    for piece in range(sizes.pieces):
        rows = slice(piece * sizes.pair, (piece + 1) * sizes.pair)
        if sizes.main:
            first = piece * sizes.main_lanes
            tall[:, rows, : sizes.main_lanes] = values[:, :, first : first + sizes.main_lanes]
        if sizes.rest:
            last = values[:, :, sizes.rest_first :]
            if piece:
                last = pltpu.roll(last, sizes.rest_width - piece * sizes.rest_lanes, 2)
            tall[:, rows, sizes.main_lanes :] = last
    out = []
    for first in range(0, sizes.main_lanes, LANES):
        tiles = [tall[at, :, first : first + LANES] for at in range(2 * sizes.nx)]
        out += turn_groups(tiles, group, sizes)
    for r in range(sizes.rest):
        value = jnp.zeros((sizes.cells, LANES), F32)
        tile, have = divmod(r, sizes.groups)
        first = sizes.main_lanes + tile * LANES
        for at in range(2 * sizes.nx):
            value = put_group(value, tall[at, :, first : first + LANES], have, at, group, sizes)
        out.append(value)
    for w, value in enumerate(out):
        scratch[w * sizes.cells : (w + 1) * sizes.cells, :] = value
    return scratch[...]


def dot(left, right, contract=((1,), (0,))):
    return lax.dot_general(left, right, (contract, ((), ())), preferred_element_type=F32)


def halves(values):
    high = values.astype(BF16)
    return high, (values - high.astype(F32)).astype(BF16)


def fine_dot(left, right, contract=((1,), (0,))):
    left_high, left_low = halves(left)
    right_high, right_low = halves(right)
    small = dot(left_high, right_low, contract) + dot(left_low, right_high, contract)
    return dot(left_high, right_high, contract) + small


def fetch(sources, targets, semaphores):
    copies = [pltpu.make_async_copy(*pair, semaphores.at[at]) for at, pair in enumerate(zip(sources, targets))]
    for copy in copies:
        copy.start()
    for copy in copies:
        copy.wait()


def depth_forward(
    sizes, field, table, source, out, target,
    cells, field_here, table_here, out_here, here, semaphores, weight_semaphores,
):
    few = [
        pltpu.make_async_copy(field, field_here, semaphores.at[0]),
        pltpu.make_async_copy(table, table_here, semaphores.at[1]),
    ]
    for copy in few:
        copy.start()
    copies = start_weights(sizes, source, 1 - core_of(), here, weight_semaphores, 0, sizes.share)
    clear_weights(sizes, target)
    for copy in few:
        copy.wait()
    copies += start_weights(sizes, source, 1 - core_of(), here, weight_semaphores, sizes.share)
    values = gather_cells(field_here, cells, sizes).astype(BF16)
    send_modes(dot(values, table_here[...]), out_here, sizes)
    copy = pltpu.make_async_copy(out_here, out, semaphores.at[2])
    copy.start()
    turn_weights(sizes, copies, here, target)
    copy.wait()


def one_hot(rows, columns, step, along_rows):
    row = lax.broadcasted_iota(jnp.int32, (rows, columns), 0)
    column = lax.broadcasted_iota(jnp.int32, (rows, columns), 1)
    same = row // step == column if along_rows else row == column // step
    return jnp.where(same, 1.0, 0.0).astype(BF16)


def cell_mixer(weights, across, sizes):
    count = sizes.channels * sizes.cells
    left = one_hot(count, sizes.channels, sizes.cells, True)
    right = one_hot(sizes.channels, count, sizes.cells, False)
    tall = dot(left, weights, ((1,), (1 if across else 0,)))
    wide = dot(tall.astype(BF16), right)
    row = lax.broadcasted_iota(jnp.int32, (count, count), 0)
    column = lax.broadcasted_iota(jnp.int32, (count, count), 1)
    same = lax.rem(row, sizes.cells) == lax.rem(column, sizes.cells)
    return jnp.where(same, wide, 0.0).astype(BF16)


def emit(sizes, pre, signal, weight, inverse, layer_out, local, inverse_out, weight_here, semaphores):
    copies = [
        pltpu.make_async_copy(weight, weight_here, semaphores.at[0]),
        pltpu.make_async_copy(inverse, inverse_out, semaphores.at[1]),
    ]
    for copy in copies:
        copy.start()
    scatter_cells(gelu_parts(pre[...])[0], layer_out, sizes)
    copies[0].wait()
    local[...] = dot(cell_mixer(weight_here[...], False, sizes), signal[...])
    copies[1].wait()


def core_of():
    return lax.rem(lax.axis_index("gy"), 2)


def start_weights(sizes, source, half, here, semaphores, first=0, end=None):
    copies = []
    for at in range(2 * sizes.share)[first:end]:
        copies.append(pltpu.make_async_copy(source.at[2 * sizes.share * half + at], here.at[at], semaphores.at[at]))
        copies[-1].start()
    return copies


def clear_weights(sizes, target):
    if sizes.half > sizes.kept:
        target[...] = jnp.zeros_like(target)
    elif sizes.rows > sizes.channels:
        target[:, :, sizes.channels :, :] = jnp.zeros(
            (sizes.share, sizes.channels, sizes.rows - sizes.channels, 2 * sizes.half), F32
        )


def turn_weights(sizes, copies, here, target):
    for mode in range(sizes.share):
        for s in range(2):
            copies[2 * mode + s].wait()
        for w in range(sizes.channels):
            blocks = [here[2 * mode + s, w].reshape(sizes.kept, sizes.channels) for s in range(2)]
            if sizes.half == sizes.kept:
                target[mode, w, : sizes.channels, :] = jnp.concatenate(blocks, 0).T
            else:
                for s, block in enumerate(blocks):
                    target[mode, w, : sizes.channels, s * sizes.half : s * sizes.half + sizes.kept] = block.T


def prepare(
    sizes, source, after, tables, field, cotangent, weight, bias,
    target, table, local, cotangent_out,
    here, cells, field_here, cot_here, cot_cells, weight_here, bias_here, local_here, semaphores, small,
):
    del after
    place = lax.axis_index("gy")
    lanes = 2 * sizes.half
    moves = [(field, field_here), (cotangent, cot_here), (weight, weight_here), (bias, bias_here)]
    for s in range(2):
        for at, owner in enumerate((place, place + 1 - 2 * core_of())):
            moves.append(
                (tables.at[owner, :, pl.ds(s * lanes, lanes)], table.at[:, pl.ds((2 * s + at) * lanes, lanes)])
            )
    few = [pltpu.make_async_copy(*move, small.at[at]) for at, move in enumerate(moves)]
    for copy in few[:4]:
        copy.start()
    copies = start_weights(sizes, source, core_of(), here, semaphores)
    for copy in few[4:]:
        copy.start()
    clear_weights(sizes, target)
    for copy in few[:4]:
        copy.wait()
    values = gather_cells(field_here, cells, sizes).astype(BF16)
    spread = one_hot(sizes.channels * sizes.cells, sizes.channels, sizes.cells, True).astype(F32)
    offset = jnp.sum(spread * bias_here[...].reshape(1, sizes.channels), axis=1, keepdims=True)
    local_here[...] = dot(cell_mixer(weight_here[...], True, sizes), values) + offset
    gather_cells(cot_here, cot_cells, sizes)
    results = [
        pltpu.make_async_copy(local_here, local, small.at[0]),
        pltpu.make_async_copy(cot_cells, cotangent_out, small.at[1]),
    ]
    for copy in results:
        copy.start()
    turn_weights(sizes, copies, here, target)
    for copy in few[4:] + results:
        copy.wait()


def fetch_weights(sizes, source, after, target, semaphore):
    del after
    copy = pltpu.make_async_copy(source, target, semaphore.at[0])
    copy.start()
    copy.wait()


def plane_spectra(sizes, received, table, targets, flat):
    count = sizes.devices * sizes.pair
    for at in range(sizes.devices):
        for piece in range(sizes.pieces):
            rows = slice(piece * count + at * sizes.pair, piece * count + (at + 1) * sizes.pair)
            if sizes.main:
                first = piece * sizes.main_lanes
                flat[rows, : sizes.main_lanes] = received[at, :, first : first + sizes.main_lanes]
            if sizes.rest:
                flat[rows, sizes.main_lanes :] = received[at, :, sizes.rest_first :]
    if sizes.rest:
        for piece in range(1, sizes.pieces):
            rows = slice(piece * count, (piece + 1) * count)
            shift = sizes.rest_width - piece * sizes.rest_lanes
            flat[rows, sizes.main_lanes :] = pltpu.roll(flat[rows, sizes.main_lanes :], shift, 1)
    rows, lanes = targets[0].shape
    both = fine_dot(flat[...].T[:rows], table[...])
    total = both[:, : 2 * lanes] + pltpu.roll(both[:, 2 * lanes :], rows - sizes.share, 0)
    for at, target in enumerate(targets):
        target[...] = total[:, at * lanes : (at + 1) * lanes]


def plane_cells(sizes, spread, table, out):
    modes = jnp.concatenate([spread[at] for at in range(4)], 1)
    cells = fine_dot(table[...], modes, ((1,), (1,)))
    count = sizes.devices * sizes.pair
    if sizes.rest:
        last = side_by_side(cells[:, sizes.main_lanes :], count, sizes)
    for at in range(sizes.devices):
        rows = slice(at * sizes.pair, (at + 1) * sizes.pair)
        for piece in range(sizes.pieces):
            if sizes.main:
                first = piece * sizes.main_lanes
                out[at, :, first : first + sizes.main_lanes] = cells[
                    piece * count + at * sizes.pair : piece * count + (at + 1) * sizes.pair, : sizes.main_lanes
                ]
        if sizes.rest:
            out[at, :, sizes.rest_first :] = last[rows]


def swap_parts(values, sizes):
    return pltpu.roll(values, sizes.half, 1)


def mode_rows(first, sizes):
    return pl.ds(first, sizes.channels, stride=sizes.modes)


def put_mixed(spread, at, mode, values, sizes):
    for s in range(2):
        spread[2 * s + at, mode_rows(s * sizes.share + mode, sizes), :] = values


def first_lanes(rows, sizes):
    return lax.broadcasted_iota(jnp.int32, (rows, 2 * sizes.half), 1) < sizes.half


def mix_forward(
    sizes, received, table, weight, other_weight, local, cotangent, inverse, forward,
    spectra, other_spectra, out, local_out, cotangent_out, inverse_out, forward_out,
    spread, swapped, flat, semaphores,
):
    moves = ((local, local_out), (cotangent, cotangent_out), (inverse, inverse_out), (forward, forward_out))
    copies = [pltpu.make_async_copy(*move, semaphores.at[at]) for at, move in enumerate(moves)]
    for copy in copies:
        copy.start()
    plane_spectra(sizes, received, table, (spectra, other_spectra), flat)
    spread[...] = jnp.zeros_like(spread)
    real = first_lanes(sizes.rows, sizes)
    for at, (rows, block) in enumerate(((spectra, weight), (other_spectra, other_weight))):
        swapped[...] = swap_parts(rows[...], sizes)
        for m in range(sizes.share):
            straight = jnp.zeros((sizes.rows, 2 * sizes.half), F32)
            crossed = jnp.zeros((sizes.rows, 2 * sizes.half), F32)
            for w in range(sizes.channels):
                row = slice(w * sizes.modes + m, w * sizes.modes + m + 1)
                straight = straight + rows[row, :] * block[m, w]
                crossed = crossed + swapped[row, :] * block[m, w]
            real_part = straight - swap_parts(straight, sizes)
            imag_part = crossed + swap_parts(crossed, sizes)
            put_mixed(spread, at, m, jnp.where(real, real_part, imag_part)[: sizes.channels], sizes)
    plane_cells(sizes, spread, table, out)
    for copy in copies:
        copy.wait()


def mix_back(sizes, received, table, weight, other_weight, back, other_back, out, spread, flat):
    plane_spectra(sizes, received, table, (back, other_back), flat)
    spread[...] = jnp.zeros_like(spread)
    real = first_lanes(sizes.channels, sizes)
    for at, (source, block) in enumerate(((back, weight), (other_back, other_weight))):
        for m in range(sizes.share):
            rows = source[mode_rows(m, sizes), :]
            if sizes.rows > sizes.channels:
                rows = jnp.concatenate([rows, jnp.zeros((sizes.rows - sizes.channels, 2 * sizes.half), F32)], 0)
            turned = swap_parts(rows, sizes)
            straight, crossed = [], []
            for w in range(sizes.channels):
                straight.append(jnp.sum(block[m, w] * rows, axis=0, keepdims=True))
                crossed.append(jnp.sum(block[m, w] * turned, axis=0, keepdims=True))
            straight = jnp.concatenate(straight, 0)
            crossed = jnp.concatenate(crossed, 0)
            real_part = straight + swap_parts(straight, sizes)
            imag_part = swap_parts(crossed, sizes) - crossed
            put_mixed(spread, at, m, jnp.where(real, real_part, imag_part), sizes)
    plane_cells(sizes, spread, table, out)


def grad_weights(
    sizes, spectra, back, given_spectra, given_back, target, here, straight, crossed, semaphores
):
    copies = []
    for which, (source, backward) in enumerate(((spectra, back), (given_spectra, given_back))):
        half = core_of() if which == 0 else 1 - core_of()
        values = source[...]
        turned = swap_parts(values, sizes)
        real = first_lanes(values.shape[0], sizes)
        straight[...] = jnp.where(real, values, turned)
        crossed[...] = jnp.where(real, turned, -values)
        for mode in range(sizes.share):
            rows = backward[mode_rows(mode, sizes), :]
            if sizes.rows > sizes.channels:
                rows = jnp.concatenate([rows, jnp.zeros((sizes.rows - sizes.channels, 2 * sizes.half), F32)], 0)
            turned = swap_parts(rows, sizes)
            local = 2 * (which * sizes.share + mode)
            for w in range(sizes.channels):
                at = slice(w * sizes.modes + mode, w * sizes.modes + mode + 1)
                block = (straight[at, :] * rows + crossed[at, :] * turned).T
                for s in range(2):
                    part = block[s * sizes.half : s * sizes.half + sizes.kept, : sizes.channels]
                    here[local + s, w] = part.reshape(sizes.local_x, sizes.kept_y, sizes.channels)
            for s in range(2):
                to = 2 * (half * sizes.share + mode) + s
                copies.append(pltpu.make_async_copy(here.at[local + s], target.at[to], semaphores.at[local + s]))
                copies[-1].start()
    for copy in copies:
        copy.wait()


def gelu_parts(pre):
    slope = math.sqrt(2.0 / math.pi)
    squared = pre * pre
    bend = jnp.tanh(slope * (pre + 0.044715 * (squared * pre)))
    value = 0.5 * pre * (1.0 + bend)
    derivative = 0.5 * (1.0 + bend) + 0.5 * pre * (1.0 - bend * bend) * (slope * (1.0 + 3.0 * 0.044715 * squared))
    return value, derivative


def activate(
    sizes, received, local, cotangent, inverse, forward, pre_out, signal_out, out, spectrum, tall
):
    pre = fine_dot(receive_modes(received, spectrum, tall, sizes), inverse[...]) + local[...]
    pre_out[...] = pre
    signal = (cotangent[...] * gelu_parts(pre)[1]).astype(BF16)
    signal_out[...] = signal
    send_modes(dot(signal, forward[...]), out, sizes)


def finish(sizes, received, local, inverse, grad_field, spectrum, tall):
    spatial = fine_dot(receive_modes(received, spectrum, tall, sizes), inverse[...])
    scatter_cells(spatial + local[...], grad_field, sizes)


def shape_of(shape, dtype=F32):
    return jax.ShapeDtypeStruct(shape, dtype)


VMEM = pl.BlockSpec(memory_space=pltpu.VMEM)
HELD = pl.BlockSpec(memory_space=pltpu.VMEM)
HBM = pl.BlockSpec(memory_space=pltpu.HBM)
ANYWHERE = pl.BlockSpec(memory_space=pl.ANY)


def settings(mebibytes):
    return pltpu.CompilerParams(vmem_limit_bytes=mebibytes * 1024 * 1024)


def cost(nanoseconds):
    return pl.CostEstimate(flops=0, bytes_accessed=3000 * nanoseconds, transcendentals=0)


def whole_call(body, sizes, nanoseconds, out_shape, scratch, *args, specs=None, out_specs=None, room=16):
    def kernel(*refs):
        body(sizes, *refs)

    if specs:
        spaces = [pltpu.HBM if spec is HBM else pltpu.VMEM if spec is HELD else None for spec in specs]
        args = [
            pltpu.with_memory_space_constraint(arg, space) if space else arg for arg, space in zip(args, spaces)
        ]
    return pl.pallas_call(
        kernel,
        out_shape=out_shape,
        in_specs=specs or [VMEM] * len(args),
        out_specs=out_specs or jax.tree.map(lambda _: VMEM, out_shape),
        scratch_shapes=scratch,
        name=body.__name__,
        cost_estimate=cost(nanoseconds),
        compiler_params=settings(room),
    )(*args)


def on_device(field, cotangent, spectral_weight, pointwise_weight, channel_bias):
    z = Sizes(field, spectral_weight)
    depth_table = depth_time_table(z.depth)
    modes = depth_table.shape[2]
    kappa = np.where(np.arange(modes) % KT == 0, 1.0, 2.0).astype(np.float32)
    shares = (z.nx, 2, z.share)
    ordered = depth_table.reshape((z.depth, 2) + shares).transpose(0, 2, 3, 1, 4).reshape(z.depth, z.all_modes)
    doubled = np.repeat(kappa.reshape(z.nx, 2, 1, z.share), 2, axis=2).reshape(z.all_modes)
    forward_first = jnp.asarray(ordered.astype(ml_dtypes.bfloat16))
    forward_back = jnp.asarray((ordered.astype(ml_dtypes.bfloat16).astype(np.float32) * doubled).astype(ml_dtypes.bfloat16))
    inverse_back = jnp.asarray(np.ascontiguousarray(ordered.T))
    inverse_first = jnp.asarray(np.ascontiguousarray((ordered * doubled).T))
    pairs = [(s, s ^ 1) for s in range(z.ny)]

    def exchange(payload):
        return lax.all_to_all(payload, ("gx", "gy"), split_axis=0, concat_axis=0, tiled=True)

    def other_core(values):
        return lax.ppermute(values, "gy", pairs)

    payload = shape_of((z.devices, z.pair, z.width))
    cell_rows = z.channels * z.cells
    cells_shape = (cell_rows, z.depth)
    cells_scratch = pltpu.VMEM(cells_shape, F32)
    spectrum_scratch = pltpu.VMEM((cell_rows, z.all_modes), F32)
    spectra_shape = (z.channels * z.modes, 2 * z.half)
    spectra_scratch = pltpu.VMEM(spectra_shape, F32)
    flat_scratch = pltpu.VMEM((z.devices * z.cells, z.spread_rows), F32)
    spread_scratch = pltpu.VMEM((4, z.spread_rows, 2 * z.half), F32)
    tall_scratch = pltpu.VMEM((2 * z.nx, z.cells, z.spread_rows), F32)
    field_scratch = pltpu.VMEM(field.shape, BF16)
    weight_here = pltpu.VMEM(pointwise_weight.shape, BF16)
    native = jnp.transpose(spectral_weight, (0, 1, 2, 4, 5, 3))
    weight_shape = (2 * z.modes,) + native.shape[2:]
    half_scratch = pltpu.VMEM((z.modes,) + native.shape[2:], F32)
    turned_shape = shape_of((z.share, z.channels, z.rows, 2 * z.half))

    def flags(count):
        return pltpu.SemaphoreType.DMA((count,))

    weights = native.reshape(weight_shape)
    sent, turned_away = whole_call(
        depth_forward, z, 1500, (payload, turned_shape),
        [
            cells_scratch, field_scratch, pltpu.VMEM(forward_first.shape, BF16), pltpu.VMEM(payload.shape, F32),
            half_scratch, flags(3), flags(z.modes),
        ],
        field, forward_first, weights, specs=[HBM] * 3, out_specs=(HBM, VMEM),
    )
    received = exchange(sent)
    other_turned = other_core(turned_away)
    turned, plane, local, cot_cells = whole_call(
        prepare, z, 100,
        (turned_shape, shape_of((z.devices * z.cells, 8 * z.half)), pltpu.HBM(cells_shape, F32), pltpu.HBM(cells_shape, F32)),
        [
            half_scratch, cells_scratch, field_scratch, field_scratch, cells_scratch, weight_here,
            pltpu.VMEM(channel_bias.shape, F32), cells_scratch, flags(z.modes), flags(8),
        ],
        weights, turned_away, jnp.asarray(plane_tables(z)), field, cotangent, pointwise_weight, channel_bias,
        specs=[HBM, ANYWHERE] + [HBM] * 5, out_specs=(VMEM, VMEM, HBM, HBM),
    )
    other_turned = whole_call(
        fetch_weights, z, 100, turned_shape, [flags(1)], other_turned, turned, specs=[HBM, ANYWHERE]
    )
    received, other_turned, turned, plane, local, cot_cells = lax.optimization_barrier(
        (received, other_turned, turned, plane, local, cot_cells)
    )
    spectra, other_spectra, sent, local, cot_cells, inverse_here, forward_here = whole_call(
        mix_forward, z, 1000,
        (
            shape_of(spectra_shape), shape_of(spectra_shape), payload, shape_of(cells_shape), shape_of(cells_shape),
            shape_of(inverse_first.shape), shape_of(forward_back.shape, BF16),
        ),
        [spread_scratch, spectra_scratch, flat_scratch, flags(4)],
        received, plane, turned, other_turned, local, cot_cells, inverse_first, forward_back,
        specs=[HELD] + [VMEM] * 3 + [HBM] * 4,
    )
    pre, signal, sent = whole_call(
        activate, z, 2000,
        (shape_of(cells_shape), shape_of(cells_shape, BF16), payload), [spectrum_scratch, tall_scratch],
        exchange(sent), local, cot_cells, inverse_here, forward_here,
    )
    back, other_back, sent = whole_call(
        mix_back, z, 1000, (shape_of(spectra_shape), shape_of(spectra_shape), payload),
        [spread_scratch, flat_scratch], exchange(sent), plane, turned, other_turned,
    )
    sent, spectra, other_spectra, back, other_back, pre, signal = lax.optimization_barrier(
        (sent, spectra, other_spectra, back, other_back, pre, signal)
    )
    returned = exchange(sent)
    given_spectra, given_back = other_core(other_spectra), other_core(other_back)
    layer_out, local, inverse_here = whole_call(
        emit, z, 1500,
        (shape_of(field.shape, BF16), shape_of(cells_shape), shape_of(inverse_back.shape)),
        [weight_here, flags(2)],
        pre, signal, pointwise_weight, inverse_back, specs=[VMEM, VMEM, HBM, HBM],
    )
    gradient = whole_call(
        grad_weights, z, 5000, shape_of(weight_shape),
        [pltpu.VMEM(weight_shape, F32), spectra_scratch, spectra_scratch, flags(2 * z.modes)],
        spectra, back, given_spectra, given_back, out_specs=HBM, room=28,
    )
    returned, gradient, layer_out, local, inverse_here = lax.optimization_barrier(
        (returned, gradient, layer_out, local, inverse_here)
    )
    grad_field = whole_call(
        finish, z, 1000, shape_of(field.shape, BF16), [spectrum_scratch, tall_scratch], returned, local, inverse_here
    )
    return (layer_out, grad_field, jnp.transpose(gradient.reshape(native.shape), (0, 1, 2, 5, 3, 4)))


def solution(mesh):
    return jax.shard_map(
        on_device,
        mesh=mesh,
        in_specs=(
            P(None, "gx", "gy", None),
            P(None, "gx", "gy", None),
            P("gx", None, None, None, "gy", None),
            P(),
            P(),
        ),
        out_specs=(
            P(None, "gx", "gy", None),
            P(None, "gx", "gy", None),
            P("gx", None, None, None, "gy", None),
        ),
        check_vma=False,
    )
```

```python
import math

import jax
import jax.numpy as jnp
import ml_dtypes
import numpy as np
from jax import lax
from jax.experimental import pallas as pl
from jax.experimental.pallas import tpu as pltpu
from jax.sharding import PartitionSpec as P

KZ = 16
KT = 4
NT = 16
LANES = 128
F32 = jnp.float32
BF16 = jnp.bfloat16


def round_up(value, step):
    return -(-value // step) * step


def split_table(table):
    high = table.astype(ml_dtypes.bfloat16)
    low = (table - high.astype(np.float32)).astype(ml_dtypes.bfloat16)
    return jnp.asarray(high), jnp.asarray(low)


def frequencies(kept):
    index = np.arange(kept)
    return np.where(index < kept // 2, index, index - kept)


def depth_time_table(cells):
    depth_cells = cells // NT
    depth = np.arange(depth_cells)[:, None, None, None] * frequencies(KZ)[None, None, :, None] * NT
    time = np.arange(NT)[None, :, None, None] * np.arange(KT)[None, None, None, :] * depth_cells
    phase = np.mod(depth + time, cells).reshape(cells, KZ * KT)
    angles = phase.astype(np.float32) * np.float32(2.0 * math.pi / cells)
    factor = np.float32(1.0 / math.sqrt(cells))
    return np.stack([np.cos(angles) * factor, -np.sin(angles) * factor], axis=1).astype(np.float32)


def plane_tables(sizes):
    length_x, length_y = sizes.nx * sizes.cells_x, sizes.ny * sizes.cells_y
    phase_x = np.mod(np.arange(length_x)[:, None] * frequencies(sizes.kept_x), length_x) / length_x
    phase_y = np.mod(np.arange(length_y)[:, None] * frequencies(sizes.kept_y), length_y) / length_y
    angle = 2.0 * math.pi * (phase_x[:, None, :, None] + phase_y[None, :, None, :])
    scale = 1.0 / math.sqrt(length_x * length_y)
    cosine, sine = np.cos(angle) * scale, np.sin(angle) * scale
    parts = np.stack([np.stack([cosine, -sine]), np.stack([sine, cosine])])
    pairs = sizes.cells_y // sizes.pair
    parts = parts.reshape(
        2, 2, sizes.nx, sizes.cells_x, sizes.ny, pairs, sizes.pair, sizes.ny, sizes.kept
    ).transpose(7, 3, 5, 2, 4, 6, 0, 1, 8)
    padded = np.zeros(parts.shape[:-1] + (sizes.half,), np.float32)
    padded[..., : sizes.kept] = parts
    return padded.reshape(sizes.ny, sizes.devices * sizes.cells, 4 * sizes.half)


class Sizes:
    def __init__(self, field, weight):
        self.nx, self.ny = lax.axis_size("gx"), lax.axis_size("gy")
        self.channels, self.cells_x, self.cells_y, self.depth = field.shape
        self.modes = weight.shape[0]
        self.local_x, self.kept_y = weight.shape[4:]
        self.kept_x = self.local_x * self.ny
        self.cells = self.cells_x * self.cells_y
        self.devices = self.nx * self.ny
        self.share = self.modes // 2
        self.kept = self.local_x * self.kept_y
        self.half = round_up(self.kept, LANES // 2)
        self.all_modes = 2 * self.modes * self.nx
        self.groups = LANES // self.modes
        self.main = self.channels // self.groups * self.groups if self.all_modes == LANES else 0
        self.rest = self.channels - self.main
        self.main_lanes = self.main * self.modes
        self.rest_lanes = self.rest * self.modes
        self.rest_tiles = round_up(self.rest_lanes, LANES) // LANES
        self.pair = math.gcd(self.cells_y, 2)
        self.pieces = self.cells // self.pair
        self.rest_first = self.pieces * self.main_lanes
        self.rest_width = round_up(self.pieces * self.rest_lanes, LANES)
        self.width = self.rest_first + self.rest_width
        self.spread_rows = self.main_lanes + self.rest_width
        self.rows = round_up(self.channels, 8)


def gather_cells(source, scratch, sizes):
    for w in range(sizes.channels):
        for x in range(sizes.cells_x):
            first = (w * sizes.cells_x + x) * sizes.cells_y
            scratch[first : first + sizes.cells_y, :] = source[w, x].astype(F32)
    return scratch[...]


def scatter_cells(values, target, sizes):
    for w in range(sizes.channels):
        for x in range(sizes.cells_x):
            first = (w * sizes.cells_x + x) * sizes.cells_y
            target[w, x] = values[first : first + sizes.cells_y, :].astype(target.dtype)


def lane_group(sizes):
    return lax.broadcasted_iota(jnp.int32, (sizes.cells, LANES), 1) // sizes.modes


def turn_groups(tiles, group, sizes):
    tiles = list(tiles)
    step = 1
    while step < sizes.groups:
        low = group // step % 2 == 0
        for first in range(sizes.groups):
            if first // step % 2 == 0:
                one, two = tiles[first], tiles[first + step]
                tiles[first] = jnp.where(low, one, pltpu.roll(two, step * sizes.modes, 1))
                tiles[first + step] = jnp.where(low, pltpu.roll(one, LANES - step * sizes.modes, 1), two)
        step *= 2
    return tiles


def put_group(target, source, have, want, group, sizes):
    if have != want:
        source = pltpu.roll(source, (want - have) % sizes.groups * sizes.modes, 1)
    return jnp.where(group == want, source, target)


def send_modes(values, target, sizes):
    group = lane_group(sizes)
    tiles = [values[w * sizes.cells : (w + 1) * sizes.cells, :] for w in range(sizes.channels)]
    turned = []
    for first in range(0, sizes.main, sizes.groups):
        turned.append(turn_groups(tiles[first : first + sizes.groups], group, sizes))
    for at in range(2 * sizes.nx):
        main = [block[at] for block in turned]
        last = [jnp.zeros((sizes.cells, LANES), F32) for _ in range(sizes.rest_width // LANES)]
        for r in range(sizes.rest):
            tile, want = divmod(r, sizes.groups)
            last[tile] = put_group(last[tile], tiles[sizes.main + r], at, want, group, sizes)
        if last:
            last = side_by_side(jnp.concatenate(last, 1), sizes.pair, sizes)
        for y in range(sizes.ny // 2):
            device = at // 2 * sizes.ny + 2 * y + at % 2
            for piece in range(sizes.pieces):
                rows = slice(piece * sizes.pair, (piece + 1) * sizes.pair)
                for k, value in enumerate(main):
                    first = piece * sizes.main_lanes + k * LANES
                    target[device, :, first : first + LANES] = value[rows]
            if sizes.rest:
                target[device, :, sizes.rest_first :] = last


def side_by_side(values, rows, sizes):
    total = values[:rows]
    for piece in range(1, sizes.pieces):
        moved = pltpu.roll(values, piece * sizes.rest_lanes, 1)
        total = total + moved[piece * rows : (piece + 1) * rows]
    return total


def receive_modes(source, scratch, tall, sizes):
    group = lane_group(sizes)
    parts = source[...].reshape(sizes.nx, sizes.ny // 2, 2, sizes.pair, sizes.width)
    values = parts[:, 0]
    for y in range(1, sizes.ny // 2):
        values = values + parts[:, y]
    values = values.reshape(2 * sizes.nx, sizes.pair, sizes.width)
    for piece in range(sizes.pieces):
        rows = slice(piece * sizes.pair, (piece + 1) * sizes.pair)
        if sizes.main:
            first = piece * sizes.main_lanes
            tall[:, rows, : sizes.main_lanes] = values[:, :, first : first + sizes.main_lanes]
        if sizes.rest:
            last = values[:, :, sizes.rest_first :]
            if piece:
                last = pltpu.roll(last, sizes.rest_width - piece * sizes.rest_lanes, 2)
            tall[:, rows, sizes.main_lanes :] = last
    out = []
    for first in range(0, sizes.main_lanes, LANES):
        tiles = [tall[at, :, first : first + LANES] for at in range(2 * sizes.nx)]
        out += turn_groups(tiles, group, sizes)
    for r in range(sizes.rest):
        value = jnp.zeros((sizes.cells, LANES), F32)
        tile, have = divmod(r, sizes.groups)
        first = sizes.main_lanes + tile * LANES
        for at in range(2 * sizes.nx):
            value = put_group(value, tall[at, :, first : first + LANES], have, at, group, sizes)
        out.append(value)
    for w, value in enumerate(out):
        scratch[w * sizes.cells : (w + 1) * sizes.cells, :] = value
    return scratch[...]


def dot(left, right, contract=((1,), (0,))):
    return lax.dot_general(left, right, (contract, ((), ())), preferred_element_type=F32)


def halves(values):
    if isinstance(values, tuple):
        return values
    high = values.astype(BF16)
    return high, (values - high.astype(F32)).astype(BF16)


def fine_dot(left, right, contract=((1,), (0,))):
    left_high, left_low = halves(left)
    right_high, right_low = halves(right)
    small = dot(left_high, right_low, contract) + dot(left_low, right_high, contract)
    return dot(left_high, right_high, contract) + small


def fetch(sources, targets, semaphores):
    copies = [pltpu.make_async_copy(*pair, semaphores.at[at]) for at, pair in enumerate(zip(sources, targets))]
    for copy in copies:
        copy.start()
    for copy in copies:
        copy.wait()


def depth_forward(
    sizes, field, table, source, out, target,
    cells, field_here, table_here, out_here, here, semaphores, weight_semaphores,
):
    few = [
        pltpu.make_async_copy(field, field_here, semaphores.at[0]),
        pltpu.make_async_copy(table, table_here, semaphores.at[1]),
    ]
    for copy in few:
        copy.start()
    copies = start_weights(sizes, source, 1 - core_of(), here, weight_semaphores, 0, sizes.share)
    clear_weights(sizes, target)
    for copy in few:
        copy.wait()
    copies += start_weights(sizes, source, 1 - core_of(), here, weight_semaphores, sizes.share)
    values = gather_cells(field_here, cells, sizes).astype(BF16)
    send_modes(dot(values, table_here[...]), out_here, sizes)
    copy = pltpu.make_async_copy(out_here, out, semaphores.at[2])
    copy.start()
    turn_weights(sizes, copies, here, target)
    copy.wait()


def one_hot(rows, columns, step, along_rows):
    row = lax.broadcasted_iota(jnp.int32, (rows, columns), 0)
    column = lax.broadcasted_iota(jnp.int32, (rows, columns), 1)
    same = row // step == column if along_rows else row == column // step
    return jnp.where(same, 1.0, 0.0).astype(BF16)


def cell_mixer(weights, across, sizes):
    count = sizes.channels * sizes.cells
    left = one_hot(count, sizes.channels, sizes.cells, True)
    right = one_hot(sizes.channels, count, sizes.cells, False)
    tall = dot(left, weights, ((1,), (1 if across else 0,)))
    wide = dot(tall.astype(BF16), right)
    row = lax.broadcasted_iota(jnp.int32, (count, count), 0)
    column = lax.broadcasted_iota(jnp.int32, (count, count), 1)
    same = lax.rem(row, sizes.cells) == lax.rem(column, sizes.cells)
    return jnp.where(same, wide, 0.0).astype(BF16)


def emit(
    sizes, pre, signal, weight, inverse_high, inverse_low, layer_out, local, high_out, low_out, weight_here, semaphores
):
    copies = [
        pltpu.make_async_copy(weight, weight_here, semaphores.at[0]),
        pltpu.make_async_copy(inverse_high, high_out, semaphores.at[1]),
        pltpu.make_async_copy(inverse_low, low_out, semaphores.at[2]),
    ]
    for copy in copies:
        copy.start()
    scatter_cells(gelu_parts(pre[...])[0], layer_out, sizes)
    copies[0].wait()
    local[...] = dot(cell_mixer(weight_here[...], False, sizes), signal[...])
    copies[1].wait()
    copies[2].wait()


def core_of():
    return lax.rem(lax.axis_index("gy"), 2)


def start_weights(sizes, source, half, here, semaphores, first=0, end=None):
    copies = []
    for at in range(2 * sizes.share)[first:end]:
        copies.append(pltpu.make_async_copy(source.at[2 * sizes.share * half + at], here.at[at], semaphores.at[at]))
        copies[-1].start()
    return copies


def clear_weights(sizes, target):
    if sizes.half > sizes.kept:
        target[...] = jnp.zeros_like(target)
    elif sizes.rows > sizes.channels:
        target[:, :, sizes.channels :, :] = jnp.zeros(
            (sizes.share, sizes.channels, sizes.rows - sizes.channels, 2 * sizes.half), F32
        )


def turn_weights(sizes, copies, here, target):
    for mode in range(sizes.share):
        for s in range(2):
            copies[2 * mode + s].wait()
        for w in range(sizes.channels):
            blocks = [here[2 * mode + s, w].reshape(sizes.kept, sizes.channels) for s in range(2)]
            if sizes.half == sizes.kept:
                target[mode, w, : sizes.channels, :] = jnp.concatenate(blocks, 0).T
            else:
                for s, block in enumerate(blocks):
                    target[mode, w, : sizes.channels, s * sizes.half : s * sizes.half + sizes.kept] = block.T


def prepare(
    sizes, source, after, tables, field, cotangent, weight, bias,
    target, table_high, table_low, local, cotangent_out,
    here, cells, field_here, cot_here, cot_cells, weight_here, bias_here, local_here, table, semaphores, small,
):
    del after
    place = lax.axis_index("gy")
    lanes = 2 * sizes.half
    moves = [(field, field_here), (cotangent, cot_here), (weight, weight_here), (bias, bias_here)]
    for s in range(2):
        for at, owner in enumerate((place, place + 1 - 2 * core_of())):
            moves.append(
                (tables.at[owner, :, pl.ds(s * lanes, lanes)], table.at[:, pl.ds((2 * s + at) * lanes, lanes)])
            )
    few = [pltpu.make_async_copy(*move, small.at[at]) for at, move in enumerate(moves)]
    for copy in few[:4]:
        copy.start()
    copies = start_weights(sizes, source, core_of(), here, semaphores)
    for copy in few[4:]:
        copy.start()
    clear_weights(sizes, target)
    for copy in few[:4]:
        copy.wait()
    values = gather_cells(field_here, cells, sizes).astype(BF16)
    spread = one_hot(sizes.channels * sizes.cells, sizes.channels, sizes.cells, True).astype(F32)
    offset = jnp.sum(spread * bias_here[...].reshape(1, sizes.channels), axis=1, keepdims=True)
    local_here[...] = dot(cell_mixer(weight_here[...], True, sizes), values) + offset
    gather_cells(cot_here, cot_cells, sizes)
    results = [
        pltpu.make_async_copy(local_here, local, small.at[0]),
        pltpu.make_async_copy(cot_cells, cotangent_out, small.at[1]),
    ]
    for copy in results:
        copy.start()
    turn_weights(sizes, copies, here, target)
    for copy in few[4:] + results:
        copy.wait()
    table_high[...], table_low[...] = halves(table[...])


def fetch_weights(sizes, source, after, target, semaphore):
    del after
    copy = pltpu.make_async_copy(source, target, semaphore.at[0])
    copy.start()
    copy.wait()


def plane_spectra(sizes, received, table, targets, flat):
    count = sizes.devices * sizes.pair
    for at in range(sizes.devices):
        for piece in range(sizes.pieces):
            rows = slice(piece * count + at * sizes.pair, piece * count + (at + 1) * sizes.pair)
            if sizes.main:
                first = piece * sizes.main_lanes
                flat[rows, : sizes.main_lanes] = received[at, :, first : first + sizes.main_lanes]
            if sizes.rest:
                flat[rows, sizes.main_lanes :] = received[at, :, sizes.rest_first :]
    if sizes.rest:
        for piece in range(1, sizes.pieces):
            rows = slice(piece * count, (piece + 1) * count)
            shift = sizes.rest_width - piece * sizes.rest_lanes
            flat[rows, sizes.main_lanes :] = pltpu.roll(flat[rows, sizes.main_lanes :], shift, 1)
    rows, lanes = targets[0].shape
    both = fine_dot(flat[...].T[:rows], table)
    total = both[:, : 2 * lanes] + pltpu.roll(both[:, 2 * lanes :], rows - sizes.share, 0)
    for at, target in enumerate(targets):
        target[...] = total[:, at * lanes : (at + 1) * lanes]


def plane_cells(sizes, spread, table, out):
    modes = jnp.concatenate([spread[at] for at in range(4)], 1)
    cells = fine_dot(table, modes, ((1,), (1,)))
    count = sizes.devices * sizes.pair
    if sizes.rest:
        last = side_by_side(cells[:, sizes.main_lanes :], count, sizes)
    for at in range(sizes.devices):
        rows = slice(at * sizes.pair, (at + 1) * sizes.pair)
        for piece in range(sizes.pieces):
            if sizes.main:
                first = piece * sizes.main_lanes
                out[at, :, first : first + sizes.main_lanes] = cells[
                    piece * count + at * sizes.pair : piece * count + (at + 1) * sizes.pair, : sizes.main_lanes
                ]
        if sizes.rest:
            out[at, :, sizes.rest_first :] = last[rows]


def swap_parts(values, sizes):
    return pltpu.roll(values, sizes.half, 1)


def mode_rows(first, sizes):
    return pl.ds(first, sizes.channels, stride=sizes.modes)


def put_mixed(spread, at, mode, values, sizes):
    for s in range(2):
        spread[2 * s + at, mode_rows(s * sizes.share + mode, sizes), :] = values


def first_lanes(rows, sizes):
    return lax.broadcasted_iota(jnp.int32, (rows, 2 * sizes.half), 1) < sizes.half


def mix_forward(
    sizes, received, table_high, table_low, weight, other_weight, local, cotangent, inverse_high, inverse_low, forward,
    spectra, other_spectra, out, local_out, cotangent_out, high_out, low_out, forward_out,
    spread, swapped, flat, semaphores,
):
    table = (table_high[...], table_low[...])
    moves = (
        (local, local_out), (cotangent, cotangent_out), (inverse_high, high_out), (inverse_low, low_out),
        (forward, forward_out),
    )
    copies = [pltpu.make_async_copy(*move, semaphores.at[at]) for at, move in enumerate(moves)]
    for copy in copies:
        copy.start()
    plane_spectra(sizes, received, table, (spectra, other_spectra), flat)
    spread[...] = jnp.zeros_like(spread)
    real = first_lanes(sizes.rows, sizes)
    for at, (rows, block) in enumerate(((spectra, weight), (other_spectra, other_weight))):
        swapped[...] = swap_parts(rows[...], sizes)
        for m in range(sizes.share):
            straight = jnp.zeros((sizes.rows, 2 * sizes.half), F32)
            crossed = jnp.zeros((sizes.rows, 2 * sizes.half), F32)
            for w in range(sizes.channels):
                row = slice(w * sizes.modes + m, w * sizes.modes + m + 1)
                straight = straight + rows[row, :] * block[m, w]
                crossed = crossed + swapped[row, :] * block[m, w]
            real_part = straight - swap_parts(straight, sizes)
            imag_part = crossed + swap_parts(crossed, sizes)
            put_mixed(spread, at, m, jnp.where(real, real_part, imag_part)[: sizes.channels], sizes)
    plane_cells(sizes, spread, table, out)
    for copy in copies:
        copy.wait()


def mix_back(sizes, received, table_high, table_low, weight, other_weight, back, other_back, out, spread, flat):
    table = (table_high[...], table_low[...])
    plane_spectra(sizes, received, table, (back, other_back), flat)
    spread[...] = jnp.zeros_like(spread)
    real = first_lanes(sizes.channels, sizes)
    for at, (source, block) in enumerate(((back, weight), (other_back, other_weight))):
        for m in range(sizes.share):
            rows = source[mode_rows(m, sizes), :]
            if sizes.rows > sizes.channels:
                rows = jnp.concatenate([rows, jnp.zeros((sizes.rows - sizes.channels, 2 * sizes.half), F32)], 0)
            turned = swap_parts(rows, sizes)
            straight, crossed = [], []
            for w in range(sizes.channels):
                straight.append(jnp.sum(block[m, w] * rows, axis=0, keepdims=True))
                crossed.append(jnp.sum(block[m, w] * turned, axis=0, keepdims=True))
            straight = jnp.concatenate(straight, 0)
            crossed = jnp.concatenate(crossed, 0)
            real_part = straight + swap_parts(straight, sizes)
            imag_part = swap_parts(crossed, sizes) - crossed
            put_mixed(spread, at, m, jnp.where(real, real_part, imag_part), sizes)
    plane_cells(sizes, spread, table, out)


def grad_weights(
    sizes, spectra, back, given_spectra, given_back, target, here, straight, crossed, semaphores
):
    copies = []
    for which, (source, backward) in enumerate(((spectra, back), (given_spectra, given_back))):
        half = core_of() if which == 0 else 1 - core_of()
        values = source[...]
        turned = swap_parts(values, sizes)
        real = first_lanes(values.shape[0], sizes)
        straight[...] = jnp.where(real, values, turned)
        crossed[...] = jnp.where(real, turned, -values)
        for mode in range(sizes.share):
            rows = backward[mode_rows(mode, sizes), :]
            if sizes.rows > sizes.channels:
                rows = jnp.concatenate([rows, jnp.zeros((sizes.rows - sizes.channels, 2 * sizes.half), F32)], 0)
            turned = swap_parts(rows, sizes)
            local = 2 * (which * sizes.share + mode)
            for w in range(sizes.channels):
                at = slice(w * sizes.modes + mode, w * sizes.modes + mode + 1)
                block = (straight[at, :] * rows + crossed[at, :] * turned).T
                for s in range(2):
                    part = block[s * sizes.half : s * sizes.half + sizes.kept, : sizes.channels]
                    here[local + s, w] = part.reshape(sizes.local_x, sizes.kept_y, sizes.channels)
            for s in range(2):
                to = 2 * (half * sizes.share + mode) + s
                copies.append(pltpu.make_async_copy(here.at[local + s], target.at[to], semaphores.at[local + s]))
                copies[-1].start()
    for copy in copies:
        copy.wait()


def gelu_parts(pre):
    slope = math.sqrt(2.0 / math.pi)
    squared = pre * pre
    bend = jnp.tanh(slope * (pre + 0.044715 * (squared * pre)))
    value = 0.5 * pre * (1.0 + bend)
    derivative = 0.5 * (1.0 + bend) + 0.5 * pre * (1.0 - bend * bend) * (slope * (1.0 + 3.0 * 0.044715 * squared))
    return value, derivative


def activate(
    sizes, received, local, cotangent, inverse_high, inverse_low, forward, pre_out, signal_out, out, spectrum, tall
):
    inverse = (inverse_high[...], inverse_low[...])
    pre = fine_dot(receive_modes(received, spectrum, tall, sizes), inverse) + local[...]
    pre_out[...] = pre
    signal = (cotangent[...] * gelu_parts(pre)[1]).astype(BF16)
    signal_out[...] = signal
    send_modes(dot(signal, forward[...]), out, sizes)


def finish(sizes, received, local, inverse_high, inverse_low, grad_field, spectrum, tall):
    spatial = fine_dot(receive_modes(received, spectrum, tall, sizes), (inverse_high[...], inverse_low[...]))
    scatter_cells(spatial + local[...], grad_field, sizes)


def shape_of(shape, dtype=F32):
    return jax.ShapeDtypeStruct(shape, dtype)


VMEM = pl.BlockSpec(memory_space=pltpu.VMEM)
HELD = pl.BlockSpec(memory_space=pltpu.VMEM)
HBM = pl.BlockSpec(memory_space=pltpu.HBM)
ANYWHERE = pl.BlockSpec(memory_space=pl.ANY)


def settings(mebibytes):
    return pltpu.CompilerParams(vmem_limit_bytes=mebibytes * 1024 * 1024)


def cost(nanoseconds):
    return pl.CostEstimate(flops=0, bytes_accessed=3000 * nanoseconds, transcendentals=0)


def whole_call(body, sizes, nanoseconds, out_shape, scratch, *args, specs=None, out_specs=None, room=16):
    def kernel(*refs):
        body(sizes, *refs)

    if specs:
        spaces = [pltpu.HBM if spec is HBM else pltpu.VMEM if spec is HELD else None for spec in specs]
        args = [
            pltpu.with_memory_space_constraint(arg, space) if space else arg for arg, space in zip(args, spaces)
        ]
    return pl.pallas_call(
        kernel,
        out_shape=out_shape,
        in_specs=specs or [VMEM] * len(args),
        out_specs=out_specs or jax.tree.map(lambda _: VMEM, out_shape),
        scratch_shapes=scratch,
        name=body.__name__,
        cost_estimate=cost(nanoseconds),
        compiler_params=settings(room),
    )(*args)


def on_device(field, cotangent, spectral_weight, pointwise_weight, channel_bias):
    z = Sizes(field, spectral_weight)
    depth_table = depth_time_table(z.depth)
    modes = depth_table.shape[2]
    kappa = np.where(np.arange(modes) % KT == 0, 1.0, 2.0).astype(np.float32)
    shares = (z.nx, 2, z.share)
    ordered = depth_table.reshape((z.depth, 2) + shares).transpose(0, 2, 3, 1, 4).reshape(z.depth, z.all_modes)
    doubled = np.repeat(kappa.reshape(z.nx, 2, 1, z.share), 2, axis=2).reshape(z.all_modes)
    forward_first = jnp.asarray(ordered.astype(ml_dtypes.bfloat16))
    forward_back = jnp.asarray((ordered.astype(ml_dtypes.bfloat16).astype(np.float32) * doubled).astype(ml_dtypes.bfloat16))
    inverse_back = split_table(np.ascontiguousarray(ordered.T))
    inverse_first = split_table(np.ascontiguousarray((ordered * doubled).T))
    inverse_shape = shape_of(inverse_first[0].shape, BF16)
    pairs = [(s, s ^ 1) for s in range(z.ny)]

    def exchange(payload):
        return lax.all_to_all(payload, ("gx", "gy"), split_axis=0, concat_axis=0, tiled=True)

    def other_core(values):
        return lax.ppermute(values, "gy", pairs)

    payload = shape_of((z.devices, z.pair, z.width))
    cell_rows = z.channels * z.cells
    cells_shape = (cell_rows, z.depth)
    cells_scratch = pltpu.VMEM(cells_shape, F32)
    spectrum_scratch = pltpu.VMEM((cell_rows, z.all_modes), F32)
    spectra_shape = (z.channels * z.modes, 2 * z.half)
    spectra_scratch = pltpu.VMEM(spectra_shape, F32)
    flat_scratch = pltpu.VMEM((z.devices * z.cells, z.spread_rows), F32)
    spread_scratch = pltpu.VMEM((4, z.spread_rows, 2 * z.half), F32)
    tall_scratch = pltpu.VMEM((2 * z.nx, z.cells, z.spread_rows), F32)
    field_scratch = pltpu.VMEM(field.shape, BF16)
    weight_here = pltpu.VMEM(pointwise_weight.shape, BF16)
    native = jnp.transpose(spectral_weight, (0, 1, 2, 4, 5, 3))
    weight_shape = (2 * z.modes,) + native.shape[2:]
    half_scratch = pltpu.VMEM((z.modes,) + native.shape[2:], F32)
    turned_shape = shape_of((z.share, z.channels, z.rows, 2 * z.half))

    def flags(count):
        return pltpu.SemaphoreType.DMA((count,))

    weights = native.reshape(weight_shape)
    sent, turned_away = whole_call(
        depth_forward, z, 1500, (payload, turned_shape),
        [
            cells_scratch, field_scratch, pltpu.VMEM(forward_first.shape, BF16), pltpu.VMEM(payload.shape, F32),
            half_scratch, flags(3), flags(z.modes),
        ],
        field, forward_first, weights, specs=[HBM] * 3, out_specs=(HBM, VMEM),
    )
    received = exchange(sent)
    other_turned = other_core(turned_away)
    table_shape = shape_of((z.devices * z.cells, 8 * z.half), BF16)
    turned, plane_high, plane_low, local, cot_cells = whole_call(
        prepare, z, 100,
        (turned_shape, table_shape, table_shape, pltpu.HBM(cells_shape, F32), pltpu.HBM(cells_shape, F32)),
        [
            half_scratch, cells_scratch, field_scratch, field_scratch, cells_scratch, weight_here,
            pltpu.VMEM(channel_bias.shape, F32), cells_scratch, pltpu.VMEM(table_shape.shape, F32), flags(z.modes), flags(8),
        ],
        weights, turned_away, jnp.asarray(plane_tables(z)), field, cotangent, pointwise_weight, channel_bias,
        specs=[HBM, ANYWHERE] + [HBM] * 5, out_specs=(VMEM, VMEM, VMEM, HBM, HBM),
    )
    other_turned = whole_call(
        fetch_weights, z, 100, turned_shape, [flags(1)], other_turned, turned, specs=[HBM, ANYWHERE]
    )
    received, other_turned, turned, plane_high, plane_low, local, cot_cells = lax.optimization_barrier(
        (received, other_turned, turned, plane_high, plane_low, local, cot_cells)
    )
    spectra, other_spectra, sent, local, cot_cells, high_here, low_here, forward_here = whole_call(
        mix_forward, z, 1000,
        (
            shape_of(spectra_shape), shape_of(spectra_shape), payload, shape_of(cells_shape), shape_of(cells_shape),
            inverse_shape, inverse_shape, shape_of(forward_back.shape, BF16),
        ),
        [spread_scratch, spectra_scratch, flat_scratch, flags(5)],
        received, plane_high, plane_low, turned, other_turned, local, cot_cells, *inverse_first, forward_back,
        specs=[HELD] + [VMEM] * 4 + [HBM] * 5,
    )
    pre, signal, sent = whole_call(
        activate, z, 2000,
        (shape_of(cells_shape), shape_of(cells_shape, BF16), payload), [spectrum_scratch, tall_scratch],
        exchange(sent), local, cot_cells, high_here, low_here, forward_here,
    )
    back, other_back, sent = whole_call(
        mix_back, z, 1000, (shape_of(spectra_shape), shape_of(spectra_shape), payload),
        [spread_scratch, flat_scratch], exchange(sent), plane_high, plane_low, turned, other_turned,
    )
    sent, spectra, other_spectra, back, other_back, pre, signal = lax.optimization_barrier(
        (sent, spectra, other_spectra, back, other_back, pre, signal)
    )
    returned = exchange(sent)
    given_spectra, given_back = other_core(other_spectra), other_core(other_back)
    layer_out, local, high_here, low_here = whole_call(
        emit, z, 1500,
        (shape_of(field.shape, BF16), shape_of(cells_shape), inverse_shape, inverse_shape),
        [weight_here, flags(3)],
        pre, signal, pointwise_weight, *inverse_back, specs=[VMEM, VMEM, HBM, HBM, HBM],
    )
    gradient = whole_call(
        grad_weights, z, 5000, shape_of(weight_shape),
        [pltpu.VMEM(weight_shape, F32), spectra_scratch, spectra_scratch, flags(2 * z.modes)],
        spectra, back, given_spectra, given_back, out_specs=HBM, room=28,
    )
    returned, gradient, layer_out, local, high_here, low_here = lax.optimization_barrier(
        (returned, gradient, layer_out, local, high_here, low_here)
    )
    grad_field = whole_call(
        finish, z, 1000, shape_of(field.shape, BF16), [spectrum_scratch, tall_scratch], returned, local, high_here, low_here
    )
    return (layer_out, grad_field, jnp.transpose(gradient.reshape(native.shape), (0, 1, 2, 5, 3, 4)))


def solution(mesh):
    return jax.shard_map(
        on_device,
        mesh=mesh,
        in_specs=(
            P(None, "gx", "gy", None),
            P(None, "gx", "gy", None),
            P("gx", None, None, None, "gy", None),
            P(),
            P(),
        ),
        out_specs=(
            P(None, "gx", "gy", None),
            P(None, "gx", "gy", None),
            P("gx", None, None, None, "gy", None),
        ),
        check_vma=False,
    )
```

```python
import math

import jax
import jax.numpy as jnp
import ml_dtypes
import numpy as np
from jax import lax
from jax.experimental import pallas as pl
from jax.experimental.pallas import tpu as pltpu
from jax.sharding import PartitionSpec as P

KZ = 16
KT = 4
NT = 16
LANES = 128
F32 = jnp.float32
BF16 = jnp.bfloat16


def round_up(value, step):
    return -(-value // step) * step


def frequencies(kept):
    index = np.arange(kept)
    return np.where(index < kept // 2, index, index - kept)


def depth_time_table(cells):
    depth_cells = cells // NT
    depth = np.arange(depth_cells)[:, None, None, None] * frequencies(KZ)[None, None, :, None] * NT
    time = np.arange(NT)[None, :, None, None] * np.arange(KT)[None, None, None, :] * depth_cells
    phase = np.mod(depth + time, cells).reshape(cells, KZ * KT)
    angles = phase.astype(np.float32) * np.float32(2.0 * math.pi / cells)
    factor = np.float32(1.0 / math.sqrt(cells))
    return np.stack([np.cos(angles) * factor, -np.sin(angles) * factor], axis=1).astype(np.float32)


def plane_tables(sizes):
    length_x, length_y = sizes.nx * sizes.cells_x, sizes.ny * sizes.cells_y
    phase_x = np.mod(np.arange(length_x)[:, None] * frequencies(sizes.kept_x), length_x) / length_x
    phase_y = np.mod(np.arange(length_y)[:, None] * frequencies(sizes.kept_y), length_y) / length_y
    angle = 2.0 * math.pi * (phase_x[:, None, :, None] + phase_y[None, :, None, :])
    scale = 1.0 / math.sqrt(length_x * length_y)
    cosine, sine = np.cos(angle) * scale, np.sin(angle) * scale
    parts = np.stack([np.stack([cosine, -sine]), np.stack([sine, cosine])])
    pairs = sizes.cells_y // sizes.pair
    parts = parts.reshape(
        2, 2, sizes.nx, sizes.cells_x, sizes.ny, pairs, sizes.pair, sizes.ny, sizes.kept
    ).transpose(7, 3, 5, 2, 4, 6, 0, 1, 8)
    padded = np.zeros(parts.shape[:-1] + (sizes.half,), np.float32)
    padded[..., : sizes.kept] = parts
    return padded.reshape(sizes.ny, sizes.devices * sizes.cells, 4 * sizes.half)


class Sizes:
    def __init__(self, field, weight):
        self.nx, self.ny = lax.axis_size("gx"), lax.axis_size("gy")
        self.channels, self.cells_x, self.cells_y, self.depth = field.shape
        self.modes = weight.shape[0]
        self.local_x, self.kept_y = weight.shape[4:]
        self.kept_x = self.local_x * self.ny
        self.cells = self.cells_x * self.cells_y
        self.devices = self.nx * self.ny
        self.share = self.modes // 2
        self.kept = self.local_x * self.kept_y
        self.half = round_up(self.kept, LANES // 2)
        self.all_modes = 2 * self.modes * self.nx
        self.groups = LANES // self.modes
        self.main = self.channels // self.groups * self.groups if self.all_modes == LANES else 0
        self.rest = self.channels - self.main
        self.main_lanes = self.main * self.modes
        self.rest_lanes = self.rest * self.modes
        self.rest_tiles = round_up(self.rest_lanes, LANES) // LANES
        self.pair = math.gcd(self.cells_y, 2)
        self.pieces = self.cells // self.pair
        self.rest_first = self.pieces * self.main_lanes
        self.rest_width = round_up(self.pieces * self.rest_lanes, LANES)
        self.width = self.rest_first + self.rest_width
        self.spread_rows = self.main_lanes + self.rest_width
        self.rows = round_up(self.channels, 8)


def gather_cells(source, scratch, sizes):
    for w in range(sizes.channels):
        for x in range(sizes.cells_x):
            first = (w * sizes.cells_x + x) * sizes.cells_y
            scratch[first : first + sizes.cells_y, :] = source[w, x].astype(F32)
    return scratch[...]


def scatter_cells(values, target, sizes):
    for w in range(sizes.channels):
        for x in range(sizes.cells_x):
            first = (w * sizes.cells_x + x) * sizes.cells_y
            target[w, x] = values[first : first + sizes.cells_y, :].astype(target.dtype)


def lane_group(sizes):
    return lax.broadcasted_iota(jnp.int32, (sizes.cells, LANES), 1) // sizes.modes


def turn_groups(tiles, group, sizes):
    tiles = list(tiles)
    step = 1
    while step < sizes.groups:
        low = group // step % 2 == 0
        for first in range(sizes.groups):
            if first // step % 2 == 0:
                one, two = tiles[first], tiles[first + step]
                tiles[first] = jnp.where(low, one, pltpu.roll(two, step * sizes.modes, 1))
                tiles[first + step] = jnp.where(low, pltpu.roll(one, LANES - step * sizes.modes, 1), two)
        step *= 2
    return tiles


def put_group(target, source, have, want, group, sizes):
    if have != want:
        source = pltpu.roll(source, (want - have) % sizes.groups * sizes.modes, 1)
    return jnp.where(group == want, source, target)


def send_modes(values, target, sizes):
    group = lane_group(sizes)
    tiles = [values[w * sizes.cells : (w + 1) * sizes.cells, :] for w in range(sizes.channels)]
    turned = []
    for first in range(0, sizes.main, sizes.groups):
        turned.append(turn_groups(tiles[first : first + sizes.groups], group, sizes))
    for at in range(2 * sizes.nx):
        main = [block[at] for block in turned]
        last = [jnp.zeros((sizes.cells, LANES), F32) for _ in range(sizes.rest_width // LANES)]
        for r in range(sizes.rest):
            tile, want = divmod(r, sizes.groups)
            last[tile] = put_group(last[tile], tiles[sizes.main + r], at, want, group, sizes)
        if last:
            last = side_by_side(jnp.concatenate(last, 1), sizes.pair, sizes)
        for y in range(sizes.ny // 2):
            device = at // 2 * sizes.ny + 2 * y + at % 2
            for piece in range(sizes.pieces):
                rows = slice(piece * sizes.pair, (piece + 1) * sizes.pair)
                for k, value in enumerate(main):
                    first = piece * sizes.main_lanes + k * LANES
                    target[device, :, first : first + LANES] = value[rows]
            if sizes.rest:
                target[device, :, sizes.rest_first :] = last


def side_by_side(values, rows, sizes):
    total = values[:rows]
    for piece in range(1, sizes.pieces):
        moved = pltpu.roll(values, piece * sizes.rest_lanes, 1)
        total = total + moved[piece * rows : (piece + 1) * rows]
    return total


def receive_modes(source, scratch, tall, sizes):
    group = lane_group(sizes)
    parts = source[...].reshape(sizes.nx, sizes.ny // 2, 2, sizes.pair, sizes.width)
    values = parts[:, 0]
    for y in range(1, sizes.ny // 2):
        values = values + parts[:, y]
    values = values.reshape(2 * sizes.nx, sizes.pair, sizes.width)
    for piece in range(sizes.pieces):
        rows = slice(piece * sizes.pair, (piece + 1) * sizes.pair)
        if sizes.main:
            first = piece * sizes.main_lanes
            tall[:, rows, : sizes.main_lanes] = values[:, :, first : first + sizes.main_lanes]
        if sizes.rest:
            last = values[:, :, sizes.rest_first :]
            if piece:
                last = pltpu.roll(last, sizes.rest_width - piece * sizes.rest_lanes, 2)
            tall[:, rows, sizes.main_lanes :] = last
    out = []
    for first in range(0, sizes.main_lanes, LANES):
        tiles = [tall[at, :, first : first + LANES] for at in range(2 * sizes.nx)]
        out += turn_groups(tiles, group, sizes)
    for r in range(sizes.rest):
        value = jnp.zeros((sizes.cells, LANES), F32)
        tile, have = divmod(r, sizes.groups)
        first = sizes.main_lanes + tile * LANES
        for at in range(2 * sizes.nx):
            value = put_group(value, tall[at, :, first : first + LANES], have, at, group, sizes)
        out.append(value)
    for w, value in enumerate(out):
        scratch[w * sizes.cells : (w + 1) * sizes.cells, :] = value
    return scratch[...]


def dot(left, right, contract=((1,), (0,))):
    return lax.dot_general(left, right, (contract, ((), ())), preferred_element_type=F32)


def halves(values):
    high = values.astype(BF16)
    return high, (values - high.astype(F32)).astype(BF16)


def fine_dot(left, right, contract=((1,), (0,))):
    left_high, left_low = halves(left)
    right_high, right_low = halves(right)
    small = dot(left_high, right_low, contract) + dot(left_low, right_high, contract)
    return dot(left_high, right_high, contract) + small


def fetch(sources, targets, semaphores):
    copies = [pltpu.make_async_copy(*pair, semaphores.at[at]) for at, pair in enumerate(zip(sources, targets))]
    for copy in copies:
        copy.start()
    for copy in copies:
        copy.wait()


def depth_forward(
    sizes, field, table, source, out, target,
    cells, field_here, table_here, out_here, here, semaphores, weight_semaphores,
):
    few = [
        pltpu.make_async_copy(field, field_here, semaphores.at[0]),
        pltpu.make_async_copy(table, table_here, semaphores.at[1]),
    ]
    for copy in few:
        copy.start()
    copies = start_weights(sizes, source, 1 - core_of(), here, weight_semaphores, 0, sizes.share)
    clear_weights(sizes, target)
    for copy in few:
        copy.wait()
    copies += start_weights(sizes, source, 1 - core_of(), here, weight_semaphores, sizes.share)
    values = gather_cells(field_here, cells, sizes).astype(BF16)
    send_modes(dot(values, table_here[...]), out_here, sizes)
    copy = pltpu.make_async_copy(out_here, out, semaphores.at[2])
    copy.start()
    turn_weights(sizes, copies, here, target)
    copy.wait()


def one_hot(rows, columns, step, along_rows):
    row = lax.broadcasted_iota(jnp.int32, (rows, columns), 0)
    column = lax.broadcasted_iota(jnp.int32, (rows, columns), 1)
    same = row // step == column if along_rows else row == column // step
    return jnp.where(same, 1.0, 0.0).astype(BF16)


def cell_mixer(weights, across, sizes):
    count = sizes.channels * sizes.cells
    left = one_hot(count, sizes.channels, sizes.cells, True)
    right = one_hot(sizes.channels, count, sizes.cells, False)
    tall = dot(left, weights, ((1,), (1 if across else 0,)))
    wide = dot(tall.astype(BF16), right)
    row = lax.broadcasted_iota(jnp.int32, (count, count), 0)
    column = lax.broadcasted_iota(jnp.int32, (count, count), 1)
    same = lax.rem(row, sizes.cells) == lax.rem(column, sizes.cells)
    return jnp.where(same, wide, 0.0).astype(BF16)


def emit(sizes, pre, signal, weight, inverse, layer_out, local, inverse_out, weight_here, semaphores):
    copies = [
        pltpu.make_async_copy(weight, weight_here, semaphores.at[0]),
        pltpu.make_async_copy(inverse, inverse_out, semaphores.at[1]),
    ]
    for copy in copies:
        copy.start()
    scatter_cells(gelu_parts(pre[...])[0], layer_out, sizes)
    copies[0].wait()
    local[...] = dot(cell_mixer(weight_here[...], False, sizes), signal[...])
    copies[1].wait()


def core_of():
    return lax.rem(lax.axis_index("gy"), 2)


def start_weights(sizes, source, half, here, semaphores, first=0, end=None):
    copies = []
    for at in range(2 * sizes.share)[first:end]:
        copies.append(pltpu.make_async_copy(source.at[2 * sizes.share * half + at], here.at[at], semaphores.at[at]))
        copies[-1].start()
    return copies


def clear_weights(sizes, target):
    if sizes.half > sizes.kept:
        target[...] = jnp.zeros_like(target)
    elif sizes.rows > sizes.channels:
        target[:, :, sizes.channels :, :] = jnp.zeros(
            (sizes.share, sizes.channels, sizes.rows - sizes.channels, 2 * sizes.half), F32
        )


def turn_weights(sizes, copies, here, target):
    for mode in range(sizes.share):
        for s in range(2):
            copies[2 * mode + s].wait()
        for w in range(sizes.channels):
            blocks = [here[2 * mode + s, w].reshape(sizes.kept, sizes.channels) for s in range(2)]
            if sizes.half == sizes.kept:
                target[mode, w, : sizes.channels, :] = jnp.concatenate(blocks, 0).T
            else:
                for s, block in enumerate(blocks):
                    target[mode, w, : sizes.channels, s * sizes.half : s * sizes.half + sizes.kept] = block.T


def prepare(
    sizes, source, after, tables, field, cotangent, weight, bias,
    target, table, local, cotangent_out,
    here, cells, field_here, cot_here, cot_cells, weight_here, bias_here, local_here, semaphores, small,
):
    del after
    place = lax.axis_index("gy")
    lanes = 2 * sizes.half
    moves = [(field, field_here), (cotangent, cot_here), (weight, weight_here), (bias, bias_here)]
    for s in range(2):
        for at, owner in enumerate((place, place + 1 - 2 * core_of())):
            moves.append(
                (tables.at[owner, :, pl.ds(s * lanes, lanes)], table.at[:, pl.ds((2 * s + at) * lanes, lanes)])
            )
    few = [pltpu.make_async_copy(*move, small.at[at]) for at, move in enumerate(moves)]
    for copy in few[:4]:
        copy.start()
    copies = start_weights(sizes, source, core_of(), here, semaphores)
    for copy in few[4:]:
        copy.start()
    clear_weights(sizes, target)
    for copy in few[:4]:
        copy.wait()
    values = gather_cells(field_here, cells, sizes).astype(BF16)
    spread = one_hot(sizes.channels * sizes.cells, sizes.channels, sizes.cells, True).astype(F32)
    offset = jnp.sum(spread * bias_here[...].reshape(1, sizes.channels), axis=1, keepdims=True)
    local_here[...] = dot(cell_mixer(weight_here[...], True, sizes), values) + offset
    gather_cells(cot_here, cot_cells, sizes)
    results = [
        pltpu.make_async_copy(local_here, local, small.at[0]),
        pltpu.make_async_copy(cot_cells, cotangent_out, small.at[1]),
    ]
    for copy in results:
        copy.start()
    turn_weights(sizes, copies, here, target)
    for copy in few[4:] + results:
        copy.wait()


def fetch_weights(sizes, source, after, target, semaphore):
    del after
    copy = pltpu.make_async_copy(source, target, semaphore.at[0])
    copy.start()
    copy.wait()


def plane_spectra(sizes, received, table, targets, flat):
    count = sizes.devices * sizes.pair
    for at in range(sizes.devices):
        for piece in range(sizes.pieces):
            rows = slice(piece * count + at * sizes.pair, piece * count + (at + 1) * sizes.pair)
            if sizes.main:
                first = piece * sizes.main_lanes
                flat[rows, : sizes.main_lanes] = received[at, :, first : first + sizes.main_lanes]
            if sizes.rest:
                flat[rows, sizes.main_lanes :] = received[at, :, sizes.rest_first :]
    if sizes.rest:
        for piece in range(1, sizes.pieces):
            rows = slice(piece * count, (piece + 1) * count)
            shift = sizes.rest_width - piece * sizes.rest_lanes
            flat[rows, sizes.main_lanes :] = pltpu.roll(flat[rows, sizes.main_lanes :], shift, 1)
    rows, lanes = targets[0].shape
    both = fine_dot(flat[...].T[:rows], table[...])
    total = both[:, : 2 * lanes] + pltpu.roll(both[:, 2 * lanes :], rows - sizes.share, 0)
    for at, target in enumerate(targets):
        target[...] = total[:, at * lanes : (at + 1) * lanes]


def plane_cells(sizes, spread, table, out):
    modes = jnp.concatenate([spread[at] for at in range(4)], 1)
    cells = fine_dot(table[...], modes, ((1,), (1,)))
    count = sizes.devices * sizes.pair
    if sizes.rest:
        last = side_by_side(cells[:, sizes.main_lanes :], count, sizes)
    for at in range(sizes.devices):
        rows = slice(at * sizes.pair, (at + 1) * sizes.pair)
        for piece in range(sizes.pieces):
            if sizes.main:
                first = piece * sizes.main_lanes
                out[at, :, first : first + sizes.main_lanes] = cells[
                    piece * count + at * sizes.pair : piece * count + (at + 1) * sizes.pair, : sizes.main_lanes
                ]
        if sizes.rest:
            out[at, :, sizes.rest_first :] = last[rows]


def swap_parts(values, sizes):
    return pltpu.roll(values, sizes.half, 1)


def mode_rows(first, sizes):
    return pl.ds(first, sizes.channels, stride=sizes.modes)


def put_mixed(spread, at, mode, values, sizes):
    for s in range(2):
        spread[2 * s + at, mode_rows(s * sizes.share + mode, sizes), :] = values


def first_lanes(rows, sizes):
    return lax.broadcasted_iota(jnp.int32, (rows, 2 * sizes.half), 1) < sizes.half


def mix_forward(
    sizes, received, table, weight, other_weight, local, cotangent, inverse, forward,
    spectra, other_spectra, out, local_out, cotangent_out, inverse_out, forward_out,
    spread, swapped, flat, semaphores,
):
    moves = ((local, local_out), (cotangent, cotangent_out), (inverse, inverse_out), (forward, forward_out))
    copies = [pltpu.make_async_copy(*move, semaphores.at[at]) for at, move in enumerate(moves)]
    for copy in copies:
        copy.start()
    plane_spectra(sizes, received, table, (spectra, other_spectra), flat)
    spread[...] = jnp.zeros_like(spread)
    real = first_lanes(sizes.rows, sizes)
    for at, (rows, block) in enumerate(((spectra, weight), (other_spectra, other_weight))):
        swapped[...] = swap_parts(rows[...], sizes)
        for m in range(sizes.share):
            straight = jnp.zeros((sizes.rows, 2 * sizes.half), F32)
            crossed = jnp.zeros((sizes.rows, 2 * sizes.half), F32)
            for w in range(sizes.channels):
                row = slice(w * sizes.modes + m, w * sizes.modes + m + 1)
                straight = straight + rows[row, :] * block[m, w]
                crossed = crossed + swapped[row, :] * block[m, w]
            real_part = straight - swap_parts(straight, sizes)
            imag_part = crossed + swap_parts(crossed, sizes)
            put_mixed(spread, at, m, jnp.where(real, real_part, imag_part)[: sizes.channels], sizes)
    plane_cells(sizes, spread, table, out)
    for copy in copies:
        copy.wait()


def sum_rows(blocks):
    row = lax.broadcasted_iota(jnp.int32, blocks[0].shape, 0)
    step = 4
    while step:
        low = row // step % 2 == 0
        count = len(blocks) // 2
        blocks = [
            jnp.where(low, one, pltpu.roll(two, step, 0)) + jnp.where(low, pltpu.roll(one, 8 - step, 0), two)
            for one, two in zip(blocks[:count], blocks[count:])
        ]
        step //= 2
    return blocks[0]


def column_sums(products, sizes):
    short = [sum(value[first : first + 8] for first in range(8, sizes.rows, 8)) + value[:8] for value in products]
    short += [jnp.zeros_like(short[0])] * (round_up(len(short), 8) - len(short))
    sums = [sum_rows(short[first : first + 8]) for first in range(0, len(short), 8)]
    return jnp.concatenate(sums, 0)[: sizes.channels]


def mix_back(sizes, received, table, weight, other_weight, back, other_back, out, spread, flat):
    plane_spectra(sizes, received, table, (back, other_back), flat)
    spread[...] = jnp.zeros_like(spread)
    real = first_lanes(sizes.channels, sizes)
    for at, (source, block) in enumerate(((back, weight), (other_back, other_weight))):
        for m in range(sizes.share):
            rows = source[mode_rows(m, sizes), :]
            if sizes.rows > sizes.channels:
                rows = jnp.concatenate([rows, jnp.zeros((sizes.rows - sizes.channels, 2 * sizes.half), F32)], 0)
            turned = swap_parts(rows, sizes)
            straight, crossed = [], []
            for w in range(sizes.channels):
                straight.append(block[m, w] * rows)
                crossed.append(block[m, w] * turned)
            straight = column_sums(straight, sizes)
            crossed = column_sums(crossed, sizes)
            real_part = straight + swap_parts(straight, sizes)
            imag_part = swap_parts(crossed, sizes) - crossed
            put_mixed(spread, at, m, jnp.where(real, real_part, imag_part), sizes)
    plane_cells(sizes, spread, table, out)


def grad_weights(
    sizes, spectra, back, given_spectra, given_back, target, here, straight, crossed, semaphores
):
    copies = []
    for which, (source, backward) in enumerate(((spectra, back), (given_spectra, given_back))):
        half = core_of() if which == 0 else 1 - core_of()
        values = source[...]
        turned = swap_parts(values, sizes)
        real = first_lanes(values.shape[0], sizes)
        straight[...] = jnp.where(real, values, turned)
        crossed[...] = jnp.where(real, turned, -values)
        for mode in range(sizes.share):
            rows = backward[mode_rows(mode, sizes), :]
            if sizes.rows > sizes.channels:
                rows = jnp.concatenate([rows, jnp.zeros((sizes.rows - sizes.channels, 2 * sizes.half), F32)], 0)
            turned = swap_parts(rows, sizes)
            local = 2 * (which * sizes.share + mode)
            for w in range(sizes.channels):
                at = slice(w * sizes.modes + mode, w * sizes.modes + mode + 1)
                block = (straight[at, :] * rows + crossed[at, :] * turned).T
                for s in range(2):
                    part = block[s * sizes.half : s * sizes.half + sizes.kept, : sizes.channels]
                    here[local + s, w] = part.reshape(sizes.local_x, sizes.kept_y, sizes.channels)
            for s in range(2):
                to = 2 * (half * sizes.share + mode) + s
                copies.append(pltpu.make_async_copy(here.at[local + s], target.at[to], semaphores.at[local + s]))
                copies[-1].start()
    for copy in copies:
        copy.wait()


def gelu_parts(pre):
    slope = math.sqrt(2.0 / math.pi)
    squared = pre * pre
    bend = jnp.tanh(slope * (pre + 0.044715 * (squared * pre)))
    value = 0.5 * pre * (1.0 + bend)
    derivative = 0.5 * (1.0 + bend) + 0.5 * pre * (1.0 - bend * bend) * (slope * (1.0 + 3.0 * 0.044715 * squared))
    return value, derivative


def activate(
    sizes, received, local, cotangent, inverse, forward, pre_out, signal_out, out, spectrum, tall
):
    pre = fine_dot(receive_modes(received, spectrum, tall, sizes), inverse[...]) + local[...]
    pre_out[...] = pre
    signal = (cotangent[...] * gelu_parts(pre)[1]).astype(BF16)
    signal_out[...] = signal
    send_modes(dot(signal, forward[...]), out, sizes)


def finish(sizes, received, local, inverse, grad_field, spectrum, tall):
    spatial = fine_dot(receive_modes(received, spectrum, tall, sizes), inverse[...])
    scatter_cells(spatial + local[...], grad_field, sizes)


def shape_of(shape, dtype=F32):
    return jax.ShapeDtypeStruct(shape, dtype)


VMEM = pl.BlockSpec(memory_space=pltpu.VMEM)
HELD = pl.BlockSpec(memory_space=pltpu.VMEM)
HBM = pl.BlockSpec(memory_space=pltpu.HBM)
ANYWHERE = pl.BlockSpec(memory_space=pl.ANY)


def settings(mebibytes):
    return pltpu.CompilerParams(vmem_limit_bytes=mebibytes * 1024 * 1024)


def cost(nanoseconds):
    return pl.CostEstimate(flops=0, bytes_accessed=3000 * nanoseconds, transcendentals=0)


def whole_call(body, sizes, nanoseconds, out_shape, scratch, *args, specs=None, out_specs=None, room=16):
    def kernel(*refs):
        body(sizes, *refs)

    if specs:
        spaces = [pltpu.HBM if spec is HBM else pltpu.VMEM if spec is HELD else None for spec in specs]
        args = [
            pltpu.with_memory_space_constraint(arg, space) if space else arg for arg, space in zip(args, spaces)
        ]
    return pl.pallas_call(
        kernel,
        out_shape=out_shape,
        in_specs=specs or [VMEM] * len(args),
        out_specs=out_specs or jax.tree.map(lambda _: VMEM, out_shape),
        scratch_shapes=scratch,
        name=body.__name__,
        cost_estimate=cost(nanoseconds),
        compiler_params=settings(room),
    )(*args)


def on_device(field, cotangent, spectral_weight, pointwise_weight, channel_bias):
    z = Sizes(field, spectral_weight)
    depth_table = depth_time_table(z.depth)
    modes = depth_table.shape[2]
    kappa = np.where(np.arange(modes) % KT == 0, 1.0, 2.0).astype(np.float32)
    shares = (z.nx, 2, z.share)
    ordered = depth_table.reshape((z.depth, 2) + shares).transpose(0, 2, 3, 1, 4).reshape(z.depth, z.all_modes)
    doubled = np.repeat(kappa.reshape(z.nx, 2, 1, z.share), 2, axis=2).reshape(z.all_modes)
    forward_first = jnp.asarray(ordered.astype(ml_dtypes.bfloat16))
    forward_back = jnp.asarray((ordered.astype(ml_dtypes.bfloat16).astype(np.float32) * doubled).astype(ml_dtypes.bfloat16))
    inverse_back = jnp.asarray(np.ascontiguousarray(ordered.T))
    inverse_first = jnp.asarray(np.ascontiguousarray((ordered * doubled).T))
    pairs = [(s, s ^ 1) for s in range(z.ny)]

    def exchange(payload):
        return lax.all_to_all(payload, ("gx", "gy"), split_axis=0, concat_axis=0, tiled=True)

    def other_core(values):
        return lax.ppermute(values, "gy", pairs)

    payload = shape_of((z.devices, z.pair, z.width))
    cell_rows = z.channels * z.cells
    cells_shape = (cell_rows, z.depth)
    cells_scratch = pltpu.VMEM(cells_shape, F32)
    spectrum_scratch = pltpu.VMEM((cell_rows, z.all_modes), F32)
    spectra_shape = (z.channels * z.modes, 2 * z.half)
    spectra_scratch = pltpu.VMEM(spectra_shape, F32)
    flat_scratch = pltpu.VMEM((z.devices * z.cells, z.spread_rows), F32)
    spread_scratch = pltpu.VMEM((4, z.spread_rows, 2 * z.half), F32)
    tall_scratch = pltpu.VMEM((2 * z.nx, z.cells, z.spread_rows), F32)
    field_scratch = pltpu.VMEM(field.shape, BF16)
    weight_here = pltpu.VMEM(pointwise_weight.shape, BF16)
    native = jnp.transpose(spectral_weight, (0, 1, 2, 4, 5, 3))
    weight_shape = (2 * z.modes,) + native.shape[2:]
    half_scratch = pltpu.VMEM((z.modes,) + native.shape[2:], F32)
    turned_shape = shape_of((z.share, z.channels, z.rows, 2 * z.half))

    def flags(count):
        return pltpu.SemaphoreType.DMA((count,))

    weights = native.reshape(weight_shape)
    sent, turned_away = whole_call(
        depth_forward, z, 1500, (payload, turned_shape),
        [
            cells_scratch, field_scratch, pltpu.VMEM(forward_first.shape, BF16), pltpu.VMEM(payload.shape, F32),
            half_scratch, flags(3), flags(z.modes),
        ],
        field, forward_first, weights, specs=[HBM] * 3, out_specs=(HBM, VMEM),
    )
    received = exchange(sent)
    other_turned = other_core(turned_away)
    turned, plane, local, cot_cells = whole_call(
        prepare, z, 100,
        (turned_shape, shape_of((z.devices * z.cells, 8 * z.half)), pltpu.HBM(cells_shape, F32), pltpu.HBM(cells_shape, F32)),
        [
            half_scratch, cells_scratch, field_scratch, field_scratch, cells_scratch, weight_here,
            pltpu.VMEM(channel_bias.shape, F32), cells_scratch, flags(z.modes), flags(8),
        ],
        weights, turned_away, jnp.asarray(plane_tables(z)), field, cotangent, pointwise_weight, channel_bias,
        specs=[HBM, ANYWHERE] + [HBM] * 5, out_specs=(VMEM, VMEM, HBM, HBM),
    )
    other_turned = whole_call(
        fetch_weights, z, 100, turned_shape, [flags(1)], other_turned, turned, specs=[HBM, ANYWHERE]
    )
    received, other_turned, turned, plane, local, cot_cells = lax.optimization_barrier(
        (received, other_turned, turned, plane, local, cot_cells)
    )
    spectra, other_spectra, sent, local, cot_cells, inverse_here, forward_here = whole_call(
        mix_forward, z, 1000,
        (
            shape_of(spectra_shape), shape_of(spectra_shape), payload, shape_of(cells_shape), shape_of(cells_shape),
            shape_of(inverse_first.shape), shape_of(forward_back.shape, BF16),
        ),
        [spread_scratch, spectra_scratch, flat_scratch, flags(4)],
        received, plane, turned, other_turned, local, cot_cells, inverse_first, forward_back,
        specs=[HELD] + [VMEM] * 3 + [HBM] * 4,
    )
    pre, signal, sent = whole_call(
        activate, z, 2000,
        (shape_of(cells_shape), shape_of(cells_shape, BF16), payload), [spectrum_scratch, tall_scratch],
        exchange(sent), local, cot_cells, inverse_here, forward_here,
    )
    back, other_back, sent = whole_call(
        mix_back, z, 1000, (shape_of(spectra_shape), shape_of(spectra_shape), payload),
        [spread_scratch, flat_scratch], exchange(sent), plane, turned, other_turned,
    )
    sent, spectra, other_spectra, back, other_back, pre, signal = lax.optimization_barrier(
        (sent, spectra, other_spectra, back, other_back, pre, signal)
    )
    returned = exchange(sent)
    given_spectra, given_back = other_core(other_spectra), other_core(other_back)
    layer_out, local, inverse_here = whole_call(
        emit, z, 1500,
        (shape_of(field.shape, BF16), shape_of(cells_shape), shape_of(inverse_back.shape)),
        [weight_here, flags(2)],
        pre, signal, pointwise_weight, inverse_back, specs=[VMEM, VMEM, HBM, HBM],
    )
    gradient = whole_call(
        grad_weights, z, 5000, shape_of(weight_shape),
        [pltpu.VMEM(weight_shape, F32), spectra_scratch, spectra_scratch, flags(2 * z.modes)],
        spectra, back, given_spectra, given_back, out_specs=HBM, room=28,
    )
    returned, gradient, layer_out, local, inverse_here = lax.optimization_barrier(
        (returned, gradient, layer_out, local, inverse_here)
    )
    grad_field = whole_call(
        finish, z, 1000, shape_of(field.shape, BF16), [spectrum_scratch, tall_scratch], returned, local, inverse_here
    )
    return (layer_out, grad_field, jnp.transpose(gradient.reshape(native.shape), (0, 1, 2, 5, 3, 4)))


def solution(mesh):
    return jax.shard_map(
        on_device,
        mesh=mesh,
        in_specs=(
            P(None, "gx", "gy", None),
            P(None, "gx", "gy", None),
            P("gx", None, None, None, "gy", None),
            P(),
            P(),
        ),
        out_specs=(
            P(None, "gx", "gy", None),
            P(None, "gx", "gy", None),
            P("gx", None, None, None, "gy", None),
        ),
        check_vma=False,
    )
```

```python
import math

import jax
import jax.numpy as jnp
import ml_dtypes
import numpy as np
from jax import lax
from jax.experimental import pallas as pl
from jax.experimental.pallas import tpu as pltpu
from jax.sharding import PartitionSpec as P

KZ = 16
KT = 4
NT = 16
LANES = 128
F32 = jnp.float32
BF16 = jnp.bfloat16


def round_up(value, step):
    return -(-value // step) * step


def frequencies(kept):
    index = np.arange(kept)
    return np.where(index < kept // 2, index, index - kept)


def depth_time_table(cells):
    depth_cells = cells // NT
    depth = np.arange(depth_cells)[:, None, None, None] * frequencies(KZ)[None, None, :, None] * NT
    time = np.arange(NT)[None, :, None, None] * np.arange(KT)[None, None, None, :] * depth_cells
    phase = np.mod(depth + time, cells).reshape(cells, KZ * KT)
    angles = phase.astype(np.float32) * np.float32(2.0 * math.pi / cells)
    factor = np.float32(1.0 / math.sqrt(cells))
    return np.stack([np.cos(angles) * factor, -np.sin(angles) * factor], axis=1).astype(np.float32)


def plane_tables(sizes):
    length_x, length_y = sizes.nx * sizes.cells_x, sizes.ny * sizes.cells_y
    phase_x = np.mod(np.arange(length_x)[:, None] * frequencies(sizes.kept_x), length_x) / length_x
    phase_y = np.mod(np.arange(length_y)[:, None] * frequencies(sizes.kept_y), length_y) / length_y
    angle = 2.0 * math.pi * (phase_x[:, None, :, None] + phase_y[None, :, None, :])
    scale = 1.0 / math.sqrt(length_x * length_y)
    cosine, sine = np.cos(angle) * scale, np.sin(angle) * scale
    parts = np.stack([np.stack([cosine, -sine]), np.stack([sine, cosine])])
    pairs = sizes.cells_y // sizes.pair
    parts = parts.reshape(
        2, 2, sizes.nx, sizes.cells_x, sizes.ny, pairs, sizes.pair, sizes.ny, sizes.kept
    ).transpose(7, 3, 5, 2, 4, 6, 0, 1, 8)
    padded = np.zeros(parts.shape[:-1] + (sizes.half,), np.float32)
    padded[..., : sizes.kept] = parts
    return padded.reshape(sizes.ny, sizes.devices * sizes.cells, 4 * sizes.half)


class Sizes:
    def __init__(self, field, weight):
        self.nx, self.ny = lax.axis_size("gx"), lax.axis_size("gy")
        self.channels, self.cells_x, self.cells_y, self.depth = field.shape
        self.modes = weight.shape[0]
        self.local_x, self.kept_y = weight.shape[4:]
        self.kept_x = self.local_x * self.ny
        self.cells = self.cells_x * self.cells_y
        self.devices = self.nx * self.ny
        self.share = self.modes // 2
        self.kept = self.local_x * self.kept_y
        self.half = round_up(self.kept, LANES // 2)
        self.all_modes = 2 * self.modes * self.nx
        self.groups = LANES // self.modes
        self.main = self.channels // self.groups * self.groups if self.all_modes == LANES else 0
        self.rest = self.channels - self.main
        self.main_lanes = self.main * self.modes
        self.rest_lanes = self.rest * self.modes
        self.rest_tiles = round_up(self.rest_lanes, LANES) // LANES
        self.pair = math.gcd(self.cells_y, 2)
        self.pieces = self.cells // self.pair
        self.rest_first = self.pieces * self.main_lanes
        self.rest_width = round_up(self.pieces * self.rest_lanes, LANES)
        self.width = self.rest_first + self.rest_width
        self.spread_rows = self.main_lanes + self.rest_width
        self.rows = round_up(self.channels, 8)


def gather_cells(source, scratch, sizes):
    for w in range(sizes.channels):
        for x in range(sizes.cells_x):
            first = (w * sizes.cells_x + x) * sizes.cells_y
            scratch[first : first + sizes.cells_y, :] = source[w, x].astype(F32)
    return scratch[...]


def scatter_cells(values, target, sizes):
    for w in range(sizes.channels):
        for x in range(sizes.cells_x):
            first = (w * sizes.cells_x + x) * sizes.cells_y
            target[w, x] = values[first : first + sizes.cells_y, :].astype(target.dtype)


def lane_group(sizes):
    return lax.broadcasted_iota(jnp.int32, (sizes.cells, LANES), 1) // sizes.modes


def turn_groups(tiles, group, sizes):
    tiles = list(tiles)
    step = 1
    while step < sizes.groups:
        low = group // step % 2 == 0
        for first in range(sizes.groups):
            if first // step % 2 == 0:
                one, two = tiles[first], tiles[first + step]
                tiles[first] = jnp.where(low, one, pltpu.roll(two, step * sizes.modes, 1))
                tiles[first + step] = jnp.where(low, pltpu.roll(one, LANES - step * sizes.modes, 1), two)
        step *= 2
    return tiles


def put_group(target, source, have, want, group, sizes):
    if have != want:
        source = pltpu.roll(source, (want - have) % sizes.groups * sizes.modes, 1)
    return jnp.where(group == want, source, target)


def send_modes(values, target, sizes):
    group = lane_group(sizes)
    tiles = [values[w * sizes.cells : (w + 1) * sizes.cells, :] for w in range(sizes.channels)]
    turned = []
    for first in range(0, sizes.main, sizes.groups):
        turned.append(turn_groups(tiles[first : first + sizes.groups], group, sizes))
    for at in range(2 * sizes.nx):
        main = [block[at] for block in turned]
        last = [jnp.zeros((sizes.cells, LANES), F32) for _ in range(sizes.rest_width // LANES)]
        for r in range(sizes.rest):
            tile, want = divmod(r, sizes.groups)
            last[tile] = put_group(last[tile], tiles[sizes.main + r], at, want, group, sizes)
        if last:
            last = side_by_side(jnp.concatenate(last, 1), sizes.pair, sizes)
        for y in range(sizes.ny // 2):
            device = at // 2 * sizes.ny + 2 * y + at % 2
            for piece in range(sizes.pieces):
                rows = slice(piece * sizes.pair, (piece + 1) * sizes.pair)
                for k, value in enumerate(main):
                    first = piece * sizes.main_lanes + k * LANES
                    target[device, :, first : first + LANES] = value[rows]
            if sizes.rest:
                target[device, :, sizes.rest_first :] = last


def side_by_side(values, rows, sizes):
    total = values[:rows]
    for piece in range(1, sizes.pieces):
        moved = pltpu.roll(values, piece * sizes.rest_lanes, 1)
        total = total + moved[piece * rows : (piece + 1) * rows]
    return total


def receive_modes(source, scratch, tall, sizes):
    group = lane_group(sizes)
    parts = source[...].reshape(sizes.nx, sizes.ny // 2, 2, sizes.pair, sizes.width)
    values = parts[:, 0]
    for y in range(1, sizes.ny // 2):
        values = values + parts[:, y]
    values = values.reshape(2 * sizes.nx, sizes.pair, sizes.width)
    for piece in range(sizes.pieces):
        rows = slice(piece * sizes.pair, (piece + 1) * sizes.pair)
        if sizes.main:
            first = piece * sizes.main_lanes
            tall[:, rows, : sizes.main_lanes] = values[:, :, first : first + sizes.main_lanes]
        if sizes.rest:
            last = values[:, :, sizes.rest_first :]
            if piece:
                last = pltpu.roll(last, sizes.rest_width - piece * sizes.rest_lanes, 2)
            tall[:, rows, sizes.main_lanes :] = last
    out = []
    for first in range(0, sizes.main_lanes, LANES):
        tiles = [tall[at, :, first : first + LANES] for at in range(2 * sizes.nx)]
        out += turn_groups(tiles, group, sizes)
    for r in range(sizes.rest):
        value = jnp.zeros((sizes.cells, LANES), F32)
        tile, have = divmod(r, sizes.groups)
        first = sizes.main_lanes + tile * LANES
        for at in range(2 * sizes.nx):
            value = put_group(value, tall[at, :, first : first + LANES], have, at, group, sizes)
        out.append(value)
    for w, value in enumerate(out):
        scratch[w * sizes.cells : (w + 1) * sizes.cells, :] = value
    return scratch[...]


def dot(left, right, contract=((1,), (0,))):
    return lax.dot_general(left, right, (contract, ((), ())), preferred_element_type=F32)


def halves(values):
    high = values.astype(BF16)
    return high, (values - high.astype(F32)).astype(BF16)


def fine_dot(left, right, contract=((1,), (0,))):
    left_high, left_low = halves(left)
    right_high, right_low = halves(right)
    small = dot(left_high, right_low, contract) + dot(left_low, right_high, contract)
    return dot(left_high, right_high, contract) + small


def fetch(sources, targets, semaphores):
    copies = [pltpu.make_async_copy(*pair, semaphores.at[at]) for at, pair in enumerate(zip(sources, targets))]
    for copy in copies:
        copy.start()
    for copy in copies:
        copy.wait()


def depth_forward(
    sizes, field, table, source, out, target,
    cells, field_here, table_here, out_here, here, semaphores, weight_semaphores,
):
    few = [
        pltpu.make_async_copy(field, field_here, semaphores.at[0]),
        pltpu.make_async_copy(table, table_here, semaphores.at[1]),
    ]
    for copy in few:
        copy.start()
    copies = start_weights(sizes, source, 1 - core_of(), here, weight_semaphores, 0, sizes.share + 1)
    clear_weights(sizes, target)
    for copy in few:
        copy.wait()
    copies += start_weights(sizes, source, 1 - core_of(), here, weight_semaphores, sizes.share + 1)
    values = gather_cells(field_here, cells, sizes).astype(BF16)
    send_modes(dot(values, table_here[...]), out_here, sizes)
    copy = pltpu.make_async_copy(out_here, out, semaphores.at[2])
    copy.start()
    turn_weights(sizes, copies, here, target)
    copy.wait()


def one_hot(rows, columns, step, along_rows):
    row = lax.broadcasted_iota(jnp.int32, (rows, columns), 0)
    column = lax.broadcasted_iota(jnp.int32, (rows, columns), 1)
    same = row // step == column if along_rows else row == column // step
    return jnp.where(same, 1.0, 0.0).astype(BF16)


def cell_mixer(weights, across, sizes):
    count = sizes.channels * sizes.cells
    left = one_hot(count, sizes.channels, sizes.cells, True)
    right = one_hot(sizes.channels, count, sizes.cells, False)
    tall = dot(left, weights, ((1,), (1 if across else 0,)))
    wide = dot(tall.astype(BF16), right)
    row = lax.broadcasted_iota(jnp.int32, (count, count), 0)
    column = lax.broadcasted_iota(jnp.int32, (count, count), 1)
    same = lax.rem(row, sizes.cells) == lax.rem(column, sizes.cells)
    return jnp.where(same, wide, 0.0).astype(BF16)


def emit(sizes, pre, signal, weight, inverse, layer_out, local, inverse_out, weight_here, semaphores):
    copies = [
        pltpu.make_async_copy(weight, weight_here, semaphores.at[0]),
        pltpu.make_async_copy(inverse, inverse_out, semaphores.at[1]),
    ]
    for copy in copies:
        copy.start()
    scatter_cells(gelu_parts(pre[...])[0], layer_out, sizes)
    copies[0].wait()
    local[...] = dot(cell_mixer(weight_here[...], False, sizes), signal[...])
    copies[1].wait()


def core_of():
    return lax.rem(lax.axis_index("gy"), 2)


def start_weights(sizes, source, half, here, semaphores, first=0, end=None):
    copies = []
    for at in range(2 * sizes.share)[first:end]:
        copies.append(pltpu.make_async_copy(source.at[2 * sizes.share * half + at], here.at[at], semaphores.at[at]))
        copies[-1].start()
    return copies


def clear_weights(sizes, target):
    if sizes.half > sizes.kept:
        target[...] = jnp.zeros_like(target)
    elif sizes.rows > sizes.channels:
        target[:, :, sizes.channels :, :] = jnp.zeros(
            (sizes.share, sizes.channels, sizes.rows - sizes.channels, 2 * sizes.half), F32
        )


def turn_weights(sizes, copies, here, target):
    for mode in range(sizes.share):
        for s in range(2):
            copies[2 * mode + s].wait()
        for w in range(sizes.channels):
            blocks = [here[2 * mode + s, w].reshape(sizes.kept, sizes.channels) for s in range(2)]
            if sizes.half == sizes.kept:
                target[mode, w, : sizes.channels, :] = jnp.concatenate(blocks, 0).T
            else:
                for s, block in enumerate(blocks):
                    target[mode, w, : sizes.channels, s * sizes.half : s * sizes.half + sizes.kept] = block.T


def prepare(
    sizes, source, after, tables, field, cotangent, weight, bias,
    target, table, local, cotangent_out,
    here, cells, field_here, cot_here, cot_cells, weight_here, bias_here, local_here, semaphores, small,
):
    del after
    place = lax.axis_index("gy")
    lanes = 2 * sizes.half
    moves = [(field, field_here), (cotangent, cot_here), (weight, weight_here), (bias, bias_here)]
    for s in range(2):
        for at, owner in enumerate((place, place + 1 - 2 * core_of())):
            moves.append(
                (tables.at[owner, :, pl.ds(s * lanes, lanes)], table.at[:, pl.ds((2 * s + at) * lanes, lanes)])
            )
    few = [pltpu.make_async_copy(*move, small.at[at]) for at, move in enumerate(moves)]
    for copy in few[:4]:
        copy.start()
    copies = start_weights(sizes, source, core_of(), here, semaphores)
    for copy in few[4:]:
        copy.start()
    clear_weights(sizes, target)
    for copy in few[:4]:
        copy.wait()
    values = gather_cells(field_here, cells, sizes).astype(BF16)
    spread = one_hot(sizes.channels * sizes.cells, sizes.channels, sizes.cells, True).astype(F32)
    offset = jnp.sum(spread * bias_here[...].reshape(1, sizes.channels), axis=1, keepdims=True)
    local_here[...] = dot(cell_mixer(weight_here[...], True, sizes), values) + offset
    gather_cells(cot_here, cot_cells, sizes)
    results = [
        pltpu.make_async_copy(local_here, local, small.at[0]),
        pltpu.make_async_copy(cot_cells, cotangent_out, small.at[1]),
    ]
    for copy in results:
        copy.start()
    turn_weights(sizes, copies, here, target)
    for copy in few[4:] + results:
        copy.wait()


def fetch_weights(sizes, source, after, target, semaphore):
    del after
    copy = pltpu.make_async_copy(source, target, semaphore.at[0])
    copy.start()
    copy.wait()


def plane_spectra(sizes, received, table, targets, flat):
    count = sizes.devices * sizes.pair
    for at in range(sizes.devices):
        for piece in range(sizes.pieces):
            rows = slice(piece * count + at * sizes.pair, piece * count + (at + 1) * sizes.pair)
            if sizes.main:
                first = piece * sizes.main_lanes
                flat[rows, : sizes.main_lanes] = received[at, :, first : first + sizes.main_lanes]
            if sizes.rest:
                flat[rows, sizes.main_lanes :] = received[at, :, sizes.rest_first :]
    if sizes.rest:
        for piece in range(1, sizes.pieces):
            rows = slice(piece * count, (piece + 1) * count)
            shift = sizes.rest_width - piece * sizes.rest_lanes
            flat[rows, sizes.main_lanes :] = pltpu.roll(flat[rows, sizes.main_lanes :], shift, 1)
    rows, lanes = targets[0].shape
    both = fine_dot(flat[...].T[:rows], table[...])
    total = both[:, : 2 * lanes] + pltpu.roll(both[:, 2 * lanes :], rows - sizes.share, 0)
    for at, target in enumerate(targets):
        target[...] = total[:, at * lanes : (at + 1) * lanes]


def plane_cells(sizes, spread, table, out):
    modes = jnp.concatenate([spread[at] for at in range(4)], 1)
    cells = fine_dot(table[...], modes, ((1,), (1,)))
    count = sizes.devices * sizes.pair
    if sizes.rest:
        last = side_by_side(cells[:, sizes.main_lanes :], count, sizes)
    for at in range(sizes.devices):
        rows = slice(at * sizes.pair, (at + 1) * sizes.pair)
        for piece in range(sizes.pieces):
            if sizes.main:
                first = piece * sizes.main_lanes
                out[at, :, first : first + sizes.main_lanes] = cells[
                    piece * count + at * sizes.pair : piece * count + (at + 1) * sizes.pair, : sizes.main_lanes
                ]
        if sizes.rest:
            out[at, :, sizes.rest_first :] = last[rows]


def swap_parts(values, sizes):
    return pltpu.roll(values, sizes.half, 1)


def mode_rows(first, sizes):
    return pl.ds(first, sizes.channels, stride=sizes.modes)


def put_mixed(spread, at, mode, values, sizes):
    for s in range(2):
        spread[2 * s + at, mode_rows(s * sizes.share + mode, sizes), :] = values


def first_lanes(rows, sizes):
    return lax.broadcasted_iota(jnp.int32, (rows, 2 * sizes.half), 1) < sizes.half


def mix_forward(
    sizes, received, table, weight, other_weight, local, cotangent, inverse, forward,
    spectra, other_spectra, out, local_out, cotangent_out, inverse_out, forward_out,
    spread, swapped, flat, semaphores,
):
    moves = ((local, local_out), (cotangent, cotangent_out), (inverse, inverse_out), (forward, forward_out))
    copies = [pltpu.make_async_copy(*move, semaphores.at[at]) for at, move in enumerate(moves)]
    for copy in copies:
        copy.start()
    plane_spectra(sizes, received, table, (spectra, other_spectra), flat)
    spread[...] = jnp.zeros_like(spread)
    real = first_lanes(sizes.rows, sizes)
    for at, (rows, block) in enumerate(((spectra, weight), (other_spectra, other_weight))):
        swapped[...] = swap_parts(rows[...], sizes)
        for m in range(sizes.share):
            straight = jnp.zeros((sizes.rows, 2 * sizes.half), F32)
            crossed = jnp.zeros((sizes.rows, 2 * sizes.half), F32)
            for w in range(sizes.channels):
                row = slice(w * sizes.modes + m, w * sizes.modes + m + 1)
                straight = straight + rows[row, :] * block[m, w]
                crossed = crossed + swapped[row, :] * block[m, w]
            real_part = straight - swap_parts(straight, sizes)
            imag_part = crossed + swap_parts(crossed, sizes)
            put_mixed(spread, at, m, jnp.where(real, real_part, imag_part)[: sizes.channels], sizes)
    plane_cells(sizes, spread, table, out)
    for copy in copies:
        copy.wait()


def sum_rows(blocks):
    row = lax.broadcasted_iota(jnp.int32, blocks[0].shape, 0)
    step = 4
    while step:
        low = row // step % 2 == 0
        count = len(blocks) // 2
        blocks = [
            jnp.where(low, one, pltpu.roll(two, step, 0)) + jnp.where(low, pltpu.roll(one, 8 - step, 0), two)
            for one, two in zip(blocks[:count], blocks[count:])
        ]
        step //= 2
    return blocks[0]


def column_sums(products, sizes):
    short = [sum(value[first : first + 8] for first in range(8, sizes.rows, 8)) + value[:8] for value in products]
    short += [jnp.zeros_like(short[0])] * (round_up(len(short), 8) - len(short))
    sums = [sum_rows(short[first : first + 8]) for first in range(0, len(short), 8)]
    return jnp.concatenate(sums, 0)[: sizes.channels]


def mix_back(sizes, received, table, weight, other_weight, back, other_back, out, spread, flat):
    plane_spectra(sizes, received, table, (back, other_back), flat)
    spread[...] = jnp.zeros_like(spread)
    real = first_lanes(sizes.channels, sizes)
    for at, (source, block) in enumerate(((back, weight), (other_back, other_weight))):
        for m in range(sizes.share):
            rows = source[mode_rows(m, sizes), :]
            if sizes.rows > sizes.channels:
                rows = jnp.concatenate([rows, jnp.zeros((sizes.rows - sizes.channels, 2 * sizes.half), F32)], 0)
            turned = swap_parts(rows, sizes)
            straight, crossed = [], []
            for w in range(sizes.channels):
                straight.append(block[m, w] * rows)
                crossed.append(block[m, w] * turned)
            straight = column_sums(straight, sizes)
            crossed = column_sums(crossed, sizes)
            real_part = straight + swap_parts(straight, sizes)
            imag_part = swap_parts(crossed, sizes) - crossed
            put_mixed(spread, at, m, jnp.where(real, real_part, imag_part), sizes)
    plane_cells(sizes, spread, table, out)


def grad_weights(
    sizes, spectra, back, given_spectra, given_back, target, here, straight, crossed, semaphores
):
    copies = []
    for which, (source, backward) in enumerate(((spectra, back), (given_spectra, given_back))):
        half = core_of() if which == 0 else 1 - core_of()
        values = source[...]
        turned = swap_parts(values, sizes)
        real = first_lanes(values.shape[0], sizes)
        straight[...] = jnp.where(real, values, turned)
        crossed[...] = jnp.where(real, turned, -values)
        for mode in range(sizes.share):
            rows = backward[mode_rows(mode, sizes), :]
            if sizes.rows > sizes.channels:
                rows = jnp.concatenate([rows, jnp.zeros((sizes.rows - sizes.channels, 2 * sizes.half), F32)], 0)
            turned = swap_parts(rows, sizes)
            local = 2 * (which * sizes.share + mode)
            for w in range(sizes.channels):
                at = slice(w * sizes.modes + mode, w * sizes.modes + mode + 1)
                block = (straight[at, :] * rows + crossed[at, :] * turned).T
                for s in range(2):
                    part = block[s * sizes.half : s * sizes.half + sizes.kept, : sizes.channels]
                    here[local + s, w] = part.reshape(sizes.local_x, sizes.kept_y, sizes.channels)
            for s in range(2):
                to = 2 * (half * sizes.share + mode) + s
                copies.append(pltpu.make_async_copy(here.at[local + s], target.at[to], semaphores.at[local + s]))
                copies[-1].start()
    for copy in copies:
        copy.wait()


def gelu_parts(pre):
    slope = math.sqrt(2.0 / math.pi)
    squared = pre * pre
    bend = jnp.tanh(slope * (pre + 0.044715 * (squared * pre)))
    value = 0.5 * pre * (1.0 + bend)
    derivative = 0.5 * (1.0 + bend) + 0.5 * pre * (1.0 - bend * bend) * (slope * (1.0 + 3.0 * 0.044715 * squared))
    return value, derivative


def activate(
    sizes, received, local, cotangent, inverse, forward, pre_out, signal_out, out, spectrum, tall
):
    pre = fine_dot(receive_modes(received, spectrum, tall, sizes), inverse[...]) + local[...]
    pre_out[...] = pre
    signal = (cotangent[...] * gelu_parts(pre)[1]).astype(BF16)
    signal_out[...] = signal
    send_modes(dot(signal, forward[...]), out, sizes)


def finish(sizes, received, local, inverse, grad_field, spectrum, tall):
    spatial = fine_dot(receive_modes(received, spectrum, tall, sizes), inverse[...])
    scatter_cells(spatial + local[...], grad_field, sizes)


def shape_of(shape, dtype=F32):
    return jax.ShapeDtypeStruct(shape, dtype)


VMEM = pl.BlockSpec(memory_space=pltpu.VMEM)
HELD = pl.BlockSpec(memory_space=pltpu.VMEM)
HBM = pl.BlockSpec(memory_space=pltpu.HBM)
ANYWHERE = pl.BlockSpec(memory_space=pl.ANY)


def settings(mebibytes):
    return pltpu.CompilerParams(vmem_limit_bytes=mebibytes * 1024 * 1024)


def cost(nanoseconds):
    return pl.CostEstimate(flops=0, bytes_accessed=3000 * nanoseconds, transcendentals=0)


def whole_call(body, sizes, nanoseconds, out_shape, scratch, *args, specs=None, out_specs=None, room=16):
    def kernel(*refs):
        body(sizes, *refs)

    if specs:
        spaces = [pltpu.HBM if spec is HBM else pltpu.VMEM if spec is HELD else None for spec in specs]
        args = [
            pltpu.with_memory_space_constraint(arg, space) if space else arg for arg, space in zip(args, spaces)
        ]
    return pl.pallas_call(
        kernel,
        out_shape=out_shape,
        in_specs=specs or [VMEM] * len(args),
        out_specs=out_specs or jax.tree.map(lambda _: VMEM, out_shape),
        scratch_shapes=scratch,
        name=body.__name__,
        cost_estimate=cost(nanoseconds),
        compiler_params=settings(room),
    )(*args)


def on_device(field, cotangent, spectral_weight, pointwise_weight, channel_bias):
    z = Sizes(field, spectral_weight)
    depth_table = depth_time_table(z.depth)
    modes = depth_table.shape[2]
    kappa = np.where(np.arange(modes) % KT == 0, 1.0, 2.0).astype(np.float32)
    shares = (z.nx, 2, z.share)
    ordered = depth_table.reshape((z.depth, 2) + shares).transpose(0, 2, 3, 1, 4).reshape(z.depth, z.all_modes)
    doubled = np.repeat(kappa.reshape(z.nx, 2, 1, z.share), 2, axis=2).reshape(z.all_modes)
    forward_first = jnp.asarray(ordered.astype(ml_dtypes.bfloat16))
    forward_back = jnp.asarray((ordered.astype(ml_dtypes.bfloat16).astype(np.float32) * doubled).astype(ml_dtypes.bfloat16))
    inverse_back = jnp.asarray(np.ascontiguousarray(ordered.T))
    inverse_first = jnp.asarray(np.ascontiguousarray((ordered * doubled).T))
    pairs = [(s, s ^ 1) for s in range(z.ny)]

    def exchange(payload):
        return lax.all_to_all(payload, ("gx", "gy"), split_axis=0, concat_axis=0, tiled=True)

    def other_core(values):
        return lax.ppermute(values, "gy", pairs)

    payload = shape_of((z.devices, z.pair, z.width))
    cell_rows = z.channels * z.cells
    cells_shape = (cell_rows, z.depth)
    cells_scratch = pltpu.VMEM(cells_shape, F32)
    spectrum_scratch = pltpu.VMEM((cell_rows, z.all_modes), F32)
    spectra_shape = (z.channels * z.modes, 2 * z.half)
    spectra_scratch = pltpu.VMEM(spectra_shape, F32)
    flat_scratch = pltpu.VMEM((z.devices * z.cells, z.spread_rows), F32)
    spread_scratch = pltpu.VMEM((4, z.spread_rows, 2 * z.half), F32)
    tall_scratch = pltpu.VMEM((2 * z.nx, z.cells, z.spread_rows), F32)
    field_scratch = pltpu.VMEM(field.shape, BF16)
    weight_here = pltpu.VMEM(pointwise_weight.shape, BF16)
    native = jnp.transpose(spectral_weight, (0, 1, 2, 4, 5, 3))
    weight_shape = (2 * z.modes,) + native.shape[2:]
    half_scratch = pltpu.VMEM((z.modes,) + native.shape[2:], F32)
    turned_shape = shape_of((z.share, z.channels, z.rows, 2 * z.half))

    def flags(count):
        return pltpu.SemaphoreType.DMA((count,))

    weights = native.reshape(weight_shape)
    sent, turned_away = whole_call(
        depth_forward, z, 1500, (payload, turned_shape),
        [
            cells_scratch, field_scratch, pltpu.VMEM(forward_first.shape, BF16), pltpu.VMEM(payload.shape, F32),
            half_scratch, flags(3), flags(z.modes),
        ],
        field, forward_first, weights, specs=[HBM] * 3, out_specs=(HBM, VMEM),
    )
    received = exchange(sent)
    other_turned = other_core(turned_away)
    turned, plane, local, cot_cells = whole_call(
        prepare, z, 100,
        (turned_shape, shape_of((z.devices * z.cells, 8 * z.half)), pltpu.HBM(cells_shape, F32), pltpu.HBM(cells_shape, F32)),
        [
            half_scratch, cells_scratch, field_scratch, field_scratch, cells_scratch, weight_here,
            pltpu.VMEM(channel_bias.shape, F32), cells_scratch, flags(z.modes), flags(8),
        ],
        weights, turned_away, jnp.asarray(plane_tables(z)), field, cotangent, pointwise_weight, channel_bias,
        specs=[HBM, ANYWHERE] + [HBM] * 5, out_specs=(VMEM, VMEM, HBM, HBM),
    )
    other_turned = whole_call(
        fetch_weights, z, 100, turned_shape, [flags(1)], other_turned, turned, specs=[HBM, ANYWHERE]
    )
    received, other_turned, turned, plane, local, cot_cells = lax.optimization_barrier(
        (received, other_turned, turned, plane, local, cot_cells)
    )
    spectra, other_spectra, sent, local, cot_cells, inverse_here, forward_here = whole_call(
        mix_forward, z, 1000,
        (
            shape_of(spectra_shape), shape_of(spectra_shape), payload, shape_of(cells_shape), shape_of(cells_shape),
            shape_of(inverse_first.shape), shape_of(forward_back.shape, BF16),
        ),
        [spread_scratch, spectra_scratch, flat_scratch, flags(4)],
        received, plane, turned, other_turned, local, cot_cells, inverse_first, forward_back,
        specs=[HELD] + [VMEM] * 3 + [HBM] * 4,
    )
    pre, signal, sent = whole_call(
        activate, z, 2000,
        (shape_of(cells_shape), shape_of(cells_shape, BF16), payload), [spectrum_scratch, tall_scratch],
        exchange(sent), local, cot_cells, inverse_here, forward_here,
    )
    back, other_back, sent = whole_call(
        mix_back, z, 1000, (shape_of(spectra_shape), shape_of(spectra_shape), payload),
        [spread_scratch, flat_scratch], exchange(sent), plane, turned, other_turned,
    )
    sent, spectra, other_spectra, back, other_back, pre, signal = lax.optimization_barrier(
        (sent, spectra, other_spectra, back, other_back, pre, signal)
    )
    returned = exchange(sent)
    given_spectra, given_back = other_core(other_spectra), other_core(other_back)
    layer_out, local, inverse_here = whole_call(
        emit, z, 1500,
        (shape_of(field.shape, BF16), shape_of(cells_shape), shape_of(inverse_back.shape)),
        [weight_here, flags(2)],
        pre, signal, pointwise_weight, inverse_back, specs=[VMEM, VMEM, HBM, HBM],
    )
    gradient = whole_call(
        grad_weights, z, 5000, shape_of(weight_shape),
        [pltpu.VMEM(weight_shape, F32), spectra_scratch, spectra_scratch, flags(2 * z.modes)],
        spectra, back, given_spectra, given_back, out_specs=HBM, room=28,
    )
    returned, gradient, layer_out, local, inverse_here = lax.optimization_barrier(
        (returned, gradient, layer_out, local, inverse_here)
    )
    grad_field = whole_call(
        finish, z, 1000, shape_of(field.shape, BF16), [spectrum_scratch, tall_scratch], returned, local, inverse_here
    )
    return (layer_out, grad_field, jnp.transpose(gradient.reshape(native.shape), (0, 1, 2, 5, 3, 4)))


def solution(mesh):
    return jax.shard_map(
        on_device,
        mesh=mesh,
        in_specs=(
            P(None, "gx", "gy", None),
            P(None, "gx", "gy", None),
            P("gx", None, None, None, "gy", None),
            P(),
            P(),
        ),
        out_specs=(
            P(None, "gx", "gy", None),
            P(None, "gx", "gy", None),
            P("gx", None, None, None, "gy", None),
        ),
        check_vma=False,
    )
```
